32 devices in a mesh: gx: 8 (over y, x, core), gy: 4 (over z).
Axes of the slice: x: 2, y: 2, z: 4, core: 2. Of those that a mesh axis runs over, the one named last changes fastest.
Arguments:
- particles: bfloat16 [4096, 128], P(('gx', 'gy')), may hold values from -6 to 6
- send_counts: int32 [32, 32], P(('gx', 'gy')), may hold values from 0 to 8, as said below
- cell_lists: int32 [32, 256], P(('gx', 'gy')), may hold values from 0 to 4095
- base_field: bfloat16 [64, 8, 64, 256], P(None, 'gx', 'gy'), may hold values from -6 to 6
- proj_weight: bfloat16 [128, 64], replicated, may hold values from -0.5 to 0.5
- conv_weight: bfloat16 [27, 64, 64], replicated, may hold values from -0.15625 to 0.15625
- cotangent: bfloat16 [64, 8, 64, 256], P(None, 'gx', 'gy'), may hold values from -6 to 6
Outputs:
- out_field: bfloat16 [64, 8, 64, 256], P(None, 'gx', 'gy')
- row_grads: float32 [4096, 128], P(('gx', 'gy'))
- conv_grad: float32 [27, 64, 64], replicated
- proj_grad: float32 [128, 64], replicated
The draws below stay inside these ranges and needn't reach their ends.
Inputs may be any that keep to these rules, and one draw needn't show every extreme that they name: `send_counts`: row s holds how many of source s's 128 rows go to each owner; each row sums to 128; source s's particle rows are listed grouped by owner in increasing order; at most 8 from one source to one owner, and some owner receives 8 from every source. `cell_lists`: entry s * 8 + r of owner d's row is the local cell of the r-th row that source s sends to d; entries of unused slots are ignored.
All inputs are finite; a program needn't handle non-finite values.
Results may differ from the reference program's by a relative error of at most 0.0041.
Values may be sent and summed in bfloat16 or wider, within the bound.
No kernel may reach another device: no remote copies, remote signals or barrier semaphores. Data moves between devices by JAX's collectives and lax.ppermute only.
A program may use at most 64 MiB of HBM per device.

```python
import jax
import jax.numpy as jnp
from jax import lax

C = 64
F = 128
CX = 1
CY = 16
NZ = 256
CAP = 8
NDEV = 32
P_SIZE = 128
CELLS = 4096
NX = 8
NY = 64
N_GY = 4


def draw_send_counts(key, part):
    half = CAP // 2
    key_perm, key_shift = jax.random.split(key)
    order = jax.random.permutation(key_perm, NDEV).astype(jnp.int32)
    shifts = jax.random.randint(key_shift, (NDEV, NDEV // 2), 0, half + 1).astype(jnp.int32)
    shifts = shifts.at[:, 0].set(half)
    counts = jnp.zeros((NDEV, NDEV), jnp.int32)
    counts = counts.at[:, order[0::2]].set(half + shifts)
    counts = counts.at[:, order[1::2]].set(half - shifts)
    return counts


def set_ends(array, own_key, least, largest):
    longest = array.shape.index(max(array.shape))
    spots = []
    for shift in (0, 1):
        where = [jax.random.randint(jax.random.fold_in(own_key, axis), (), 0, length) for axis, length in enumerate(array.shape)]
        where[longest] = (where[longest] + shift) % array.shape[longest]
        spots.append(tuple(where))
    return array.at[spots[0]].set(least).at[spots[1]].set(largest)


def steps_of(key, shape, pieces, smallest, high):
    factor_of = 1.0
    for dim, blocks in pieces:
        heights = jax.random.uniform(jax.random.fold_in(jax.random.fold_in(key, 6), dim), (blocks,), jnp.float32, smallest / len(pieces), high / len(pieces))
        factor_of = factor_of * jnp.repeat(jnp.exp(heights), shape[dim] // blocks).reshape((-1,) + (1,) * (len(shape) - 1 - dim))
    return factor_of


def gaussian(rng, extent, spread, bound, shards=(), held_as=jnp.bfloat16):
    array = spread * jax.random.normal(rng, extent, jnp.float32)
    if shards:
        array = array * steps_of(rng, extent, shards, -0.22, 0.18)
    return jnp.clip(array, -bound, bound).astype(held_as)


def setup_inputs(seed: int = 0) -> dict:
    key_list = jax.random.split(jax.random.key(seed), 8)
    particles = gaussian(key_list[0], (NDEV * P_SIZE, F), 1.0, 6.0, ((0, 32),))
    send_counts = draw_send_counts(jax.random.fold_in(key_list[7], 71), 0)
    cell_lists = set_ends(jax.random.randint(key_list[2], (NDEV, NDEV * CAP), 0, CELLS), jax.random.fold_in(key_list[2], 1), 0, CELLS - 1).astype(jnp.int32)
    base_field = gaussian(key_list[3], (C, NX, NY, NZ), 1.0, 6.0, ((1, 8), (2, 4)))
    proj_weight = gaussian(key_list[4], (F, C), F ** -0.5, 0.5)
    conv_weight = gaussian(key_list[5], (27, C, C), (27 * C) ** -0.5, 0.15625)
    cotangent = gaussian(key_list[6], (C, NX, NY, NZ), 1.0, 6.0, ((1, 8), (2, 4)))
    return dict(particles=particles, send_counts=send_counts, cell_lists=cell_lists, base_field=base_field, proj_weight=proj_weight, conv_weight=conv_weight, cotangent=cotangent)


def pack(rows, counts):
    offsets = jnp.cumsum(counts).astype(jnp.int32) - counts
    slots = jnp.arange(CAP, dtype=jnp.int32)
    index = offsets[:, None] + slots[None, :]
    valid = slots[None, :] < counts[:, None]
    picked = jnp.take(rows, jnp.clip(index, 0, P_SIZE - 1).reshape(-1), axis=0)
    outgoing = jnp.where(valid.reshape(-1, 1), picked, jnp.zeros_like(picked))
    places = jnp.arange(P_SIZE, dtype=jnp.int32)
    ends = offsets + counts
    owner = lax.optimization_barrier(jnp.sum((ends[None, :] <= places[:, None]).astype(jnp.int32), axis=1)).astype(jnp.int32)
    slot_of = owner * CAP + places - jnp.take(offsets, owner)
    return (outgoing, slot_of.astype(jnp.int32))

def taps():
    return [(dx, dy, dz) for dx in (-1, 0, 1) for dy in (-1, 0, 1) for dz in (-1, 0, 1)]

def reference(particles, send_counts, cell_lists, base_field, proj_weight, conv_weight, cotangent):
    parts = particles.reshape(NDEV, P_SIZE, F)
    outgoing, slot_of = jax.vmap(pack)(parts, send_counts)
    recv = outgoing.reshape(NDEV, NDEV, CAP, F).transpose(1, 0, 2, 3).reshape(NDEV * NDEV * CAP, F)
    projected = jnp.dot(recv, proj_weight, preferred_element_type=jnp.float32).astype(jnp.bfloat16)
    owner = jnp.arange(NDEV, dtype=jnp.int32)
    gxi = (owner // N_GY)[:, None]
    gyi = (owner % N_GY)[:, None]
    cxl = cell_lists // (CY * NZ)
    cyl = cell_lists // NZ % CY
    czl = cell_lists % NZ
    gidx = (((gxi * CX + cxl) * NY + gyi * CY + cyl) * NZ + czl).astype(jnp.int32).reshape(-1)
    painted = jnp.zeros((NX * NY * NZ, C), jnp.float32).at[gidx].add(projected.astype(jnp.float32))
    painted = painted.T.reshape(C, NX, NY, NZ)
    field = (base_field.astype(jnp.float32) + painted).astype(jnp.bfloat16)
    pre = jnp.zeros((C, NX * NY * NZ), jnp.float32)
    for k, (dx, dy, dz) in enumerate(taps()):
        moved = jnp.roll(field, (-dx, -dy, -dz), axis=(1, 2, 3)).reshape(C, -1)
        pre = pre + jnp.dot(conv_weight[k], moved, preferred_element_type=jnp.float32)
    pre = pre.reshape(C, NX, NY, NZ)
    sig = jax.nn.sigmoid(pre)
    out_field = (field.astype(jnp.float32) + pre * sig).astype(jnp.bfloat16)
    pre_grad = (cotangent.astype(jnp.float32) * sig * (1.0 + pre * (1.0 - sig))).astype(jnp.bfloat16)
    field_grad = cotangent.astype(jnp.float32).reshape(C, -1)
    flat_grad = pre_grad.reshape(C, -1)
    tap_grads = []
    for k, (dx, dy, dz) in enumerate(taps()):
        back = jnp.roll(pre_grad, (dx, dy, dz), axis=(1, 2, 3)).reshape(C, -1)
        field_grad = field_grad + jnp.dot(conv_weight[k].T, back, preferred_element_type=jnp.float32)
        moved = jnp.roll(field, (-dx, -dy, -dz), axis=(1, 2, 3)).reshape(C, -1)
        tap_grads.append(lax.dot_general(flat_grad, moved, (((1,), (1,)), ((), ())), preferred_element_type=jnp.float32))
    conv_grad = jnp.stack(tap_grads) / jnp.sqrt(jnp.float32(NX * NY * NZ))
    slot_grad = jnp.take(field_grad, gidx, axis=1).T.astype(jnp.bfloat16)
    grad_slots = jnp.dot(slot_grad, proj_weight.T, preferred_element_type=jnp.float32)
    grad_slots = grad_slots.reshape(NDEV, NDEV, CAP, F).transpose(1, 0, 2, 3).reshape(NDEV, NDEV * CAP, F)
    proj_grad = jnp.dot(recv.T, slot_grad, preferred_element_type=jnp.float32)
    proj_grad = proj_grad / jnp.sqrt(jnp.float32(NDEV * P_SIZE))
    row_grads = jax.vmap(lambda grads, slot: jnp.take(grads, slot, axis=0))(grad_slots, slot_of).reshape(NDEV * P_SIZE, F)
    return (out_field, row_grads, conv_grad, proj_grad)
```

```python
import functools
import math

import jax
import jax.numpy as jnp
from jax import lax
from jax.experimental import pallas as pl
from jax.experimental.pallas import tpu as pltpu
from jax.sharding import PartitionSpec as P

AXES = ("gx", "gy")
F32, BF16, I32 = jnp.float32, jnp.bfloat16, jnp.int32
LIMIT = 40 * 1024 * 1024
PAIRS = (((-1, 0), (1, 0)), ((0, -1), (0, 1)), ((-1, -1), (-1, 1)), ((1, -1), (1, 1)))
NT = (((1,), (1,)), ((), ()))
NN = (((1,), (0,)), ((), ()))


def mm(a, b, dims=NN):
    return lax.dot_general(a, b, dims, preferred_element_type=F32)


def call(kernel, outs, args, flops, scratch=()):
    traffic = sum(math.prod(a.shape) * a.dtype.itemsize for a in (*args, *outs))
    return pl.pallas_call(
        kernel,
        out_shape=[jax.ShapeDtypeStruct(o.shape, o.dtype) for o in outs],
        in_specs=[pl.BlockSpec(memory_space=pltpu.VMEM)] * len(args),
        out_specs=[pl.BlockSpec(memory_space=pltpu.VMEM)] * len(outs),
        scratch_shapes=list(scratch),
        compiler_params=pltpu.CompilerParams(vmem_limit_bytes=LIMIT),
        cost_estimate=pl.CostEstimate(flops=flops, bytes_accessed=traffic, transcendentals=0),
    )(*args)


def shape(dims, dtype):
    return jax.ShapeDtypeStruct(dims, dtype)


def send(block, di, dj, ngx, ngy):
    pairs = []
    for i in range(ngx):
        for j in range(ngy):
            pairs.append((i * ngy + j, ((i + di) % ngx) * ngy + (j + dj) % ngy))
    return lax.ppermute(block, AXES, pairs)


def exchange(payload, ndev):
    rows, width = payload.shape
    moved = lax.all_to_all(
        payload.reshape(ndev, rows // ndev, width), AXES, split_axis=0, concat_axis=0, tiled=True
    )
    return moved.reshape(rows, width)


def rolled(x, di, dj):
    for axis, shift in ((0, di), (1, dj)):
        if shift == 1:
            head, tail = lax.slice_in_dim(x, 1, None, axis=axis), lax.slice_in_dim(x, 0, 1, axis=axis)
            x = jnp.concatenate([head, tail], axis=axis)
        elif shift == -1:
            count = x.shape[axis]
            head = lax.slice_in_dim(x, count - 1, count, axis=axis)
            x = jnp.concatenate([head, lax.slice_in_dim(x, 0, count - 1, axis=axis)], axis=axis)
    return x


def pick_kernel(ngx, ngy, cap, counts_ref, rows_ref, proj_t_ref, out_ref):
    ndev = ngx * ngy
    nrows, feats = rows_ref.shape
    slots = ndev * cap
    counts = counts_ref[...].astype(F32)
    rows = rows_ref[...]
    proj_t = proj_t_ref[...]
    both = mm(rows, jnp.concatenate([proj_t, proj_t], axis=0), NT).astype(BF16)
    slot = lax.broadcasted_iota(I32, (slots, ndev), 0)
    lane = lax.broadcasted_iota(I32, (slots, ndev), 1)
    owner = slot // cap
    start = jnp.sum(jnp.where(lane < owner, counts, 0.0), axis=1, keepdims=True)
    held = jnp.sum(jnp.where(lane == owner, counts, 0.0), axis=1, keepdims=True)
    place = (lax.broadcasted_iota(I32, (slots, nrows), 0) % cap).astype(F32)
    row = lax.broadcasted_iota(I32, (slots, nrows), 1).astype(F32)
    onehot = jnp.where((row == place + start) & (place < held), 1.0, 0.0).astype(BF16)
    raw = mm(onehot, rows).reshape(ndev, cap, feats)
    projected = mm(onehot, both).reshape(ngx, ngy, cap, feats)
    left = lax.broadcasted_iota(I32, projected.shape, 3) < feats // 2
    parts = [raw]
    for first, second in PAIRS:
        pair = jnp.where(left, rolled(projected, *first), rolled(projected, *second))
        parts.append(pair.reshape(ndev, cap, feats))
    out = jnp.stack(parts, axis=1)
    out_ref[...] = out.reshape(out_ref.shape).astype(BF16)


def lists_of(block, nl, slots):
    block = block.astype(F32)
    y = jnp.concatenate([block[n : n + 1] for n in range(nl)], axis=1)[:, :slots]
    z = jnp.concatenate([block[nl + n : nl + n + 1] for n in range(nl)], axis=1)[:, :slots]
    return y.astype(I32), z.astype(I32)


def field_kernel(
    ndev, cap, chans, cy, nz,
    recv_ref, cells_ref, base_ref, cot_ref, west_ref, east_ref, north_ref, south_ref,
    nw_ref, sw_ref, ne_ref, se_ref, proj_t_ref, wf_ref, wb_ref,
    out_ref, x_ref, s_ref, raw_ref, to_west_ref, to_east_ref, own_ref,
    masked, hot, ylist, cot_all,
):
    slots = ndev * cap
    nl = -(-slots // nz)
    width = recv_ref.shape[1]
    arrived = recv_ref[...].astype(F32).reshape(ndev, 1 + len(PAIRS), cap, width)
    raw = arrived[:, 0].reshape(slots, width).astype(BF16)
    raw_ref[...] = raw
    rows_of = {(0, 0): mm(proj_t_ref[...], raw, NT).astype(BF16)}
    for q, (first, second) in enumerate(PAIRS):
        flipped = arrived[:, q + 1].reshape(slots, width).T.astype(BF16)
        rows_of[first], rows_of[second] = flipped[:chans], flipped[chans:]
    cells = cells_ref[...]
    where = {
        (0, 0): (cells // nz, cells % nz),
        (-1, 0): lists_of(west_ref[cy], nl, slots),
        (1, 0): lists_of(east_ref[cy], nl, slots),
    }
    for key, ref in (
        ((0, -1), north_ref), ((0, 1), south_ref), ((-1, -1), nw_ref),
        ((-1, 1), sw_ref), ((1, -1), ne_ref), ((1, 1), se_ref),
    ):
        where[key] = lists_of(ref[2], nl, slots)
    depth = lax.broadcasted_iota(I32, (nz, slots), 0)
    mains = {-1: west_ref, 0: base_ref, 1: east_ref}
    edges = {
        (-1, -1): nw_ref, (-1, 1): sw_ref, (0, -1): north_ref,
        (0, 1): south_ref, (1, -1): ne_ref, (1, 1): se_ref,
    }
    for dx in (-1, 0, 1):
        lanes = pl.ds((dx + 1) * chans, chans)
        y, z = where[dx, 0]
        onehot = jnp.where(depth == z, 1.0, 0.0).astype(BF16)
        hot[dx + 1] = onehot
        ylist[dx + 1] = jnp.broadcast_to(y, ylist.shape[1:])
        values = rows_of[dx, 0]
        for n in range(cy):
            masked[pl.ds(n * chans, chans)] = values * jnp.where(y == n, 1.0, 0.0).astype(BF16)
        painted = mm(masked[...], onehot, NT)
        for n in range(cy):
            part = painted[n * chans : (n + 1) * chans]
            x_ref[n + 2, lanes] = (mains[dx][n].astype(F32) + part).astype(BF16)
        for dj in (-1, 1):
            y, z = where[dx, dj]
            onehot = jnp.where(depth == z, 1.0, 0.0).astype(BF16)
            values = rows_of[dx, dj]
            first = cy - 2 if dj < 0 else 0
            lhs = jnp.concatenate(
                [values * jnp.where(y == first + n, 1.0, 0.0).astype(BF16) for n in range(2)], axis=0
            )
            painted = mm(lhs, onehot, NT)
            for n in range(2):
                part = painted[n * chans : (n + 1) * chans]
                target = n if dj < 0 else cy + 2 + n
                x_ref[target, lanes] = (edges[dx, dj][n].astype(F32) + part).astype(BF16)
    cot_all[0] = north_ref[3]
    cot_all[1 : cy + 1] = cot_ref[...]
    cot_all[cy + 1] = south_ref[3]
    own = pl.ds(chans, chans)

    def forward(t, carry):
        taps = x_ref[pl.ds(t, 3)].reshape(9 * chans, nz)
        acc = mm(wf_ref[...], taps)
        pre = acc[chans : 2 * chans]
        pre = pre + pltpu.roll(acc[:chans], 1, 1) + pltpu.roll(acc[2 * chans :], nz - 1, 1)
        sig = jax.nn.sigmoid(pre)
        out_ref[t] = (x_ref[t + 1, own].astype(F32) + pre * sig).astype(BF16)
        grad = cot_all[t].astype(F32) * sig * (1.0 + pre * (1.0 - sig))
        grad = grad.astype(BF16)
        wide = grad.astype(F32)
        s_ref[t, pl.ds(0, chans)] = pltpu.roll(wide, nz - 1, 1).astype(BF16)
        s_ref[t, own] = grad
        s_ref[t, pl.ds(2 * chans, chans)] = pltpu.roll(wide, 1, 1).astype(BF16)
        return carry

    lax.fori_loop(0, cy + 2, forward, 0)

    def slot_terms(n, sums):
        taps = s_ref[pl.ds(n, 3)].reshape(9 * chans, nz)
        plane = mm(wb_ref[...], taps)
        new = []
        for dx in range(3):
            part = plane[dx * chans : (dx + 1) * chans]
            if dx == 1:
                part = part + cot_all[n + 1].astype(F32)
            at_slots = mm(part.astype(BF16), hot[dx])
            here = ylist[dx][:1] == n
            new.append(sums[dx] + jnp.where(here, at_slots, 0.0))
        return tuple(new)

    zero = jnp.zeros((chans, slots), F32)
    west, mine, east = lax.fori_loop(0, cy, slot_terms, (zero, zero, zero))
    to_west_ref[...] = west.astype(BF16)
    to_east_ref[...] = east.astype(BF16)
    own_ref[...] = mine


def taps_kernel(chans, cy, x_ref, s_ref, out_ref, total):
    nz = x_ref.shape[2]
    total[...] = jnp.zeros_like(total)

    def step(n, carry):
        taps = x_ref[pl.ds(n + 1, 3)].reshape(9 * chans, nz)
        total[...] += mm(s_ref[n + 1], taps, NT)
        return carry

    lax.fori_loop(0, cy, step, 0)
    rows = 3 * chans
    width = 2 * chans
    for n in range(4):
        out_ref[pl.ds(n * rows, rows)] = total[:, n * width : (n + 1) * width].astype(BF16)
    last = total[:, 4 * width :]
    last = jnp.concatenate([last[: rows // 2], last[rows // 2 :]], axis=1)
    out_ref[pl.ds(4 * rows, rows // 2)] = last.astype(BF16)


def slots_kernel(ndev, cap, own_ref, a_ref, b_ref, raw_ref, grads_ref, out_ref):
    chans, slots = own_ref.shape
    width = raw_ref.shape[1]
    total = own_ref[...] + a_ref[...].astype(F32) + b_ref[...].astype(F32)
    grad = total.astype(BF16)
    proj = mm(grad, raw_ref[...])
    back = grad.astype(F32).T
    back = jnp.concatenate([back, jnp.zeros((slots, width - chans), F32)], axis=1)
    share = out_ref.shape[0] // ndev - cap
    rows = grads_ref.shape[0] + chans
    pad = jnp.zeros((share * ndev - rows, width), F32)
    sums = jnp.concatenate([grads_ref[...].astype(F32), proj, pad], axis=0)
    out = jnp.concatenate(
        [sums.reshape(ndev, share, width), back.reshape(ndev, cap, width)], axis=1
    )
    out_ref[...] = out.reshape(out_ref.shape).astype(BF16)


def rows_kernel(ndev, cap, recv_ref, counts_ref, proj_t_ref, rows_ref, sums_ref):
    nrows = rows_ref.shape[0]
    chans = proj_t_ref.shape[0]
    width = recv_ref.shape[1]
    slots = ndev * cap
    share = recv_ref.shape[0] // ndev - cap
    arrived = recv_ref[...].astype(F32).reshape(ndev, share + cap, width)
    sums = jnp.sum(arrived[:, :share], axis=0)
    sums_ref[...] = jnp.broadcast_to(sums[None], (ndev, share, width)).reshape(
        sums_ref.shape
    ).astype(BF16)
    back = arrived[:, share:].reshape(slots, width)[:, :chans].astype(BF16)
    counts = counts_ref[...].astype(F32)
    place = lax.broadcasted_iota(I32, (nrows, ndev), 0).astype(F32)
    lane = lax.broadcasted_iota(I32, (ndev, ndev), 1)
    upto = lax.broadcasted_iota(I32, (ndev, ndev), 0) <= lane
    ends = mm(counts.astype(BF16), jnp.where(upto, 1.0, 0.0).astype(BF16))
    before = ends <= place
    owner = jnp.sum(jnp.where(before, 1.0, 0.0), axis=1, keepdims=True)
    start = jnp.sum(jnp.where(before, counts, 0.0), axis=1, keepdims=True)
    slot = owner * cap + place[:, :1] - start
    onehot = jnp.where(
        lax.broadcasted_iota(I32, (nrows, slots), 1).astype(F32) == slot, 1.0, 0.0
    ).astype(BF16)
    picked = mm(onehot, back).astype(BF16)
    rows_ref[...] = mm(picked, proj_t_ref[...])


def finish_kernel(conv_scale, proj_scale, recv_ref, conv_ref, proj_ref):
    taps, chans, _ = conv_ref.shape
    rows, width = 3 * chans, 2 * chans
    half = rows // 2
    for t in range(9):
        dy, dx = t // 3, t % 3
        for dz in range(3):
            if t < 8:
                block = recv_ref[pl.ds((t // 2) * rows + dz * chans, chans)].astype(F32)
                part = block[:, :chans] if t % 2 == 0 else block[:, chans:]
                conv_ref[dx * 9 + dy * 3 + dz] = part * conv_scale
        if t == 8:
            block = recv_ref[pl.ds(4 * rows, half)].astype(F32)
            column = jnp.concatenate([block[:, :chans], block[:, chans:]], axis=0)
            for dz in range(3):
                conv_ref[dx * 9 + dy * 3 + dz] = column[dz * chans : (dz + 1) * chans] * conv_scale
    proj_ref[...] = recv_ref[pl.ds(4 * rows + half, chans)].astype(F32) * proj_scale


def local(particles, send_counts, cell_lists, base_field, proj_weight, conv_weight, cotangent):
    ngx, ngy = lax.axis_size("gx"), lax.axis_size("gy")
    ndev = ngx * ngy
    nrows, feats = particles.shape
    chans, cx, cy, nz = base_field.shape
    slots = cell_lists.shape[1]
    cap = slots // ndev
    count = cx * cy * nz
    assert cx == 1 and feats == 2 * chans
    proj_t = proj_weight.T

    base = base_field[:, 0].transpose(1, 0, 2)
    cot = cotangent[:, 0].transpose(1, 0, 2)
    nl = -(-slots // nz)
    lists = jnp.stack([cell_lists[0] // nz, cell_lists[0] % nz]).astype(BF16)
    lists = jnp.pad(lists, ((0, 0), (0, nl * nz - slots))).reshape(2 * nl, nz)
    lists = jnp.pad(lists, ((0, chans - 2 * nl), (0, 0)))[None]
    whole = jnp.concatenate([base, lists], axis=0)
    low = jnp.concatenate([base[:2], lists], axis=0)
    high = jnp.concatenate([base[cy - 2 :], lists], axis=0)
    move = functools.partial(send, ngx=ngx, ngy=ngy)
    west, east = move(whole, 1, 0), move(whole, -1, 0)
    north = move(jnp.concatenate([high, cot[cy - 1 :]], axis=0), 0, 1)
    south = move(jnp.concatenate([low, cot[:1]], axis=0), 0, -1)
    nw, sw = move(high, 1, 1), move(low, 1, -1)
    ne, se = move(high, -1, 1), move(low, -1, -1)

    (payload,) = call(
        functools.partial(pick_kernel, ngx, ngy, cap),
        [shape((ndev * (1 + len(PAIRS)) * cap, feats), BF16)],
        (send_counts, particles, proj_t),
        4 * slots * nrows * feats,
    )
    recv = exchange(payload, ndev)

    taps = conv_weight.reshape(3, 3, 3, chans, chans)
    wf = taps.transpose(2, 3, 1, 0, 4).reshape(3 * chans, 9 * chans)
    wb = taps[:, ::-1].transpose(0, 4, 1, 2, 3).reshape(3 * chans, 9 * chans)

    rows = 3 * chans
    out_rows, x_all, s_all, raw, to_west, to_east, own = call(
        functools.partial(field_kernel, ndev, cap, chans, cy, nz),
        [
            shape((cy + 2, chans, nz), BF16),
            shape((cy + 4, rows, nz), BF16),
            shape((cy + 2, rows, nz), BF16),
            shape((slots, feats), BF16),
            shape((chans, slots), BF16),
            shape((chans, slots), BF16),
            shape((chans, slots), F32),
        ],
        (recv, cell_lists, base, cot, west, east, north, south, nw, sw, ne, se, proj_t, wf, wb),
        4 * rows * rows * 3 * count,
        (
            pltpu.VMEM((cy * chans, slots), BF16),
            pltpu.VMEM((3, nz, slots), BF16),
            pltpu.VMEM((3, 8, slots), I32),
            pltpu.VMEM((cy + 2, chans, nz), BF16),
        ),
    )
    from_east = move(to_west, -1, 0)
    from_west = move(to_east, 1, 0)
    grad_rows = 27 * chans * chans // feats
    (tap_grads,) = call(
        functools.partial(taps_kernel, chans, cy),
        [shape((grad_rows, feats), BF16)],
        (x_all, s_all),
        2 * rows * rows * 3 * count,
        (pltpu.VMEM((rows, 9 * chans), F32),),
    )
    share = -(-(grad_rows + chans) // (8 * ndev)) * 8
    (payload,) = call(
        functools.partial(slots_kernel, ndev, cap),
        [shape((ndev * (share + cap), feats), BF16)],
        (own, from_east, from_west, raw, tap_grads),
        2 * chans * slots * feats,
    )
    recv = exchange(payload, ndev)
    row_grads, sums = call(
        functools.partial(rows_kernel, ndev, cap),
        [shape((nrows, feats), F32), shape((ndev * share, feats), BF16)],
        (recv, send_counts, proj_t),
        2 * nrows * slots * chans,
    )
    recv = exchange(sums, ndev)
    conv_grad, proj_grad = call(
        functools.partial(
            finish_kernel, 1.0 / math.sqrt(count * ndev), 1.0 / math.sqrt(nrows * ndev)
        ),
        [shape((27, chans, chans), F32), shape((chans, feats), F32)],
        (recv,),
        1000,
    )
    out_field = out_rows[1 : cy + 1].transpose(1, 0, 2)[:, None]
    return (out_field, row_grads, conv_grad, proj_grad.T)


def solution(mesh):
    in_specs = (
        P(("gx", "gy"), None),
        P(("gx", "gy"), None),
        P(("gx", "gy"), None),
        P(None, "gx", "gy", None),
        P(),
        P(),
        P(None, "gx", "gy", None),
    )
    out_specs = (P(None, "gx", "gy", None), P(("gx", "gy"), None), P(), P())
    return jax.shard_map(local, mesh=mesh, in_specs=in_specs, out_specs=out_specs, check_vma=False)
```

```python
import functools
import math

import jax
import jax.numpy as jnp
from jax import lax
from jax.experimental import pallas as pl
from jax.experimental.pallas import tpu as pltpu
from jax.sharding import PartitionSpec as P

AXES = ("gx", "gy")
F32, BF16, I32 = jnp.float32, jnp.bfloat16, jnp.int32
LIMIT = 40 * 1024 * 1024
NT = (((1,), (1,)), ((), ()))
NN = (((1,), (0,)), ((), ()))


def mm(a, b, dims=NN):
    return lax.dot_general(a, b, dims, preferred_element_type=F32)


def call(kernel, outs, args, flops, scratch=()):
    traffic = sum(math.prod(a.shape) * a.dtype.itemsize for a in (*args, *outs))
    return pl.pallas_call(
        kernel,
        out_shape=[jax.ShapeDtypeStruct(o.shape, o.dtype) for o in outs],
        in_specs=[pl.BlockSpec(memory_space=pltpu.VMEM)] * len(args),
        out_specs=[pl.BlockSpec(memory_space=pltpu.VMEM)] * len(outs),
        scratch_shapes=list(scratch),
        compiler_params=pltpu.CompilerParams(vmem_limit_bytes=LIMIT),
        cost_estimate=pl.CostEstimate(flops=flops, bytes_accessed=traffic, transcendentals=0),
    )(*args)


def shape(dims, dtype):
    return jax.ShapeDtypeStruct(dims, dtype)


def send(block, di, dj, ngx, ngy):
    pairs = []
    for i in range(ngx):
        for j in range(ngy):
            pairs.append((i * ngy + j, ((i + di) % ngx) * ngy + (j + dj) % ngy))
    return lax.ppermute(block, AXES, pairs)


def exchange(payload, ndev):
    rows, width = payload.shape
    moved = lax.all_to_all(
        payload.reshape(ndev, rows // ndev, width), AXES, split_axis=0, concat_axis=0, tiled=True
    )
    return moved.reshape(rows, width)


def rolled(x, di, dj):
    for axis, shift in ((0, di), (1, dj)):
        if shift == 1:
            head, tail = lax.slice_in_dim(x, 1, None, axis=axis), lax.slice_in_dim(x, 0, 1, axis=axis)
            x = jnp.concatenate([head, tail], axis=axis)
        elif shift == -1:
            count = x.shape[axis]
            head = lax.slice_in_dim(x, count - 1, count, axis=axis)
            x = jnp.concatenate([head, lax.slice_in_dim(x, 0, count - 1, axis=axis)], axis=axis)
    return x


def widths(nl, slots, block):
    block = block.astype(F32)
    y = jnp.concatenate([block[n : n + 1] for n in range(nl)], axis=1)[:, :slots]
    z = jnp.concatenate([block[nl + n : nl + n + 1] for n in range(nl)], axis=1)[:, :slots]
    return y.astype(I32), z.astype(I32)


def picked_depth(z, nz):
    depth = lax.broadcasted_iota(I32, (nz, z.shape[1]), 0)
    return jnp.where(depth == z, 1.0, 0.0).astype(BF16)


def rows_in(recv_ref, ndev, cap):
    width = recv_ref.shape[1]
    arrived = recv_ref[...].astype(F32).reshape(ndev, 3, cap, width)
    return [arrived[:, n].reshape(ndev * cap, width).astype(BF16) for n in range(3)]


def stacked(grad):
    nz = grad.shape[1]
    wide = grad.astype(F32)
    return jnp.concatenate(
        [pltpu.roll(wide, nz - 1, 1), wide, pltpu.roll(wide, 1, 1)], axis=0
    ).astype(BF16)


def finish_row(acc, field, cot):
    chans, nz = field.shape
    pre = acc[chans : 2 * chans]
    pre = pre + pltpu.roll(acc[:chans], 1, 1) + pltpu.roll(acc[2 * chans :], nz - 1, 1)
    sig = jax.nn.sigmoid(pre)
    out = field.astype(F32) + pre * sig
    grad = cot.astype(F32) * sig * (1.0 + pre * (1.0 - sig))
    return out.astype(BF16), grad.astype(BF16)


def plane_kernel(base_ref, lists_ref, out_ref):
    chans, cy, nz = base_ref.shape
    turned = jnp.swapaxes(base_ref[...].astype(F32), 0, 1)
    out_ref[pl.ds(0, cy * chans)] = turned.reshape(cy * chans, nz).astype(BF16)
    out_ref[pl.ds(cy * chans, lists_ref.shape[0])] = lists_ref[...]


def pick_kernel(ngx, ngy, cap, counts_ref, rows_ref, plane_ref, out_ref):
    ndev = ngx * ngy
    nrows, feats = rows_ref.shape
    slots = ndev * cap
    counts = counts_ref[...].astype(F32)
    slot = lax.broadcasted_iota(I32, (slots, ndev), 0)
    lane = lax.broadcasted_iota(I32, (slots, ndev), 1)
    owner = slot // cap
    start = jnp.sum(jnp.where(lane < owner, counts, 0.0), axis=1, keepdims=True)
    held = jnp.sum(jnp.where(lane == owner, counts, 0.0), axis=1, keepdims=True)
    place = (lax.broadcasted_iota(I32, (slots, nrows), 0) % cap).astype(F32)
    row = lax.broadcasted_iota(I32, (slots, nrows), 1).astype(F32)
    onehot = jnp.where((row == place + start) & (place < held), 1.0, 0.0).astype(BF16)
    raw = mm(onehot, rows_ref[...]).reshape(ngx, ngy, cap, feats)
    parts = [rolled(raw, dx, 0).reshape(ndev, cap, feats) for dx in (-1, 0, 1)]
    out_ref[...] = jnp.stack(parts, axis=1).reshape(out_ref.shape).astype(BF16)


def paint_kernel(
    ndev, cap, chans, cy, nz,
    recv_ref, own_ref, west_ref, east_ref, proj_t_ref,
    x_ref, first_ref, last_ref, masked,
):
    slots = ndev * cap
    nl = -(-slots // nz)
    raws = rows_in(recv_ref, ndev, cap)
    for dx, ref in enumerate((west_ref, own_ref, east_ref)):
        lanes = pl.ds(dx * chans, chans)
        y, z = widths(nl, slots, ref[pl.ds(cy * chans, ref.shape[0] - cy * chans)])
        values = mm(proj_t_ref[...], raws[dx], NT).astype(BF16)
        for n in range(cy):
            masked[pl.ds(n * chans, chans)] = values * jnp.where(y == n, 1.0, 0.0).astype(BF16)
        painted = mm(masked[...], picked_depth(z, nz), NT)
        for n in range(cy):
            rows = pl.ds(n * chans, chans)
            part = painted[n * chans : (n + 1) * chans]
            field = (ref[rows].astype(F32) + part).astype(BF16)
            x_ref[n, lanes] = field
            if n == 0:
                first_ref[lanes] = field
            if n == cy - 1:
                last_ref[lanes] = field


def conv_kernel(
    chans, cy, x_ref, cot_ref, wf_ref,
    out_ref, s_ref, top_ref, bottom_ref, total_ref, acc,
):
    rows = 3 * chans
    own = pl.ds(chans, chans)
    zeros = jnp.zeros(s_ref.shape[1:], BF16)
    for t in (0, 1, cy, cy + 1):
        s_ref[t] = zeros
    out_ref[0] = zeros[:chans]
    out_ref[cy - 1] = zeros[:chans]
    acc[0] = jnp.zeros(acc.shape[1:], F32)

    def spread(n):
        terms = mm(wf_ref[...], x_ref[n])
        acc[n + 1] = terms[:rows]
        acc[n] += terms[rows : 2 * rows]
        return terms[2 * rows :]

    spread(0)
    top_ref[...] = acc[0] + spread(1)

    def forward(n, carry):
        done = spread(n) + acc[n - 1]
        y = n - 1
        out, grad = finish_row(done, x_ref[y, own], cot_ref[y])
        out_ref[y] = out
        s_ref[y + 1] = stacked(grad)
        return carry

    lax.fori_loop(2, cy, forward, 0, unroll=2)
    bottom_ref[...] = acc[cy - 1]
    total_ref[...] = jnp.zeros_like(total_ref)

    def taps(n, carry):
        grads = s_ref[pl.ds(n, 3)].reshape(3 * rows, s_ref.shape[2])
        total_ref[...] += mm(grads, x_ref[n], NT)
        return carry

    lax.fori_loop(0, cy, taps, 0, unroll=2)


def edge_kernel(
    chans, cy, top_ref, bottom_ref, north_ref, south_ref, first_ref, last_ref, cot_ref, wf_ref,
    out_ref, up_ref, down_ref,
):
    rows = 3 * chans
    own = pl.ds(chans, chans)
    top = top_ref[...] + mm(wf_ref[pl.ds(0, rows)], north_ref[...])
    out_ref[0], up_ref[...] = finish_row(top, first_ref[own], cot_ref[0])
    bottom = bottom_ref[...] + mm(wf_ref[pl.ds(2 * rows, rows)], south_ref[...])
    out_ref[1], down_ref[...] = finish_row(bottom, last_ref[own], cot_ref[cy - 1])


def at_slots(parts, ylists, hots, first, total):
    chans = total[0].shape[0]
    new = []
    for dx in range(3):
        found = mm(parts[dx], hots[dx])
        value = total[dx]
        for n in range(len(first)):
            here = ylists[dx] == first[n]
            value = value + jnp.where(here, found[n * chans : (n + 1) * chans], 0.0)
        new.append(value)
    return new


def slot_kernel(
    ndev, cap, chans, cy, nz,
    x_ref, s_ref, north_ref, south_ref, up_ref, down_ref, cot_ref, total_ref, wb_ref,
    own_ref, west_ref, east_ref,
    grads_ref, sums_ref, edge_ref, acc, plane, total,
):
    rows = 3 * chans
    slots = ndev * cap
    nl = -(-slots // nz)
    up, down = stacked(up_ref[...]), stacked(down_ref[...])
    for block, high, middle, low in (
        (0, x_ref[1], x_ref[0], north_ref[...]),
        (cy - 1, south_ref[...], x_ref[cy - 1], x_ref[cy - 2]),
    ):
        grads = up if block == 0 else down
        for n, field in enumerate((high, middle, low)):
            at = pl.ds(n * rows, rows)
            base = total_ref[at] if block == 0 else total[at]
            total[at] = base + mm(grads, field, NT)
    grads_ref[pl.ds(0, 3 * rows)] = total[:, : 2 * chans].astype(BF16)
    last = total[:, 2 * chans :]
    half = 3 * rows // 2
    last = jnp.concatenate([last[:half], last[half:]], axis=1)
    grads_ref[pl.ds(3 * rows, half)] = last.astype(BF16)

    def keep(n, value):
        for dx in range(3):
            part = value[dx * chans : (dx + 1) * chans]
            if dx == 1:
                part = part + cot_ref[n].astype(F32)
            plane[dx, pl.ds((n - 1) * chans, chans)] = part.astype(BF16)

    def spread(n, grads):
        terms = mm(wb_ref[...], grads)
        acc[n + 1] = terms[2 * rows :]
        acc[n] += terms[rows : 2 * rows]
        return terms[:rows]

    acc[0] = jnp.zeros(acc.shape[1:], F32)
    spread(0, up)
    edge_ref[0] = acc[0] + spread(1, s_ref[2])

    def backward(n, carry):
        keep(n - 1, spread(n, s_ref[n + 1]) + acc[n - 1])
        return carry

    lax.fori_loop(2, cy - 1, backward, 0, unroll=2)
    keep(cy - 2, spread(cy - 1, down) + acc[cy - 2])
    edge_ref[1] = acc[cy - 1]
    ylists, hots = [], []
    for ref in (west_ref, own_ref, east_ref):
        y, z = widths(nl, slots, ref[pl.ds(cy * chans, ref.shape[0] - cy * chans)])
        ylists.append(y)
        hots.append(picked_depth(z, nz))
    zero = jnp.zeros((chans, slots), F32)
    found = at_slots([plane[dx] for dx in range(3)], ylists, hots, range(1, cy - 1), [zero] * 3)
    for dx in range(3):
        sums_ref[dx] = found[dx]


def return_kernel(
    ndev, cap, chans, cy, nz,
    sums_ref, edge_ref, before_ref, after_ref, cot_ref, wb_ref,
    own_ref, west_ref, east_ref, recv_ref, grads_ref, out_ref,
):
    rows = 3 * chans
    slots = ndev * cap
    nl = -(-slots // nz)
    top = edge_ref[0] + mm(wb_ref[pl.ds(2 * rows, rows)], stacked(before_ref[...]))
    bottom = edge_ref[1] + mm(wb_ref[pl.ds(0, rows)], stacked(after_ref[...]))
    ylists, hots, parts = [], [], []
    for dx, ref in enumerate((west_ref, own_ref, east_ref)):
        y, z = widths(nl, slots, ref[pl.ds(cy * chans, ref.shape[0] - cy * chans)])
        ylists.append(y)
        hots.append(picked_depth(z, nz))
        at = slice(dx * chans, (dx + 1) * chans)
        pair = [top[at], bottom[at]]
        if dx == 1:
            pair = [pair[0] + cot_ref[0].astype(F32), pair[1] + cot_ref[cy - 1].astype(F32)]
        parts.append(jnp.concatenate(pair, axis=0).astype(BF16))
    found = at_slots(parts, ylists, hots, (0, cy - 1), [sums_ref[dx] for dx in range(3)])
    raws = rows_in(recv_ref, ndev, cap)
    proj = sum(mm(found[dx].astype(BF16), raws[dx]) for dx in range(3))
    proj_high = proj.astype(BF16).astype(F32)
    sides = jnp.concatenate([found[0], found[2]], axis=0).T
    middle = jnp.concatenate([found[1], jnp.zeros_like(found[1])], axis=0).T
    width = out_ref.shape[1]
    share = out_ref.shape[0] // ndev - 2 * cap
    used = grads_ref.shape[0] + 2 * chans
    pad = jnp.zeros((share * ndev - used, width), F32)
    halves = [v.reshape(2 * chans // share, share // 2, width) for v in (proj_high, proj - proj_high)]
    proj = jnp.stack(halves, axis=1).reshape(2 * chans, width)
    sums = jnp.concatenate([grads_ref[...].astype(F32), proj, pad], axis=0)
    out = jnp.concatenate(
        [
            sums.reshape(ndev, share, width),
            sides.reshape(ndev, cap, width),
            middle.reshape(ndev, cap, width),
        ],
        axis=1,
    )
    out_ref[...] = out.reshape(out_ref.shape).astype(BF16)


def rows_kernel(
    ngx, ngy, cap, chans, recv_ref, index_ref, counts_ref, proj_t_ref, rows_ref, sums_ref
):
    ndev = ngx * ngy
    nrows = rows_ref.shape[0]
    width = recv_ref.shape[1]
    slots = ndev * cap
    share = recv_ref.shape[0] // ndev - 2 * cap
    arrived = recv_ref[...].astype(F32).reshape(ndev, share + 2 * cap, width)
    sums = jnp.sum(arrived[:, :share], axis=0)
    half = share // 2
    whole = sums[:half] + sums[half:]
    high = whole.astype(BF16).astype(F32)
    split = jnp.concatenate([high, whole - high], axis=0)
    device = jnp.broadcast_to(index_ref[...], sums.shape)
    sums = jnp.where(device * share >= 27 * chans * chans // width, split, sums)
    sums_ref[...] = jnp.broadcast_to(sums[None], (ndev, share, width)).reshape(
        sums_ref.shape
    ).astype(BF16)
    sides = arrived[:, share : share + cap].reshape(ngx, ngy, cap, width)
    left = lax.broadcasted_iota(I32, sides.shape, 3) < chans
    sides = jnp.where(left, rolled(sides, 1, 0), rolled(sides, -1, 0)).reshape(slots, width)
    middle = arrived[:, share + cap :].reshape(slots, width)
    counts = counts_ref[...].astype(F32)
    place = lax.broadcasted_iota(I32, (nrows, ndev), 0).astype(F32)
    lane = lax.broadcasted_iota(I32, (ndev, ndev), 1)
    upto = lax.broadcasted_iota(I32, (ndev, ndev), 0) <= lane
    ends = mm(counts.astype(BF16), jnp.where(upto, 1.0, 0.0).astype(BF16))
    before = ends <= place
    owner = jnp.sum(jnp.where(before, 1.0, 0.0), axis=1, keepdims=True)
    start = jnp.sum(jnp.where(before, counts, 0.0), axis=1, keepdims=True)
    slot = owner * cap + place[:, :1] - start
    onehot = jnp.where(
        lax.broadcasted_iota(I32, (nrows, slots), 1).astype(F32) == slot, 1.0, 0.0
    ).astype(BF16)
    proj_t = proj_t_ref[...]
    both = jnp.concatenate([proj_t, proj_t], axis=0)
    sides = mm(onehot, sides.astype(BF16)).astype(BF16)
    middle = mm(onehot, middle.astype(BF16)).astype(BF16)
    rows_ref[...] = mm(sides, both) + mm(middle, both)


def finish_kernel(conv_scale, proj_scale, share, recv_ref, conv_ref, proj_ref):
    taps, chans, _ = conv_ref.shape
    rows = 9 * chans
    half = rows // 2
    packed = recv_ref[pl.ds(rows, half)].astype(F32)
    column = jnp.concatenate([packed[:, :chans], packed[:, chans:]], axis=0)
    for b in range(3):
        for dz in range(3):
            first = (b * 3 + dz) * chans
            block = recv_ref[pl.ds(first, chans)].astype(F32)
            k = (2 - b) * 3 + dz
            conv_ref[k] = block[:, :chans] * conv_scale
            conv_ref[9 + k] = block[:, chans:] * conv_scale
            conv_ref[18 + k] = column[first : first + chans] * conv_scale
    width = recv_ref.shape[1]
    terms = recv_ref[pl.ds(rows + half, 2 * chans)].astype(F32)
    terms = terms.reshape(2 * chans // share, 2, share // 2, width)
    proj_ref[...] = jnp.sum(terms, axis=1).reshape(chans, width) * proj_scale


def local(particles, send_counts, cell_lists, base_field, proj_weight, conv_weight, cotangent):
    ngx, ngy = lax.axis_size("gx"), lax.axis_size("gy")
    ndev = ngx * ngy
    nrows, feats = particles.shape
    chans, cx, cy, nz = base_field.shape
    slots = cell_lists.shape[1]
    cap = slots // ndev
    count = cx * cy * nz
    assert cx == 1 and feats == 2 * chans
    proj_t = proj_weight.T
    move = functools.partial(send, ngx=ngx, ngy=ngy)
    rows = 3 * chans
    one = 2 * rows * rows * nz

    nl = -(-slots // nz)
    tail = -(-2 * nl // 16) * 16
    lists = jnp.stack([cell_lists[0] // nz, cell_lists[0] % nz]).astype(BF16)
    lists = jnp.pad(lists, ((0, 0), (0, nl * nz - slots))).reshape(2 * nl, nz)
    lists = jnp.pad(lists, ((0, tail - 2 * nl), (0, 0)))
    (plane,) = call(
        plane_kernel,
        [shape((cy * chans + tail, nz), BF16)],
        (base_field.reshape(chans, cy, nz), lists),
        1000,
    )
    west, east = move(plane, 1, 0), move(plane, -1, 0)
    (payload,) = call(
        functools.partial(pick_kernel, ngx, ngy, cap),
        [shape((ndev * 3 * cap, feats), BF16)],
        (send_counts, particles, plane),
        2 * slots * nrows * feats,
    )
    recv = exchange(payload, ndev)

    cot = cotangent[:, 0].transpose(1, 0, 2)
    taps = conv_weight.reshape(3, 3, 3, chans, chans)
    wf = taps.transpose(1, 2, 3, 0, 4).reshape(9 * chans, rows)
    wb = taps.transpose(1, 0, 4, 2, 3).reshape(9 * chans, rows)

    x_all, first, last = call(
        functools.partial(paint_kernel, ndev, cap, chans, cy, nz),
        [shape((cy, rows, nz), BF16), shape((rows, nz), BF16), shape((rows, nz), BF16)],
        (recv, plane, west, east, proj_t),
        6 * slots * count * chans // nz * nz // 16,
        (pltpu.VMEM((cy * chans, slots), BF16),),
    )
    north, south = move(last, 0, 1), move(first, 0, -1)
    out_rows, s_all, top, bottom, total = call(
        functools.partial(conv_kernel, chans, cy),
        [
            shape((cy, chans, nz), BF16),
            shape((cy + 2, rows, nz), BF16),
            shape((rows, nz), F32),
            shape((rows, nz), F32),
            shape((9 * chans, rows), F32),
        ],
        (x_all, cot, wf),
        2 * cy * 3 * one,
        (pltpu.VMEM((cy + 1, rows, nz), F32),),
    )
    out_edge, up, down = call(
        functools.partial(edge_kernel, chans, cy),
        [shape((2, chans, nz), BF16), shape((chans, nz), BF16), shape((chans, nz), BF16)],
        (top, bottom, north, south, first, last, cot, wf),
        2 * one,
    )
    before, after = move(down, 0, 1), move(up, 0, -1)
    grad_rows = 27 * chans * chans // feats
    tap_grads, sums, edge = call(
        functools.partial(slot_kernel, ndev, cap, chans, cy, nz),
        [
            shape((grad_rows, feats), BF16),
            shape((3, chans, slots), F32),
            shape((2, rows, nz), F32),
        ],
        (x_all, s_all, north, south, up, down, cot, total, wb, plane, west, east),
        cy * 3 * one,
        (
            pltpu.VMEM((cy + 1, rows, nz), F32),
            pltpu.VMEM((3, (cy - 2) * chans, nz), BF16),
            pltpu.VMEM((9 * chans, rows), F32),
        ),
    )
    share = -(-(grad_rows + 2 * chans) // (16 * ndev)) * 16
    (payload,) = call(
        functools.partial(return_kernel, ndev, cap, chans, cy, nz),
        [shape((ndev * (share + 2 * cap), feats), BF16)],
        (sums, edge, before, after, cot, wb, plane, west, east, recv, tap_grads),
        2 * one,
    )
    recv = exchange(payload, ndev)
    index = (lax.axis_index("gx") * ngy + lax.axis_index("gy")).astype(I32).reshape(1, 1)
    row_grads, sums = call(
        functools.partial(rows_kernel, ngx, ngy, cap, chans),
        [shape((nrows, feats), F32), shape((ndev * share, feats), BF16)],
        (recv, index, send_counts, proj_t),
        2 * nrows * slots * chans,
    )
    recv = exchange(sums, ndev)
    conv_grad, proj_grad = call(
        functools.partial(
            finish_kernel, 1.0 / math.sqrt(count * ndev), 1.0 / math.sqrt(nrows * ndev), share
        ),
        [shape((27, chans, chans), F32), shape((chans, feats), F32)],
        (recv,),
        1000,
    )
    out_field = jnp.concatenate([out_edge[:1], out_rows[1 : cy - 1], out_edge[1:]], axis=0)
    return (out_field.transpose(1, 0, 2)[:, None], row_grads, conv_grad, proj_grad.T)


def solution(mesh):
    in_specs = (
        P(("gx", "gy"), None),
        P(("gx", "gy"), None),
        P(("gx", "gy"), None),
        P(None, "gx", "gy", None),
        P(),
        P(),
        P(None, "gx", "gy", None),
    )
    out_specs = (P(None, "gx", "gy", None), P(("gx", "gy"), None), P(), P())
    return jax.shard_map(local, mesh=mesh, in_specs=in_specs, out_specs=out_specs, check_vma=False)
```

```python
import functools
import math

import jax
import jax.numpy as jnp
from jax import lax
from jax.experimental import pallas as pl
from jax.experimental.pallas import tpu as pltpu
from jax.sharding import PartitionSpec as P

AXES = ("gx", "gy")
F32, BF16, I32 = jnp.float32, jnp.bfloat16, jnp.int32
LIMIT = 40 * 1024 * 1024
NT = (((1,), (1,)), ((), ()))
NN = (((1,), (0,)), ((), ()))


def mm(a, b, dims=NN):
    return lax.dot_general(a, b, dims, preferred_element_type=F32)


def call(kernel, outs, args, flops, scratch=()):
    traffic = sum(math.prod(a.shape) * a.dtype.itemsize for a in (*args, *outs))
    return pl.pallas_call(
        kernel,
        out_shape=[jax.ShapeDtypeStruct(o.shape, o.dtype) for o in outs],
        in_specs=[pl.BlockSpec(memory_space=pltpu.VMEM)] * len(args),
        out_specs=[pl.BlockSpec(memory_space=pltpu.VMEM)] * len(outs),
        scratch_shapes=list(scratch),
        compiler_params=pltpu.CompilerParams(vmem_limit_bytes=LIMIT),
        cost_estimate=pl.CostEstimate(flops=flops, bytes_accessed=traffic, transcendentals=0),
    )(*args)


def shape(dims, dtype):
    return jax.ShapeDtypeStruct(dims, dtype)


def send(block, di, dj, ngx, ngy):
    pairs = []
    for i in range(ngx):
        for j in range(ngy):
            pairs.append((i * ngy + j, ((i + di) % ngx) * ngy + (j + dj) % ngy))
    return lax.ppermute(block, AXES, pairs)


def exchange(payload, ndev):
    rows, width = payload.shape
    moved = lax.all_to_all(
        payload.reshape(ndev, rows // ndev, width), AXES, split_axis=0, concat_axis=0, tiled=True
    )
    return moved.reshape(rows, width)


def rolled(x, di, dj):
    for axis, shift in ((0, di), (1, dj)):
        if shift == 1:
            head, tail = lax.slice_in_dim(x, 1, None, axis=axis), lax.slice_in_dim(x, 0, 1, axis=axis)
            x = jnp.concatenate([head, tail], axis=axis)
        elif shift == -1:
            count = x.shape[axis]
            head = lax.slice_in_dim(x, count - 1, count, axis=axis)
            x = jnp.concatenate([head, lax.slice_in_dim(x, 0, count - 1, axis=axis)], axis=axis)
    return x


def widths(nl, slots, block):
    block = block.astype(F32)
    y = jnp.concatenate([block[n : n + 1] for n in range(nl)], axis=1)[:, :slots]
    z = jnp.concatenate([block[nl + n : nl + n + 1] for n in range(nl)], axis=1)[:, :slots]
    return y.astype(I32), z.astype(I32)


def picked_depth(z, nz):
    depth = lax.broadcasted_iota(I32, (nz, z.shape[1]), 0)
    return jnp.where(depth == z, 1.0, 0.0).astype(BF16)


def rows_in(recv_ref, ndev, cap):
    width = recv_ref.shape[1]
    arrived = recv_ref[...].astype(F32).reshape(ndev, 3, cap, width)
    return [arrived[:, n].reshape(ndev * cap, width).astype(BF16) for n in range(3)]


def stacked(grad):
    nz = grad.shape[1]
    wide = grad.astype(F32)
    return jnp.concatenate(
        [pltpu.roll(wide, nz - 1, 1), wide, pltpu.roll(wide, 1, 1)], axis=0
    ).astype(BF16)


def finish_row(acc, field, cot):
    chans, nz = field.shape
    pre = acc[chans : 2 * chans]
    pre = pre + pltpu.roll(acc[:chans], 1, 1) + pltpu.roll(acc[2 * chans :], nz - 1, 1)
    sig = jax.nn.sigmoid(pre)
    out = field.astype(F32) + pre * sig
    grad = cot.astype(F32) * sig * (1.0 + pre * (1.0 - sig))
    return out.astype(BF16), grad.astype(BF16)


def plane_kernel(base_ref, cells_ref, rows_ref, counts_ref, out_ref, rows_out_ref, counts_out_ref):
    chans, cy, nz = base_ref.shape
    rows_out_ref[...] = rows_ref[...]
    counts_out_ref[...] = counts_ref[...]
    turned = jnp.swapaxes(base_ref[...].astype(F32), 0, 1)
    out_ref[pl.ds(0, cy * chans)] = turned.reshape(cy * chans, nz).astype(BF16)
    cells = cells_ref[...]
    slots = cells.shape[1]
    nl = -(-slots // nz)
    tail = out_ref.shape[0] - cy * chans
    lines = []
    for values in (cells // nz, cells % nz):
        values = values.astype(F32)
        if nl * nz > slots:
            values = jnp.concatenate([values, jnp.zeros((1, nl * nz - slots), F32)], axis=1)
        lines += [values[:, n * nz : (n + 1) * nz] for n in range(nl)]
    if tail > 2 * nl:
        lines.append(jnp.zeros((tail - 2 * nl, nz), F32))
    out_ref[pl.ds(cy * chans, tail)] = jnp.concatenate(lines, axis=0).astype(BF16)


def pick_kernel(ngx, ngy, cap, counts_ref, rows_ref, plane_ref, out_ref):
    ndev = ngx * ngy
    nrows, feats = rows_ref.shape
    slots = ndev * cap
    counts = counts_ref[...].astype(F32)
    slot = lax.broadcasted_iota(I32, (slots, ndev), 0)
    lane = lax.broadcasted_iota(I32, (slots, ndev), 1)
    owner = slot // cap
    start = jnp.sum(jnp.where(lane < owner, counts, 0.0), axis=1, keepdims=True)
    held = jnp.sum(jnp.where(lane == owner, counts, 0.0), axis=1, keepdims=True)
    place = (lax.broadcasted_iota(I32, (slots, nrows), 0) % cap).astype(F32)
    row = lax.broadcasted_iota(I32, (slots, nrows), 1).astype(F32)
    onehot = jnp.where((row == place + start) & (place < held), 1.0, 0.0).astype(BF16)
    raw = mm(onehot, rows_ref[...]).reshape(ngx, ngy, cap, feats)
    parts = [rolled(raw, dx, 0).reshape(ndev, cap, feats) for dx in (-1, 0, 1)]
    out_ref[...] = jnp.stack(parts, axis=1).reshape(out_ref.shape).astype(BF16)


def paint_kernel(
    ndev, cap, chans, cy, nz,
    recv_ref, own_ref, west_ref, east_ref, proj_t_ref, cot_ref,
    x_ref, first_ref, last_ref, masked,
):
    slots = ndev * cap
    nl = -(-slots // nz)
    raws = rows_in(recv_ref, ndev, cap)
    for dx, ref in enumerate((west_ref, own_ref, east_ref)):
        lanes = pl.ds(dx * chans, chans)
        y, z = widths(nl, slots, ref[pl.ds(cy * chans, ref.shape[0] - cy * chans)])
        values = mm(proj_t_ref[...], raws[dx], NT).astype(BF16)
        for n in range(cy):
            masked[pl.ds(n * chans, chans)] = values * jnp.where(y == n, 1.0, 0.0).astype(BF16)
        painted = mm(masked[...], picked_depth(z, nz), NT)
        for n in range(cy):
            rows = pl.ds(n * chans, chans)
            part = painted[n * chans : (n + 1) * chans]
            field = (ref[rows].astype(F32) + part).astype(BF16)
            x_ref[n, lanes] = field
            if n < 2:
                first_ref[pl.ds((3 * n + dx) * chans, chans)] = field
            if n >= cy - 2:
                last_ref[pl.ds((3 * (n - cy + 2) + dx) * chans, chans)] = field
    first_ref[pl.ds(6 * chans, chans)] = cot_ref[0]
    last_ref[pl.ds(6 * chans, chans)] = cot_ref[cy - 1]


def list_of(ref, cy, chans, slots):
    tail = ref.shape[0] - cy * chans
    return widths(-(-slots // ref.shape[1]), slots, ref[pl.ds(cy * chans, tail)])


def conv_kernel(
    ndev, cap, chans, cy, x_ref, cot_ref, wf_ref, wb_ref, own_ref, west_ref, east_ref,
    out_ref, total_ref, pre_ref, slot_ref, sums_ref, acc, grads, back, plane,
):
    rows = 3 * chans
    nz = x_ref.shape[2]
    slots = ndev * cap
    own = pl.ds(chans, chans)
    zeros = jnp.zeros((rows, nz), BF16)
    for t in (0, 1, cy, cy + 1):
        grads[t] = zeros
    out_ref[0] = zeros[:chans]
    out_ref[cy - 1] = zeros[:chans]
    acc[0] = jnp.zeros((rows, nz), F32)

    def spread(n):
        terms = mm(wf_ref[...], x_ref[n])
        acc[n + 1] = terms[:rows]
        acc[n] += terms[rows : 2 * rows]
        return terms[2 * rows :]

    pre_ref[0] = spread(0)
    pre_ref[1] = acc[0] + spread(1)

    def forward(n, carry):
        done = spread(n) + acc[n - 1]
        y = n - 1
        out, grad = finish_row(done, x_ref[y, own], cot_ref[y])
        out_ref[y] = out
        grads[y + 1] = stacked(grad)
        return carry

    lax.fori_loop(2, cy, forward, 0, unroll=2)
    pre_ref[2] = acc[cy - 1]
    pre_ref[3] = acc[cy]
    total_ref[...] = jnp.zeros_like(total_ref)
    back[0] = jnp.zeros((rows, nz), F32)
    back[1] = jnp.zeros((rows, nz), F32)

    def taps(n):
        window = grads[pl.ds(n, 3)].reshape(3 * rows, nz)
        total_ref[...] += mm(window, x_ref[n], NT)

    def spread_back(n):
        terms = mm(wb_ref[...], grads[n + 1])
        back[n + 1] = terms[2 * rows :]
        back[n] += terms[rows : 2 * rows]
        return terms[:rows]

    def backward(n, carry):
        taps(n)
        value = spread_back(n) + back[n - 1]
        for dx in range(3):
            part = value[dx * chans : (dx + 1) * chans]
            if dx == 1:
                part = part + cot_ref[n - 1].astype(F32)
            plane[dx, pl.ds((n - 3) * chans, chans)] = part.astype(BF16)
        return carry

    taps(0)
    taps(1)
    slot_ref[0] = spread_back(1)
    taps(2)
    slot_ref[1] = spread_back(2) + back[1]
    lax.fori_loop(3, cy - 1, backward, 0, unroll=2)
    taps(cy - 1)
    slot_ref[2] = back[cy - 2]
    slot_ref[3] = back[cy - 1]
    zero = jnp.zeros((chans, slots), F32)
    for dx, ref in enumerate((west_ref, own_ref, east_ref)):
        sums_ref[dx] = at_slots(plane[dx], list_of(ref, cy, chans, slots), range(2, cy - 2), zero)


def at_slots(part, cells, first, total):
    chans = total.shape[0]
    y, z = cells
    found = mm(part, picked_depth(z, part.shape[1]))
    for n, row in enumerate(first):
        total = total + jnp.where(y == row, found[n * chans : (n + 1) * chans], 0.0)
    return total


def edge_kernel(
    ndev, cap, chans, cy,
    pre_ref, slot_ref, sums_ref, total_ref, north_ref, south_ref, first_ref, last_ref,
    wf_ref, wb_ref, cot_ref, own_ref, west_ref, east_ref, recv_ref,
    out_ref, send_ref, total,
):
    rows = 3 * chans
    slots = ndev * cap
    own = slice(chans, 2 * chans)
    fields = [ref[pl.ds(n * rows, rows)] for ref in (north_ref, first_ref, last_ref, south_ref) for n in (0, 1)]
    cots = [ref[pl.ds(2 * rows, chans)] for ref in (north_ref, first_ref, last_ref, south_ref)]
    near = mm(wf_ref[pl.ds(0, 2 * rows)], fields[1])
    pre = [pre_ref[0] + near[rows:] + mm(wf_ref[pl.ds(0, rows)], fields[0]), pre_ref[1] + near[:rows]]
    near = mm(wf_ref[pl.ds(rows, 2 * rows)], fields[6])
    pre += [pre_ref[2] + near[rows:], pre_ref[3] + near[:rows] + mm(wf_ref[pl.ds(2 * rows, rows)], fields[7])]
    at = (1, 2, 5, 6)
    ends = [finish_row(pre[n], fields[at[n]][own], cots[n]) for n in range(4)]
    out_ref[0], out_ref[1] = ends[1][0], ends[2][0]
    grads = [stacked(grad) for _, grad in ends]
    for n in range(3):
        here = pl.ds(n * rows, rows)
        total[here] = total_ref[here] + (mm(grads[1], fields[3 - n], NT) + mm(grads[2], fields[6 - n], NT))
    inner = mm(wb_ref[pl.ds(rows, 2 * rows)], grads[1])
    top = slot_ref[0] + inner[:rows] + mm(wb_ref[pl.ds(2 * rows, rows)], grads[0])
    second = slot_ref[1] + inner[rows:]
    inner = mm(wb_ref[pl.ds(0, 2 * rows)], grads[2])
    third = slot_ref[2] + inner[:rows]
    bottom = slot_ref[3] + inner[rows:] + mm(wb_ref[pl.ds(0, rows)], grads[3])
    found = []
    for dx, ref in enumerate((west_ref, own_ref, east_ref)):
        parts = [value[dx * chans : (dx + 1) * chans] for value in (top, second, third, bottom)]
        if dx == 1:
            inner = (cots[1], cot_ref[1], cot_ref[cy - 2], cots[2])
            parts = [part + cot.astype(F32) for part, cot in zip(parts, inner)]
        part = jnp.concatenate(parts, axis=0).astype(BF16)
        cells = list_of(ref, cy, chans, slots)
        found.append(at_slots(part, cells, (0, 1, cy - 2, cy - 1), sums_ref[dx]))
    raws = rows_in(recv_ref, ndev, cap)
    proj = sum(mm(found[dx].astype(BF16), raws[dx]) for dx in range(3))
    proj_high = proj.astype(BF16).astype(F32)
    sides = jnp.concatenate([found[0], found[2]], axis=0).T
    middle = jnp.concatenate([found[1], jnp.zeros_like(found[1])], axis=0).T
    width = send_ref.shape[1]
    share = send_ref.shape[0] // ndev - 2 * cap
    taps = total[:, 2 * chans :]
    half = 3 * rows // 2
    taps = jnp.concatenate([taps[:half], taps[half:]], axis=1)
    halves = [v.reshape(2 * chans // share, share // 2, width) for v in (proj_high, proj - proj_high)]
    proj = jnp.stack(halves, axis=1).reshape(2 * chans, width)
    pad = jnp.zeros((share * ndev - 3 * rows - half - 2 * chans, width), F32)
    sums = jnp.concatenate([total[:, : 2 * chans], taps, proj, pad], axis=0)
    out = jnp.concatenate(
        [
            sums.reshape(ndev, share, width),
            sides.reshape(ndev, cap, width),
            middle.reshape(ndev, cap, width),
        ],
        axis=1,
    )
    send_ref[...] = out.reshape(send_ref.shape).astype(BF16)


def rows_kernel(
    ngx, ngy, cap, chans, recv_ref, index_ref, counts_ref, proj_t_ref, rows_ref, sums_ref
):
    ndev = ngx * ngy
    nrows = rows_ref.shape[0]
    width = recv_ref.shape[1]
    slots = ndev * cap
    share = recv_ref.shape[0] // ndev - 2 * cap
    arrived = recv_ref[...].astype(F32).reshape(ndev, share + 2 * cap, width)
    sums = jnp.sum(arrived[:, :share], axis=0)
    half = share // 2
    whole = sums[:half] + sums[half:]
    high = whole.astype(BF16).astype(F32)
    split = jnp.concatenate([high, whole - high], axis=0)
    device = jnp.broadcast_to(index_ref[...], sums.shape)
    sums = jnp.where(device * share >= 27 * chans * chans // width, split, sums)
    sums_ref[...] = jnp.broadcast_to(sums[None], (ndev, share, width)).reshape(
        sums_ref.shape
    ).astype(BF16)
    sides = arrived[:, share : share + cap].reshape(ngx, ngy, cap, width)
    left = lax.broadcasted_iota(I32, sides.shape, 3) < chans
    sides = jnp.where(left, rolled(sides, 1, 0), rolled(sides, -1, 0)).reshape(slots, width)
    middle = arrived[:, share + cap :].reshape(slots, width)
    counts = counts_ref[...].astype(F32)
    place = lax.broadcasted_iota(I32, (nrows, ndev), 0).astype(F32)
    lane = lax.broadcasted_iota(I32, (ndev, ndev), 1)
    upto = lax.broadcasted_iota(I32, (ndev, ndev), 0) <= lane
    ends = mm(counts.astype(BF16), jnp.where(upto, 1.0, 0.0).astype(BF16))
    before = ends <= place
    owner = jnp.sum(jnp.where(before, 1.0, 0.0), axis=1, keepdims=True)
    start = jnp.sum(jnp.where(before, counts, 0.0), axis=1, keepdims=True)
    slot = owner * cap + place[:, :1] - start
    onehot = jnp.where(
        lax.broadcasted_iota(I32, (nrows, slots), 1).astype(F32) == slot, 1.0, 0.0
    ).astype(BF16)
    proj_t = proj_t_ref[...]
    both = jnp.concatenate([proj_t, proj_t], axis=0)
    sides = mm(onehot, sides.astype(BF16)).astype(BF16)
    middle = mm(onehot, middle.astype(BF16)).astype(BF16)
    rows_ref[...] = mm(sides, both) + mm(middle, both)


def finish_kernel(conv_scale, proj_scale, share, recv_ref, conv_ref, proj_ref):
    taps, chans, _ = conv_ref.shape
    rows = 9 * chans
    half = rows // 2
    packed = recv_ref[pl.ds(rows, half)].astype(F32)
    column = jnp.concatenate([packed[:, :chans], packed[:, chans:]], axis=0)
    for b in range(3):
        for dz in range(3):
            first = (b * 3 + dz) * chans
            block = recv_ref[pl.ds(first, chans)].astype(F32)
            k = (2 - b) * 3 + dz
            conv_ref[k] = block[:, :chans] * conv_scale
            conv_ref[9 + k] = block[:, chans:] * conv_scale
            conv_ref[18 + k] = column[first : first + chans] * conv_scale
    width = recv_ref.shape[1]
    terms = recv_ref[pl.ds(rows + half, 2 * chans)].astype(F32)
    terms = terms.reshape(2 * chans // share, 2, share // 2, width)
    proj_ref[...] = jnp.sum(terms, axis=1).reshape(chans, width) * proj_scale


def local(particles, send_counts, cell_lists, base_field, proj_weight, conv_weight, cotangent):
    ngx, ngy = lax.axis_size("gx"), lax.axis_size("gy")
    ndev = ngx * ngy
    nrows, feats = particles.shape
    chans, cx, cy, nz = base_field.shape
    slots = cell_lists.shape[1]
    cap = slots // ndev
    count = cx * cy * nz
    assert cx == 1 and feats == 2 * chans
    proj_t = proj_weight.T
    move = functools.partial(send, ngx=ngx, ngy=ngy)
    rows = 3 * chans
    one = 2 * rows * rows * nz

    tail = -(-2 * -(-slots // nz) // 16) * 16
    plane, particles, counts = call(
        plane_kernel,
        [shape((cy * chans + tail, nz), BF16), particles, send_counts],
        (base_field.reshape(chans, cy, nz), cell_lists, particles, send_counts),
        1000,
    )
    west, east = move(plane, 1, 0), move(plane, -1, 0)
    (payload,) = call(
        functools.partial(pick_kernel, ngx, ngy, cap),
        [shape((ndev * 3 * cap, feats), BF16)],
        (counts, particles, plane),
        2 * slots * nrows * feats,
    )
    recv = exchange(payload, ndev)

    cot = cotangent[:, 0].transpose(1, 0, 2)
    taps = conv_weight.reshape(3, 3, 3, chans, chans)
    wf = taps.transpose(1, 2, 3, 0, 4).reshape(9 * chans, rows)
    wb = taps.transpose(1, 0, 4, 2, 3).reshape(9 * chans, rows)

    x_all, first, last = call(
        functools.partial(paint_kernel, ndev, cap, chans, cy, nz),
        [shape((cy, rows, nz), BF16)] + [shape((2 * rows + chans, nz), BF16)] * 2,
        (recv, plane, west, east, proj_t, cot),
        6 * slots * count * chans,
        (pltpu.VMEM((cy * chans, slots), BF16),),
    )
    north, south = move(last, 0, 1), move(first, 0, -1)
    out_rows, total, pre_edge, slot_edge, sums = call(
        functools.partial(conv_kernel, ndev, cap, chans, cy),
        [
            shape((cy, chans, nz), BF16),
            shape((9 * chans, rows), F32),
            shape((4, rows, nz), F32),
            shape((4, rows, nz), F32),
            shape((3, chans, slots), F32),
        ],
        (x_all, cot, wf, wb, plane, west, east),
        3 * cy * 3 * one,
        (
            pltpu.VMEM((cy + 1, rows, nz), F32),
            pltpu.VMEM((cy + 2, rows, nz), BF16),
            pltpu.VMEM((cy, rows, nz), F32),
            pltpu.VMEM((3, (cy - 4) * chans, nz), BF16),
        ),
    )
    grad_rows = 27 * chans * chans // feats
    share = -(-(grad_rows + 2 * chans) // (16 * ndev)) * 16
    out_edge, payload = call(
        functools.partial(edge_kernel, ndev, cap, chans, cy),
        [shape((2, chans, nz), BF16), shape((ndev * (share + 2 * cap), feats), BF16)],
        (
            pre_edge, slot_edge, sums, total, north, south, first, last,
            wf, wb, cot, plane, west, east, recv,
        ),
        12 * one,
        (pltpu.VMEM((9 * chans, rows), F32),),
    )
    recv = exchange(payload, ndev)
    index = (lax.axis_index("gx") * ngy + lax.axis_index("gy")).astype(I32).reshape(1, 1)
    row_grads, sums = call(
        functools.partial(rows_kernel, ngx, ngy, cap, chans),
        [shape((nrows, feats), F32), shape((ndev * share, feats), BF16)],
        (recv, index, counts, proj_t),
        2 * nrows * slots * chans,
    )
    recv = exchange(sums, ndev)
    conv_grad, proj_grad = call(
        functools.partial(
            finish_kernel, 1.0 / math.sqrt(count * ndev), 1.0 / math.sqrt(nrows * ndev), share
        ),
        [shape((27, chans, chans), F32), shape((chans, feats), F32)],
        (recv,),
        1000,
    )
    out_field = jnp.concatenate([out_edge[:1], out_rows[1 : cy - 1], out_edge[1:]], axis=0)
    return (out_field.transpose(1, 0, 2)[:, None], row_grads, conv_grad, proj_grad.T)


def solution(mesh):
    in_specs = (
        P(("gx", "gy"), None),
        P(("gx", "gy"), None),
        P(("gx", "gy"), None),
        P(None, "gx", "gy", None),
        P(),
        P(),
        P(None, "gx", "gy", None),
    )
    out_specs = (P(None, "gx", "gy", None), P(("gx", "gy"), None), P(), P())
    return jax.shard_map(local, mesh=mesh, in_specs=in_specs, out_specs=out_specs, check_vma=False)
```

```python
import functools
import math

import jax
import jax.numpy as jnp
from jax import lax
from jax.experimental import pallas as pl
from jax.experimental.pallas import tpu as pltpu
from jax.sharding import PartitionSpec as P

AXES = ("gx", "gy")
F32, BF16, I32 = jnp.float32, jnp.bfloat16, jnp.int32
LIMIT = 40 * 1024 * 1024
NT = (((1,), (1,)), ((), ()))
NN = (((1,), (0,)), ((), ()))


def mm(a, b, dims=NN):
    return lax.dot_general(a, b, dims, preferred_element_type=F32)


def call(kernel, outs, args, flops, scratch=(), far=(), far_out=(), aliases=None):
    traffic = sum(math.prod(a.shape) * a.dtype.itemsize for a in (*args, *outs))
    near = pl.BlockSpec(memory_space=pltpu.VMEM)
    there = pl.BlockSpec(memory_space=pltpu.HBM)
    return pl.pallas_call(
        kernel,
        out_shape=[jax.ShapeDtypeStruct(o.shape, o.dtype) for o in outs],
        in_specs=[there if n in far else near for n in range(len(args))],
        out_specs=[there if n in far_out else near for n in range(len(outs))],
        scratch_shapes=list(scratch),
        input_output_aliases=aliases or {},
        compiler_params=pltpu.CompilerParams(vmem_limit_bytes=LIMIT),
        cost_estimate=pl.CostEstimate(flops=flops, bytes_accessed=traffic, transcendentals=0),
    )(*args)


def shape(dims, dtype):
    return jax.ShapeDtypeStruct(dims, dtype)


def send(block, di, dj, ngx, ngy):
    pairs = []
    for i in range(ngx):
        for j in range(ngy):
            pairs.append((i * ngy + j, ((i + di) % ngx) * ngy + (j + dj) % ngy))
    return lax.ppermute(block, AXES, pairs)


def exchange(payload, ndev):
    rows, width = payload.shape
    moved = lax.all_to_all(
        payload.reshape(ndev, rows // ndev, width), AXES, split_axis=0, concat_axis=0, tiled=True
    )
    return moved.reshape(rows, width)


def rolled(x, di, dj):
    for axis, shift in ((0, di), (1, dj)):
        if shift == 1:
            head, tail = lax.slice_in_dim(x, 1, None, axis=axis), lax.slice_in_dim(x, 0, 1, axis=axis)
            x = jnp.concatenate([head, tail], axis=axis)
        elif shift == -1:
            count = x.shape[axis]
            head = lax.slice_in_dim(x, count - 1, count, axis=axis)
            x = jnp.concatenate([head, lax.slice_in_dim(x, 0, count - 1, axis=axis)], axis=axis)
    return x


def widths(nl, slots, block):
    block = block.astype(F32)
    y = jnp.concatenate([block[n : n + 1] for n in range(nl)], axis=1)[:, :slots]
    z = jnp.concatenate([block[nl + n : nl + n + 1] for n in range(nl)], axis=1)[:, :slots]
    return y.astype(I32), z.astype(I32)


def picked_depth(z, nz):
    depth = lax.broadcasted_iota(I32, (nz, z.shape[1]), 0)
    return jnp.where(depth == z, 1.0, 0.0).astype(BF16)


def rows_in(recv_ref, ndev, cap):
    width = recv_ref.shape[1]
    arrived = recv_ref[...].astype(F32).reshape(ndev, 3, cap, width)
    return [arrived[:, n].reshape(ndev * cap, width).astype(BF16) for n in range(3)]


def stacked(grad):
    nz = grad.shape[1]
    wide = grad.astype(F32)
    return jnp.concatenate(
        [pltpu.roll(wide, nz - 1, 1), wide, pltpu.roll(wide, 1, 1)], axis=0
    ).astype(BF16)


def finish_row(acc, field, cot):
    chans, nz = field.shape
    pre = acc[chans : 2 * chans]
    pre = pre + pltpu.roll(acc[:chans], 1, 1) + pltpu.roll(acc[2 * chans :], nz - 1, 1)
    sig = jax.nn.sigmoid(pre)
    out = field.astype(F32) + pre * sig
    grad = cot.astype(F32) * sig * (1.0 + pre * (1.0 - sig))
    return out.astype(BF16), grad.astype(BF16)


def first_kernel(
    ngx, ngy, cap, base_far, cells_far, rows_far, counts_far,
    out_ref, send_ref, base_ref, cells_ref, rows_ref, counts_ref, sems,
):
    pairs = (
        (rows_far, rows_ref), (counts_far, counts_ref), (cells_far, cells_ref), (base_far, base_ref)
    )
    copies = [pltpu.make_async_copy(src, dst, sems.at[n]) for n, (src, dst) in enumerate(pairs)]
    for copy in copies:
        copy.start()
    chans, cy, nz = base_ref.shape
    for copy in copies[:3]:
        copy.wait()
    pick(ngx, ngy, cap, counts_ref, rows_ref, send_ref)
    cells = cells_ref[...]
    slots = cells.shape[1]
    nl = -(-slots // nz)
    tail = out_ref.shape[0] - cy * chans
    lines = []
    for values in (cells // nz, cells % nz):
        values = values.astype(F32)
        if nl * nz > slots:
            values = jnp.concatenate([values, jnp.zeros((1, nl * nz - slots), F32)], axis=1)
        lines += [values[:, n * nz : (n + 1) * nz] for n in range(nl)]
    if tail > 2 * nl:
        lines.append(jnp.zeros((tail - 2 * nl, nz), F32))
    out_ref[pl.ds(cy * chans, tail)] = jnp.concatenate(lines, axis=0).astype(BF16)
    copies[3].wait()
    turned = jnp.swapaxes(base_ref[...].astype(F32), 0, 1)
    out_ref[pl.ds(0, cy * chans)] = turned.reshape(cy * chans, nz).astype(BF16)


def same_kernel(in_ref, out_ref):
    pass


def pick(ngx, ngy, cap, counts_ref, rows_ref, out_ref):
    ndev = ngx * ngy
    nrows, feats = rows_ref.shape
    slots = ndev * cap
    counts = counts_ref[...].astype(F32)
    slot = lax.broadcasted_iota(I32, (slots, ndev), 0)
    lane = lax.broadcasted_iota(I32, (slots, ndev), 1)
    owner = slot // cap
    start = jnp.sum(jnp.where(lane < owner, counts, 0.0), axis=1, keepdims=True)
    held = jnp.sum(jnp.where(lane == owner, counts, 0.0), axis=1, keepdims=True)
    place = (lax.broadcasted_iota(I32, (slots, nrows), 0) % cap).astype(F32)
    row = lax.broadcasted_iota(I32, (slots, nrows), 1).astype(F32)
    onehot = jnp.where((row == place + start) & (place < held), 1.0, 0.0).astype(BF16)
    raw = mm(onehot, rows_ref[...]).reshape(ngx, ngy, cap, feats)
    parts = [rolled(raw, dx, 0).reshape(ndev, cap, feats) for dx in (-1, 0, 1)]
    out_ref[...] = jnp.stack(parts, axis=1).reshape(out_ref.shape).astype(BF16)


def painted_rows(values, cells, nz, ns, masked):
    chans = values.shape[0]
    y, z = cells
    for n, row in enumerate(ns):
        masked[pl.ds(n * chans, chans)] = values * jnp.where(y == row, 1.0, 0.0).astype(BF16)
    return mm(masked[pl.ds(0, len(ns) * chans)], picked_depth(z, nz), NT)


def outer_kernel(
    ndev, cap, chans, cy, recv_ref, own_ref, west_ref, east_ref, proj_t_ref, cot_ref,
    first_ref, last_ref, masked,
):
    slots = ndev * cap
    nz = own_ref.shape[1]
    raws = rows_in(recv_ref, ndev, cap)
    ns = (0, 1, cy - 2, cy - 1)
    for dx, ref in enumerate((west_ref, own_ref, east_ref)):
        values = mm(proj_t_ref[...], raws[dx], NT).astype(BF16)
        painted = painted_rows(values, list_of(ref, cy, chans, slots), nz, ns, masked)
        for n, row in enumerate(ns):
            part = painted[n * chans : (n + 1) * chans]
            field = (ref[pl.ds(row * chans, chans)].astype(F32) + part).astype(BF16)
            target = first_ref if n < 2 else last_ref
            target[pl.ds((3 * (n % 2) + dx) * chans, chans)] = field
    first_ref[pl.ds(6 * chans, chans)] = cot_ref[0]
    last_ref[pl.ds(6 * chans, chans)] = cot_ref[cy - 1]


def list_of(ref, cy, chans, slots):
    tail = ref.shape[0] - cy * chans
    return widths(-(-slots // ref.shape[1]), slots, ref[pl.ds(cy * chans, tail)])


def conv_kernel(
    ndev, cap, chans, cy, recv_ref, proj_t_ref, cot_ref, wf_ref, wb_ref, own_ref, west_ref, east_ref,
    out_ref, total_ref, pre_ref, slot_ref, sums_ref, x_ref, acc, grads, back, plane, masked,
):
    rows = 3 * chans
    nz = x_ref.shape[2]
    slots = ndev * cap
    raws = rows_in(recv_ref, ndev, cap)
    for dx, ref in enumerate((west_ref, own_ref, east_ref)):
        values = mm(proj_t_ref[...], raws[dx], NT).astype(BF16)
        painted = painted_rows(values, list_of(ref, cy, chans, slots), nz, range(cy), masked)
        for n in range(cy):
            part = painted[n * chans : (n + 1) * chans]
            field = ref[pl.ds(n * chans, chans)].astype(F32) + part
            x_ref[n, pl.ds(dx * chans, chans)] = field.astype(BF16)
    own = pl.ds(chans, chans)
    zeros = jnp.zeros((rows, nz), BF16)
    for t in (0, 1, cy, cy + 1):
        grads[t] = zeros
    out_ref[0] = zeros[:chans]
    out_ref[cy - 1] = zeros[:chans]
    acc[0] = jnp.zeros((rows, nz), F32)

    def spread(n):
        terms = mm(wf_ref[...], x_ref[n])
        acc[n + 1] = terms[:rows]
        acc[n] += terms[rows : 2 * rows]
        return terms[2 * rows :]

    pre_ref[0] = spread(0)
    pre_ref[1] = acc[0] + spread(1)

    def forward(n, carry):
        done = spread(n) + acc[n - 1]
        y = n - 1
        out, grad = finish_row(done, x_ref[y, own], cot_ref[y])
        out_ref[y] = out
        grads[y + 1] = stacked(grad)
        return carry

    lax.fori_loop(2, cy, forward, 0, unroll=2)
    pre_ref[2] = acc[cy - 1]
    pre_ref[3] = acc[cy]
    total_ref[...] = jnp.zeros_like(total_ref)
    back[0] = jnp.zeros((rows, nz), F32)
    back[1] = jnp.zeros((rows, nz), F32)

    def taps(n):
        window = grads[pl.ds(n, 3)].reshape(3 * rows, nz)
        total_ref[...] += mm(window, x_ref[n], NT)

    def spread_back(n):
        terms = mm(wb_ref[...], grads[n + 1])
        back[n + 1] = terms[2 * rows :]
        back[n] += terms[rows : 2 * rows]
        return terms[:rows]

    def backward(n, carry):
        taps(n)
        value = spread_back(n) + back[n - 1]
        for dx in range(3):
            part = value[dx * chans : (dx + 1) * chans]
            if dx == 1:
                part = part + cot_ref[n - 1].astype(F32)
            plane[dx, pl.ds((n - 3) * chans, chans)] = part.astype(BF16)
        return carry

    taps(0)
    taps(1)
    slot_ref[0] = spread_back(1)
    taps(2)
    slot_ref[1] = spread_back(2) + back[1]
    lax.fori_loop(3, cy - 1, backward, 0, unroll=2)
    taps(cy - 1)
    slot_ref[2] = back[cy - 2]
    slot_ref[3] = back[cy - 1]
    zero = jnp.zeros((chans, slots), F32)
    for dx, ref in enumerate((west_ref, own_ref, east_ref)):
        sums_ref[dx] = at_slots(plane[dx], list_of(ref, cy, chans, slots), range(2, cy - 2), zero)


def at_slots(part, cells, first, total):
    chans = total.shape[0]
    y, z = cells
    found = mm(part, picked_depth(z, part.shape[1]))
    for n, row in enumerate(first):
        total = total + jnp.where(y == row, found[n * chans : (n + 1) * chans], 0.0)
    return total


def edge_kernel(
    ndev, cap, chans, cy,
    pre_ref, slot_ref, sums_ref, total_ref, north_ref, south_ref, first_ref, last_ref,
    wf_ref, wb_ref, cot_ref, own_ref, west_ref, east_ref, recv_ref,
    out_ref, send_far, total, sums_send, slots_send, sems,
):
    rows = 3 * chans
    slots = ndev * cap
    own = slice(chans, 2 * chans)
    fields = [ref[pl.ds(n * rows, rows)] for ref in (north_ref, first_ref, last_ref, south_ref) for n in (0, 1)]
    cots = [ref[pl.ds(2 * rows, chans)] for ref in (north_ref, first_ref, last_ref, south_ref)]
    near = mm(wf_ref[pl.ds(0, 2 * rows)], fields[1])
    pre = [pre_ref[0] + near[rows:] + mm(wf_ref[pl.ds(0, rows)], fields[0]), pre_ref[1] + near[:rows]]
    near = mm(wf_ref[pl.ds(rows, 2 * rows)], fields[6])
    pre += [pre_ref[2] + near[rows:], pre_ref[3] + near[:rows] + mm(wf_ref[pl.ds(2 * rows, rows)], fields[7])]
    at = (1, 2, 5, 6)
    ends = [finish_row(pre[n], fields[at[n]][own], cots[n]) for n in range(4)]
    out_ref[0], out_ref[1] = ends[1][0], ends[2][0]
    grads = [stacked(grad) for _, grad in ends]
    for n in range(3):
        here = pl.ds(n * rows, rows)
        total[here] = total_ref[here] + (mm(grads[1], fields[3 - n], NT) + mm(grads[2], fields[6 - n], NT))
    inner = mm(wb_ref[pl.ds(rows, 2 * rows)], grads[1])
    top = slot_ref[0] + inner[:rows] + mm(wb_ref[pl.ds(2 * rows, rows)], grads[0])
    second = slot_ref[1] + inner[rows:]
    inner = mm(wb_ref[pl.ds(0, 2 * rows)], grads[2])
    third = slot_ref[2] + inner[:rows]
    bottom = slot_ref[3] + inner[rows:] + mm(wb_ref[pl.ds(0, rows)], grads[3])
    found = []
    for dx, ref in enumerate((west_ref, own_ref, east_ref)):
        parts = [value[dx * chans : (dx + 1) * chans] for value in (top, second, third, bottom)]
        if dx == 1:
            inner = (cots[1], cot_ref[1], cot_ref[cy - 2], cots[2])
            parts = [part + cot.astype(F32) for part, cot in zip(parts, inner)]
        part = jnp.concatenate(parts, axis=0).astype(BF16)
        cells = list_of(ref, cy, chans, slots)
        found.append(at_slots(part, cells, (0, 1, cy - 2, cy - 1), sums_ref[dx]))
    raws = rows_in(recv_ref, ndev, cap)
    proj = sum(mm(found[dx].astype(BF16), raws[dx]) for dx in range(3))
    proj_high = proj.astype(BF16).astype(F32)
    sides = jnp.concatenate([found[0], found[2]], axis=0).T
    middle = jnp.concatenate([found[1], jnp.zeros_like(found[1])], axis=0).T
    width = send_far.shape[2]
    share = send_far.shape[1] - 2 * cap
    taps = total[:, 2 * chans :]
    half = 3 * rows // 2
    taps = jnp.concatenate([taps[:half], taps[half:]], axis=1)
    halves = [v.reshape(2 * chans // share, share // 2, width) for v in (proj_high, proj - proj_high)]
    proj = jnp.stack(halves, axis=1).reshape(2 * chans, width)
    pad = jnp.zeros((share * ndev - 3 * rows - half - 2 * chans, width), F32)
    sums = jnp.concatenate([total[:, : 2 * chans], taps, proj, pad], axis=0)
    sums_send[...] = sums.reshape(sums_send.shape).astype(BF16)
    back = [sides.reshape(ndev, cap, width), middle.reshape(ndev, cap, width)]
    slots_send[...] = jnp.concatenate(back, axis=1).astype(BF16)
    copies = [
        pltpu.make_async_copy(sums_send, send_far.at[:, pl.ds(0, share)], sems.at[0]),
        pltpu.make_async_copy(slots_send, send_far.at[:, pl.ds(share, 2 * cap)], sems.at[1]),
    ]
    for copy in copies:
        copy.start()
    for copy in copies:
        copy.wait()


def rows_kernel(
    ngx, ngy, cap, chans, recv_ref, index_ref, counts_ref, proj_t_ref, rows_ref, sums_ref
):
    ndev = ngx * ngy
    nrows = rows_ref.shape[0]
    width = recv_ref.shape[1]
    slots = ndev * cap
    share = recv_ref.shape[0] // ndev - 2 * cap
    arrived = recv_ref[...].astype(F32).reshape(ndev, share + 2 * cap, width)
    sums = jnp.sum(arrived[:, :share], axis=0)
    half = share // 2
    whole = sums[:half] + sums[half:]
    high = whole.astype(BF16).astype(F32)
    split = jnp.concatenate([high, whole - high], axis=0)
    device = jnp.broadcast_to(index_ref[...], sums.shape)
    sums = jnp.where(device * share >= 27 * chans * chans // width, split, sums)
    sums_ref[...] = jnp.broadcast_to(sums[None], (ndev, share, width)).reshape(
        sums_ref.shape
    ).astype(BF16)
    sides = arrived[:, share : share + cap].reshape(ngx, ngy, cap, width)
    left = lax.broadcasted_iota(I32, sides.shape, 3) < chans
    sides = jnp.where(left, rolled(sides, 1, 0), rolled(sides, -1, 0)).reshape(slots, width)
    middle = arrived[:, share + cap :].reshape(slots, width)
    counts = counts_ref[...].astype(F32)
    place = lax.broadcasted_iota(I32, (nrows, ndev), 0).astype(F32)
    lane = lax.broadcasted_iota(I32, (ndev, ndev), 1)
    upto = lax.broadcasted_iota(I32, (ndev, ndev), 0) <= lane
    ends = mm(counts.astype(BF16), jnp.where(upto, 1.0, 0.0).astype(BF16))
    before = ends <= place
    owner = jnp.sum(jnp.where(before, 1.0, 0.0), axis=1, keepdims=True)
    start = jnp.sum(jnp.where(before, counts, 0.0), axis=1, keepdims=True)
    slot = owner * cap + place[:, :1] - start
    onehot = jnp.where(
        lax.broadcasted_iota(I32, (nrows, slots), 1).astype(F32) == slot, 1.0, 0.0
    ).astype(BF16)
    proj_t = proj_t_ref[...]
    both = jnp.concatenate([proj_t, proj_t], axis=0)
    sides = mm(onehot, sides.astype(BF16)).astype(BF16)
    middle = mm(onehot, middle.astype(BF16)).astype(BF16)
    rows_ref[...] = mm(sides, both) + mm(middle, both)


def finish_kernel(conv_scale, proj_scale, share, recv_ref, conv_ref, proj_ref):
    taps, chans, _ = conv_ref.shape
    rows = 9 * chans
    half = rows // 2
    packed = recv_ref[pl.ds(rows, half)].astype(F32)
    column = jnp.concatenate([packed[:, :chans], packed[:, chans:]], axis=0)
    for b in range(3):
        for dz in range(3):
            first = (b * 3 + dz) * chans
            block = recv_ref[pl.ds(first, chans)].astype(F32)
            k = (2 - b) * 3 + dz
            conv_ref[k] = block[:, :chans] * conv_scale
            conv_ref[9 + k] = block[:, chans:] * conv_scale
            conv_ref[18 + k] = column[first : first + chans] * conv_scale
    width = recv_ref.shape[1]
    terms = recv_ref[pl.ds(rows + half, 2 * chans)].astype(F32)
    terms = terms.reshape(2 * chans // share, 2, share // 2, width)
    proj_ref[...] = jnp.sum(terms, axis=1).reshape(chans, width) * proj_scale


def local(particles, send_counts, cell_lists, base_field, proj_weight, conv_weight, cotangent):
    ngx, ngy = lax.axis_size("gx"), lax.axis_size("gy")
    ndev = ngx * ngy
    nrows, feats = particles.shape
    chans, cx, cy, nz = base_field.shape
    slots = cell_lists.shape[1]
    cap = slots // ndev
    count = cx * cy * nz
    assert cx == 1 and feats == 2 * chans
    proj_t = proj_weight.T
    move = functools.partial(send, ngx=ngx, ngy=ngy)
    rows = 3 * chans
    one = 2 * rows * rows * nz

    tail = -(-2 * -(-slots // nz) // 16) * 16
    base = base_field.reshape(chans, cy, nz)
    plane, payload = call(
        functools.partial(first_kernel, ngx, ngy, cap),
        [shape((cy * chans + tail, nz), BF16), shape((ndev * 3 * cap, feats), BF16)],
        (base, cell_lists, particles, send_counts),
        2 * slots * nrows * feats,
        (
            pltpu.VMEM(base.shape, BF16),
            pltpu.VMEM(cell_lists.shape, I32),
            pltpu.VMEM(particles.shape, BF16),
            pltpu.VMEM(send_counts.shape, I32),
            pltpu.SemaphoreType.DMA((4,)),
        ),
        far=range(4),
    )
    west, east = move(plane, 1, 0), move(plane, -1, 0)
    (payload,) = call(same_kernel, [payload], (payload,), 0, far=(0,), far_out=(0,), aliases={0: 0})
    recv = exchange(payload, ndev)

    cot = cotangent[:, 0].transpose(1, 0, 2)
    taps = conv_weight.reshape(3, 3, 3, chans, chans)
    wf = taps.transpose(1, 2, 3, 0, 4).reshape(9 * chans, rows)
    wb = taps.transpose(1, 0, 4, 2, 3).reshape(9 * chans, rows)

    first, last = call(
        functools.partial(outer_kernel, ndev, cap, chans, cy),
        [shape((2 * rows + chans, nz), BF16)] * 2,
        (recv, plane, west, east, proj_t, cot),
        2 * slots * count * chans,
        (pltpu.VMEM((4 * chans, slots), BF16),),
    )
    north, south = move(last, 0, 1), move(first, 0, -1)
    out_rows, total, pre_edge, slot_edge, sums = call(
        functools.partial(conv_kernel, ndev, cap, chans, cy),
        [
            shape((cy, chans, nz), BF16),
            shape((9 * chans, rows), F32),
            shape((4, rows, nz), F32),
            shape((4, rows, nz), F32),
            shape((3, chans, slots), F32),
        ],
        (recv, proj_t, cot, wf, wb, plane, west, east),
        3 * cy * 3 * one,
        (
            pltpu.VMEM((cy, rows, nz), BF16),
            pltpu.VMEM((cy + 1, rows, nz), F32),
            pltpu.VMEM((cy + 2, rows, nz), BF16),
            pltpu.VMEM((cy, rows, nz), F32),
            pltpu.VMEM((3, (cy - 4) * chans, nz), BF16),
            pltpu.VMEM((cy * chans, slots), BF16),
        ),
    )
    grad_rows = 27 * chans * chans // feats
    share = -(-(grad_rows + 2 * chans) // (16 * ndev)) * 16
    out_edge, payload = call(
        functools.partial(edge_kernel, ndev, cap, chans, cy),
        [shape((2, chans, nz), BF16), shape((ndev, share + 2 * cap, feats), BF16)],
        (
            pre_edge, slot_edge, sums, total, north, south, first, last,
            wf, wb, cot, plane, west, east, recv,
        ),
        12 * one,
        (
            pltpu.VMEM((9 * chans, rows), F32),
            pltpu.VMEM((ndev, share, feats), BF16),
            pltpu.VMEM((ndev, 2 * cap, feats), BF16),
            pltpu.SemaphoreType.DMA((2,)),
        ),
        far_out=(1,),
    )
    payload = payload.reshape(-1, feats)
    recv = exchange(payload, ndev)
    index = (lax.axis_index("gx") * ngy + lax.axis_index("gy")).astype(I32).reshape(1, 1)
    row_grads, sums = call(
        functools.partial(rows_kernel, ngx, ngy, cap, chans),
        [shape((nrows, feats), F32), shape((ndev * share, feats), BF16)],
        (recv, index, send_counts, proj_t),
        2 * nrows * slots * chans,
    )
    recv = exchange(sums, ndev)
    conv_grad, proj_grad = call(
        functools.partial(
            finish_kernel, 1.0 / math.sqrt(count * ndev), 1.0 / math.sqrt(nrows * ndev), share
        ),
        [shape((27, chans, chans), F32), shape((chans, feats), F32)],
        (recv,),
        1000,
    )
    out_field = jnp.concatenate([out_edge[:1], out_rows[1 : cy - 1], out_edge[1:]], axis=0)
    return (out_field.transpose(1, 0, 2)[:, None], row_grads, conv_grad, proj_grad.T)


def solution(mesh):
    in_specs = (
        P(("gx", "gy"), None),
        P(("gx", "gy"), None),
        P(("gx", "gy"), None),
        P(None, "gx", "gy", None),
        P(),
        P(),
        P(None, "gx", "gy", None),
    )
    out_specs = (P(None, "gx", "gy", None), P(("gx", "gy"), None), P(), P())
    return jax.shard_map(local, mesh=mesh, in_specs=in_specs, out_specs=out_specs, check_vma=False)
```

```python
import functools
import math

import jax
import jax.numpy as jnp
from jax import lax
from jax.experimental import pallas as pl
from jax.experimental.pallas import tpu as pltpu
from jax.sharding import PartitionSpec as P

AXES = ("gx", "gy")
F32, BF16, I32 = jnp.float32, jnp.bfloat16, jnp.int32
LIMIT = 40 * 1024 * 1024
ALL = 60 * 1024 * 1024
NT = (((1,), (1,)), ((), ()))
NN = (((1,), (0,)), ((), ()))


def mm(a, b, dims=NN):
    return lax.dot_general(a, b, dims, preferred_element_type=F32)


def call(kernel, outs, args, flops, scratch=(), far=(), far_out=(), aliases=None, limit=LIMIT):
    traffic = sum(math.prod(a.shape) * a.dtype.itemsize for a in (*args, *outs))
    near = pl.BlockSpec(memory_space=pltpu.VMEM)
    there = pl.BlockSpec(memory_space=pltpu.HBM)
    return pl.pallas_call(
        kernel,
        out_shape=[jax.ShapeDtypeStruct(o.shape, o.dtype) for o in outs],
        in_specs=[there if n in far else near for n in range(len(args))],
        out_specs=[there if n in far_out else near for n in range(len(outs))],
        scratch_shapes=list(scratch),
        input_output_aliases=aliases or {},
        compiler_params=pltpu.CompilerParams(vmem_limit_bytes=limit),
        cost_estimate=pl.CostEstimate(flops=flops, bytes_accessed=traffic, transcendentals=0),
    )(*args)


def shape(dims, dtype):
    return jax.ShapeDtypeStruct(dims, dtype)


def send(block, di, dj, ngx, ngy):
    pairs = []
    for i in range(ngx):
        for j in range(ngy):
            pairs.append((i * ngy + j, ((i + di) % ngx) * ngy + (j + dj) % ngy))
    return lax.ppermute(block, AXES, pairs)


def exchange(payload, ndev):
    rows, width = payload.shape
    moved = lax.all_to_all(
        payload.reshape(ndev, rows // ndev, width), AXES, split_axis=0, concat_axis=0, tiled=True
    )
    return moved.reshape(rows, width)


def rolled(x, di, dj):
    for axis, shift in ((0, di), (1, dj)):
        if shift == 1:
            head, tail = lax.slice_in_dim(x, 1, None, axis=axis), lax.slice_in_dim(x, 0, 1, axis=axis)
            x = jnp.concatenate([head, tail], axis=axis)
        elif shift == -1:
            count = x.shape[axis]
            head = lax.slice_in_dim(x, count - 1, count, axis=axis)
            x = jnp.concatenate([head, lax.slice_in_dim(x, 0, count - 1, axis=axis)], axis=axis)
    return x


def widths(nl, slots, block):
    block = block.astype(F32)
    y = jnp.concatenate([block[n : n + 1] for n in range(nl)], axis=1)[:, :slots]
    z = jnp.concatenate([block[nl + n : nl + n + 1] for n in range(nl)], axis=1)[:, :slots]
    return y.astype(I32), z.astype(I32)


def picked_depth(z, nz):
    depth = lax.broadcasted_iota(I32, (nz, z.shape[1]), 0)
    return jnp.where(depth == z, 1.0, 0.0).astype(BF16)


def rows_in(recv_ref, ndev, cap):
    width = recv_ref.shape[1]
    arrived = recv_ref[...].astype(F32).reshape(ndev, 3, cap, width)
    return [arrived[:, n].reshape(ndev * cap, width).astype(BF16) for n in range(3)]


def stacked(grad):
    nz = grad.shape[1]
    wide = grad.astype(F32)
    return jnp.concatenate(
        [pltpu.roll(wide, nz - 1, 1), wide, pltpu.roll(wide, 1, 1)], axis=0
    ).astype(BF16)


def finish_row(acc, field, cot):
    chans, nz = field.shape
    pre = acc[chans : 2 * chans]
    pre = pre + pltpu.roll(acc[:chans], 1, 1) + pltpu.roll(acc[2 * chans :], nz - 1, 1)
    sig = jax.nn.sigmoid(pre)
    out = field.astype(F32) + pre * sig
    grad = cot.astype(F32) * sig * (1.0 + pre * (1.0 - sig))
    return out.astype(BF16), grad.astype(BF16)


def first_kernel(
    ngx, ngy, cap, base_far, cells_far, rows_far, counts_far,
    out_ref, send_ref, base_ref, cells_ref, rows_ref, counts_ref, sems,
):
    pairs = (
        (rows_far, rows_ref), (counts_far, counts_ref), (cells_far, cells_ref), (base_far, base_ref)
    )
    copies = [pltpu.make_async_copy(src, dst, sems.at[n]) for n, (src, dst) in enumerate(pairs)]
    for copy in copies:
        copy.start()
    chans, cy, nz = base_ref.shape
    for copy in copies[:3]:
        copy.wait()
    pick(ngx, ngy, cap, counts_ref, rows_ref, send_ref)
    cells = cells_ref[...]
    slots = cells.shape[1]
    nl = -(-slots // nz)
    tail = out_ref.shape[0] - cy * chans
    lines = []
    for values in (cells // nz, cells % nz):
        values = values.astype(F32)
        if nl * nz > slots:
            values = jnp.concatenate([values, jnp.zeros((1, nl * nz - slots), F32)], axis=1)
        lines += [values[:, n * nz : (n + 1) * nz] for n in range(nl)]
    if tail > 2 * nl:
        lines.append(jnp.zeros((tail - 2 * nl, nz), F32))
    out_ref[pl.ds(cy * chans, tail)] = jnp.concatenate(lines, axis=0).astype(BF16)
    copies[3].wait()
    turned = jnp.swapaxes(base_ref[...].astype(F32), 0, 1)
    out_ref[pl.ds(0, cy * chans)] = turned.reshape(cy * chans, nz).astype(BF16)


def same_kernel(in_ref, out_ref):
    pass


def pick(ngx, ngy, cap, counts_ref, rows_ref, out_ref):
    ndev = ngx * ngy
    nrows, feats = rows_ref.shape
    slots = ndev * cap
    counts = counts_ref[...].astype(F32)
    slot = lax.broadcasted_iota(I32, (slots, ndev), 0)
    lane = lax.broadcasted_iota(I32, (slots, ndev), 1)
    owner = slot // cap
    start = jnp.sum(jnp.where(lane < owner, counts, 0.0), axis=1, keepdims=True)
    held = jnp.sum(jnp.where(lane == owner, counts, 0.0), axis=1, keepdims=True)
    place = (lax.broadcasted_iota(I32, (slots, nrows), 0) % cap).astype(F32)
    row = lax.broadcasted_iota(I32, (slots, nrows), 1).astype(F32)
    onehot = jnp.where((row == place + start) & (place < held), 1.0, 0.0).astype(BF16)
    raw = mm(onehot, rows_ref[...]).reshape(ngx, ngy, cap, feats)
    parts = [rolled(raw, dx, 0).reshape(ndev, cap, feats) for dx in (-1, 0, 1)]
    out_ref[...] = jnp.stack(parts, axis=1).reshape(out_ref.shape).astype(BF16)


def painted_rows(values, cells, nz, ns, masked):
    chans = values.shape[0]
    y, z = cells
    for n, row in enumerate(ns):
        masked[pl.ds(n * chans, chans)] = values * jnp.where(y == row, 1.0, 0.0).astype(BF16)
    return mm(masked[pl.ds(0, len(ns) * chans)], picked_depth(z, nz), NT)


def outer_kernel(
    ndev, cap, chans, cy, recv_ref, own_ref, west_ref, east_ref, proj_t_ref, cot_ref,
    first_ref, last_ref, masked,
):
    slots = ndev * cap
    nz = own_ref.shape[1]
    raws = rows_in(recv_ref, ndev, cap)
    ns = (0, 1, cy - 2, cy - 1)
    for dx, ref in enumerate((west_ref, own_ref, east_ref)):
        values = mm(proj_t_ref[...], raws[dx], NT).astype(BF16)
        painted = painted_rows(values, list_of(ref, cy, chans, slots), nz, ns, masked)
        for n, row in enumerate(ns):
            part = painted[n * chans : (n + 1) * chans]
            field = (ref[pl.ds(row * chans, chans)].astype(F32) + part).astype(BF16)
            target = first_ref if n < 2 else last_ref
            target[pl.ds((3 * (n % 2) + dx) * chans, chans)] = field
    first_ref[pl.ds(6 * chans, chans)] = cot_ref[0]
    last_ref[pl.ds(6 * chans, chans)] = cot_ref[cy - 1]


def list_of(ref, cy, chans, slots):
    tail = ref.shape[0] - cy * chans
    return widths(-(-slots // ref.shape[1]), slots, ref[pl.ds(cy * chans, tail)])


def conv_kernel(
    ndev, cap, chans, cy, recv_ref, proj_t_ref, cot_ref, wf_ref, wb_ref, own_ref, west_ref, east_ref,
    out_ref, total_ref, pre_ref, slot_ref, sums_ref, x_ref, acc, grads, back, plane, masked,
):
    rows = 3 * chans
    nz = x_ref.shape[2]
    slots = ndev * cap
    raws = rows_in(recv_ref, ndev, cap)
    for dx, ref in enumerate((west_ref, own_ref, east_ref)):
        values = mm(proj_t_ref[...], raws[dx], NT).astype(BF16)
        painted = painted_rows(values, list_of(ref, cy, chans, slots), nz, range(cy), masked)
        for n in range(cy):
            part = painted[n * chans : (n + 1) * chans]
            field = ref[pl.ds(n * chans, chans)].astype(F32) + part
            x_ref[n, pl.ds(dx * chans, chans)] = field.astype(BF16)
    own = pl.ds(chans, chans)
    zeros = jnp.zeros((rows, nz), BF16)
    for t in (0, 1, cy, cy + 1):
        grads[t] = zeros
    out_ref[0] = zeros[:chans]
    out_ref[cy - 1] = zeros[:chans]
    acc[0] = jnp.zeros((rows, nz), F32)

    def spread(n):
        terms = mm(wf_ref[...], x_ref[n])
        acc[n + 1] = terms[:rows]
        acc[n] += terms[rows : 2 * rows]
        return terms[2 * rows :]

    pre_ref[0] = spread(0)
    pre_ref[1] = acc[0] + spread(1)

    def forward(n, carry):
        done = spread(n) + acc[n - 1]
        y = n - 1
        out, grad = finish_row(done, x_ref[y, own], cot_ref[y])
        out_ref[y] = out
        grads[y + 1] = stacked(grad)
        return carry

    lax.fori_loop(2, cy, forward, 0, unroll=2)
    pre_ref[2] = acc[cy - 1]
    pre_ref[3] = acc[cy]
    total_ref[...] = jnp.zeros_like(total_ref)
    back[0] = jnp.zeros((rows, nz), F32)
    back[1] = jnp.zeros((rows, nz), F32)

    def taps(n):
        window = grads[pl.ds(n, 3)].reshape(3 * rows, nz)
        total_ref[...] += mm(window, x_ref[n], NT)

    def spread_back(n):
        terms = mm(wb_ref[...], grads[n + 1])
        back[n + 1] = terms[2 * rows :]
        back[n] += terms[rows : 2 * rows]
        return terms[:rows]

    def backward(n, carry):
        taps(n)
        value = spread_back(n) + back[n - 1]
        for dx in range(3):
            part = value[dx * chans : (dx + 1) * chans]
            if dx == 1:
                part = part + cot_ref[n - 1].astype(F32)
            plane[dx, pl.ds((n - 3) * chans, chans)] = part.astype(BF16)
        return carry

    taps(0)
    taps(1)
    slot_ref[0] = spread_back(1)
    taps(2)
    slot_ref[1] = spread_back(2) + back[1]
    lax.fori_loop(3, cy - 1, backward, 0, unroll=2)
    taps(cy - 1)
    slot_ref[2] = back[cy - 2]
    slot_ref[3] = back[cy - 1]
    zero = jnp.zeros((chans, slots), F32)
    for dx, ref in enumerate((west_ref, own_ref, east_ref)):
        sums_ref[dx] = at_slots(plane[dx], list_of(ref, cy, chans, slots), range(2, cy - 2), zero)


def at_slots(part, cells, first, total):
    chans = total.shape[0]
    y, z = cells
    found = mm(part, picked_depth(z, part.shape[1]))
    for n, row in enumerate(first):
        total = total + jnp.where(y == row, found[n * chans : (n + 1) * chans], 0.0)
    return total


def edge_kernel(
    ndev, cap, chans, cy,
    pre_ref, slot_ref, sums_ref, total_ref, north_ref, south_ref, first_ref, last_ref,
    wf_ref, wb_ref, cot_ref, own_ref, west_ref, east_ref, recv_ref,
    out_ref, send_far, total, sums_send, slots_send, sems,
):
    rows = 3 * chans
    slots = ndev * cap
    own = slice(chans, 2 * chans)
    fields = [ref[pl.ds(n * rows, rows)] for ref in (north_ref, first_ref, last_ref, south_ref) for n in (0, 1)]
    cots = [ref[pl.ds(2 * rows, chans)] for ref in (north_ref, first_ref, last_ref, south_ref)]
    near = mm(wf_ref[pl.ds(0, 2 * rows)], fields[1])
    pre = [pre_ref[0] + near[rows:] + mm(wf_ref[pl.ds(0, rows)], fields[0]), pre_ref[1] + near[:rows]]
    near = mm(wf_ref[pl.ds(rows, 2 * rows)], fields[6])
    pre += [pre_ref[2] + near[rows:], pre_ref[3] + near[:rows] + mm(wf_ref[pl.ds(2 * rows, rows)], fields[7])]
    at = (1, 2, 5, 6)
    ends = [finish_row(pre[n], fields[at[n]][own], cots[n]) for n in range(4)]
    out_ref[0], out_ref[1] = ends[1][0], ends[2][0]
    grads = [stacked(grad) for _, grad in ends]
    for n in range(3):
        here = pl.ds(n * rows, rows)
        total[here] = total_ref[here] + (mm(grads[1], fields[3 - n], NT) + mm(grads[2], fields[6 - n], NT))
    width = send_far.shape[2]
    share = send_far.shape[1] - 2 * cap
    half = 3 * rows // 2
    taps = total[:, 2 * chans :]
    taps = jnp.concatenate([taps[:half], taps[half:]], axis=1)
    taps = jnp.concatenate([total[:, : 2 * chans], taps], axis=0)
    full = taps.shape[0] // share
    sums_send[pl.ds(0, full)] = taps.reshape(full, share, width).astype(BF16)
    early = pltpu.make_async_copy(
        sums_send.at[pl.ds(0, full)], send_far.at[pl.ds(0, full), pl.ds(0, share)], sems.at[0]
    )
    early.start()
    inner = mm(wb_ref[pl.ds(rows, 2 * rows)], grads[1])
    top = slot_ref[0] + inner[:rows] + mm(wb_ref[pl.ds(2 * rows, rows)], grads[0])
    second = slot_ref[1] + inner[rows:]
    inner = mm(wb_ref[pl.ds(0, 2 * rows)], grads[2])
    third = slot_ref[2] + inner[:rows]
    bottom = slot_ref[3] + inner[rows:] + mm(wb_ref[pl.ds(0, rows)], grads[3])
    found = []
    for dx, ref in enumerate((west_ref, own_ref, east_ref)):
        parts = [value[dx * chans : (dx + 1) * chans] for value in (top, second, third, bottom)]
        if dx == 1:
            inner = (cots[1], cot_ref[1], cot_ref[cy - 2], cots[2])
            parts = [part + cot.astype(F32) for part, cot in zip(parts, inner)]
        part = jnp.concatenate(parts, axis=0).astype(BF16)
        cells = list_of(ref, cy, chans, slots)
        found.append(at_slots(part, cells, (0, 1, cy - 2, cy - 1), sums_ref[dx]))
    raws = rows_in(recv_ref, ndev, cap)
    proj = sum(mm(found[dx].astype(BF16), raws[dx]) for dx in range(3))
    proj_high = proj.astype(BF16).astype(F32)
    sides = jnp.concatenate([found[0], found[2]], axis=0).T
    middle = jnp.concatenate([found[1], jnp.zeros_like(found[1])], axis=0).T
    halves = [v.reshape(2 * chans // share, share // 2, width) for v in (proj_high, proj - proj_high)]
    proj = jnp.stack(halves, axis=1).reshape(2 * chans // share * 2, share // 2, width)
    rest = ndev - full
    pad = jnp.zeros(((rest * 2 - proj.shape[0]), share // 2, width), F32)
    proj = jnp.concatenate([proj, pad], axis=0).reshape(rest, share, width)
    sums_send[pl.ds(full, rest)] = proj.astype(BF16)
    back = [sides.reshape(ndev, cap, width), middle.reshape(ndev, cap, width)]
    slots_send[...] = jnp.concatenate(back, axis=1).astype(BF16)
    copies = [
        pltpu.make_async_copy(
            sums_send.at[pl.ds(full, rest)], send_far.at[pl.ds(full, rest), pl.ds(0, share)], sems.at[1]
        ),
        pltpu.make_async_copy(slots_send, send_far.at[:, pl.ds(share, 2 * cap)], sems.at[2]),
    ]
    for copy in copies:
        copy.start()
    early.wait()
    for copy in copies:
        copy.wait()


def sums_kernel(chans, cap, recv_ref, index_ref, sums_ref):
    ndev, each, width = recv_ref.shape
    share = each - 2 * cap
    sums = jnp.sum(recv_ref[:, pl.ds(0, share)].astype(F32), axis=0)
    half = share // 2
    whole = sums[:half] + sums[half:]
    high = whole.astype(BF16).astype(F32)
    split = jnp.concatenate([high, whole - high], axis=0)
    device = jnp.broadcast_to(index_ref[...], sums.shape)
    sums = jnp.where(device * share >= 27 * chans * chans // width, split, sums).astype(BF16)
    for n in range(ndev):
        sums_ref[n] = sums


def rows_kernel(ngx, ngy, cap, chans, recv_ref, counts_ref, proj_t_ref, rows_ref):
    ndev = ngx * ngy
    nrows = rows_ref.shape[0]
    width = recv_ref.shape[2]
    slots = ndev * cap
    share = recv_ref.shape[1] - 2 * cap
    arrived = recv_ref[:, pl.ds(share, 2 * cap)].astype(F32)
    sides = arrived[:, :cap].reshape(ngx, ngy, cap, width)
    left = lax.broadcasted_iota(I32, sides.shape, 3) < chans
    sides = jnp.where(left, rolled(sides, 1, 0), rolled(sides, -1, 0)).reshape(slots, width)
    middle = arrived[:, cap:].reshape(slots, width)
    counts = counts_ref[...].astype(F32)
    place = lax.broadcasted_iota(I32, (nrows, ndev), 0).astype(F32)
    lane = lax.broadcasted_iota(I32, (ndev, ndev), 1)
    upto = lax.broadcasted_iota(I32, (ndev, ndev), 0) <= lane
    ends = mm(counts.astype(BF16), jnp.where(upto, 1.0, 0.0).astype(BF16))
    before = ends <= place
    owner = jnp.sum(jnp.where(before, 1.0, 0.0), axis=1, keepdims=True)
    start = jnp.sum(jnp.where(before, counts, 0.0), axis=1, keepdims=True)
    slot = owner * cap + place[:, :1] - start
    onehot = jnp.where(
        lax.broadcasted_iota(I32, (nrows, slots), 1).astype(F32) == slot, 1.0, 0.0
    ).astype(BF16)
    proj_t = proj_t_ref[...]
    both = jnp.concatenate([proj_t, proj_t], axis=0)
    sides = mm(onehot, sides.astype(BF16)).astype(BF16)
    middle = mm(onehot, middle.astype(BF16)).astype(BF16)
    rows_ref[...] = mm(sides, both) + mm(middle, both)


def finish_kernel(conv_scale, proj_scale, share, recv_ref, conv_far, proj_ref, conv_ref, sems):
    taps, chans, _ = conv_ref.shape
    rows = 9 * chans
    half = rows // 2
    third = taps // 3
    packed = recv_ref[pl.ds(rows, half)].astype(F32)
    column = jnp.concatenate([packed[:, :chans], packed[:, chans:]], axis=0)
    copies = []
    for dx in range(3):
        for b in range(3):
            for dz in range(3):
                at = (b * 3 + dz) * chans
                if dx < 2:
                    block = recv_ref[pl.ds(at, chans)].astype(F32)[:, dx * chans : (dx + 1) * chans]
                else:
                    block = column[at : at + chans]
                conv_ref[dx * 9 + (2 - b) * 3 + dz] = block * conv_scale
        part = pl.ds(dx * third, third)
        copies.append(pltpu.make_async_copy(conv_ref.at[part], conv_far.at[part], sems.at[dx]))
        copies[-1].start()
    width = recv_ref.shape[1]
    terms = recv_ref[pl.ds(rows + half, 2 * chans)].astype(F32)
    terms = terms.reshape(2 * chans // share, 2, share // 2, width)
    proj_ref[...] = jnp.sum(terms, axis=1).reshape(chans, width) * proj_scale
    for copy in copies:
        copy.wait()


def local(particles, send_counts, cell_lists, base_field, proj_weight, conv_weight, cotangent):
    ngx, ngy = lax.axis_size("gx"), lax.axis_size("gy")
    ndev = ngx * ngy
    nrows, feats = particles.shape
    chans, cx, cy, nz = base_field.shape
    slots = cell_lists.shape[1]
    cap = slots // ndev
    count = cx * cy * nz
    assert cx == 1 and feats == 2 * chans
    proj_t = proj_weight.T
    move = functools.partial(send, ngx=ngx, ngy=ngy)
    rows = 3 * chans
    one = 2 * rows * rows * nz

    tail = -(-2 * -(-slots // nz) // 16) * 16
    base = base_field.reshape(chans, cy, nz)
    plane, payload = call(
        functools.partial(first_kernel, ngx, ngy, cap),
        [shape((cy * chans + tail, nz), BF16), shape((ndev * 3 * cap, feats), BF16)],
        (base, cell_lists, particles, send_counts),
        2 * slots * nrows * feats,
        (
            pltpu.VMEM(base.shape, BF16),
            pltpu.VMEM(cell_lists.shape, I32),
            pltpu.VMEM(particles.shape, BF16),
            pltpu.VMEM(send_counts.shape, I32),
            pltpu.SemaphoreType.DMA((4,)),
        ),
        far=range(4),
        limit=ALL,
    )
    west, east = move(plane, 1, 0), move(plane, -1, 0)
    (payload,) = call(same_kernel, [payload], (payload,), 0, far=(0,), far_out=(0,), aliases={0: 0})
    recv = exchange(payload, ndev)

    cot = cotangent[:, 0].transpose(1, 0, 2)
    taps = conv_weight.reshape(3, 3, 3, chans, chans)
    wf = taps.transpose(1, 2, 3, 0, 4).reshape(9 * chans, rows)
    wb = taps.transpose(1, 0, 4, 2, 3).reshape(9 * chans, rows)

    first, last = call(
        functools.partial(outer_kernel, ndev, cap, chans, cy),
        [shape((2 * rows + chans, nz), BF16)] * 2,
        (recv, plane, west, east, proj_t, cot),
        2 * slots * count * chans,
        (pltpu.VMEM((4 * chans, slots), BF16),),
    )
    north, south = move(last, 0, 1), move(first, 0, -1)
    out_rows, total, pre_edge, slot_edge, sums = call(
        functools.partial(conv_kernel, ndev, cap, chans, cy),
        [
            shape((cy, chans, nz), BF16),
            shape((9 * chans, rows), F32),
            shape((4, rows, nz), F32),
            shape((4, rows, nz), F32),
            shape((3, chans, slots), F32),
        ],
        (recv, proj_t, cot, wf, wb, plane, west, east),
        3 * cy * 3 * one,
        (
            pltpu.VMEM((cy, rows, nz), BF16),
            pltpu.VMEM((cy + 1, rows, nz), F32),
            pltpu.VMEM((cy + 2, rows, nz), BF16),
            pltpu.VMEM((cy, rows, nz), F32),
            pltpu.VMEM((3, (cy - 4) * chans, nz), BF16),
            pltpu.VMEM((cy * chans, slots), BF16),
        ),
    )
    grad_rows = 27 * chans * chans // feats
    share = -(-(grad_rows + 2 * chans) // (16 * ndev)) * 16
    out_edge, payload = call(
        functools.partial(edge_kernel, ndev, cap, chans, cy),
        [shape((2, chans, nz), BF16), shape((ndev, share + 2 * cap, feats), BF16)],
        (
            pre_edge, slot_edge, sums, total, north, south, first, last,
            wf, wb, cot, plane, west, east, recv,
        ),
        12 * one,
        (
            pltpu.VMEM((9 * chans, rows), F32),
            pltpu.VMEM((ndev, share, feats), BF16),
            pltpu.VMEM((ndev, 2 * cap, feats), BF16),
            pltpu.SemaphoreType.DMA((3,)),
        ),
        far_out=(1,),
    )
    (payload,) = call(same_kernel, [payload], (payload,), 0, far=(0,), far_out=(0,), aliases={0: 0})
    payload = payload.reshape(-1, feats)
    recv = exchange(payload, ndev).reshape(ndev, share + 2 * cap, feats)
    index = (lax.axis_index("gx") * ngy + lax.axis_index("gy")).astype(I32).reshape(1, 1)
    (sums,) = call(
        functools.partial(sums_kernel, chans, cap),
        [shape((ndev, share, feats), BF16)],
        (recv, index),
        1000,
    )
    (row_grads,) = call(
        functools.partial(rows_kernel, ngx, ngy, cap, chans),
        [shape((nrows, feats), F32)],
        (recv, send_counts, proj_t),
        2 * nrows * slots * chans,
    )
    sums = sums.reshape(-1, feats)
    recv = exchange(sums, ndev)
    conv_grad, proj_grad = call(
        functools.partial(
            finish_kernel, 1.0 / math.sqrt(count * ndev), 1.0 / math.sqrt(nrows * ndev), share
        ),
        [shape((27, chans, chans), F32), shape((chans, feats), F32)],
        (recv,),
        1000,
        (pltpu.VMEM((27, chans, chans), F32), pltpu.SemaphoreType.DMA((3,))),
        far_out=(0,),
    )
    out_field = jnp.concatenate([out_edge[:1], out_rows[1 : cy - 1], out_edge[1:]], axis=0)
    return (out_field.transpose(1, 0, 2)[:, None], row_grads, conv_grad, proj_grad.T)


def solution(mesh):
    in_specs = (
        P(("gx", "gy"), None),
        P(("gx", "gy"), None),
        P(("gx", "gy"), None),
        P(None, "gx", "gy", None),
        P(),
        P(),
        P(None, "gx", "gy", None),
    )
    out_specs = (P(None, "gx", "gy", None), P(("gx", "gy"), None), P(), P())
    return jax.shard_map(local, mesh=mesh, in_specs=in_specs, out_specs=out_specs, check_vma=False)
```

```python
import functools
import math

import jax
import jax.numpy as jnp
from jax import lax
from jax.experimental import pallas as pl
from jax.experimental.pallas import tpu as pltpu
from jax.sharding import PartitionSpec as P

AXES = ("gx", "gy")
F32, BF16, I32 = jnp.float32, jnp.bfloat16, jnp.int32
LIMIT = 40 * 1024 * 1024
ALL = 60 * 1024 * 1024
NT = (((1,), (1,)), ((), ()))
NN = (((1,), (0,)), ((), ()))


def mm(a, b, dims=NN):
    return lax.dot_general(a, b, dims, preferred_element_type=F32)


def call(kernel, outs, args, flops, scratch=(), far=(), far_out=(), aliases=None, limit=LIMIT):
    traffic = sum(math.prod(a.shape) * a.dtype.itemsize for a in (*args, *outs))
    near = pl.BlockSpec(memory_space=pltpu.VMEM)
    there = pl.BlockSpec(memory_space=pltpu.HBM)
    return pl.pallas_call(
        kernel,
        out_shape=[jax.ShapeDtypeStruct(o.shape, o.dtype) for o in outs],
        in_specs=[there if n in far else near for n in range(len(args))],
        out_specs=[there if n in far_out else near for n in range(len(outs))],
        scratch_shapes=list(scratch),
        input_output_aliases=aliases or {},
        compiler_params=pltpu.CompilerParams(vmem_limit_bytes=limit),
        cost_estimate=pl.CostEstimate(flops=flops, bytes_accessed=traffic, transcendentals=0),
    )(*args)


def shape(dims, dtype):
    return jax.ShapeDtypeStruct(dims, dtype)


def send(block, di, dj, ngx, ngy):
    pairs = []
    for i in range(ngx):
        for j in range(ngy):
            pairs.append((i * ngy + j, ((i + di) % ngx) * ngy + (j + dj) % ngy))
    return lax.ppermute(block, AXES, pairs)


def exchange(payload, ndev):
    rows, width = payload.shape
    moved = lax.all_to_all(
        payload.reshape(ndev, rows // ndev, width), AXES, split_axis=0, concat_axis=0, tiled=True
    )
    return moved.reshape(rows, width)


def rolled(x, di, dj):
    for axis, shift in ((0, di), (1, dj)):
        if shift == 1:
            head, tail = lax.slice_in_dim(x, 1, None, axis=axis), lax.slice_in_dim(x, 0, 1, axis=axis)
            x = jnp.concatenate([head, tail], axis=axis)
        elif shift == -1:
            count = x.shape[axis]
            head = lax.slice_in_dim(x, count - 1, count, axis=axis)
            x = jnp.concatenate([head, lax.slice_in_dim(x, 0, count - 1, axis=axis)], axis=axis)
    return x


def picked_depth(z, nz):
    depth = lax.broadcasted_iota(I32, (nz, z.shape[1]), 0)
    return jnp.where(depth == z, 1.0, 0.0).astype(BF16)


def rows_in(recv_ref, ndev, cap):
    width = recv_ref.shape[1]
    arrived = recv_ref[...].astype(F32).reshape(ndev, 3, cap, width)
    return [arrived[:, n].reshape(ndev * cap, width).astype(BF16) for n in range(3)]


def stacked(grad):
    nz = grad.shape[1]
    wide = grad.astype(F32)
    return jnp.concatenate(
        [pltpu.roll(wide, nz - 1, 1), wide, pltpu.roll(wide, 1, 1)], axis=0
    ).astype(BF16)


def finish_row(acc, field, cot):
    chans, nz = field.shape
    pre = acc[chans : 2 * chans]
    pre = pre + pltpu.roll(acc[:chans], 1, 1) + pltpu.roll(acc[2 * chans :], nz - 1, 1)
    sig = jax.nn.sigmoid(pre)
    out = field.astype(F32) + pre * sig
    grad = cot.astype(F32) * sig * (1.0 + pre * (1.0 - sig))
    return out.astype(BF16), grad.astype(BF16)


def first_kernel(
    ngx, ngy, cap, rows_far, counts_far, send_ref, rows_ref, counts_ref, sems
):
    copies = [
        pltpu.make_async_copy(rows_far, rows_ref, sems.at[0]),
        pltpu.make_async_copy(counts_far, counts_ref, sems.at[1]),
    ]
    for copy in copies:
        copy.start()
    for copy in copies:
        copy.wait()
    pick(ngx, ngy, cap, counts_ref, rows_ref, send_ref)


def same_kernel(in_ref, out_ref):
    pass


def pick(ngx, ngy, cap, counts_ref, rows_ref, out_ref):
    ndev = ngx * ngy
    nrows, feats = rows_ref.shape
    slots = ndev * cap
    counts = counts_ref[...].astype(F32)
    slot = lax.broadcasted_iota(I32, (slots, ndev), 0)
    lane = lax.broadcasted_iota(I32, (slots, ndev), 1)
    owner = slot // cap
    start = jnp.sum(jnp.where(lane < owner, counts, 0.0), axis=1, keepdims=True)
    held = jnp.sum(jnp.where(lane == owner, counts, 0.0), axis=1, keepdims=True)
    place = (lax.broadcasted_iota(I32, (slots, nrows), 0) % cap).astype(F32)
    row = lax.broadcasted_iota(I32, (slots, nrows), 1).astype(F32)
    onehot = jnp.where((row == place + start) & (place < held), 1.0, 0.0).astype(BF16)
    raw = mm(onehot, rows_ref[...]).reshape(ngx, ngy, cap, feats)
    parts = [rolled(raw, dx, 0).reshape(ndev, cap, feats) for dx in (-1, 0, 1)]
    out_ref[...] = jnp.stack(parts, axis=1).reshape(out_ref.shape).astype(BF16)


def painted_rows(values, cells, nz, ns, masked):
    chans = values.shape[0]
    y, z = cells
    for n, row in enumerate(ns):
        masked[pl.ds(n * chans, chans)] = values * jnp.where(y == row, 1.0, 0.0).astype(BF16)
    return mm(masked[pl.ds(0, len(ns) * chans)], picked_depth(z, nz), NT)


def outer_kernel(
    ndev, cap, recv_ref, own_ref, west_ref, east_ref, own_cells, west_cells, east_cells,
    proj_t_ref, cot_ref, first_ref, last_ref, masked,
):
    chans, cy, nz = own_ref.shape
    raws = rows_in(recv_ref, ndev, cap)
    ns = (0, 1, cy - 2, cy - 1)
    planes = ((west_ref, west_cells), (own_ref, own_cells), (east_ref, east_cells))
    for dx, (ref, cells_ref) in enumerate(planes):
        values = mm(proj_t_ref[...], raws[dx], NT).astype(BF16)
        painted = painted_rows(values, place(cells_ref, nz), nz, ns, masked)
        base = turned(ref)
        for n, row in enumerate(ns):
            part = painted[n * chans : (n + 1) * chans]
            field = (base[row] + part).astype(BF16)
            target = first_ref if n < 2 else last_ref
            target[pl.ds((3 * (n % 2) + dx) * chans, chans)] = field
    first_ref[pl.ds(6 * chans, chans)] = cot_ref[0]
    last_ref[pl.ds(6 * chans, chans)] = cot_ref[cy - 1]


def place(cells_ref, nz):
    cells = cells_ref[...]
    return cells // nz, cells % nz


def turned(ref):
    return jnp.swapaxes(ref[...].astype(F32), 0, 1)


def conv_kernel(
    ndev, cap, recv_ref, proj_t_ref, cot_ref, wf_ref, wb_ref,
    own_ref, west_ref, east_ref, own_cells, west_cells, east_cells,
    out_ref, total_ref, pre_ref, slot_ref, sums_ref, x_ref, acc, grads, back, plane, masked,
):
    chans, cy, nz = own_ref.shape
    rows = 3 * chans
    slots = ndev * cap
    raws = rows_in(recv_ref, ndev, cap)
    planes = ((west_ref, west_cells), (own_ref, own_cells), (east_ref, east_cells))
    for dx, (ref, cells_ref) in enumerate(planes):
        values = mm(proj_t_ref[...], raws[dx], NT).astype(BF16)
        painted = painted_rows(values, place(cells_ref, nz), nz, range(cy), masked)
        field = turned(ref) + painted.reshape(cy, chans, nz)
        x_ref[:, pl.ds(dx * chans, chans)] = field.astype(BF16)
    own = pl.ds(chans, chans)
    zeros = jnp.zeros((rows, nz), BF16)
    for t in (0, 1, cy, cy + 1):
        grads[t] = zeros
    out_ref[0] = zeros[:chans]
    out_ref[cy - 1] = zeros[:chans]
    acc[0] = jnp.zeros((rows, nz), F32)

    def spread(n):
        terms = mm(wf_ref[...], x_ref[n])
        acc[n + 1] = terms[:rows]
        acc[n] += terms[rows : 2 * rows]
        return terms[2 * rows :]

    pre_ref[0] = spread(0)
    pre_ref[1] = acc[0] + spread(1)

    def forward(n, carry):
        done = spread(n) + acc[n - 1]
        y = n - 1
        out, grad = finish_row(done, x_ref[y, own], cot_ref[y])
        out_ref[y] = out
        grads[y + 1] = stacked(grad)
        return carry

    lax.fori_loop(2, cy, forward, 0, unroll=2)
    pre_ref[2] = acc[cy - 1]
    pre_ref[3] = acc[cy]
    total_ref[...] = jnp.zeros_like(total_ref)
    back[0] = jnp.zeros((rows, nz), F32)
    back[1] = jnp.zeros((rows, nz), F32)

    def taps(n):
        window = grads[pl.ds(n, 3)].reshape(3 * rows, nz)
        total_ref[...] += mm(window, x_ref[n], NT)

    def spread_back(n):
        terms = mm(wb_ref[...], grads[n + 1])
        back[n + 1] = terms[2 * rows :]
        back[n] += terms[rows : 2 * rows]
        return terms[:rows]

    def backward(n, carry):
        taps(n)
        value = spread_back(n) + back[n - 1]
        for dx in range(3):
            part = value[dx * chans : (dx + 1) * chans]
            if dx == 1:
                part = part + cot_ref[n - 1].astype(F32)
            plane[dx, pl.ds((n - 3) * chans, chans)] = part.astype(BF16)
        return carry

    taps(0)
    taps(1)
    slot_ref[0] = spread_back(1)
    taps(2)
    slot_ref[1] = spread_back(2) + back[1]
    lax.fori_loop(3, cy - 1, backward, 0, unroll=2)
    taps(cy - 1)
    slot_ref[2] = back[cy - 2]
    slot_ref[3] = back[cy - 1]
    zero = jnp.zeros((chans, slots), F32)
    for dx, (_, cells_ref) in enumerate(planes):
        sums_ref[dx] = at_slots(plane[dx], place(cells_ref, nz), range(2, cy - 2), zero)


def at_slots(part, cells, first, total):
    chans = total.shape[0]
    y, z = cells
    found = mm(part, picked_depth(z, part.shape[1]))
    for n, row in enumerate(first):
        total = total + jnp.where(y == row, found[n * chans : (n + 1) * chans], 0.0)
    return total


def edge_kernel(
    ndev, cap,
    pre_ref, slot_ref, sums_ref, total_ref, north_ref, south_ref, first_ref, last_ref,
    wf_ref, wb_ref, cot_ref, own_cells, west_cells, east_cells, recv_ref,
    out_ref, send_far, total, sums_send, slots_send, sems,
):
    cy, chans, nz = cot_ref.shape
    rows = 3 * chans
    own = slice(chans, 2 * chans)
    fields = [ref[pl.ds(n * rows, rows)] for ref in (north_ref, first_ref, last_ref, south_ref) for n in (0, 1)]
    cots = [ref[pl.ds(2 * rows, chans)] for ref in (north_ref, first_ref, last_ref, south_ref)]
    near = mm(wf_ref[pl.ds(0, 2 * rows)], fields[1])
    pre = [pre_ref[0] + near[rows:] + mm(wf_ref[pl.ds(0, rows)], fields[0]), pre_ref[1] + near[:rows]]
    near = mm(wf_ref[pl.ds(rows, 2 * rows)], fields[6])
    pre += [pre_ref[2] + near[rows:], pre_ref[3] + near[:rows] + mm(wf_ref[pl.ds(2 * rows, rows)], fields[7])]
    at = (1, 2, 5, 6)
    ends = [finish_row(pre[n], fields[at[n]][own], cots[n]) for n in range(4)]
    out_ref[0], out_ref[1] = ends[1][0], ends[2][0]
    grads = [stacked(grad) for _, grad in ends]
    for n in range(3):
        here = pl.ds(n * rows, rows)
        total[here] = total_ref[here] + (mm(grads[1], fields[3 - n], NT) + mm(grads[2], fields[6 - n], NT))
    width = send_far.shape[2]
    share = send_far.shape[1] - 2 * cap
    half = 3 * rows // 2
    taps = total[:, 2 * chans :]
    taps = jnp.concatenate([taps[:half], taps[half:]], axis=1)
    taps = jnp.concatenate([total[:, : 2 * chans], taps], axis=0)
    full = taps.shape[0] // share
    sums_send[pl.ds(0, full)] = taps.reshape(full, share, width).astype(BF16)
    early = pltpu.make_async_copy(
        sums_send.at[pl.ds(0, full)], send_far.at[pl.ds(0, full), pl.ds(0, share)], sems.at[0]
    )
    early.start()
    inner = mm(wb_ref[pl.ds(rows, 2 * rows)], grads[1])
    top = slot_ref[0] + inner[:rows] + mm(wb_ref[pl.ds(2 * rows, rows)], grads[0])
    second = slot_ref[1] + inner[rows:]
    inner = mm(wb_ref[pl.ds(0, 2 * rows)], grads[2])
    third = slot_ref[2] + inner[:rows]
    bottom = slot_ref[3] + inner[rows:] + mm(wb_ref[pl.ds(0, rows)], grads[3])
    found = []
    for dx, cells_ref in enumerate((west_cells, own_cells, east_cells)):
        parts = [value[dx * chans : (dx + 1) * chans] for value in (top, second, third, bottom)]
        if dx == 1:
            inner = (cots[1], cot_ref[1], cot_ref[cy - 2], cots[2])
            parts = [part + cot.astype(F32) for part, cot in zip(parts, inner)]
        part = jnp.concatenate(parts, axis=0).astype(BF16)
        cells = place(cells_ref, nz)
        found.append(at_slots(part, cells, (0, 1, cy - 2, cy - 1), sums_ref[dx]))
    raws = rows_in(recv_ref, ndev, cap)
    proj = sum(mm(found[dx].astype(BF16), raws[dx]) for dx in range(3))
    proj_high = proj.astype(BF16).astype(F32)
    sides = jnp.concatenate([found[0], found[2]], axis=0).T
    middle = jnp.concatenate([found[1], jnp.zeros_like(found[1])], axis=0).T
    halves = [v.reshape(2 * chans // share, share // 2, width) for v in (proj_high, proj - proj_high)]
    proj = jnp.stack(halves, axis=1).reshape(2 * chans // share * 2, share // 2, width)
    rest = ndev - full
    pad = jnp.zeros(((rest * 2 - proj.shape[0]), share // 2, width), F32)
    proj = jnp.concatenate([proj, pad], axis=0).reshape(rest, share, width)
    sums_send[pl.ds(full, rest)] = proj.astype(BF16)
    back = [sides.reshape(ndev, cap, width), middle.reshape(ndev, cap, width)]
    slots_send[...] = jnp.concatenate(back, axis=1).astype(BF16)
    copies = [
        pltpu.make_async_copy(
            sums_send.at[pl.ds(full, rest)], send_far.at[pl.ds(full, rest), pl.ds(0, share)], sems.at[1]
        ),
        pltpu.make_async_copy(slots_send, send_far.at[:, pl.ds(share, 2 * cap)], sems.at[2]),
    ]
    for copy in copies:
        copy.start()
    early.wait()
    for copy in copies:
        copy.wait()


def sums_kernel(chans, cap, recv_ref, index_ref, sums_ref):
    ndev, each, width = recv_ref.shape
    share = each - 2 * cap
    sums = jnp.sum(recv_ref[:, pl.ds(0, share)].astype(F32), axis=0)
    half = share // 2
    whole = sums[:half] + sums[half:]
    high = whole.astype(BF16).astype(F32)
    split = jnp.concatenate([high, whole - high], axis=0)
    device = jnp.broadcast_to(index_ref[...], sums.shape)
    sums = jnp.where(device * share >= 27 * chans * chans // width, split, sums).astype(BF16)
    for n in range(ndev):
        sums_ref[n] = sums


def rows_kernel(ngx, ngy, cap, chans, recv_ref, counts_ref, proj_t_ref, rows_ref):
    ndev = ngx * ngy
    nrows = rows_ref.shape[0]
    width = recv_ref.shape[2]
    slots = ndev * cap
    share = recv_ref.shape[1] - 2 * cap
    arrived = recv_ref[:, pl.ds(share, 2 * cap)].astype(F32)
    sides = arrived[:, :cap].reshape(ngx, ngy, cap, width)
    left = lax.broadcasted_iota(I32, sides.shape, 3) < chans
    sides = jnp.where(left, rolled(sides, 1, 0), rolled(sides, -1, 0)).reshape(slots, width)
    middle = arrived[:, cap:].reshape(slots, width)
    counts = counts_ref[...].astype(F32)
    place = lax.broadcasted_iota(I32, (nrows, ndev), 0).astype(F32)
    lane = lax.broadcasted_iota(I32, (ndev, ndev), 1)
    upto = lax.broadcasted_iota(I32, (ndev, ndev), 0) <= lane
    ends = mm(counts.astype(BF16), jnp.where(upto, 1.0, 0.0).astype(BF16))
    before = ends <= place
    owner = jnp.sum(jnp.where(before, 1.0, 0.0), axis=1, keepdims=True)
    start = jnp.sum(jnp.where(before, counts, 0.0), axis=1, keepdims=True)
    slot = owner * cap + place[:, :1] - start
    onehot = jnp.where(
        lax.broadcasted_iota(I32, (nrows, slots), 1).astype(F32) == slot, 1.0, 0.0
    ).astype(BF16)
    proj_t = proj_t_ref[...]
    both = jnp.concatenate([proj_t, proj_t], axis=0)
    sides = mm(onehot, sides.astype(BF16)).astype(BF16)
    middle = mm(onehot, middle.astype(BF16)).astype(BF16)
    rows_ref[...] = mm(sides, both) + mm(middle, both)


def finish_kernel(conv_scale, proj_scale, share, recv_ref, conv_ref, proj_ref):
    taps, chans, _ = conv_ref.shape
    rows = 9 * chans
    half = rows // 2
    packed = recv_ref[pl.ds(rows, half)].astype(F32)
    column = jnp.concatenate([packed[:, :chans], packed[:, chans:]], axis=0)
    for b in range(3):
        for dz in range(3):
            first = (b * 3 + dz) * chans
            block = recv_ref[pl.ds(first, chans)].astype(F32)
            k = (2 - b) * 3 + dz
            conv_ref[k] = block[:, :chans] * conv_scale
            conv_ref[9 + k] = block[:, chans:] * conv_scale
            conv_ref[18 + k] = column[first : first + chans] * conv_scale
    width = recv_ref.shape[1]
    terms = recv_ref[pl.ds(rows + half, 2 * chans)].astype(F32)
    terms = terms.reshape(2 * chans // share, 2, share // 2, width)
    proj_ref[...] = jnp.sum(terms, axis=1).reshape(chans, width) * proj_scale


def local(particles, send_counts, cell_lists, base_field, proj_weight, conv_weight, cotangent):
    ngx, ngy = lax.axis_size("gx"), lax.axis_size("gy")
    ndev = ngx * ngy
    nrows, feats = particles.shape
    chans, cx, cy, nz = base_field.shape
    slots = cell_lists.shape[1]
    cap = slots // ndev
    count = cx * cy * nz
    assert cx == 1 and feats == 2 * chans
    proj_t = proj_weight.T
    move = functools.partial(send, ngx=ngx, ngy=ngy)
    rows = 3 * chans
    one = 2 * rows * rows * nz

    base = base_field.reshape(chans, cy, nz)
    west, east = move(base_field, 1, 0), move(base_field, -1, 0)
    planes = (base, west.reshape(base.shape), east.reshape(base.shape))
    lists = (cell_lists, move(cell_lists, 1, 0), move(cell_lists, -1, 0))
    (payload,) = call(
        functools.partial(first_kernel, ngx, ngy, cap),
        [shape((ndev * 3 * cap, feats), BF16)],
        (particles, send_counts),
        2 * slots * nrows * feats,
        (
            pltpu.VMEM(particles.shape, BF16),
            pltpu.VMEM(send_counts.shape, I32),
            pltpu.SemaphoreType.DMA((2,)),
        ),
        far=range(2),
        limit=ALL,
    )
    recv = exchange(payload, ndev)

    cot = cotangent[:, 0].transpose(1, 0, 2)
    taps = conv_weight.reshape(3, 3, 3, chans, chans)
    wf = taps.transpose(1, 2, 3, 0, 4).reshape(9 * chans, rows)
    wb = taps.transpose(1, 0, 4, 2, 3).reshape(9 * chans, rows)

    first, last = call(
        functools.partial(outer_kernel, ndev, cap),
        [shape((2 * rows + chans, nz), BF16)] * 2,
        (recv, *planes, *lists, proj_t, cot),
        2 * slots * count * chans,
        (pltpu.VMEM((4 * chans, slots), BF16),),
    )
    north, south = move(last, 0, 1), move(first, 0, -1)
    out_rows, total, pre_edge, slot_edge, sums = call(
        functools.partial(conv_kernel, ndev, cap),
        [
            shape((cy, chans, nz), BF16),
            shape((9 * chans, rows), F32),
            shape((4, rows, nz), F32),
            shape((4, rows, nz), F32),
            shape((3, chans, slots), F32),
        ],
        (recv, proj_t, cot, wf, wb, *planes, *lists),
        3 * cy * 3 * one,
        (
            pltpu.VMEM((cy, rows, nz), BF16),
            pltpu.VMEM((cy + 1, rows, nz), F32),
            pltpu.VMEM((cy + 2, rows, nz), BF16),
            pltpu.VMEM((cy, rows, nz), F32),
            pltpu.VMEM((3, (cy - 4) * chans, nz), BF16),
            pltpu.VMEM((cy * chans, slots), BF16),
        ),
    )
    grad_rows = 27 * chans * chans // feats
    share = -(-(grad_rows + 2 * chans) // (16 * ndev)) * 16
    out_edge, payload = call(
        functools.partial(edge_kernel, ndev, cap),
        [shape((2, chans, nz), BF16), shape((ndev, share + 2 * cap, feats), BF16)],
        (
            pre_edge, slot_edge, sums, total, north, south, first, last,
            wf, wb, cot, *lists, recv,
        ),
        12 * one,
        (
            pltpu.VMEM((9 * chans, rows), F32),
            pltpu.VMEM((ndev, share, feats), BF16),
            pltpu.VMEM((ndev, 2 * cap, feats), BF16),
            pltpu.SemaphoreType.DMA((3,)),
        ),
        far_out=(1,),
    )
    (payload,) = call(same_kernel, [payload], (payload,), 0, far=(0,), far_out=(0,), aliases={0: 0})
    payload = payload.reshape(-1, feats)
    recv = exchange(payload, ndev).reshape(ndev, share + 2 * cap, feats)
    index = (lax.axis_index("gx") * ngy + lax.axis_index("gy")).astype(I32).reshape(1, 1)
    (sums,) = call(
        functools.partial(sums_kernel, chans, cap),
        [shape((ndev, share, feats), BF16)],
        (recv, index),
        1000,
    )
    (row_grads,) = call(
        functools.partial(rows_kernel, ngx, ngy, cap, chans),
        [shape((nrows, feats), F32)],
        (recv, send_counts, proj_t),
        2 * nrows * slots * chans,
    )
    sums = sums.reshape(-1, feats)
    recv = exchange(sums, ndev)
    conv_grad, proj_grad = call(
        functools.partial(
            finish_kernel, 1.0 / math.sqrt(count * ndev), 1.0 / math.sqrt(nrows * ndev), share
        ),
        [shape((27, chans, chans), F32), shape((chans, feats), F32)],
        (recv,),
        1000,
    )
    out_field = jnp.concatenate([out_edge[:1], out_rows[1 : cy - 1], out_edge[1:]], axis=0)
    return (out_field.transpose(1, 0, 2)[:, None], row_grads, conv_grad, proj_grad.T)


def solution(mesh):
    in_specs = (
        P(("gx", "gy"), None),
        P(("gx", "gy"), None),
        P(("gx", "gy"), None),
        P(None, "gx", "gy", None),
        P(),
        P(),
        P(None, "gx", "gy", None),
    )
    out_specs = (P(None, "gx", "gy", None), P(("gx", "gy"), None), P(), P())
    return jax.shard_map(local, mesh=mesh, in_specs=in_specs, out_specs=out_specs, check_vma=False)
```

```python
import functools
import math

import jax
import jax.numpy as jnp
from jax import lax
from jax.experimental import pallas as pl
from jax.experimental.pallas import tpu as pltpu
from jax.sharding import PartitionSpec as P

AXES = ("gx", "gy")
F32, BF16, I32 = jnp.float32, jnp.bfloat16, jnp.int32
LIMIT = 40 * 1024 * 1024
ALL = 60 * 1024 * 1024
NT = (((1,), (1,)), ((), ()))
NN = (((1,), (0,)), ((), ()))


def mm(a, b, dims=NN):
    return lax.dot_general(a, b, dims, preferred_element_type=F32)


def call(kernel, outs, args, flops, scratch=(), far=(), far_out=(), aliases=None, limit=LIMIT):
    traffic = sum(math.prod(a.shape) * a.dtype.itemsize for a in (*args, *outs))
    near = pl.BlockSpec(memory_space=pltpu.VMEM)
    there = pl.BlockSpec(memory_space=pltpu.HBM)
    return pl.pallas_call(
        kernel,
        out_shape=[jax.ShapeDtypeStruct(o.shape, o.dtype) for o in outs],
        in_specs=[there if n in far else near for n in range(len(args))],
        out_specs=[there if n in far_out else near for n in range(len(outs))],
        scratch_shapes=list(scratch),
        input_output_aliases=aliases or {},
        compiler_params=pltpu.CompilerParams(vmem_limit_bytes=limit),
        cost_estimate=pl.CostEstimate(flops=flops, bytes_accessed=traffic, transcendentals=0),
    )(*args)


def shape(dims, dtype):
    return jax.ShapeDtypeStruct(dims, dtype)


def send(block, di, dj, ngx, ngy):
    pairs = []
    for i in range(ngx):
        for j in range(ngy):
            pairs.append((i * ngy + j, ((i + di) % ngx) * ngy + (j + dj) % ngy))
    return lax.ppermute(block, AXES, pairs)


def exchange(payload, ndev):
    rows, width = payload.shape
    moved = lax.all_to_all(
        payload.reshape(ndev, rows // ndev, width), AXES, split_axis=0, concat_axis=0, tiled=True
    )
    return moved.reshape(rows, width)


def rolled(x, di, dj):
    for axis, shift in ((0, di), (1, dj)):
        if shift == 1:
            head, tail = lax.slice_in_dim(x, 1, None, axis=axis), lax.slice_in_dim(x, 0, 1, axis=axis)
            x = jnp.concatenate([head, tail], axis=axis)
        elif shift == -1:
            count = x.shape[axis]
            head = lax.slice_in_dim(x, count - 1, count, axis=axis)
            x = jnp.concatenate([head, lax.slice_in_dim(x, 0, count - 1, axis=axis)], axis=axis)
    return x


def picked_depth(z, nz):
    depth = lax.broadcasted_iota(I32, (nz, z.shape[1]), 0)
    return jnp.where(depth == z, 1.0, 0.0).astype(BF16)


def rows_in(recv_ref, ndev, cap):
    width = recv_ref.shape[1]
    arrived = recv_ref[...].astype(F32).reshape(ndev, 3, cap, width)
    return [arrived[:, n].reshape(ndev * cap, width).astype(BF16) for n in range(3)]


def stacked(grad):
    nz = grad.shape[1]
    wide = grad.astype(F32)
    return jnp.concatenate(
        [pltpu.roll(wide, nz - 1, 1), wide, pltpu.roll(wide, 1, 1)], axis=0
    ).astype(BF16)


def over_depth(acc):
    chans, nz = acc.shape[0] // 3, acc.shape[1]
    total = acc[chans : 2 * chans] + pltpu.roll(acc[:chans], 1, 1)
    return total + pltpu.roll(acc[2 * chans :], nz - 1, 1)


def finish_row(pre, field, cot):
    sig = jax.nn.sigmoid(pre)
    out = field.astype(F32) + pre * sig
    grad = cot.astype(F32) * sig * (1.0 + pre * (1.0 - sig))
    return out.astype(BF16), grad.astype(BF16)


def first_kernel(
    ngx, ngy, cap, rows_far, counts_far, send_ref, rows_ref, counts_ref, sems
):
    copies = [
        pltpu.make_async_copy(rows_far, rows_ref, sems.at[0]),
        pltpu.make_async_copy(counts_far, counts_ref, sems.at[1]),
    ]
    for copy in copies:
        copy.start()
    for copy in copies:
        copy.wait()
    pick(ngx, ngy, cap, counts_ref, rows_ref, send_ref)


def same_kernel(in_ref, out_ref):
    pass


def pick(ngx, ngy, cap, counts_ref, rows_ref, out_ref):
    ndev = ngx * ngy
    nrows, feats = rows_ref.shape
    slots = ndev * cap
    counts = counts_ref[...].astype(F32)
    owner = lax.broadcasted_iota(I32, (ndev, cap, ndev), 0).reshape(slots, ndev)
    lane = lax.broadcasted_iota(I32, (slots, ndev), 1)
    start = jnp.sum(jnp.where(lane < owner, counts, 0.0), axis=1, keepdims=True)
    held = jnp.sum(jnp.where(lane == owner, counts, 0.0), axis=1, keepdims=True)
    place = lax.broadcasted_iota(I32, (ndev, cap, nrows), 1).reshape(slots, nrows).astype(F32)
    row = lax.broadcasted_iota(I32, (slots, nrows), 1).astype(F32)
    onehot = jnp.where((row == place + start) & (place < held), 1.0, 0.0).astype(BF16)
    raw = mm(onehot, rows_ref[...]).reshape(ngx, ngy, cap, feats)
    parts = [rolled(raw, dx, 0).reshape(ndev, cap, feats) for dx in (-1, 0, 1)]
    out_ref[...] = jnp.stack(parts, axis=1).reshape(out_ref.shape).astype(BF16)


def painted_rows(values, cells, nz, ns, masked):
    chans = values.shape[0]
    y, z = cells
    for n, row in enumerate(ns):
        masked[pl.ds(n * chans, chans)] = values * jnp.where(y == row, 1.0, 0.0).astype(BF16)
    return mm(masked[pl.ds(0, len(ns) * chans)], picked_depth(z, nz), NT)


def outer_kernel(
    ndev, cap, recv_ref, own_ref, west_ref, east_ref, own_cells, west_cells, east_cells,
    proj_t_ref, cot_ref, wf_ref, first_ref, last_ref, field_ref, masked,
):
    chans, cy, nz = own_ref.shape
    rows = 3 * chans
    raws = rows_in(recv_ref, ndev, cap)
    ns = (0, 1, cy - 2, cy - 1)
    planes = ((west_ref, west_cells), (own_ref, own_cells), (east_ref, east_cells))
    for dx, (ref, cells_ref) in enumerate(planes):
        values = mm(proj_t_ref[...], raws[dx], NT).astype(BF16)
        painted = painted_rows(values, place(cells_ref, nz), nz, ns, masked)
        base = turned(ref)
        for n, row in enumerate(ns):
            part = painted[n * chans : (n + 1) * chans]
            field_ref[n, pl.ds(dx * chans, chans)] = (base[row] + part).astype(BF16)
    near = mm(wf_ref[pl.ds(0, 2 * rows)], field_ref[3])
    far = mm(wf_ref[pl.ds(0, rows)], field_ref[2])
    last_ref[pl.ds(0, chans)] = over_depth(near[:rows]).astype(BF16)
    last_ref[pl.ds(chans, chans)] = over_depth(near[rows:] + far).astype(BF16)
    last_ref[pl.ds(2 * chans, chans)] = cot_ref[cy - 1]
    near = mm(wf_ref[pl.ds(rows, 2 * rows)], field_ref[0])
    far = mm(wf_ref[pl.ds(2 * rows, rows)], field_ref[1])
    first_ref[pl.ds(0, chans)] = over_depth(near[rows:]).astype(BF16)
    first_ref[pl.ds(chans, chans)] = over_depth(near[:rows] + far).astype(BF16)
    first_ref[pl.ds(2 * chans, chans)] = cot_ref[0]


def place(cells_ref, nz):
    cells = cells_ref[...]
    return cells // nz, cells % nz


def turned(ref):
    return jnp.swapaxes(ref[...].astype(F32), 0, 1)


def conv_kernel(
    ndev, cap, recv_ref, proj_t_ref, cot_ref, wf_ref, wb_ref,
    own_ref, west_ref, east_ref, own_cells, west_cells, east_cells,
    out_ref, total_ref, pre_ref, slot_ref, sums_ref, x_ref, acc, grads, back, plane, masked,
):
    chans, cy, nz = own_ref.shape
    rows = 3 * chans
    slots = ndev * cap
    raws = rows_in(recv_ref, ndev, cap)
    planes = ((west_ref, west_cells), (own_ref, own_cells), (east_ref, east_cells))
    for dx, (ref, cells_ref) in enumerate(planes):
        values = mm(proj_t_ref[...], raws[dx], NT).astype(BF16)
        painted = painted_rows(values, place(cells_ref, nz), nz, range(cy), masked)
        field = turned(ref) + painted.reshape(cy, chans, nz)
        x_ref[:, pl.ds(dx * chans, chans)] = field.astype(BF16)
    own = pl.ds(chans, chans)
    zeros = jnp.zeros((rows, nz), BF16)
    for t in (0, 1, cy, cy + 1):
        grads[t] = zeros
    out_ref[0] = zeros[:chans]
    out_ref[cy - 1] = zeros[:chans]
    acc[0] = jnp.zeros((rows, nz), F32)

    def spread(n):
        terms = mm(wf_ref[...], x_ref[n])
        acc[n + 1] = terms[:rows]
        acc[n] += terms[rows : 2 * rows]
        return terms[2 * rows :]

    pre_ref[0] = over_depth(spread(0))
    pre_ref[1] = over_depth(acc[0] + spread(1))

    def forward(n):
        done = spread(n) + acc[n - 1]
        y = n - 1
        out, grad = finish_row(over_depth(done), x_ref[y, own], cot_ref[y])
        out_ref[y] = out
        grads[y + 1] = stacked(grad)

    for n in range(2, cy):
        forward(n)
    pre_ref[2] = over_depth(acc[cy - 1])
    pre_ref[3] = over_depth(acc[cy])
    total_ref[...] = jnp.zeros_like(total_ref)
    back[0] = jnp.zeros((rows, nz), F32)
    back[1] = jnp.zeros((rows, nz), F32)

    def taps(n):
        window = grads[pl.ds(n, 3)].reshape(3 * rows, nz)
        total_ref[...] += mm(window, x_ref[n], NT)

    def spread_back(n):
        terms = mm(wb_ref[...], grads[n + 1])
        back[n + 1] = terms[2 * rows :]
        back[n] += terms[rows : 2 * rows]
        return terms[:rows]

    def backward(n):
        taps(n)
        value = spread_back(n) + back[n - 1]
        for dx in range(3):
            part = value[dx * chans : (dx + 1) * chans]
            if dx == 1:
                part = part + cot_ref[n - 1].astype(F32)
            plane[dx, pl.ds((n - 3) * chans, chans)] = part.astype(BF16)

    taps(0)
    taps(1)
    slot_ref[0] = spread_back(1)
    taps(2)
    slot_ref[1] = spread_back(2) + back[1]
    for n in range(3, cy - 1):
        backward(n)
    taps(cy - 1)
    slot_ref[2] = back[cy - 2]
    slot_ref[3] = back[cy - 1]
    zero = jnp.zeros((chans, slots), F32)
    for dx, (_, cells_ref) in enumerate(planes):
        sums_ref[dx] = at_slots(plane[dx], place(cells_ref, nz), range(2, cy - 2), zero)


def at_slots(part, cells, first, total):
    chans = total.shape[0]
    y, z = cells
    found = mm(part, picked_depth(z, part.shape[1]))
    for n, row in enumerate(first):
        total = total + jnp.where(y == row, found[n * chans : (n + 1) * chans], 0.0)
    return total


def edge_kernel(
    ndev, cap,
    pre_ref, slot_ref, sums_ref, total_ref, north_ref, south_ref, field_ref, wb_ref, cot_ref,
    own_cells, west_cells, east_cells, recv_ref,
    out_ref, send_far, total, sums_send, slots_send, sems,
):
    cy, chans, nz = cot_ref.shape
    rows = 3 * chans
    own = pl.ds(chans, chans)
    cots = (north_ref[pl.ds(2 * chans, chans)], cot_ref[0], cot_ref[cy - 1], south_ref[pl.ds(2 * chans, chans)])
    added = [ref[pl.ds(n * chans, chans)].astype(F32) for ref, n in ((north_ref, 1), (north_ref, 0), (south_ref, 0), (south_ref, 1))]
    ends = [
        finish_row(pre_ref[n] + added[n], field_ref[0 if n < 2 else 3, own], cots[n]) for n in range(4)
    ]
    out_ref[0], out_ref[1] = ends[1][0], ends[2][0]
    grads = [stacked(grad) for _, grad in ends]
    top = mm(jnp.concatenate([grads[0], grads[1]], axis=0), field_ref[0], NT)
    bottom = mm(jnp.concatenate([grads[2], grads[3]], axis=0), field_ref[3], NT)
    here = [pl.ds(n * rows, rows) for n in range(3)]
    total[here[0]] = total_ref[here[0]] + (top[:rows] + mm(grads[1], field_ref[1], NT))
    total[here[1]] = total_ref[here[1]] + (top[rows:] + bottom[:rows])
    total[here[2]] = total_ref[here[2]] + (bottom[rows:] + mm(grads[2], field_ref[2], NT))
    width = send_far.shape[2]
    share = send_far.shape[1] - 2 * cap
    half = 3 * rows // 2
    taps = total[:, 2 * chans :]
    taps = jnp.concatenate([taps[:half], taps[half:]], axis=1)
    taps = jnp.concatenate([total[:, : 2 * chans], taps], axis=0)
    full = taps.shape[0] // share
    sums_send[pl.ds(0, full)] = taps.reshape(full, share, width).astype(BF16)
    early = pltpu.make_async_copy(
        sums_send.at[pl.ds(0, full)], send_far.at[pl.ds(0, full), pl.ds(0, share)], sems.at[0]
    )
    early.start()
    inner = mm(wb_ref[pl.ds(rows, 2 * rows)], grads[1])
    top = slot_ref[0] + inner[:rows] + mm(wb_ref[pl.ds(2 * rows, rows)], grads[0])
    second = slot_ref[1] + inner[rows:]
    inner = mm(wb_ref[pl.ds(0, 2 * rows)], grads[2])
    third = slot_ref[2] + inner[:rows]
    bottom = slot_ref[3] + inner[rows:] + mm(wb_ref[pl.ds(0, rows)], grads[3])
    found = []
    for dx, cells_ref in enumerate((west_cells, own_cells, east_cells)):
        parts = [value[dx * chans : (dx + 1) * chans] for value in (top, second, third, bottom)]
        if dx == 1:
            inner = (cots[1], cot_ref[1], cot_ref[cy - 2], cots[2])
            parts = [part + cot.astype(F32) for part, cot in zip(parts, inner)]
        part = jnp.concatenate(parts, axis=0).astype(BF16)
        cells = place(cells_ref, nz)
        found.append(at_slots(part, cells, (0, 1, cy - 2, cy - 1), sums_ref[dx]))
    raws = rows_in(recv_ref, ndev, cap)
    proj = sum(mm(found[dx].astype(BF16), raws[dx]) for dx in range(3))
    proj_high = proj.astype(BF16).astype(F32)
    sides = jnp.concatenate([found[0], found[2]], axis=0).T
    middle = jnp.concatenate([found[1], jnp.zeros_like(found[1])], axis=0).T
    halves = [v.reshape(2 * chans // share, share // 2, width) for v in (proj_high, proj - proj_high)]
    proj = jnp.stack(halves, axis=1).reshape(2 * chans // share * 2, share // 2, width)
    rest = ndev - full
    pad = jnp.zeros(((rest * 2 - proj.shape[0]), share // 2, width), F32)
    proj = jnp.concatenate([proj, pad], axis=0).reshape(rest, share, width)
    sums_send[pl.ds(full, rest)] = proj.astype(BF16)
    back = [sides.reshape(ndev, cap, width), middle.reshape(ndev, cap, width)]
    slots_send[...] = jnp.concatenate(back, axis=1).astype(BF16)
    copies = [
        pltpu.make_async_copy(
            sums_send.at[pl.ds(full, rest)], send_far.at[pl.ds(full, rest), pl.ds(0, share)], sems.at[1]
        ),
        pltpu.make_async_copy(slots_send, send_far.at[:, pl.ds(share, 2 * cap)], sems.at[2]),
    ]
    for copy in copies:
        copy.start()
    early.wait()
    for copy in copies:
        copy.wait()


def sums_kernel(chans, cap, recv_ref, index_ref, sums_ref):
    ndev, each, width = recv_ref.shape
    share = each - 2 * cap
    sums = jnp.sum(recv_ref[:, pl.ds(0, share)].astype(F32), axis=0)
    half = share // 2
    whole = sums[:half] + sums[half:]
    high = whole.astype(BF16).astype(F32)
    split = jnp.concatenate([high, whole - high], axis=0)
    device = jnp.broadcast_to(index_ref[...], sums.shape)
    sums = jnp.where(device * share >= 27 * chans * chans // width, split, sums).astype(BF16)
    for n in range(ndev):
        sums_ref[n] = sums


def rows_kernel(ngx, ngy, cap, chans, recv_ref, counts_ref, proj_t_ref, rows_ref):
    ndev = ngx * ngy
    nrows = rows_ref.shape[0]
    width = recv_ref.shape[2]
    slots = ndev * cap
    share = recv_ref.shape[1] - 2 * cap
    arrived = recv_ref[:, pl.ds(share, 2 * cap)].astype(F32)
    sides = arrived[:, :cap].reshape(ngx, ngy, cap, width)
    left = lax.broadcasted_iota(I32, sides.shape, 3) < chans
    sides = jnp.where(left, rolled(sides, 1, 0), rolled(sides, -1, 0)).reshape(slots, width)
    middle = arrived[:, cap:].reshape(slots, width)
    counts = counts_ref[...].astype(F32)
    place = lax.broadcasted_iota(I32, (nrows, ndev), 0).astype(F32)
    lane = lax.broadcasted_iota(I32, (ndev, ndev), 1)
    upto = lax.broadcasted_iota(I32, (ndev, ndev), 0) <= lane
    ends = mm(counts.astype(BF16), jnp.where(upto, 1.0, 0.0).astype(BF16))
    before = ends <= place
    owner = jnp.sum(jnp.where(before, 1.0, 0.0), axis=1, keepdims=True)
    start = jnp.sum(jnp.where(before, counts, 0.0), axis=1, keepdims=True)
    slot = owner * cap + place[:, :1] - start
    onehot = jnp.where(
        lax.broadcasted_iota(I32, (nrows, slots), 1).astype(F32) == slot, 1.0, 0.0
    ).astype(BF16)
    proj_t = proj_t_ref[...]
    both = jnp.concatenate([proj_t, proj_t], axis=0)
    sides = mm(onehot, sides.astype(BF16)).astype(BF16)
    middle = mm(onehot, middle.astype(BF16)).astype(BF16)
    rows_ref[...] = mm(sides, both) + mm(middle, both)


def finish_kernel(conv_scale, proj_scale, share, recv_ref, conv_ref, proj_ref):
    taps, chans, _ = conv_ref.shape
    rows = 9 * chans
    half = rows // 2
    packed = recv_ref[pl.ds(rows, half)].astype(F32)
    column = jnp.concatenate([packed[:, :chans], packed[:, chans:]], axis=0)
    for b in range(3):
        for dz in range(3):
            first = (b * 3 + dz) * chans
            block = recv_ref[pl.ds(first, chans)].astype(F32)
            k = (2 - b) * 3 + dz
            conv_ref[k] = block[:, :chans] * conv_scale
            conv_ref[9 + k] = block[:, chans:] * conv_scale
            conv_ref[18 + k] = column[first : first + chans] * conv_scale
    width = recv_ref.shape[1]
    terms = recv_ref[pl.ds(rows + half, 2 * chans)].astype(F32)
    terms = terms.reshape(2 * chans // share, 2, share // 2, width)
    proj_ref[...] = jnp.sum(terms, axis=1).reshape(chans, width) * proj_scale


def local(particles, send_counts, cell_lists, base_field, proj_weight, conv_weight, cotangent):
    ngx, ngy = lax.axis_size("gx"), lax.axis_size("gy")
    ndev = ngx * ngy
    nrows, feats = particles.shape
    chans, cx, cy, nz = base_field.shape
    slots = cell_lists.shape[1]
    cap = slots // ndev
    count = cx * cy * nz
    assert cx == 1 and feats == 2 * chans
    proj_t = proj_weight.T
    move = functools.partial(send, ngx=ngx, ngy=ngy)
    rows = 3 * chans
    one = 2 * rows * rows * nz

    base = base_field.reshape(chans, cy, nz)
    west, east = move(base_field, 1, 0), move(base_field, -1, 0)
    planes = (base, west.reshape(base.shape), east.reshape(base.shape))
    lists = (cell_lists, move(cell_lists, 1, 0), move(cell_lists, -1, 0))
    (payload,) = call(
        functools.partial(first_kernel, ngx, ngy, cap),
        [shape((ndev * 3 * cap, feats), BF16)],
        (particles, send_counts),
        2 * slots * nrows * feats,
        (
            pltpu.VMEM(particles.shape, BF16),
            pltpu.VMEM(send_counts.shape, I32),
            pltpu.SemaphoreType.DMA((2,)),
        ),
        far=range(2),
        limit=ALL,
    )
    recv = exchange(payload, ndev)

    cot = cotangent[:, 0].transpose(1, 0, 2)
    taps = conv_weight.reshape(3, 3, 3, chans, chans)
    wf = taps.transpose(1, 2, 3, 0, 4).reshape(9 * chans, rows)
    wb = taps.transpose(1, 0, 4, 2, 3).reshape(9 * chans, rows)

    first, last, outer = call(
        functools.partial(outer_kernel, ndev, cap),
        [shape((rows, nz), BF16)] * 2 + [shape((4, rows, nz), BF16)],
        (recv, *planes, *lists, proj_t, cot, wf),
        2 * slots * count * chans,
        (pltpu.VMEM((4 * chans, slots), BF16),),
    )
    north, south = move(last, 0, 1), move(first, 0, -1)
    out_rows, total, pre_edge, slot_edge, sums = call(
        functools.partial(conv_kernel, ndev, cap),
        [
            shape((cy, chans, nz), BF16),
            shape((9 * chans, rows), F32),
            shape((4, chans, nz), F32),
            shape((4, rows, nz), F32),
            shape((3, chans, slots), F32),
        ],
        (recv, proj_t, cot, wf, wb, *planes, *lists),
        3 * cy * 3 * one,
        (
            pltpu.VMEM((cy, rows, nz), BF16),
            pltpu.VMEM((cy + 1, rows, nz), F32),
            pltpu.VMEM((cy + 2, rows, nz), BF16),
            pltpu.VMEM((cy, rows, nz), F32),
            pltpu.VMEM((3, (cy - 4) * chans, nz), BF16),
            pltpu.VMEM((cy * chans, slots), BF16),
        ),
    )
    grad_rows = 27 * chans * chans // feats
    share = -(-(grad_rows + 2 * chans) // (16 * ndev)) * 16
    out_edge, payload = call(
        functools.partial(edge_kernel, ndev, cap),
        [shape((2, chans, nz), BF16), shape((ndev, share + 2 * cap, feats), BF16)],
        (
            pre_edge, slot_edge, sums, total, north, south, outer, wb, cot, *lists, recv,
        ),
        12 * one,
        (
            pltpu.VMEM((9 * chans, rows), F32),
            pltpu.VMEM((ndev, share, feats), BF16),
            pltpu.VMEM((ndev, 2 * cap, feats), BF16),
            pltpu.SemaphoreType.DMA((3,)),
        ),
        far_out=(1,),
    )
    (payload,) = call(same_kernel, [payload], (payload,), 0, far=(0,), far_out=(0,), aliases={0: 0})
    payload = payload.reshape(-1, feats)
    recv = exchange(payload, ndev).reshape(ndev, share + 2 * cap, feats)
    index = (lax.axis_index("gx") * ngy + lax.axis_index("gy")).astype(I32).reshape(1, 1)
    (sums,) = call(
        functools.partial(sums_kernel, chans, cap),
        [shape((ndev, share, feats), BF16)],
        (recv, index),
        1000,
    )
    (row_grads,) = call(
        functools.partial(rows_kernel, ngx, ngy, cap, chans),
        [shape((nrows, feats), F32)],
        (recv, send_counts, proj_t),
        2 * nrows * slots * chans,
    )
    sums = sums.reshape(-1, feats)
    recv = exchange(sums, ndev)
    conv_grad, proj_grad = call(
        functools.partial(
            finish_kernel, 1.0 / math.sqrt(count * ndev), 1.0 / math.sqrt(nrows * ndev), share
        ),
        [shape((27, chans, chans), F32), shape((chans, feats), F32)],
        (recv,),
        1000,
    )
    out_field = jnp.concatenate([out_edge[:1], out_rows[1 : cy - 1], out_edge[1:]], axis=0)
    return (out_field.transpose(1, 0, 2)[:, None], row_grads, conv_grad, proj_grad.T)


def solution(mesh):
    in_specs = (
        P(("gx", "gy"), None),
        P(("gx", "gy"), None),
        P(("gx", "gy"), None),
        P(None, "gx", "gy", None),
        P(),
        P(),
        P(None, "gx", "gy", None),
    )
    out_specs = (P(None, "gx", "gy", None), P(("gx", "gy"), None), P(), P())
    return jax.shard_map(local, mesh=mesh, in_specs=in_specs, out_specs=out_specs, check_vma=False)
```

```python
import functools
import math

import jax
import jax.numpy as jnp
from jax import lax
from jax.experimental import pallas as pl
from jax.experimental.pallas import tpu as pltpu
from jax.sharding import PartitionSpec as P

AXES = ("gx", "gy")
F32, BF16, I32 = jnp.float32, jnp.bfloat16, jnp.int32
LIMIT = 40 * 1024 * 1024
ALL = 60 * 1024 * 1024
NT = (((1,), (1,)), ((), ()))
NN = (((1,), (0,)), ((), ()))


def mm(a, b, dims=NN):
    return lax.dot_general(a, b, dims, preferred_element_type=F32)


def call(kernel, outs, args, flops, scratch=(), far=(), far_out=(), aliases=None, limit=LIMIT, scalar=()):
    traffic = sum(math.prod(a.shape) * a.dtype.itemsize for a in (*args, *outs))
    near = pl.BlockSpec(memory_space=pltpu.VMEM)
    there = pl.BlockSpec(memory_space=pltpu.HBM)
    return pl.pallas_call(
        kernel,
        out_shape=[jax.ShapeDtypeStruct(o.shape, o.dtype) for o in outs],
        in_specs=[
            pl.BlockSpec(memory_space=pltpu.SMEM) if n in scalar else there if n in far else near
            for n in range(len(args))
        ],
        out_specs=[there if n in far_out else near for n in range(len(outs))],
        scratch_shapes=list(scratch),
        input_output_aliases=aliases or {},
        compiler_params=pltpu.CompilerParams(vmem_limit_bytes=limit),
        cost_estimate=pl.CostEstimate(flops=flops, bytes_accessed=traffic, transcendentals=0),
    )(*args)


def shape(dims, dtype):
    return jax.ShapeDtypeStruct(dims, dtype)


def send(block, di, dj, ngx, ngy):
    pairs = []
    for i in range(ngx):
        for j in range(ngy):
            pairs.append((i * ngy + j, ((i + di) % ngx) * ngy + (j + dj) % ngy))
    return lax.ppermute(block, AXES, pairs)


def swap(block):
    return lax.ppermute(block, "gx", [(i, i ^ 1) for i in range(lax.axis_size("gx"))])


def exchange(payload, ndev):
    rows, width = payload.shape
    moved = lax.all_to_all(
        payload.reshape(ndev, rows // ndev, width), AXES, split_axis=0, concat_axis=0, tiled=True
    )
    return moved.reshape(rows, width)


def rolled(x, di, dj):
    for axis, shift in ((0, di), (1, dj)):
        if shift == 1:
            head, tail = lax.slice_in_dim(x, 1, None, axis=axis), lax.slice_in_dim(x, 0, 1, axis=axis)
            x = jnp.concatenate([head, tail], axis=axis)
        elif shift == -1:
            count = x.shape[axis]
            head = lax.slice_in_dim(x, count - 1, count, axis=axis)
            x = jnp.concatenate([head, lax.slice_in_dim(x, 0, count - 1, axis=axis)], axis=axis)
    return x


def picked_depth(z, nz):
    depth = lax.broadcasted_iota(I32, (nz, z.shape[1]), 0)
    return jnp.where(depth == z, 1.0, 0.0).astype(BF16)


def rows_in(recv_ref, ndev, cap):
    width = recv_ref.shape[1]
    arrived = recv_ref[...].astype(F32).reshape(ndev, 3, cap, width)
    return [arrived[:, n].reshape(ndev * cap, width).astype(BF16) for n in range(3)]


def stacked(grad):
    nz = grad.shape[1]
    wide = grad.astype(F32)
    return jnp.concatenate(
        [pltpu.roll(wide, nz - 1, 1), wide, pltpu.roll(wide, 1, 1)], axis=0
    ).astype(BF16)


def over_depth(acc):
    chans, nz = acc.shape[0] // 3, acc.shape[1]
    total = acc[chans : 2 * chans] + pltpu.roll(acc[:chans], 1, 1)
    return total + pltpu.roll(acc[2 * chans :], nz - 1, 1)


def finish_row(pre, field, cot):
    sig = jax.nn.sigmoid(pre)
    out = field.astype(F32) + pre * sig
    grad = cot.astype(F32) * sig * (1.0 + pre * (1.0 - sig))
    return out.astype(BF16), grad.astype(BF16)


def first_kernel(
    ngx, ngy, cap, rows_far, counts_far, send_ref, rows_ref, counts_ref, sems
):
    copies = [
        pltpu.make_async_copy(rows_far, rows_ref, sems.at[0]),
        pltpu.make_async_copy(counts_far, counts_ref, sems.at[1]),
    ]
    for copy in copies:
        copy.start()
    for copy in copies:
        copy.wait()
    pick(ngx, ngy, cap, counts_ref, rows_ref, send_ref)


def same_kernel(in_ref, out_ref):
    pass


def pick(ngx, ngy, cap, counts_ref, rows_ref, out_ref):
    ndev = ngx * ngy
    nrows, feats = rows_ref.shape
    slots = ndev * cap
    counts = counts_ref[...].astype(F32)
    owner = lax.broadcasted_iota(I32, (ndev, cap, ndev), 0).reshape(slots, ndev)
    lane = lax.broadcasted_iota(I32, (slots, ndev), 1)
    start = jnp.sum(jnp.where(lane < owner, counts, 0.0), axis=1, keepdims=True)
    held = jnp.sum(jnp.where(lane == owner, counts, 0.0), axis=1, keepdims=True)
    place = lax.broadcasted_iota(I32, (ndev, cap, nrows), 1).reshape(slots, nrows).astype(F32)
    row = lax.broadcasted_iota(I32, (slots, nrows), 1).astype(F32)
    onehot = jnp.where((row == place + start) & (place < held), 1.0, 0.0).astype(BF16)
    raw = mm(onehot, rows_ref[...]).reshape(ngx, ngy, cap, feats)
    parts = [rolled(raw, dx, 0).reshape(ndev, cap, feats) for dx in (-1, 0, 1)]
    out_ref[...] = jnp.stack(parts, axis=1).reshape(out_ref.shape).astype(BF16)


def painted_rows(values, cells, nz, ns, masked):
    chans = values.shape[0]
    y, z = cells
    for n, row in enumerate(ns):
        masked[pl.ds(n * chans, chans)] = values * jnp.where(y == row, 1.0, 0.0).astype(BF16)
    return mm(masked[pl.ds(0, len(ns) * chans)], picked_depth(z, nz), NT)


def outer_kernel(
    ndev, cap, recv_ref, own_ref, west_ref, east_ref, own_cells, west_cells, east_cells,
    proj_t_ref, cot_ref, wf_ref, first_ref, last_ref, field_ref, masked,
):
    chans, cy, nz = own_ref.shape
    rows = 3 * chans
    raws = rows_in(recv_ref, ndev, cap)
    ns = (0, 1, cy - 2, cy - 1)
    planes = ((west_ref, west_cells), (own_ref, own_cells), (east_ref, east_cells))
    for dx, (ref, cells_ref) in enumerate(planes):
        values = mm(proj_t_ref[...], raws[dx], NT).astype(BF16)
        painted = painted_rows(values, place(cells_ref, nz), nz, ns, masked)
        base = turned(ref)
        for n, row in enumerate(ns):
            part = painted[n * chans : (n + 1) * chans]
            field_ref[n, pl.ds(dx * chans, chans)] = (base[row] + part).astype(BF16)
    near = mm(wf_ref[pl.ds(0, 2 * rows)], field_ref[3])
    far = mm(wf_ref[pl.ds(0, rows)], field_ref[2])
    last_ref[pl.ds(0, chans)] = over_depth(near[:rows]).astype(BF16)
    last_ref[pl.ds(chans, chans)] = over_depth(near[rows:] + far).astype(BF16)
    last_ref[pl.ds(2 * chans, chans)] = cot_ref[cy - 1]
    near = mm(wf_ref[pl.ds(rows, 2 * rows)], field_ref[0])
    far = mm(wf_ref[pl.ds(2 * rows, rows)], field_ref[1])
    first_ref[pl.ds(0, chans)] = over_depth(near[rows:]).astype(BF16)
    first_ref[pl.ds(chans, chans)] = over_depth(near[:rows] + far).astype(BF16)
    first_ref[pl.ds(2 * chans, chans)] = cot_ref[0]


def place(cells_ref, nz):
    cells = cells_ref[...]
    return cells // nz, cells % nz


def turned(ref):
    return jnp.swapaxes(ref[...].astype(F32), 0, 1)


def conv_kernel(
    ndev, cap, recv_ref, proj_t_ref, cot_ref, wf_ref, wb_ref,
    own_ref, west_ref, east_ref, own_cells, west_cells, east_cells,
    out_ref, total_ref, pre_ref, slot_ref, sums_ref, x_ref, acc, grads, back, plane, masked,
):
    chans, cy, nz = own_ref.shape
    rows = 3 * chans
    slots = ndev * cap
    raws = rows_in(recv_ref, ndev, cap)
    planes = ((west_ref, west_cells), (own_ref, own_cells), (east_ref, east_cells))
    for dx, (ref, cells_ref) in enumerate(planes):
        values = mm(proj_t_ref[...], raws[dx], NT).astype(BF16)
        painted = painted_rows(values, place(cells_ref, nz), nz, range(cy), masked)
        field = turned(ref) + painted.reshape(cy, chans, nz)
        x_ref[:, pl.ds(dx * chans, chans)] = field.astype(BF16)
    own = pl.ds(chans, chans)
    zeros = jnp.zeros((rows, nz), BF16)
    for t in (0, 1, cy, cy + 1):
        grads[t] = zeros
    out_ref[0] = zeros[:chans]
    out_ref[cy - 1] = zeros[:chans]
    acc[0] = jnp.zeros((rows, nz), F32)

    def spread(n):
        terms = mm(wf_ref[...], x_ref[n])
        acc[n + 1] = terms[:rows]
        acc[n] += terms[rows : 2 * rows]
        return terms[2 * rows :]

    pre_ref[0] = over_depth(spread(0))
    pre_ref[1] = over_depth(acc[0] + spread(1))

    def forward(n):
        done = spread(n) + acc[n - 1]
        y = n - 1
        out, grad = finish_row(over_depth(done), x_ref[y, own], cot_ref[y])
        out_ref[y] = out
        grads[y + 1] = stacked(grad)

    for n in range(2, cy):
        forward(n)
    pre_ref[2] = over_depth(acc[cy - 1])
    pre_ref[3] = over_depth(acc[cy])
    total_ref[...] = jnp.zeros_like(total_ref)
    back[0] = jnp.zeros((rows, nz), F32)
    back[1] = jnp.zeros((rows, nz), F32)

    def taps(n):
        window = grads[pl.ds(n, 3)].reshape(3 * rows, nz)
        total_ref[...] += mm(window, x_ref[n], NT)

    def spread_back(n):
        terms = mm(wb_ref[...], grads[n + 1])
        back[n + 1] = terms[2 * rows :]
        back[n] += terms[rows : 2 * rows]
        return terms[:rows]

    def backward(n):
        taps(n)
        value = spread_back(n) + back[n - 1]
        for dx in range(3):
            part = value[dx * chans : (dx + 1) * chans]
            if dx == 1:
                part = part + cot_ref[n - 1].astype(F32)
            plane[dx, pl.ds((n - 3) * chans, chans)] = part.astype(BF16)

    taps(0)
    taps(1)
    slot_ref[0] = spread_back(1)
    taps(2)
    slot_ref[1] = spread_back(2) + back[1]
    for n in range(3, cy - 1):
        backward(n)
    taps(cy - 1)
    slot_ref[2] = back[cy - 2]
    slot_ref[3] = back[cy - 1]
    zero = jnp.zeros((chans, slots), F32)
    for dx, (_, cells_ref) in enumerate(planes):
        sums_ref[dx] = at_slots(plane[dx], place(cells_ref, nz), range(2, cy - 2), zero)


def at_slots(part, cells, first, total):
    chans = total.shape[0]
    y, z = cells
    found = mm(part, picked_depth(z, part.shape[1]))
    for n, row in enumerate(first):
        total = total + jnp.where(y == row, found[n * chans : (n + 1) * chans], 0.0)
    return total


def edge_kernel(
    part, parity_ref, pre_ref, total_ref, north_ref, south_ref, field_ref, cot_ref,
    out_ref, grads_ref, keep_ref, give_ref, total, sums,
):
    cy, chans, nz = cot_ref.shape
    rows = 3 * chans
    own = pl.ds(chans, chans)
    last = pl.ds(2 * chans, chans)
    cots = (north_ref[last], cot_ref[0], cot_ref[cy - 1], south_ref[last])
    sides = ((north_ref, 1), (north_ref, 0), (south_ref, 0), (south_ref, 1))
    ends = []
    for n, (ref, at) in enumerate(sides):
        pre = pre_ref[n] + ref[pl.ds(at * chans, chans)].astype(F32)
        ends.append(finish_row(pre, field_ref[0 if n < 2 else 3, own], cots[n]))
    out_ref[0], out_ref[1] = ends[1][0], ends[2][0]
    grads = [stacked(grad) for _, grad in ends]
    for n in range(4):
        grads_ref[n] = grads[n]
    top = mm(jnp.concatenate([grads[0], grads[1]], axis=0), field_ref[0], NT)
    bottom = mm(jnp.concatenate([grads[2], grads[3]], axis=0), field_ref[3], NT)
    here = [pl.ds(n * rows, rows) for n in range(3)]
    total[here[0]] = total_ref[here[0]] + (top[:rows] + mm(grads[1], field_ref[1], NT))
    total[here[1]] = total_ref[here[1]] + (top[rows:] + bottom[:rows])
    total[here[2]] = total_ref[here[2]] + (bottom[rows:] + mm(grads[2], field_ref[2], NT))
    full, _, width = keep_ref.shape
    half = 3 * rows // 2
    split = 3 * rows // (2 * part)
    sums[pl.ds(0, split)] = total[:, :width].reshape(split, 2, part, width)
    taps = jnp.concatenate([total[pl.ds(0, half), width:], total[pl.ds(half, half), width:]], axis=1)
    sums[pl.ds(split, full - split)] = taps.reshape(full - split, 2, part, width)
    parity = parity_ref[0]
    keep_ref[...] = sums[:, parity]
    give_ref[...] = sums[:, 1 - parity]


def slots_kernel(
    ndev, cap, part, full, slot_ref, sums_ref, grads_ref, wb_ref, cot_ref,
    own_cells, west_cells, east_cells, recv_ref, send_far, slots_send, proj_send, sems,
):
    cy, chans, nz = cot_ref.shape
    rows = 3 * chans
    inner = mm(wb_ref[pl.ds(rows, 2 * rows)], grads_ref[1])
    top = slot_ref[0] + inner[:rows] + mm(wb_ref[pl.ds(2 * rows, rows)], grads_ref[0])
    second = slot_ref[1] + inner[rows:]
    inner = mm(wb_ref[pl.ds(0, 2 * rows)], grads_ref[2])
    third = slot_ref[2] + inner[:rows]
    bottom = slot_ref[3] + inner[rows:] + mm(wb_ref[pl.ds(0, rows)], grads_ref[3])
    at = (0, 1, cy - 2, cy - 1)
    found = []
    for dx, cells_ref in enumerate((west_cells, own_cells, east_cells)):
        parts = [value[dx * chans : (dx + 1) * chans] for value in (top, second, third, bottom)]
        if dx == 1:
            parts = [value + cot_ref[n].astype(F32) for value, n in zip(parts, at)]
        terms = jnp.concatenate(parts, axis=0).astype(BF16)
        found.append(at_slots(terms, place(cells_ref, nz), at, sums_ref[dx]))
    sides = jnp.concatenate([found[0], found[2]], axis=0).T
    middle = jnp.concatenate([found[1], jnp.zeros_like(found[1])], axis=0).T
    width = send_far.shape[2]
    back = [sides.reshape(ndev, cap, width), middle.reshape(ndev, cap, width)]
    slots_send[...] = jnp.concatenate(back, axis=1).astype(BF16)
    copies = [pltpu.make_async_copy(slots_send, send_far.at[:, pl.ds(part, 2 * cap)], sems.at[0])]
    copies[0].start()
    raws = rows_in(recv_ref, ndev, cap)
    proj = sum(mm(found[dx].astype(BF16), raws[dx]) for dx in range(3))
    rest = ndev - full
    pad = jnp.zeros((rest * part - chans, width), F32)
    proj = jnp.concatenate([proj, pad], axis=0).reshape(rest, part, width)
    proj_send[...] = proj.astype(BF16)
    copies.append(
        pltpu.make_async_copy(proj_send, send_far.at[pl.ds(full, rest), pl.ds(0, part)], sems.at[1])
    )
    copies[1].start()
    for copy in copies:
        copy.wait()


def pair_kernel(keep_ref, got_ref, same_far, send_far, sums_send, sem):
    full, part, _ = keep_ref.shape
    sums_send[...] = (keep_ref[...] + got_ref[...]).astype(BF16)
    copy = pltpu.make_async_copy(sums_send, send_far.at[pl.ds(0, full), pl.ds(0, part)], sem)
    copy.start()
    copy.wait()


def sums_kernel(ngx, ngy, full, cap, recv_ref, index_ref, sums_ref):
    ndev, each, width = recv_ref.shape
    part = each - 2 * cap
    terms = recv_ref[:, pl.ds(0, part)].astype(F32).reshape(ngx // 2, 2, ngy, part, width)
    sums = jnp.sum(terms, axis=(0, 2))
    whole = sums[0] + sums[1]
    high = whole.astype(BF16).astype(F32)
    last = jnp.broadcast_to(index_ref[...], whole.shape) >= full
    sums = [
        jnp.where(last, high, sums[0]).astype(BF16),
        jnp.where(last, whole - high, sums[1]).astype(BF16),
    ]
    for n in range(ndev):
        sums_ref[n] = sums[(n // ngy) % 2]


def rows_kernel(ngx, ngy, cap, chans, recv_ref, counts_ref, proj_t_ref, rows_ref):
    ndev = ngx * ngy
    nrows = rows_ref.shape[0]
    width = recv_ref.shape[2]
    slots = ndev * cap
    share = recv_ref.shape[1] - 2 * cap
    arrived = recv_ref[:, pl.ds(share, 2 * cap)].astype(F32)
    sides = arrived[:, :cap].reshape(ngx, ngy, cap, width)
    left = lax.broadcasted_iota(I32, sides.shape, 3) < chans
    sides = jnp.where(left, rolled(sides, 1, 0), rolled(sides, -1, 0)).reshape(slots, width)
    middle = arrived[:, cap:].reshape(slots, width)
    counts = counts_ref[...].astype(F32)
    place = lax.broadcasted_iota(I32, (nrows, ndev), 0).astype(F32)
    lane = lax.broadcasted_iota(I32, (ndev, ndev), 1)
    upto = lax.broadcasted_iota(I32, (ndev, ndev), 0) <= lane
    ends = mm(counts.astype(BF16), jnp.where(upto, 1.0, 0.0).astype(BF16))
    before = ends <= place
    owner = jnp.sum(jnp.where(before, 1.0, 0.0), axis=1, keepdims=True)
    start = jnp.sum(jnp.where(before, counts, 0.0), axis=1, keepdims=True)
    slot = owner * cap + place[:, :1] - start
    onehot = jnp.where(
        lax.broadcasted_iota(I32, (nrows, slots), 1).astype(F32) == slot, 1.0, 0.0
    ).astype(BF16)
    proj_t = proj_t_ref[...]
    both = jnp.concatenate([proj_t, proj_t], axis=0)
    sides = mm(onehot, sides.astype(BF16)).astype(BF16)
    middle = mm(onehot, middle.astype(BF16)).astype(BF16)
    rows_ref[...] = mm(sides, both) + mm(middle, both)


def finish_kernel(conv_scale, proj_scale, parity_ref, mine_ref, other_ref, conv_ref, proj_ref, both):
    ndev, part, width = mine_ref.shape
    parity = parity_ref[0]
    both[:, parity] = mine_ref[...]
    both[:, 1 - parity] = other_ref[...]
    sums = both[...].astype(F32).reshape(ndev * 2 * part, width)
    taps, chans, _ = conv_ref.shape
    rows = 9 * chans
    half = rows // 2
    packed = sums[rows : rows + half]
    column = jnp.concatenate([packed[:, :chans], packed[:, chans:]], axis=0)
    for b in range(3):
        for dz in range(3):
            first = (b * 3 + dz) * chans
            block = sums[first : first + chans]
            k = (2 - b) * 3 + dz
            conv_ref[k] = block[:, :chans] * conv_scale
            conv_ref[9 + k] = block[:, chans:] * conv_scale
            conv_ref[18 + k] = column[first : first + chans] * conv_scale
    terms = sums[rows + half : rows + half + 2 * chans].reshape(chans // part, 2, part, width)
    proj_ref[...] = jnp.sum(terms, axis=1).reshape(chans, width) * proj_scale


def local(particles, send_counts, cell_lists, base_field, proj_weight, conv_weight, cotangent):
    ngx, ngy = lax.axis_size("gx"), lax.axis_size("gy")
    ndev = ngx * ngy
    nrows, feats = particles.shape
    chans, cx, cy, nz = base_field.shape
    slots = cell_lists.shape[1]
    cap = slots // ndev
    count = cx * cy * nz
    assert cx == 1 and feats == 2 * chans
    proj_t = proj_weight.T
    move = functools.partial(send, ngx=ngx, ngy=ngy)
    rows = 3 * chans
    one = 2 * rows * rows * nz

    base = base_field.reshape(chans, cy, nz)
    west, east = move(base_field, 1, 0), move(base_field, -1, 0)
    planes = (base, west.reshape(base.shape), east.reshape(base.shape))
    lists = (cell_lists, move(cell_lists, 1, 0), move(cell_lists, -1, 0))
    (payload,) = call(
        functools.partial(first_kernel, ngx, ngy, cap),
        [shape((ndev * 3 * cap, feats), BF16)],
        (particles, send_counts),
        2 * slots * nrows * feats,
        (
            pltpu.VMEM(particles.shape, BF16),
            pltpu.VMEM(send_counts.shape, I32),
            pltpu.SemaphoreType.DMA((2,)),
        ),
        far=range(2),
        limit=ALL,
    )
    recv = exchange(payload, ndev)

    cot = cotangent[:, 0].transpose(1, 0, 2)
    taps = conv_weight.reshape(3, 3, 3, chans, chans)
    wf = taps.transpose(1, 2, 3, 0, 4).reshape(9 * chans, rows)
    wb = taps.transpose(1, 0, 4, 2, 3).reshape(9 * chans, rows)

    first, last, outer = call(
        functools.partial(outer_kernel, ndev, cap),
        [shape((rows, nz), BF16)] * 2 + [shape((4, rows, nz), BF16)],
        (recv, *planes, *lists, proj_t, cot, wf),
        2 * slots * count * chans,
        (pltpu.VMEM((4 * chans, slots), BF16),),
    )
    south, north = move(first, 0, -1), move(last, 0, 1)
    out_rows, total, pre_edge, slot_edge, sums = call(
        functools.partial(conv_kernel, ndev, cap),
        [
            shape((cy, chans, nz), BF16),
            shape((9 * chans, rows), F32),
            shape((4, chans, nz), F32),
            shape((4, rows, nz), F32),
            shape((3, chans, slots), F32),
        ],
        (recv, proj_t, cot, wf, wb, *planes, *lists),
        3 * cy * 3 * one,
        (
            pltpu.VMEM((cy, rows, nz), BF16),
            pltpu.VMEM((cy + 1, rows, nz), F32),
            pltpu.VMEM((cy + 2, rows, nz), BF16),
            pltpu.VMEM((cy, rows, nz), F32),
            pltpu.VMEM((3, (cy - 4) * chans, nz), BF16),
            pltpu.VMEM((cy * chans, slots), BF16),
        ),
    )
    grad_rows = 27 * chans * chans // feats
    part = -(-(grad_rows + 2 * chans) // (32 * ndev)) * 16
    full = grad_rows // (2 * part)
    assert ngx % 2 == 0 and full * 2 * part == grad_rows
    row = lax.axis_index("gx")
    parity = (row % 2).astype(I32).reshape(1)
    out_edge, grads, keep, give = call(
        functools.partial(edge_kernel, part),
        [
            shape((2, chans, nz), BF16),
            shape((4, rows, nz), BF16),
            shape((full, part, feats), F32),
            shape((full, part, feats), F32),
        ],
        (parity, pre_edge, total, north, south, outer, cot),
        6 * one,
        (pltpu.VMEM((9 * chans, rows), F32), pltpu.VMEM((full, 2, part, feats), F32)),
        scalar=(0,),
    )
    got = swap(give)
    (payload,) = call(
        functools.partial(slots_kernel, ndev, cap, part, full),
        [shape((ndev, part + 2 * cap, feats), BF16)],
        (slot_edge, sums, grads, wb, cot, *lists, recv),
        6 * one,
        (
            pltpu.VMEM((ndev, 2 * cap, feats), BF16),
            pltpu.VMEM((ndev - full, part, feats), BF16),
            pltpu.SemaphoreType.DMA((2,)),
        ),
        far_out=(0,),
    )
    (payload,) = call(
        pair_kernel,
        [payload],
        (keep, got, payload),
        1000,
        (pltpu.VMEM((full, part, feats), BF16), pltpu.SemaphoreType.DMA),
        far=(2,),
        far_out=(0,),
        aliases={2: 0},
    )
    recv = exchange(payload.reshape(-1, feats), ndev).reshape(payload.shape)
    index = (row * ngy + lax.axis_index("gy")).astype(I32).reshape(1, 1)
    (sums,) = call(
        functools.partial(sums_kernel, ngx, ngy, full, cap),
        [shape((ndev, part, feats), BF16)],
        (recv, index),
        1000,
    )
    (row_grads,) = call(
        functools.partial(rows_kernel, ngx, ngy, cap, chans),
        [shape((nrows, feats), F32)],
        (recv, send_counts, proj_t),
        2 * nrows * slots * chans,
    )
    mine = exchange(sums.reshape(-1, feats), ndev).reshape(sums.shape)
    other = swap(mine)
    conv_grad, proj_grad = call(
        functools.partial(
            finish_kernel, 1.0 / math.sqrt(count * ndev), 1.0 / math.sqrt(nrows * ndev)
        ),
        [shape((27, chans, chans), F32), shape((chans, feats), F32)],
        (parity, mine, other),
        1000,
        (pltpu.VMEM((ndev, 2, part, feats), BF16),),
        scalar=(0,),
    )
    out_field = jnp.concatenate([out_edge[:1], out_rows[1 : cy - 1], out_edge[1:]], axis=0)
    return (out_field.transpose(1, 0, 2)[:, None], row_grads, conv_grad, proj_grad.T)


def solution(mesh):
    in_specs = (
        P(("gx", "gy"), None),
        P(("gx", "gy"), None),
        P(("gx", "gy"), None),
        P(None, "gx", "gy", None),
        P(),
        P(),
        P(None, "gx", "gy", None),
    )
    out_specs = (P(None, "gx", "gy", None), P(("gx", "gy"), None), P(), P())
    return jax.shard_map(local, mesh=mesh, in_specs=in_specs, out_specs=out_specs, check_vma=False)
```

```python
import functools
import math

import jax
import jax.numpy as jnp
from jax import lax
from jax.experimental import pallas as pl
from jax.experimental.pallas import tpu as pltpu
from jax.sharding import PartitionSpec as P

AXES = ("gx", "gy")
F32, BF16, I32 = jnp.float32, jnp.bfloat16, jnp.int32
LIMIT = 40 * 1024 * 1024
ALL = 60 * 1024 * 1024
NT = (((1,), (1,)), ((), ()))
NN = (((1,), (0,)), ((), ()))


def mm(a, b, dims=NN):
    return lax.dot_general(a, b, dims, preferred_element_type=F32)


def call(kernel, outs, args, flops, scratch=(), far=(), far_out=(), aliases=None, limit=LIMIT, scalar=()):
    traffic = sum(math.prod(a.shape) * a.dtype.itemsize for a in (*args, *outs))
    near = pl.BlockSpec(memory_space=pltpu.VMEM)
    there = pl.BlockSpec(memory_space=pltpu.HBM)
    return pl.pallas_call(
        kernel,
        out_shape=[jax.ShapeDtypeStruct(o.shape, o.dtype) for o in outs],
        in_specs=[
            pl.BlockSpec(memory_space=pltpu.SMEM) if n in scalar else there if n in far else near
            for n in range(len(args))
        ],
        out_specs=[there if n in far_out else near for n in range(len(outs))],
        scratch_shapes=list(scratch),
        input_output_aliases=aliases or {},
        compiler_params=pltpu.CompilerParams(vmem_limit_bytes=limit),
        cost_estimate=pl.CostEstimate(flops=flops, bytes_accessed=traffic, transcendentals=0),
    )(*args)


def shape(dims, dtype):
    return jax.ShapeDtypeStruct(dims, dtype)


def send(block, di, dj, ngx, ngy):
    pairs = []
    for i in range(ngx):
        for j in range(ngy):
            pairs.append((i * ngy + j, ((i + di) % ngx) * ngy + (j + dj) % ngy))
    return lax.ppermute(block, AXES, pairs)


def swap(block):
    return lax.ppermute(block, "gx", [(i, i ^ 1) for i in range(lax.axis_size("gx"))])


def exchange(payload, ndev):
    rows, width = payload.shape
    moved = lax.all_to_all(
        payload.reshape(ndev, rows // ndev, width), AXES, split_axis=0, concat_axis=0, tiled=True
    )
    return moved.reshape(rows, width)


def rolled(x, di, dj):
    for axis, shift in ((0, di), (1, dj)):
        if shift == 1:
            head, tail = lax.slice_in_dim(x, 1, None, axis=axis), lax.slice_in_dim(x, 0, 1, axis=axis)
            x = jnp.concatenate([head, tail], axis=axis)
        elif shift == -1:
            count = x.shape[axis]
            head = lax.slice_in_dim(x, count - 1, count, axis=axis)
            x = jnp.concatenate([head, lax.slice_in_dim(x, 0, count - 1, axis=axis)], axis=axis)
    return x


def picked_depth(z, nz):
    depth = lax.broadcasted_iota(I32, (nz, z.shape[1]), 0)
    return jnp.where(depth == z, 1.0, 0.0).astype(BF16)


def rows_in(recv_ref, ndev, cap):
    width = recv_ref.shape[1]
    arrived = recv_ref[...].astype(F32).reshape(ndev, 3, cap, width)
    return [arrived[:, n].reshape(ndev * cap, width).astype(BF16) for n in range(3)]


def stacked(grad):
    nz = grad.shape[1]
    wide = grad.astype(F32)
    return jnp.concatenate(
        [pltpu.roll(wide, nz - 1, 1), wide, pltpu.roll(wide, 1, 1)], axis=0
    ).astype(BF16)


def over_depth(acc):
    chans, nz = acc.shape[0] // 3, acc.shape[1]
    total = acc[chans : 2 * chans] + pltpu.roll(acc[:chans], 1, 1)
    return total + pltpu.roll(acc[2 * chans :], nz - 1, 1)


def finish_row(pre, field, cot):
    sig = jax.nn.sigmoid(pre)
    out = field.astype(F32) + pre * sig
    grad = cot.astype(F32) * sig * (1.0 + pre * (1.0 - sig))
    return out.astype(BF16), grad.astype(BF16)


def first_kernel(
    ngx, ngy, cap, rows_far, counts_far, send_ref, rows_ref, counts_ref, sems
):
    copies = [
        pltpu.make_async_copy(rows_far, rows_ref, sems.at[0]),
        pltpu.make_async_copy(counts_far, counts_ref, sems.at[1]),
    ]
    for copy in copies:
        copy.start()
    for copy in copies:
        copy.wait()
    pick(ngx, ngy, cap, counts_ref, rows_ref, send_ref)


def same_kernel(in_ref, out_ref):
    pass


def pick(ngx, ngy, cap, counts_ref, rows_ref, out_ref):
    ndev = ngx * ngy
    nrows, feats = rows_ref.shape
    slots = ndev * cap
    counts = counts_ref[...].astype(F32)
    owner = lax.broadcasted_iota(I32, (ndev, cap, ndev), 0).reshape(slots, ndev)
    lane = lax.broadcasted_iota(I32, (slots, ndev), 1)
    start = jnp.sum(jnp.where(lane < owner, counts, 0.0), axis=1, keepdims=True)
    held = jnp.sum(jnp.where(lane == owner, counts, 0.0), axis=1, keepdims=True)
    place = lax.broadcasted_iota(I32, (ndev, cap, nrows), 1).reshape(slots, nrows).astype(F32)
    row = lax.broadcasted_iota(I32, (slots, nrows), 1).astype(F32)
    onehot = jnp.where((row == place + start) & (place < held), 1.0, 0.0).astype(BF16)
    raw = mm(onehot, rows_ref[...]).reshape(ngx, ngy, cap, feats)
    parts = [rolled(raw, dx, 0).reshape(ndev, cap, feats) for dx in (-1, 0, 1)]
    out_ref[...] = jnp.stack(parts, axis=1).reshape(out_ref.shape).astype(BF16)


def painted_rows(values, cells, nz, ns, masked):
    chans = values.shape[0]
    y, z = cells
    for n, row in enumerate(ns):
        masked[pl.ds(n * chans, chans)] = values * jnp.where(y == row, 1.0, 0.0).astype(BF16)
    return mm(masked[pl.ds(0, len(ns) * chans)], picked_depth(z, nz), NT)


def add_to_rows(near, far, cot, rows, back, out_ref):
    chans = cot.shape[0]
    at, over = (rows, 0) if back else (0, rows)
    out_ref[pl.ds(0, chans)] = over_depth(near[at : at + rows]).astype(BF16)
    out_ref[pl.ds(chans, chans)] = over_depth(near[over : over + rows] + far).astype(BF16)
    out_ref[pl.ds(2 * chans, chans)] = cot


def outer_kernel(
    ndev, cap, recv_ref, own_ref, west_ref, east_ref, own_cells, west_cells, east_cells,
    proj_t_ref, cot_ref, wf_ref, first_ref, masked, field,
):
    chans, cy, nz = own_ref.shape
    rows = 3 * chans
    raws = rows_in(recv_ref, ndev, cap)
    planes = ((west_ref, west_cells), (own_ref, own_cells), (east_ref, east_cells))
    for dx, (ref, cells_ref) in enumerate(planes):
        values = mm(proj_t_ref[...], raws[dx], NT).astype(BF16)
        painted = painted_rows(values, place(cells_ref, nz), nz, (0, 1), masked)
        base = turned(ref)
        for n in range(2):
            part = painted[n * chans : (n + 1) * chans]
            field[n, pl.ds(dx * chans, chans)] = (base[n] + part).astype(BF16)
    near = mm(wf_ref[pl.ds(rows, 2 * rows)], field[0])
    far = mm(wf_ref[pl.ds(2 * rows, rows)], field[1])
    add_to_rows(near, far, cot_ref[0], rows, True, first_ref)


def field_kernel(
    ndev, cap, recv_ref, own_ref, west_ref, east_ref, own_cells, west_cells, east_cells,
    proj_t_ref, cot_ref, wf_ref, x_ref, last_ref, masked,
):
    chans, cy, nz = own_ref.shape
    rows = 3 * chans
    raws = rows_in(recv_ref, ndev, cap)
    planes = ((west_ref, west_cells), (own_ref, own_cells), (east_ref, east_cells))
    for dx, (ref, cells_ref) in enumerate(planes):
        values = mm(proj_t_ref[...], raws[dx], NT).astype(BF16)
        painted = painted_rows(values, place(cells_ref, nz), nz, range(cy), masked)
        field = turned(ref) + painted.reshape(cy, chans, nz)
        x_ref[:, pl.ds(dx * chans, chans)] = field.astype(BF16)
    near = mm(wf_ref[pl.ds(0, 2 * rows)], x_ref[cy - 1])
    far = mm(wf_ref[pl.ds(0, rows)], x_ref[cy - 2])
    add_to_rows(near, far, cot_ref[cy - 1], rows, False, last_ref)


def place(cells_ref, nz):
    cells = cells_ref[...]
    return cells // nz, cells % nz


def turned(ref):
    return jnp.swapaxes(ref[...].astype(F32), 0, 1)


def conv_kernel(
    x_ref, cot_ref, wf_ref, wb_ref, own_cells, west_cells, east_cells,
    out_ref, total_ref, pre_ref, slot_ref, sums_ref, acc, grads, back, plane,
):
    cy, chans, nz = cot_ref.shape
    rows = 3 * chans
    slots = own_cells.shape[1]
    own = pl.ds(chans, chans)
    zeros = jnp.zeros((rows, nz), BF16)
    for t in (0, 1, cy, cy + 1):
        grads[t] = zeros
    out_ref[0] = zeros[:chans]
    out_ref[cy - 1] = zeros[:chans]
    acc[0] = jnp.zeros((rows, nz), F32)

    def spread(n):
        terms = mm(wf_ref[...], x_ref[n])
        acc[n + 1] = terms[:rows]
        acc[n] += terms[rows : 2 * rows]
        return terms[2 * rows :]

    pre_ref[0] = over_depth(spread(0))
    pre_ref[1] = over_depth(acc[0] + spread(1))

    def forward(n):
        done = spread(n) + acc[n - 1]
        y = n - 1
        out, grad = finish_row(over_depth(done), x_ref[y, own], cot_ref[y])
        out_ref[y] = out
        grads[y + 1] = stacked(grad)

    for n in range(2, cy):
        forward(n)
    pre_ref[2] = over_depth(acc[cy - 1])
    pre_ref[3] = over_depth(acc[cy])
    total_ref[...] = jnp.zeros_like(total_ref)
    back[0] = jnp.zeros((rows, nz), F32)
    back[1] = jnp.zeros((rows, nz), F32)

    def taps(n):
        window = grads[pl.ds(n, 3)].reshape(3 * rows, nz)
        total_ref[...] += mm(window, x_ref[n], NT)

    def spread_back(n):
        terms = mm(wb_ref[...], grads[n + 1])
        back[n + 1] = terms[2 * rows :]
        back[n] += terms[rows : 2 * rows]
        return terms[:rows]

    def backward(n):
        taps(n)
        value = spread_back(n) + back[n - 1]
        for dx in range(3):
            part = value[dx * chans : (dx + 1) * chans]
            if dx == 1:
                part = part + cot_ref[n - 1].astype(F32)
            plane[dx, pl.ds((n - 3) * chans, chans)] = part.astype(BF16)

    taps(0)
    taps(1)
    slot_ref[0] = spread_back(1)
    taps(2)
    slot_ref[1] = spread_back(2) + back[1]
    for n in range(3, cy - 1):
        backward(n)
    taps(cy - 1)
    slot_ref[2] = back[cy - 2]
    slot_ref[3] = back[cy - 1]
    zero = jnp.zeros((chans, slots), F32)
    for dx, cells_ref in enumerate((west_cells, own_cells, east_cells)):
        sums_ref[dx] = at_slots(plane[dx], place(cells_ref, nz), range(2, cy - 2), zero)


def at_slots(part, cells, first, total):
    chans = total.shape[0]
    y, z = cells
    found = mm(part, picked_depth(z, part.shape[1]))
    for n, row in enumerate(first):
        total = total + jnp.where(y == row, found[n * chans : (n + 1) * chans], 0.0)
    return total


def edge_kernel(
    part, parity_ref, pre_ref, total_ref, north_ref, south_ref, x_ref, cot_ref,
    out_ref, grads_ref, keep_ref, give_ref, total, sums,
):
    cy, chans, nz = cot_ref.shape
    rows = 3 * chans
    own = pl.ds(chans, chans)
    last = pl.ds(2 * chans, chans)
    cots = (north_ref[last], cot_ref[0], cot_ref[cy - 1], south_ref[last])
    sides = ((north_ref, 1), (north_ref, 0), (south_ref, 0), (south_ref, 1))
    ends = []
    for n, (ref, at) in enumerate(sides):
        pre = pre_ref[n] + ref[pl.ds(at * chans, chans)].astype(F32)
        ends.append(finish_row(pre, x_ref[0 if n < 2 else cy - 1, own], cots[n]))
    out_ref[0], out_ref[1] = ends[1][0], ends[2][0]
    grads = [stacked(grad) for _, grad in ends]
    for n in range(4):
        grads_ref[n] = grads[n]
    top = mm(jnp.concatenate([grads[0], grads[1]], axis=0), x_ref[0], NT)
    bottom = mm(jnp.concatenate([grads[2], grads[3]], axis=0), x_ref[cy - 1], NT)
    here = [pl.ds(n * rows, rows) for n in range(3)]
    total[here[0]] = total_ref[here[0]] + (top[:rows] + mm(grads[1], x_ref[1], NT))
    total[here[1]] = total_ref[here[1]] + (top[rows:] + bottom[:rows])
    total[here[2]] = total_ref[here[2]] + (bottom[rows:] + mm(grads[2], x_ref[cy - 2], NT))
    full, _, width = keep_ref.shape
    half = 3 * rows // 2
    split = 3 * rows // (2 * part)
    sums[pl.ds(0, split)] = total[:, :width].reshape(split, 2, part, width)
    taps = jnp.concatenate([total[pl.ds(0, half), width:], total[pl.ds(half, half), width:]], axis=1)
    sums[pl.ds(split, full - split)] = taps.reshape(full - split, 2, part, width)
    parity = parity_ref[0]
    keep_ref[...] = sums[:, parity]
    give_ref[...] = sums[:, 1 - parity].astype(BF16)


def slots_kernel(
    ndev, cap, part, full, slot_ref, sums_ref, grads_ref, wb_ref, cot_ref,
    own_cells, west_cells, east_cells, recv_ref, slots_ref, proj_ref,
):
    cy, chans, nz = cot_ref.shape
    rows = 3 * chans
    inner = mm(wb_ref[pl.ds(rows, 2 * rows)], grads_ref[1])
    top = slot_ref[0] + inner[:rows] + mm(wb_ref[pl.ds(2 * rows, rows)], grads_ref[0])
    second = slot_ref[1] + inner[rows:]
    inner = mm(wb_ref[pl.ds(0, 2 * rows)], grads_ref[2])
    third = slot_ref[2] + inner[:rows]
    bottom = slot_ref[3] + inner[rows:] + mm(wb_ref[pl.ds(0, rows)], grads_ref[3])
    at = (0, 1, cy - 2, cy - 1)
    found = []
    for dx, cells_ref in enumerate((west_cells, own_cells, east_cells)):
        parts = [value[dx * chans : (dx + 1) * chans] for value in (top, second, third, bottom)]
        if dx == 1:
            parts = [value + cot_ref[n].astype(F32) for value, n in zip(parts, at)]
        terms = jnp.concatenate(parts, axis=0).astype(BF16)
        found.append(at_slots(terms, place(cells_ref, nz), at, sums_ref[dx]))
    sides = jnp.concatenate([found[0], found[2]], axis=0).T
    middle = jnp.concatenate([found[1], jnp.zeros_like(found[1])], axis=0).T
    width = recv_ref.shape[1]
    back = [sides.reshape(ndev, cap, width), middle.reshape(ndev, cap, width)]
    slots_ref[...] = jnp.concatenate(back, axis=1).astype(BF16)
    raws = rows_in(recv_ref, ndev, cap)
    proj = sum(mm(found[dx].astype(BF16), raws[dx]) for dx in range(3))
    rest = ndev - full
    pad = jnp.zeros((rest * part - chans, width), F32)
    proj = jnp.concatenate([proj, pad], axis=0).reshape(rest, part, width)
    proj_ref[...] = proj.astype(BF16)


def pair_kernel(keep_ref, got_ref, slots_ref, proj_ref, send_far, sums_send, sems):
    full, part, _ = keep_ref.shape
    ndev, back, _ = slots_ref.shape
    pieces = (
        (slots_ref, send_far.at[:, pl.ds(part, back)]),
        (proj_ref, send_far.at[pl.ds(full, ndev - full), pl.ds(0, part)]),
        (sums_send, send_far.at[pl.ds(0, full), pl.ds(0, part)]),
    )
    copies = [pltpu.make_async_copy(src, dst, sems.at[n]) for n, (src, dst) in enumerate(pieces)]
    copies[0].start()
    copies[1].start()
    sums_send[...] = (keep_ref[...] + got_ref[...].astype(F32)).astype(BF16)
    copies[2].start()
    for copy in copies:
        copy.wait()


def sums_kernel(ngx, ngy, full, cap, recv_ref, index_ref, sums_ref):
    ndev, each, width = recv_ref.shape
    part = each - 2 * cap
    terms = recv_ref[:, pl.ds(0, part)].astype(F32).reshape(ngx // 2, 2, ngy, part, width)
    sums = jnp.sum(terms, axis=(0, 2))
    whole = sums[0] + sums[1]
    high = whole.astype(BF16).astype(F32)
    last = jnp.broadcast_to(index_ref[...], whole.shape) >= full
    sums = [
        jnp.where(last, high, sums[0]).astype(BF16),
        jnp.where(last, whole - high, sums[1]).astype(BF16),
    ]
    for n in range(ndev):
        sums_ref[n] = sums[(n // ngy) % 2]


def rows_kernel(
    ngx, ngy, cap, chans, recv_ref, counts_ref, proj_t_ref, inner_ref, ends_ref, rows_ref, out_ref
):
    ndev = ngx * ngy
    nrows = rows_ref.shape[0]
    width = recv_ref.shape[2]
    slots = ndev * cap
    share = recv_ref.shape[1] - 2 * cap
    arrived = recv_ref[:, pl.ds(share, 2 * cap)].astype(F32)
    sides = arrived[:, :cap].reshape(ngx, ngy, cap, width)
    left = lax.broadcasted_iota(I32, sides.shape, 3) < chans
    sides = jnp.where(left, rolled(sides, 1, 0), rolled(sides, -1, 0)).reshape(slots, width)
    middle = arrived[:, cap:].reshape(slots, width)
    counts = counts_ref[...].astype(F32)
    place = lax.broadcasted_iota(I32, (nrows, ndev), 0).astype(F32)
    lane = lax.broadcasted_iota(I32, (ndev, ndev), 1)
    upto = lax.broadcasted_iota(I32, (ndev, ndev), 0) <= lane
    ends = mm(counts.astype(BF16), jnp.where(upto, 1.0, 0.0).astype(BF16))
    before = ends <= place
    owner = jnp.sum(jnp.where(before, 1.0, 0.0), axis=1, keepdims=True)
    start = jnp.sum(jnp.where(before, counts, 0.0), axis=1, keepdims=True)
    slot = owner * cap + place[:, :1] - start
    onehot = jnp.where(
        lax.broadcasted_iota(I32, (nrows, slots), 1).astype(F32) == slot, 1.0, 0.0
    ).astype(BF16)
    proj_t = proj_t_ref[...]
    both = jnp.concatenate([proj_t, proj_t], axis=0)
    sides = mm(onehot, sides.astype(BF16)).astype(BF16)
    middle = mm(onehot, middle.astype(BF16)).astype(BF16)
    rows_ref[...] = mm(sides, both) + mm(middle, both)
    cy = inner_ref.shape[0]
    field = jnp.concatenate([ends_ref[:1], inner_ref[1 : cy - 1], ends_ref[1:]], axis=0)
    out_ref[...] = jnp.swapaxes(field.astype(F32), 0, 1).astype(BF16)


def finish_kernel(conv_scale, proj_scale, parity_ref, mine_ref, other_ref, conv_ref, proj_ref, both):
    ndev, part, width = mine_ref.shape
    parity = parity_ref[0]
    both[:, parity] = mine_ref[...]
    both[:, 1 - parity] = other_ref[...]
    sums = both[...].astype(F32).reshape(ndev * 2 * part, width)
    taps, chans, _ = conv_ref.shape
    rows = 9 * chans
    half = rows // 2
    packed = sums[rows : rows + half]
    column = jnp.concatenate([packed[:, :chans], packed[:, chans:]], axis=0)
    for b in range(3):
        for dz in range(3):
            first = (b * 3 + dz) * chans
            block = sums[first : first + chans]
            k = (2 - b) * 3 + dz
            conv_ref[k] = block[:, :chans] * conv_scale
            conv_ref[9 + k] = block[:, chans:] * conv_scale
            conv_ref[18 + k] = column[first : first + chans] * conv_scale
    terms = sums[rows + half : rows + half + 2 * chans].reshape(chans // part, 2, part, width)
    proj_ref[...] = jnp.sum(terms, axis=1).reshape(chans, width) * proj_scale


def local(particles, send_counts, cell_lists, base_field, proj_weight, conv_weight, cotangent):
    ngx, ngy = lax.axis_size("gx"), lax.axis_size("gy")
    ndev = ngx * ngy
    nrows, feats = particles.shape
    chans, cx, cy, nz = base_field.shape
    slots = cell_lists.shape[1]
    cap = slots // ndev
    count = cx * cy * nz
    assert cx == 1 and feats == 2 * chans
    proj_t = proj_weight.T
    move = functools.partial(send, ngx=ngx, ngy=ngy)
    rows = 3 * chans
    one = 2 * rows * rows * nz

    base = base_field.reshape(chans, cy, nz)
    west, east = move(base_field, 1, 0), move(base_field, -1, 0)
    planes = (base, west.reshape(base.shape), east.reshape(base.shape))
    lists = (cell_lists, move(cell_lists, 1, 0), move(cell_lists, -1, 0))
    (payload,) = call(
        functools.partial(first_kernel, ngx, ngy, cap),
        [shape((ndev * 3 * cap, feats), BF16)],
        (particles, send_counts),
        2 * slots * nrows * feats,
        (
            pltpu.VMEM(particles.shape, BF16),
            pltpu.VMEM(send_counts.shape, I32),
            pltpu.SemaphoreType.DMA((2,)),
        ),
        far=range(2),
        limit=ALL,
    )
    recv = exchange(payload, ndev)

    cot = cotangent[:, 0].transpose(1, 0, 2)
    taps = conv_weight.reshape(3, 3, 3, chans, chans)
    wf = taps.transpose(1, 2, 3, 0, 4).reshape(9 * chans, rows)
    wb = taps.transpose(1, 0, 4, 2, 3).reshape(9 * chans, rows)

    inputs = (recv, *planes, *lists, proj_t, cot, wf)
    (first,) = call(
        functools.partial(outer_kernel, ndev, cap),
        [shape((rows, nz), BF16)],
        inputs,
        2 * one,
        (pltpu.VMEM((2 * chans, slots), BF16), pltpu.VMEM((2, rows, nz), BF16)),
    )
    south = move(first, 0, -1)
    x_all, last = call(
        functools.partial(field_kernel, ndev, cap),
        [shape((cy, rows, nz), BF16), shape((rows, nz), BF16)],
        inputs,
        6 * slots * count * chans,
        (pltpu.VMEM((cy * chans, slots), BF16),),
    )
    north = move(last, 0, 1)
    out_rows, total, pre_edge, slot_edge, sums = call(
        conv_kernel,
        [
            shape((cy, chans, nz), BF16),
            shape((9 * chans, rows), F32),
            shape((4, chans, nz), F32),
            shape((4, rows, nz), F32),
            shape((3, chans, slots), F32),
        ],
        (x_all, cot, wf, wb, *lists),
        3 * cy * 3 * one,
        (
            pltpu.VMEM((cy + 1, rows, nz), F32),
            pltpu.VMEM((cy + 2, rows, nz), BF16),
            pltpu.VMEM((cy, rows, nz), F32),
            pltpu.VMEM((3, (cy - 4) * chans, nz), BF16),
        ),
    )
    grad_rows = 27 * chans * chans // feats
    part = -(-(grad_rows + 2 * chans) // (32 * ndev)) * 16
    full = grad_rows // (2 * part)
    assert ngx % 2 == 0 and full * 2 * part == grad_rows
    row = lax.axis_index("gx")
    parity = (row % 2).astype(I32).reshape(1)
    out_edge, grads, keep, give = call(
        functools.partial(edge_kernel, part),
        [
            shape((2, chans, nz), BF16),
            shape((4, rows, nz), BF16),
            shape((full, part, feats), F32),
            shape((full, part, feats), BF16),
        ],
        (parity, pre_edge, total, north, south, x_all, cot),
        6 * one,
        (pltpu.VMEM((9 * chans, rows), F32), pltpu.VMEM((full, 2, part, feats), F32)),
        scalar=(0,),
    )
    got = swap(give)
    back, proj = call(
        functools.partial(slots_kernel, ndev, cap, part, full),
        [shape((ndev, 2 * cap, feats), BF16), shape((ndev - full, part, feats), BF16)],
        (slot_edge, sums, grads, wb, cot, *lists, recv),
        6 * one,
    )
    (payload,) = call(
        pair_kernel,
        [shape((ndev, part + 2 * cap, feats), BF16)],
        (keep, got, back, proj),
        1000,
        (pltpu.VMEM((full, part, feats), BF16), pltpu.SemaphoreType.DMA((3,))),
        far_out=(0,),
    )
    (payload,) = call(same_kernel, [payload], (payload,), 0, far=(0,), far_out=(0,), aliases={0: 0})
    recv = exchange(payload.reshape(-1, feats), ndev).reshape(payload.shape)
    index = (row * ngy + lax.axis_index("gy")).astype(I32).reshape(1, 1)
    (sums,) = call(
        functools.partial(sums_kernel, ngx, ngy, full, cap),
        [shape((ndev, part, feats), BF16)],
        (recv, index),
        1000,
    )
    row_grads, out_field = call(
        functools.partial(rows_kernel, ngx, ngy, cap, chans),
        [shape((nrows, feats), F32), shape((chans, cy, nz), BF16)],
        (recv, send_counts, proj_t, out_rows, out_edge),
        2 * nrows * slots * chans,
    )
    mine = exchange(sums.reshape(-1, feats), ndev).reshape(sums.shape)
    mine, row_grads, out_field = lax.optimization_barrier((mine, row_grads, out_field))
    other = swap(mine)
    conv_grad, proj_grad = call(
        functools.partial(
            finish_kernel, 1.0 / math.sqrt(count * ndev), 1.0 / math.sqrt(nrows * ndev)
        ),
        [shape((27, chans, chans), F32), shape((chans, feats), F32)],
        (parity, mine, other),
        1000,
        (pltpu.VMEM((ndev, 2, part, feats), BF16),),
        scalar=(0,),
    )
    return (out_field[:, None], row_grads, conv_grad, proj_grad.T)


def solution(mesh):
    in_specs = (
        P(("gx", "gy"), None),
        P(("gx", "gy"), None),
        P(("gx", "gy"), None),
        P(None, "gx", "gy", None),
        P(),
        P(),
        P(None, "gx", "gy", None),
    )
    out_specs = (P(None, "gx", "gy", None), P(("gx", "gy"), None), P(), P())
    return jax.shard_map(local, mesh=mesh, in_specs=in_specs, out_specs=out_specs, check_vma=False)
```

```python
import functools
import math

import jax
import jax.numpy as jnp
from jax import lax
from jax.experimental import pallas as pl
from jax.experimental.pallas import tpu as pltpu
from jax.sharding import PartitionSpec as P

AXES = ("gx", "gy")
F32, BF16, I32 = jnp.float32, jnp.bfloat16, jnp.int32
LIMIT = 40 * 1024 * 1024
ALL = 60 * 1024 * 1024
NT = (((1,), (1,)), ((), ()))
NN = (((1,), (0,)), ((), ()))


def mm(a, b, dims=NN):
    return lax.dot_general(a, b, dims, preferred_element_type=F32)


def call(kernel, outs, args, flops, scratch=(), far=(), far_out=(), aliases=None, limit=LIMIT, scalar=()):
    traffic = sum(math.prod(a.shape) * a.dtype.itemsize for a in (*args, *outs))
    near = pl.BlockSpec(memory_space=pltpu.VMEM)
    there = pl.BlockSpec(memory_space=pltpu.HBM)
    return pl.pallas_call(
        kernel,
        out_shape=[jax.ShapeDtypeStruct(o.shape, o.dtype) for o in outs],
        in_specs=[
            pl.BlockSpec(memory_space=pltpu.SMEM) if n in scalar else there if n in far else near
            for n in range(len(args))
        ],
        out_specs=[there if n in far_out else near for n in range(len(outs))],
        scratch_shapes=list(scratch),
        input_output_aliases=aliases or {},
        compiler_params=pltpu.CompilerParams(vmem_limit_bytes=limit),
        cost_estimate=pl.CostEstimate(flops=flops, bytes_accessed=traffic, transcendentals=0),
    )(*args)


def shape(dims, dtype):
    return jax.ShapeDtypeStruct(dims, dtype)


def send(block, di, dj, ngx, ngy):
    pairs = []
    for i in range(ngx):
        for j in range(ngy):
            pairs.append((i * ngy + j, ((i + di) % ngx) * ngy + (j + dj) % ngy))
    return lax.ppermute(block, AXES, pairs)


def swap(block):
    return lax.ppermute(block, "gx", [(i, i ^ 1) for i in range(lax.axis_size("gx"))])


def exchange(payload, ndev):
    rows, width = payload.shape
    moved = lax.all_to_all(
        payload.reshape(ndev, rows // ndev, width), AXES, split_axis=0, concat_axis=0, tiled=True
    )
    return moved.reshape(rows, width)


def rolled(x, di, dj):
    for axis, shift in ((0, di), (1, dj)):
        if shift == 1:
            head, tail = lax.slice_in_dim(x, 1, None, axis=axis), lax.slice_in_dim(x, 0, 1, axis=axis)
            x = jnp.concatenate([head, tail], axis=axis)
        elif shift == -1:
            count = x.shape[axis]
            head = lax.slice_in_dim(x, count - 1, count, axis=axis)
            x = jnp.concatenate([head, lax.slice_in_dim(x, 0, count - 1, axis=axis)], axis=axis)
    return x


def picked_depth(z, nz):
    depth = lax.broadcasted_iota(I32, (nz, z.shape[1]), 0)
    return jnp.where(depth == z, 1.0, 0.0).astype(BF16)


def rows_in(recv_ref, ndev, cap):
    width = recv_ref.shape[1]
    arrived = recv_ref[...].astype(F32).reshape(ndev, 3, cap, width)
    return [arrived[:, n].reshape(ndev * cap, width).astype(BF16) for n in range(3)]


def stacked(grad):
    nz = grad.shape[1]
    wide = grad.astype(F32)
    return jnp.concatenate(
        [pltpu.roll(wide, nz - 1, 1), wide, pltpu.roll(wide, 1, 1)], axis=0
    ).astype(BF16)


def over_depth(acc):
    chans, nz = acc.shape[0] // 3, acc.shape[1]
    total = acc[chans : 2 * chans] + pltpu.roll(acc[:chans], 1, 1)
    return total + pltpu.roll(acc[2 * chans :], nz - 1, 1)


def finish_row(pre, field, cot):
    sig = jax.nn.sigmoid(pre)
    out = field.astype(F32) + pre * sig
    grad = cot.astype(F32) * sig * (1.0 + pre * (1.0 - sig))
    return out.astype(BF16), grad.astype(BF16)


def first_kernel(
    ngx, ngy, cap, rows_far, counts_far, send_ref, rows_ref, counts_ref, sems
):
    copies = [
        pltpu.make_async_copy(rows_far, rows_ref, sems.at[0]),
        pltpu.make_async_copy(counts_far, counts_ref, sems.at[1]),
    ]
    for copy in copies:
        copy.start()
    for copy in copies:
        copy.wait()
    pick(ngx, ngy, cap, counts_ref, rows_ref, send_ref)


def same_kernel(in_ref, out_ref):
    pass


def pick(ngx, ngy, cap, counts_ref, rows_ref, out_ref):
    ndev = ngx * ngy
    nrows, feats = rows_ref.shape
    slots = ndev * cap
    counts = counts_ref[...].astype(F32)
    owner = lax.broadcasted_iota(I32, (ndev, cap, ndev), 0).reshape(slots, ndev)
    lane = lax.broadcasted_iota(I32, (slots, ndev), 1)
    start = jnp.sum(jnp.where(lane < owner, counts, 0.0), axis=1, keepdims=True)
    held = jnp.sum(jnp.where(lane == owner, counts, 0.0), axis=1, keepdims=True)
    place = lax.broadcasted_iota(I32, (ndev, cap, nrows), 1).reshape(slots, nrows).astype(F32)
    row = lax.broadcasted_iota(I32, (slots, nrows), 1).astype(F32)
    onehot = jnp.where((row == place + start) & (place < held), 1.0, 0.0).astype(BF16)
    raw = mm(onehot, rows_ref[...]).reshape(ngx, ngy, cap, feats)
    parts = [rolled(raw, dx, 0).reshape(ndev, cap, feats) for dx in (-1, 0, 1)]
    out_ref[...] = jnp.stack(parts, axis=1).reshape(out_ref.shape).astype(BF16)


def painted_rows(values, y, onehot, ns, masked):
    chans = values.shape[0]
    for n, row in enumerate(ns):
        masked[pl.ds(n * chans, chans)] = values * jnp.where(y == row, 1.0, 0.0).astype(BF16)
    return mm(masked[pl.ds(0, len(ns) * chans)], onehot, NT)


def add_to_rows(near, far, cot, back, out_ref):
    chans = cot.shape[0]
    rows = 3 * chans
    at, over = (rows, 0) if back else (0, rows)
    out_ref[pl.ds(0, chans)] = over_depth(near[at : at + rows]).astype(BF16)
    out_ref[pl.ds(chans, chans)] = over_depth(near[over : over + rows] + far).astype(BF16)
    out_ref[pl.ds(2 * chans, chans)] = cot


def outer_kernel(
    ndev, cap, recv_ref, own_ref, west_ref, east_ref, own_cells, west_cells, east_cells,
    proj_t_ref, cot_ref, wf_ref, first_ref, last_ref, values_ref, hot_ref, masked, field,
):
    chans, cy, nz = own_ref.shape
    rows = 3 * chans
    raws = rows_in(recv_ref, ndev, cap)
    ns = (0, 1, cy - 2, cy - 1)
    planes = ((west_ref, west_cells), (own_ref, own_cells), (east_ref, east_cells))
    for dx, (ref, cells_ref) in enumerate(planes):
        values = mm(proj_t_ref[...], raws[dx], NT).astype(BF16)
        y, z = place(cells_ref, nz)
        onehot = picked_depth(z, nz)
        values_ref[dx] = values
        hot_ref[dx] = onehot
        painted = painted_rows(values, y, onehot, ns, masked)
        base = turned(ref)
        for n, row in enumerate(ns):
            part = painted[n * chans : (n + 1) * chans]
            field[n, pl.ds(dx * chans, chans)] = (base[row] + part).astype(BF16)
    near = mm(wf_ref[pl.ds(0, 2 * rows)], field[3])
    add_to_rows(near, mm(wf_ref[pl.ds(0, rows)], field[2]), cot_ref[cy - 1], False, last_ref)
    near = mm(wf_ref[pl.ds(rows, 2 * rows)], field[0])
    add_to_rows(near, mm(wf_ref[pl.ds(2 * rows, rows)], field[1]), cot_ref[0], True, first_ref)


def place(cells_ref, nz):
    cells = cells_ref[...]
    return cells // nz, cells % nz


def turned(ref):
    return jnp.swapaxes(ref[...].astype(F32), 0, 1)


def conv_kernel(
    values_ref, hot_ref, own_ref, west_ref, east_ref, own_cells, west_cells, east_cells,
    cot_ref, wf_ref, wb_ref,
    x_ref, out_ref, total_ref, pre_ref, slot_ref, plane, acc, grads, back, masked,
):
    cy, chans, nz = cot_ref.shape
    rows = 3 * chans
    planes = ((west_ref, west_cells), (own_ref, own_cells), (east_ref, east_cells))
    for dx, (ref, cells_ref) in enumerate(planes):
        y, _ = place(cells_ref, nz)
        painted = painted_rows(values_ref[dx], y, hot_ref[dx], range(cy), masked)
        field = turned(ref) + painted.reshape(cy, chans, nz)
        x_ref[:, pl.ds(dx * chans, chans)] = field.astype(BF16)
    own = pl.ds(chans, chans)
    zeros = jnp.zeros((rows, nz), BF16)
    for t in (0, 1, cy, cy + 1):
        grads[t] = zeros
    out_ref[0] = zeros[:chans]
    out_ref[cy - 1] = zeros[:chans]
    acc[0] = jnp.zeros((rows, nz), F32)

    def spread(n):
        terms = mm(wf_ref[...], x_ref[n])
        acc[n + 1] = terms[:rows]
        acc[n] += terms[rows : 2 * rows]
        return terms[2 * rows :]

    pre_ref[0] = over_depth(spread(0))
    pre_ref[1] = over_depth(acc[0] + spread(1))

    def forward(n):
        done = spread(n) + acc[n - 1]
        y = n - 1
        out, grad = finish_row(over_depth(done), x_ref[y, own], cot_ref[y])
        out_ref[y] = out
        grads[y + 1] = stacked(grad)

    for n in range(2, cy):
        forward(n)
    pre_ref[2] = over_depth(acc[cy - 1])
    pre_ref[3] = over_depth(acc[cy])
    total_ref[...] = jnp.zeros_like(total_ref)
    back[0] = jnp.zeros((rows, nz), F32)
    back[1] = jnp.zeros((rows, nz), F32)

    def taps(n):
        window = grads[pl.ds(n, 3)].reshape(3 * rows, nz)
        total_ref[...] += mm(window, x_ref[n], NT)

    def spread_back(n):
        terms = mm(wb_ref[...], grads[n + 1])
        back[n + 1] = terms[2 * rows :]
        back[n] += terms[rows : 2 * rows]
        return terms[:rows]

    def backward(n):
        taps(n)
        value = spread_back(n) + back[n - 1]
        for dx in range(3):
            part = value[dx * chans : (dx + 1) * chans]
            if dx == 1:
                part = part + cot_ref[n - 1].astype(F32)
            plane[dx, pl.ds((n - 3) * chans, chans)] = part.astype(BF16)

    taps(0)
    taps(1)
    slot_ref[0] = spread_back(1)
    taps(2)
    slot_ref[1] = spread_back(2) + back[1]
    for n in range(3, cy - 1):
        backward(n)
    taps(cy - 1)
    slot_ref[2] = back[cy - 2]
    slot_ref[3] = back[cy - 1]


def at_slots(part, y, onehot, first):
    found = mm(part, onehot)
    chans = found.shape[0] // len(first)
    total = jnp.zeros((chans, found.shape[1]), F32)
    for n, row in enumerate(first):
        total = total + jnp.where(y == row, found[n * chans : (n + 1) * chans], 0.0)
    return total


def edge_kernel(
    part, parity_ref, pre_ref, total_ref, north_ref, south_ref, x_ref, cot_ref,
    out_ref, grads_ref, keep_ref, give_ref, total, sums,
):
    cy, chans, nz = cot_ref.shape
    rows = 3 * chans
    own = pl.ds(chans, chans)
    last = pl.ds(2 * chans, chans)
    cots = (north_ref[last], cot_ref[0], cot_ref[cy - 1], south_ref[last])
    sides = ((north_ref, 1), (north_ref, 0), (south_ref, 0), (south_ref, 1))
    ends = []
    for n, (ref, at) in enumerate(sides):
        pre = pre_ref[n] + ref[pl.ds(at * chans, chans)].astype(F32)
        ends.append(finish_row(pre, x_ref[0 if n < 2 else cy - 1, own], cots[n]))
    out_ref[0], out_ref[1] = ends[1][0], ends[2][0]
    grads = [stacked(grad) for _, grad in ends]
    for n in range(4):
        grads_ref[n] = grads[n]
    top = mm(jnp.concatenate([grads[0], grads[1]], axis=0), x_ref[0], NT)
    bottom = mm(jnp.concatenate([grads[2], grads[3]], axis=0), x_ref[cy - 1], NT)
    here = [pl.ds(n * rows, rows) for n in range(3)]
    total[here[0]] = total_ref[here[0]] + (top[:rows] + mm(grads[1], x_ref[1], NT))
    total[here[1]] = total_ref[here[1]] + (top[rows:] + bottom[:rows])
    total[here[2]] = total_ref[here[2]] + (bottom[rows:] + mm(grads[2], x_ref[cy - 2], NT))
    full, _, width = keep_ref.shape
    half = 3 * rows // 2
    split = 3 * rows // (2 * part)
    sums[pl.ds(0, split)] = total[:, :width].reshape(split, 2, part, width)
    taps = jnp.concatenate([total[pl.ds(0, half), width:], total[pl.ds(half, half), width:]], axis=1)
    sums[pl.ds(split, full - split)] = taps.reshape(full - split, 2, part, width)
    parity = parity_ref[0]
    keep_ref[...] = sums[:, parity]
    give_ref[...] = sums[:, 1 - parity].astype(BF16)


def slots_kernel(
    ndev, cap, part, full, slot_ref, plane_ref, hot_ref, grads_ref, wb_ref, cot_ref,
    own_cells, west_cells, east_cells, recv_ref, slots_ref, proj_ref,
):
    cy, chans, nz = cot_ref.shape
    rows = 3 * chans
    inner = mm(wb_ref[pl.ds(rows, 2 * rows)], grads_ref[1])
    top = slot_ref[0] + inner[:rows] + mm(wb_ref[pl.ds(2 * rows, rows)], grads_ref[0])
    second = slot_ref[1] + inner[rows:]
    inner = mm(wb_ref[pl.ds(0, 2 * rows)], grads_ref[2])
    third = slot_ref[2] + inner[:rows]
    bottom = slot_ref[3] + inner[rows:] + mm(wb_ref[pl.ds(0, rows)], grads_ref[3])
    at = (0, 1, cy - 2, cy - 1)
    found = []
    for dx, cells_ref in enumerate((west_cells, own_cells, east_cells)):
        parts = [value[dx * chans : (dx + 1) * chans] for value in (top, second, third, bottom)]
        if dx == 1:
            parts = [value + cot_ref[n].astype(F32) for value, n in zip(parts, at)]
        parts = [value.astype(BF16) for value in parts]
        terms = jnp.concatenate([plane_ref[dx], *parts], axis=0)
        y, _ = place(cells_ref, nz)
        found.append(at_slots(terms, y, hot_ref[dx], (*range(2, cy - 2), *at)))
    sides = jnp.concatenate([found[0], found[2]], axis=0).T
    middle = jnp.concatenate([found[1], jnp.zeros_like(found[1])], axis=0).T
    width = recv_ref.shape[1]
    back = [sides.reshape(ndev, cap, width), middle.reshape(ndev, cap, width)]
    slots_ref[...] = jnp.concatenate(back, axis=1).astype(BF16)
    raws = rows_in(recv_ref, ndev, cap)
    proj = sum(mm(found[dx].astype(BF16), raws[dx]) for dx in range(3))
    rest = ndev - full
    pad = jnp.zeros((rest * part - chans, width), F32)
    proj = jnp.concatenate([proj, pad], axis=0).reshape(rest, part, width)
    proj_ref[...] = proj.astype(BF16)


def pair_kernel(keep_ref, got_ref, slots_ref, proj_ref, send_far, sums_send, sems):
    full, part, _ = keep_ref.shape
    ndev, back, _ = slots_ref.shape
    pieces = (
        (slots_ref, send_far.at[:, pl.ds(part, back)]),
        (proj_ref, send_far.at[pl.ds(full, ndev - full), pl.ds(0, part)]),
        (sums_send, send_far.at[pl.ds(0, full), pl.ds(0, part)]),
    )
    copies = [pltpu.make_async_copy(src, dst, sems.at[n]) for n, (src, dst) in enumerate(pieces)]
    copies[0].start()
    copies[1].start()
    sums_send[...] = (keep_ref[...] + got_ref[...].astype(F32)).astype(BF16)
    copies[2].start()
    for copy in copies:
        copy.wait()


def sums_kernel(ngx, ngy, full, cap, recv_ref, index_ref, sums_ref):
    ndev, each, width = recv_ref.shape
    part = each - 2 * cap
    terms = recv_ref[:, pl.ds(0, part)].astype(F32).reshape(ngx // 2, 2, ngy, part, width)
    sums = jnp.sum(terms, axis=(0, 2))
    whole = sums[0] + sums[1]
    high = whole.astype(BF16).astype(F32)
    last = jnp.broadcast_to(index_ref[...], whole.shape) >= full
    sums = [
        jnp.where(last, high, sums[0]).astype(BF16),
        jnp.where(last, whole - high, sums[1]).astype(BF16),
    ]
    for n in range(ndev):
        sums_ref[n] = sums[(n // ngy) % 2]


def rows_kernel(
    ngx, ngy, cap, chans, recv_ref, counts_ref, proj_t_ref, inner_ref, ends_ref, rows_ref, out_ref
):
    ndev = ngx * ngy
    nrows = rows_ref.shape[0]
    width = recv_ref.shape[2]
    slots = ndev * cap
    share = recv_ref.shape[1] - 2 * cap
    arrived = recv_ref[:, pl.ds(share, 2 * cap)].astype(F32)
    sides = arrived[:, :cap].reshape(ngx, ngy, cap, width)
    left = lax.broadcasted_iota(I32, sides.shape, 3) < chans
    sides = jnp.where(left, rolled(sides, 1, 0), rolled(sides, -1, 0)).reshape(slots, width)
    middle = arrived[:, cap:].reshape(slots, width)
    counts = counts_ref[...].astype(F32)
    place = lax.broadcasted_iota(I32, (nrows, ndev), 0).astype(F32)
    lane = lax.broadcasted_iota(I32, (ndev, ndev), 1)
    upto = lax.broadcasted_iota(I32, (ndev, ndev), 0) <= lane
    ends = mm(counts.astype(BF16), jnp.where(upto, 1.0, 0.0).astype(BF16))
    before = ends <= place
    owner = jnp.sum(jnp.where(before, 1.0, 0.0), axis=1, keepdims=True)
    start = jnp.sum(jnp.where(before, counts, 0.0), axis=1, keepdims=True)
    slot = owner * cap + place[:, :1] - start
    onehot = jnp.where(
        lax.broadcasted_iota(I32, (nrows, slots), 1).astype(F32) == slot, 1.0, 0.0
    ).astype(BF16)
    proj_t = proj_t_ref[...]
    both = jnp.concatenate([proj_t, proj_t], axis=0)
    sides = mm(onehot, sides.astype(BF16)).astype(BF16)
    middle = mm(onehot, middle.astype(BF16)).astype(BF16)
    rows_ref[...] = mm(sides, both) + mm(middle, both)
    cy = inner_ref.shape[0]
    field = jnp.concatenate([ends_ref[:1], inner_ref[1 : cy - 1], ends_ref[1:]], axis=0)
    out_ref[...] = jnp.swapaxes(field.astype(F32), 0, 1).astype(BF16)


def finish_kernel(conv_scale, proj_scale, parity_ref, mine_ref, other_ref, conv_ref, proj_ref, both):
    ndev, part, width = mine_ref.shape
    parity = parity_ref[0]
    both[:, parity] = mine_ref[...]
    both[:, 1 - parity] = other_ref[...]
    sums = both[...].astype(F32).reshape(ndev * 2 * part, width)
    taps, chans, _ = conv_ref.shape
    rows = 9 * chans
    half = rows // 2
    packed = sums[rows : rows + half]
    column = jnp.concatenate([packed[:, :chans], packed[:, chans:]], axis=0)
    for b in range(3):
        for dz in range(3):
            first = (b * 3 + dz) * chans
            block = sums[first : first + chans]
            k = (2 - b) * 3 + dz
            conv_ref[k] = block[:, :chans] * conv_scale
            conv_ref[9 + k] = block[:, chans:] * conv_scale
            conv_ref[18 + k] = column[first : first + chans] * conv_scale
    terms = sums[rows + half : rows + half + 2 * chans].reshape(chans // part, 2, part, width)
    proj_ref[...] = jnp.sum(terms, axis=1).reshape(chans, width) * proj_scale


def local(particles, send_counts, cell_lists, base_field, proj_weight, conv_weight, cotangent):
    ngx, ngy = lax.axis_size("gx"), lax.axis_size("gy")
    ndev = ngx * ngy
    nrows, feats = particles.shape
    chans, cx, cy, nz = base_field.shape
    slots = cell_lists.shape[1]
    cap = slots // ndev
    count = cx * cy * nz
    assert cx == 1 and feats == 2 * chans
    proj_t = proj_weight.T
    move = functools.partial(send, ngx=ngx, ngy=ngy)
    rows = 3 * chans
    one = 2 * rows * rows * nz

    base = base_field.reshape(chans, cy, nz)
    west, east = move(base_field, 1, 0), move(base_field, -1, 0)
    planes = (base, west.reshape(base.shape), east.reshape(base.shape))
    lists = (cell_lists, move(cell_lists, 1, 0), move(cell_lists, -1, 0))
    (payload,) = call(
        functools.partial(first_kernel, ngx, ngy, cap),
        [shape((ndev * 3 * cap, feats), BF16)],
        (particles, send_counts),
        2 * slots * nrows * feats,
        (
            pltpu.VMEM(particles.shape, BF16),
            pltpu.VMEM(send_counts.shape, I32),
            pltpu.SemaphoreType.DMA((2,)),
        ),
        far=range(2),
        limit=ALL,
    )
    recv = exchange(payload, ndev)

    cot = cotangent[:, 0].transpose(1, 0, 2)
    taps = conv_weight.reshape(3, 3, 3, chans, chans)
    wf = taps.transpose(1, 2, 3, 0, 4).reshape(9 * chans, rows)
    wb = taps.transpose(1, 0, 4, 2, 3).reshape(9 * chans, rows)

    first, last, values, hots = call(
        functools.partial(outer_kernel, ndev, cap),
        [shape((rows, nz), BF16)] * 2
        + [shape((3, chans, slots), BF16), shape((3, nz, slots), BF16)],
        (recv, *planes, *lists, proj_t, cot, wf),
        4 * one,
        (pltpu.VMEM((4 * chans, slots), BF16), pltpu.VMEM((4, rows, nz), BF16)),
    )
    south, north = move(first, 0, -1), move(last, 0, 1)
    x_all, out_rows, total, pre_edge, slot_edge, plane = call(
        conv_kernel,
        [
            shape((cy, rows, nz), BF16),
            shape((cy, chans, nz), BF16),
            shape((9 * chans, rows), F32),
            shape((4, chans, nz), F32),
            shape((4, rows, nz), F32),
            shape((3, (cy - 4) * chans, nz), BF16),
        ],
        (values, hots, *planes, *lists, cot, wf, wb),
        3 * cy * 3 * one,
        (
            pltpu.VMEM((cy + 1, rows, nz), F32),
            pltpu.VMEM((cy + 2, rows, nz), BF16),
            pltpu.VMEM((cy, rows, nz), F32),
            pltpu.VMEM((cy * chans, slots), BF16),
        ),
    )
    grad_rows = 27 * chans * chans // feats
    part = -(-(grad_rows + 2 * chans) // (32 * ndev)) * 16
    full = grad_rows // (2 * part)
    assert ngx % 2 == 0 and full * 2 * part == grad_rows
    row = lax.axis_index("gx")
    parity = (row % 2).astype(I32).reshape(1)
    out_edge, grads, keep, give = call(
        functools.partial(edge_kernel, part),
        [
            shape((2, chans, nz), BF16),
            shape((4, rows, nz), BF16),
            shape((full, part, feats), F32),
            shape((full, part, feats), BF16),
        ],
        (parity, pre_edge, total, north, south, x_all, cot),
        6 * one,
        (pltpu.VMEM((9 * chans, rows), F32), pltpu.VMEM((full, 2, part, feats), F32)),
        scalar=(0,),
    )
    got = swap(give)
    back, proj = call(
        functools.partial(slots_kernel, ndev, cap, part, full),
        [shape((ndev, 2 * cap, feats), BF16), shape((ndev - full, part, feats), BF16)],
        (slot_edge, plane, hots, grads, wb, cot, *lists, recv),
        6 * one,
    )
    (payload,) = call(
        pair_kernel,
        [shape((ndev, part + 2 * cap, feats), BF16)],
        (keep, got, back, proj),
        1000,
        (pltpu.VMEM((full, part, feats), BF16), pltpu.SemaphoreType.DMA((3,))),
        far_out=(0,),
    )
    (payload,) = call(same_kernel, [payload], (payload,), 0, far=(0,), far_out=(0,), aliases={0: 0})
    recv = exchange(payload.reshape(-1, feats), ndev).reshape(payload.shape)
    index = (row * ngy + lax.axis_index("gy")).astype(I32).reshape(1, 1)
    (sums,) = call(
        functools.partial(sums_kernel, ngx, ngy, full, cap),
        [shape((ndev, part, feats), BF16)],
        (recv, index),
        1000,
    )
    row_grads, out_field = call(
        functools.partial(rows_kernel, ngx, ngy, cap, chans),
        [shape((nrows, feats), F32), shape((chans, cy, nz), BF16)],
        (recv, send_counts, proj_t, out_rows, out_edge),
        2 * nrows * slots * chans,
    )
    mine = exchange(sums.reshape(-1, feats), ndev).reshape(sums.shape)
    mine, row_grads, out_field = lax.optimization_barrier((mine, row_grads, out_field))
    other = swap(mine)
    conv_grad, proj_grad = call(
        functools.partial(
            finish_kernel, 1.0 / math.sqrt(count * ndev), 1.0 / math.sqrt(nrows * ndev)
        ),
        [shape((27, chans, chans), F32), shape((chans, feats), F32)],
        (parity, mine, other),
        1000,
        (pltpu.VMEM((ndev, 2, part, feats), BF16),),
        scalar=(0,),
    )
    return (out_field[:, None], row_grads, conv_grad, proj_grad.T)


def solution(mesh):
    in_specs = (
        P(("gx", "gy"), None),
        P(("gx", "gy"), None),
        P(("gx", "gy"), None),
        P(None, "gx", "gy", None),
        P(),
        P(),
        P(None, "gx", "gy", None),
    )
    out_specs = (P(None, "gx", "gy", None), P(("gx", "gy"), None), P(), P())
    return jax.shard_map(local, mesh=mesh, in_specs=in_specs, out_specs=out_specs, check_vma=False)
```

```python
import functools
import math

import jax
import jax.numpy as jnp
from jax import lax
from jax.experimental import pallas as pl
from jax.experimental.pallas import tpu as pltpu
from jax.sharding import PartitionSpec as P

AXES = ("gx", "gy")
F32, BF16, I32 = jnp.float32, jnp.bfloat16, jnp.int32
LIMIT = 40 * 1024 * 1024
ALL = 60 * 1024 * 1024
NT = (((1,), (1,)), ((), ()))
NN = (((1,), (0,)), ((), ()))


def mm(a, b, dims=NN):
    return lax.dot_general(a, b, dims, preferred_element_type=F32)


def call(kernel, outs, args, flops, scratch=(), far=(), far_out=(), aliases=None, limit=LIMIT, scalar=()):
    traffic = sum(math.prod(a.shape) * a.dtype.itemsize for a in (*args, *outs))
    near = pl.BlockSpec(memory_space=pltpu.VMEM)
    there = pl.BlockSpec(memory_space=pltpu.HBM)
    return pl.pallas_call(
        kernel,
        out_shape=[jax.ShapeDtypeStruct(o.shape, o.dtype) for o in outs],
        in_specs=[
            pl.BlockSpec(memory_space=pltpu.SMEM) if n in scalar else there if n in far else near
            for n in range(len(args))
        ],
        out_specs=[there if n in far_out else near for n in range(len(outs))],
        scratch_shapes=list(scratch),
        input_output_aliases=aliases or {},
        compiler_params=pltpu.CompilerParams(vmem_limit_bytes=limit),
        cost_estimate=pl.CostEstimate(flops=flops, bytes_accessed=traffic, transcendentals=0),
    )(*args)


def shape(dims, dtype):
    return jax.ShapeDtypeStruct(dims, dtype)


def send(block, di, dj, ngx, ngy):
    pairs = []
    for i in range(ngx):
        for j in range(ngy):
            pairs.append((i * ngy + j, ((i + di) % ngx) * ngy + (j + dj) % ngy))
    return lax.ppermute(block, AXES, pairs)


def swap(block):
    return lax.ppermute(block, "gx", [(i, i ^ 1) for i in range(lax.axis_size("gx"))])


def exchange(payload, ndev):
    rows, width = payload.shape
    moved = lax.all_to_all(
        payload.reshape(ndev, rows // ndev, width), AXES, split_axis=0, concat_axis=0, tiled=True
    )
    return moved.reshape(rows, width)


def rolled(x, di, dj):
    for axis, shift in ((0, di), (1, dj)):
        if shift == 1:
            head, tail = lax.slice_in_dim(x, 1, None, axis=axis), lax.slice_in_dim(x, 0, 1, axis=axis)
            x = jnp.concatenate([head, tail], axis=axis)
        elif shift == -1:
            count = x.shape[axis]
            head = lax.slice_in_dim(x, count - 1, count, axis=axis)
            x = jnp.concatenate([head, lax.slice_in_dim(x, 0, count - 1, axis=axis)], axis=axis)
    return x


def picked_depth(z, nz):
    depth = lax.broadcasted_iota(I32, (nz, z.shape[1]), 0)
    return jnp.where(depth == z, 1.0, 0.0).astype(BF16)


def rows_in(recv_ref, ndev, cap):
    width = recv_ref.shape[1]
    arrived = recv_ref[...].astype(F32).reshape(ndev, 3, cap, width)
    return [arrived[:, n].reshape(ndev * cap, width).astype(BF16) for n in range(3)]


def stacked(grad):
    nz = grad.shape[1]
    wide = grad.astype(F32)
    return jnp.concatenate(
        [pltpu.roll(wide, nz - 1, 1), wide, pltpu.roll(wide, 1, 1)], axis=0
    ).astype(BF16)


def over_depth(acc):
    chans, nz = acc.shape[0] // 3, acc.shape[1]
    total = acc[chans : 2 * chans] + pltpu.roll(acc[:chans], 1, 1)
    return total + pltpu.roll(acc[2 * chans :], nz - 1, 1)


def finish_row(pre, field, cot):
    sig = jax.nn.sigmoid(pre)
    out = field.astype(F32) + pre * sig
    grad = cot.astype(F32) * sig * (1.0 + pre * (1.0 - sig))
    return out.astype(BF16), grad.astype(BF16)


def first_kernel(
    ngx, ngy, cap, rows_far, counts_far, send_ref, rows_ref, counts_ref, sems
):
    copies = [
        pltpu.make_async_copy(rows_far, rows_ref, sems.at[0]),
        pltpu.make_async_copy(counts_far, counts_ref, sems.at[1]),
    ]
    for copy in copies:
        copy.start()
    for copy in copies:
        copy.wait()
    pick(ngx, ngy, cap, counts_ref, rows_ref, send_ref)


def same_kernel(in_ref, out_ref):
    pass


def pick(ngx, ngy, cap, counts_ref, rows_ref, out_ref):
    ndev = ngx * ngy
    nrows, feats = rows_ref.shape
    slots = ndev * cap
    counts = counts_ref[...].astype(F32)
    owner = lax.broadcasted_iota(I32, (ndev, cap, ndev), 0).reshape(slots, ndev)
    lane = lax.broadcasted_iota(I32, (slots, ndev), 1)
    start = jnp.sum(jnp.where(lane < owner, counts, 0.0), axis=1, keepdims=True)
    held = jnp.sum(jnp.where(lane == owner, counts, 0.0), axis=1, keepdims=True)
    place = lax.broadcasted_iota(I32, (ndev, cap, nrows), 1).reshape(slots, nrows).astype(F32)
    row = lax.broadcasted_iota(I32, (slots, nrows), 1).astype(F32)
    onehot = jnp.where((row == place + start) & (place < held), 1.0, 0.0).astype(BF16)
    raw = mm(onehot, rows_ref[...]).reshape(ngx, ngy, cap, feats)
    parts = [rolled(raw, dx, 0).reshape(ndev, cap, feats) for dx in (-1, 0, 1)]
    out_ref[...] = jnp.stack(parts, axis=1).reshape(out_ref.shape).astype(BF16)


def painted_rows(values, y, onehot, ns, masked):
    chans = values.shape[0]
    for n, row in enumerate(ns):
        masked[pl.ds(n * chans, chans)] = values * jnp.where(y == row, 1.0, 0.0).astype(BF16)
    return mm(masked[pl.ds(0, len(ns) * chans)], onehot, NT)


def add_to_rows(near, far, cot, back, out_ref):
    chans = cot.shape[0]
    rows = 3 * chans
    at, over = (rows, 0) if back else (0, rows)
    out_ref[pl.ds(0, chans)] = over_depth(near[at : at + rows]).astype(BF16)
    out_ref[pl.ds(chans, chans)] = over_depth(near[over : over + rows] + far).astype(BF16)
    out_ref[pl.ds(2 * chans, chans)] = cot


def outer_kernel(
    ndev, cap, recv_ref, own_ref, west_ref, east_ref, own_cells, west_cells, east_cells,
    proj_t_ref, cot_ref, wf_ref, first_ref, last_ref, values_ref, hot_ref, masked, field,
):
    chans, cy, nz = own_ref.shape
    rows = 3 * chans
    raws = rows_in(recv_ref, ndev, cap)
    ns = (0, 1, cy - 2, cy - 1)
    planes = ((west_ref, west_cells), (own_ref, own_cells), (east_ref, east_cells))
    for dx, (ref, cells_ref) in enumerate(planes):
        values = mm(proj_t_ref[...], raws[dx], NT).astype(BF16)
        y, z = place(cells_ref, nz)
        onehot = picked_depth(z, nz)
        values_ref[dx] = values
        hot_ref[dx] = onehot
        painted = painted_rows(values, y, onehot, ns, masked)
        base = turned(ref)
        for n, row in enumerate(ns):
            part = painted[n * chans : (n + 1) * chans]
            field[n, pl.ds(dx * chans, chans)] = (base[row] + part).astype(BF16)
    near = mm(wf_ref[pl.ds(0, 2 * rows)], field[3])
    add_to_rows(near, mm(wf_ref[pl.ds(0, rows)], field[2]), cot_ref[cy - 1], False, last_ref)
    near = mm(wf_ref[pl.ds(rows, 2 * rows)], field[0])
    add_to_rows(near, mm(wf_ref[pl.ds(2 * rows, rows)], field[1]), cot_ref[0], True, first_ref)


def place(cells_ref, nz):
    cells = cells_ref[...]
    return cells // nz, cells % nz


def turned(ref):
    return jnp.swapaxes(ref[...].astype(F32), 0, 1)


def conv_kernel(
    values_ref, hot_ref, own_ref, west_ref, east_ref, own_cells, west_cells, east_cells,
    cot_ref, wf_ref, wb_ref,
    x_ref, out_ref, total_ref, pre_ref, slot_ref, plane, acc, grads, back, masked,
):
    cy, chans, nz = cot_ref.shape
    rows = 3 * chans
    planes = ((west_ref, west_cells), (own_ref, own_cells), (east_ref, east_cells))
    for dx, (ref, cells_ref) in enumerate(planes):
        y, _ = place(cells_ref, nz)
        painted = painted_rows(values_ref[dx], y, hot_ref[dx], range(cy), masked)
        field = turned(ref) + painted.reshape(cy, chans, nz)
        x_ref[:, pl.ds(dx * chans, chans)] = field.astype(BF16)
    own = pl.ds(chans, chans)
    zeros = jnp.zeros((rows, nz), BF16)
    for t in (0, 1, cy, cy + 1):
        grads[t] = zeros
    out_ref[0] = zeros[:chans]
    out_ref[cy - 1] = zeros[:chans]
    acc[0] = jnp.zeros((rows, nz), F32)

    def spread(n):
        terms = mm(wf_ref[...], x_ref[n])
        acc[n + 1] = terms[:rows]
        acc[n] += terms[rows : 2 * rows]
        return terms[2 * rows :]

    pre_ref[0] = over_depth(spread(0))
    pre_ref[1] = over_depth(acc[0] + spread(1))

    def forward(n):
        done = spread(n) + acc[n - 1]
        y = n - 1
        out, grad = finish_row(over_depth(done), x_ref[y, own], cot_ref[y])
        out_ref[y] = out
        grads[y + 1] = stacked(grad)

    for n in range(2, cy):
        forward(n)
    pre_ref[2] = over_depth(acc[cy - 1])
    pre_ref[3] = over_depth(acc[cy])
    total_ref[...] = jnp.zeros_like(total_ref)
    back[0] = jnp.zeros((rows, nz), F32)
    back[1] = jnp.zeros((rows, nz), F32)

    def taps(n):
        window = grads[pl.ds(n, 3)].reshape(3 * rows, nz)
        total_ref[...] += mm(window, x_ref[n], NT)

    def spread_back(n):
        terms = mm(wb_ref[...], grads[n + 1])
        back[n + 1] = terms[2 * rows :]
        back[n] += terms[rows : 2 * rows]
        return terms[:rows]

    def backward(n):
        taps(n)
        value = spread_back(n) + back[n - 1]
        for dx in range(3):
            part = value[dx * chans : (dx + 1) * chans]
            if dx == 1:
                part = part + cot_ref[n - 1].astype(F32)
            plane[dx, pl.ds((n - 3) * chans, chans)] = part.astype(BF16)

    taps(0)
    taps(1)
    slot_ref[0] = spread_back(1)
    taps(2)
    slot_ref[1] = spread_back(2) + back[1]
    for n in range(3, cy - 1):
        backward(n)
    taps(cy - 1)
    slot_ref[2] = back[cy - 2]
    slot_ref[3] = back[cy - 1]


def at_slots(part, y, onehot, first):
    found = mm(part, onehot)
    chans = found.shape[0] // len(first)
    total = jnp.zeros((chans, found.shape[1]), F32)
    for n, row in enumerate(first):
        total = total + jnp.where(y == row, found[n * chans : (n + 1) * chans], 0.0)
    return total


def edge_kernel(
    part, parity_ref, pre_ref, total_ref, north_ref, south_ref, x_ref, cot_ref,
    out_ref, grads_ref, keep_ref, give_ref, total, sums,
):
    cy, chans, nz = cot_ref.shape
    rows = 3 * chans
    own = pl.ds(chans, chans)
    last = pl.ds(2 * chans, chans)
    cots = (north_ref[last], cot_ref[0], cot_ref[cy - 1], south_ref[last])
    sides = ((north_ref, 1), (north_ref, 0), (south_ref, 0), (south_ref, 1))
    ends = []
    for n, (ref, at) in enumerate(sides):
        pre = pre_ref[n] + ref[pl.ds(at * chans, chans)].astype(F32)
        ends.append(finish_row(pre, x_ref[0 if n < 2 else cy - 1, own], cots[n]))
    out_ref[0], out_ref[1] = ends[1][0], ends[2][0]
    grads = [stacked(grad) for _, grad in ends]
    for n in range(4):
        grads_ref[n] = grads[n]
    top = mm(jnp.concatenate([grads[0], grads[1]], axis=0), x_ref[0], NT)
    bottom = mm(jnp.concatenate([grads[2], grads[3]], axis=0), x_ref[cy - 1], NT)
    here = [pl.ds(n * rows, rows) for n in range(3)]
    total[here[0]] = total_ref[here[0]] + (top[:rows] + mm(grads[1], x_ref[1], NT))
    total[here[1]] = total_ref[here[1]] + (top[rows:] + bottom[:rows])
    total[here[2]] = total_ref[here[2]] + (bottom[rows:] + mm(grads[2], x_ref[cy - 2], NT))
    full, _, width = keep_ref.shape
    half = 3 * rows // 2
    split = 3 * rows // (2 * part)
    sums[pl.ds(0, split)] = total[:, :width].reshape(split, 2, part, width)
    taps = jnp.concatenate([total[pl.ds(0, half), width:], total[pl.ds(half, half), width:]], axis=1)
    sums[pl.ds(split, full - split)] = taps.reshape(full - split, 2, part, width)
    parity = parity_ref[0]
    keep_ref[...] = sums[:, parity]
    give_ref[...] = sums[:, 1 - parity].astype(BF16)


def slots_kernel(
    parity_ref, slot_ref, plane_ref, hot_ref, grads_ref, wb_ref, cot_ref,
    own_cells, west_cells, east_cells, terms_ref, give_ref,
):
    cy, chans, nz = cot_ref.shape
    rows = 3 * chans
    inner = mm(wb_ref[pl.ds(rows, 2 * rows)], grads_ref[1])
    top = slot_ref[0] + inner[:rows] + mm(wb_ref[pl.ds(2 * rows, rows)], grads_ref[0])
    second = slot_ref[1] + inner[rows:]
    inner = mm(wb_ref[pl.ds(0, 2 * rows)], grads_ref[2])
    third = slot_ref[2] + inner[:rows]
    bottom = slot_ref[3] + inner[rows:] + mm(wb_ref[pl.ds(0, rows)], grads_ref[3])
    at = (0, 1, cy - 2, cy - 1)
    for dx, cells_ref in enumerate((west_cells, own_cells, east_cells)):
        parts = [value[dx * chans : (dx + 1) * chans] for value in (top, second, third, bottom)]
        if dx == 1:
            parts = [value + cot_ref[n].astype(F32) for value, n in zip(parts, at)]
        parts = [value.astype(BF16) for value in parts]
        terms = jnp.concatenate([plane_ref[dx], *parts], axis=0)
        y, _ = place(cells_ref, nz)
        terms_ref[dx] = at_slots(terms, y, hot_ref[dx], (*range(2, cy - 2), *at))
    give_ref[...] = terms_ref[2 - 2 * parity_ref[0]].astype(BF16)


def proj_kernel(ndev, cap, parity_ref, terms_ref, recv_ref, proj_ref, outer_ref):
    raws = rows_in(recv_ref, ndev, cap)
    proj = sum(mm(terms_ref[dx].astype(BF16), raws[dx]) for dx in range(3))
    rest, part, width = proj_ref.shape
    pad = jnp.zeros((rest * part - proj.shape[0], width), F32)
    proj = jnp.concatenate([proj, pad], axis=0).reshape(rest, part, width)
    proj_ref[...] = proj.astype(BF16)
    outer_ref[...] = terms_ref[2 * parity_ref[0]]


def pair_kernel(
    keep_ref, got_ref, terms_ref, got_terms_ref, outer_ref, proj_ref, send_far, sums_send, slots_send, sems
):
    full, part, width = keep_ref.shape
    ndev, back, _ = slots_send.shape
    pieces = (
        (proj_ref, send_far.at[pl.ds(full, ndev - full), pl.ds(0, part)]),
        (sums_send, send_far.at[pl.ds(0, full), pl.ds(0, part)]),
        (slots_send, send_far.at[:, pl.ds(part, back)]),
    )
    copies = [pltpu.make_async_copy(src, dst, sems.at[n]) for n, (src, dst) in enumerate(pieces)]
    copies[0].start()
    sums_send[...] = (keep_ref[...] + got_ref[...].astype(F32)).astype(BF16)
    copies[1].start()
    own = terms_ref[1] + got_terms_ref[...].astype(F32)
    terms = jnp.concatenate([own, outer_ref[...]], axis=0).T
    slots_send[...] = terms.reshape(slots_send.shape).astype(BF16)
    copies[2].start()
    for copy in copies:
        copy.wait()


def sums_kernel(ngx, ngy, full, cap, recv_ref, index_ref, sums_ref):
    ndev, each, width = recv_ref.shape
    part = each - cap
    terms = recv_ref[:, pl.ds(0, part)].astype(F32).reshape(ngx // 2, 2, ngy, part, width)
    sums = jnp.sum(terms, axis=(0, 2))
    whole = sums[0] + sums[1]
    high = whole.astype(BF16).astype(F32)
    last = jnp.broadcast_to(index_ref[...], whole.shape) >= full
    sums = [
        jnp.where(last, high, sums[0]).astype(BF16),
        jnp.where(last, whole - high, sums[1]).astype(BF16),
    ]
    for n in range(ndev):
        sums_ref[n] = sums[(n // ngy) % 2]


def rows_kernel(
    ngx, ngy, cap, chans, recv_ref, counts_ref, proj_t_ref, inner_ref, ends_ref, rows_ref, out_ref
):
    ndev = ngx * ngy
    nrows = rows_ref.shape[0]
    width = recv_ref.shape[2]
    slots = ndev * cap
    part = recv_ref.shape[1] - cap
    arrived = recv_ref[:, pl.ds(part, cap)].astype(F32).reshape(ngx, ngy, cap, width)
    outer = [arrived[(i - 1) % ngx if i % 2 == 0 else (i + 1) % ngx] for i in range(ngx)]
    left = lax.broadcasted_iota(I32, arrived.shape, 3) < chans
    terms = jnp.where(left, arrived, jnp.stack(outer, axis=0)).reshape(slots, width)
    counts = counts_ref[...].astype(F32)
    place = lax.broadcasted_iota(I32, (nrows, ndev), 0).astype(F32)
    lane = lax.broadcasted_iota(I32, (ndev, ndev), 1)
    upto = lax.broadcasted_iota(I32, (ndev, ndev), 0) <= lane
    ends = mm(counts.astype(BF16), jnp.where(upto, 1.0, 0.0).astype(BF16))
    before = ends <= place
    owner = jnp.sum(jnp.where(before, 1.0, 0.0), axis=1, keepdims=True)
    start = jnp.sum(jnp.where(before, counts, 0.0), axis=1, keepdims=True)
    slot = owner * cap + place[:, :1] - start
    onehot = jnp.where(
        lax.broadcasted_iota(I32, (nrows, slots), 1).astype(F32) == slot, 1.0, 0.0
    ).astype(BF16)
    proj_t = proj_t_ref[...]
    both = jnp.concatenate([proj_t, proj_t], axis=0)
    picked = mm(onehot, terms.astype(BF16)).astype(BF16)
    rows_ref[...] = mm(picked, both)
    cy = inner_ref.shape[0]
    field = jnp.concatenate([ends_ref[:1], inner_ref[1 : cy - 1], ends_ref[1:]], axis=0)
    out_ref[...] = jnp.swapaxes(field.astype(F32), 0, 1).astype(BF16)


def finish_kernel(conv_scale, proj_scale, parity_ref, mine_ref, other_ref, conv_ref, proj_ref, both):
    ndev, part, width = mine_ref.shape
    parity = parity_ref[0]
    both[:, parity] = mine_ref[...]
    both[:, 1 - parity] = other_ref[...]
    sums = both[...].astype(F32).reshape(ndev * 2 * part, width)
    taps, chans, _ = conv_ref.shape
    rows = 9 * chans
    half = rows // 2
    packed = sums[rows : rows + half]
    column = jnp.concatenate([packed[:, :chans], packed[:, chans:]], axis=0)
    for b in range(3):
        for dz in range(3):
            first = (b * 3 + dz) * chans
            block = sums[first : first + chans]
            k = (2 - b) * 3 + dz
            conv_ref[k] = block[:, :chans] * conv_scale
            conv_ref[9 + k] = block[:, chans:] * conv_scale
            conv_ref[18 + k] = column[first : first + chans] * conv_scale
    terms = sums[rows + half : rows + half + 2 * chans].reshape(chans // part, 2, part, width)
    proj_ref[...] = jnp.sum(terms, axis=1).reshape(chans, width) * proj_scale


def local(particles, send_counts, cell_lists, base_field, proj_weight, conv_weight, cotangent):
    ngx, ngy = lax.axis_size("gx"), lax.axis_size("gy")
    ndev = ngx * ngy
    nrows, feats = particles.shape
    chans, cx, cy, nz = base_field.shape
    slots = cell_lists.shape[1]
    cap = slots // ndev
    count = cx * cy * nz
    assert cx == 1 and feats == 2 * chans
    proj_t = proj_weight.T
    move = functools.partial(send, ngx=ngx, ngy=ngy)
    rows = 3 * chans
    one = 2 * rows * rows * nz

    base = base_field.reshape(chans, cy, nz)
    west, east = move(base_field, 1, 0), move(base_field, -1, 0)
    planes = (base, west.reshape(base.shape), east.reshape(base.shape))
    lists = (cell_lists, move(cell_lists, 1, 0), move(cell_lists, -1, 0))
    (payload,) = call(
        functools.partial(first_kernel, ngx, ngy, cap),
        [shape((ndev * 3 * cap, feats), BF16)],
        (particles, send_counts),
        2 * slots * nrows * feats,
        (
            pltpu.VMEM(particles.shape, BF16),
            pltpu.VMEM(send_counts.shape, I32),
            pltpu.SemaphoreType.DMA((2,)),
        ),
        far=range(2),
        limit=ALL,
    )
    recv = exchange(payload, ndev)

    cot = cotangent[:, 0].transpose(1, 0, 2)
    taps = conv_weight.reshape(3, 3, 3, chans, chans)
    wf = taps.transpose(1, 2, 3, 0, 4).reshape(9 * chans, rows)
    wb = taps.transpose(1, 0, 4, 2, 3).reshape(9 * chans, rows)

    first, last, values, hots = call(
        functools.partial(outer_kernel, ndev, cap),
        [shape((rows, nz), BF16)] * 2
        + [shape((3, chans, slots), BF16), shape((3, nz, slots), BF16)],
        (recv, *planes, *lists, proj_t, cot, wf),
        4 * one,
        (pltpu.VMEM((4 * chans, slots), BF16), pltpu.VMEM((4, rows, nz), BF16)),
    )
    south, north = move(first, 0, -1), move(last, 0, 1)
    x_all, out_rows, total, pre_edge, slot_edge, plane = call(
        conv_kernel,
        [
            shape((cy, rows, nz), BF16),
            shape((cy, chans, nz), BF16),
            shape((9 * chans, rows), F32),
            shape((4, chans, nz), F32),
            shape((4, rows, nz), F32),
            shape((3, (cy - 4) * chans, nz), BF16),
        ],
        (values, hots, *planes, *lists, cot, wf, wb),
        3 * cy * 3 * one,
        (
            pltpu.VMEM((cy + 1, rows, nz), F32),
            pltpu.VMEM((cy + 2, rows, nz), BF16),
            pltpu.VMEM((cy, rows, nz), F32),
            pltpu.VMEM((cy * chans, slots), BF16),
        ),
    )
    grad_rows = 27 * chans * chans // feats
    part = -(-(grad_rows + 2 * chans) // (32 * ndev)) * 16
    full = grad_rows // (2 * part)
    assert ngx % 2 == 0 and full * 2 * part == grad_rows
    row = lax.axis_index("gx")
    parity = (row % 2).astype(I32).reshape(1)
    out_edge, grads, keep, give = call(
        functools.partial(edge_kernel, part),
        [
            shape((2, chans, nz), BF16),
            shape((4, rows, nz), BF16),
            shape((full, part, feats), F32),
            shape((full, part, feats), BF16),
        ],
        (parity, pre_edge, total, north, south, x_all, cot),
        6 * one,
        (pltpu.VMEM((9 * chans, rows), F32), pltpu.VMEM((full, 2, part, feats), F32)),
        scalar=(0,),
    )
    got = swap(give)
    terms, give = call(
        slots_kernel,
        [shape((3, chans, slots), F32), shape((chans, slots), BF16)],
        (parity, slot_edge, plane, hots, grads, wb, cot, *lists),
        6 * one,
        scalar=(0,),
    )
    got_terms = swap(give)
    proj, outer = call(
        functools.partial(proj_kernel, ndev, cap),
        [shape((ndev - full, part, feats), BF16), shape((chans, slots), F32)],
        (parity, terms, recv),
        one,
        scalar=(0,),
    )
    (payload,) = call(
        pair_kernel,
        [shape((ndev, part + cap, feats), BF16)],
        (keep, got, terms, got_terms, outer, proj),
        1000,
        (
            pltpu.VMEM((full, part, feats), BF16),
            pltpu.VMEM((ndev, cap, feats), BF16),
            pltpu.SemaphoreType.DMA((3,)),
        ),
        far_out=(0,),
    )
    (payload,) = call(same_kernel, [payload], (payload,), 0, far=(0,), far_out=(0,), aliases={0: 0})
    recv = exchange(payload.reshape(-1, feats), ndev).reshape(payload.shape)
    index = (row * ngy + lax.axis_index("gy")).astype(I32).reshape(1, 1)
    (sums,) = call(
        functools.partial(sums_kernel, ngx, ngy, full, cap),
        [shape((ndev, part, feats), BF16)],
        (recv, index),
        1000,
    )
    row_grads, out_field = call(
        functools.partial(rows_kernel, ngx, ngy, cap, chans),
        [shape((nrows, feats), F32), shape((chans, cy, nz), BF16)],
        (recv, send_counts, proj_t, out_rows, out_edge),
        2 * nrows * slots * chans,
    )
    mine = exchange(sums.reshape(-1, feats), ndev).reshape(sums.shape)
    mine, row_grads, out_field = lax.optimization_barrier((mine, row_grads, out_field))
    other = swap(mine)
    conv_grad, proj_grad = call(
        functools.partial(
            finish_kernel, 1.0 / math.sqrt(count * ndev), 1.0 / math.sqrt(nrows * ndev)
        ),
        [shape((27, chans, chans), F32), shape((chans, feats), F32)],
        (parity, mine, other),
        1000,
        (pltpu.VMEM((ndev, 2, part, feats), BF16),),
        scalar=(0,),
    )
    return (out_field[:, None], row_grads, conv_grad, proj_grad.T)


def solution(mesh):
    in_specs = (
        P(("gx", "gy"), None),
        P(("gx", "gy"), None),
        P(("gx", "gy"), None),
        P(None, "gx", "gy", None),
        P(),
        P(),
        P(None, "gx", "gy", None),
    )
    out_specs = (P(None, "gx", "gy", None), P(("gx", "gy"), None), P(), P())
    return jax.shard_map(local, mesh=mesh, in_specs=in_specs, out_specs=out_specs, check_vma=False)
```

```python
import functools
import math

import jax
import jax.numpy as jnp
from jax import lax
from jax.experimental import pallas as pl
from jax.experimental.pallas import tpu as pltpu
from jax.sharding import PartitionSpec as P

AXES = ("gx", "gy")
F32, BF16, I32 = jnp.float32, jnp.bfloat16, jnp.int32
LIMIT = 40 * 1024 * 1024
ALL = 60 * 1024 * 1024
NT = (((1,), (1,)), ((), ()))
NN = (((1,), (0,)), ((), ()))


def mm(a, b, dims=NN):
    return lax.dot_general(a, b, dims, preferred_element_type=F32)


def call(kernel, outs, args, flops, scratch=(), far=(), far_out=(), aliases=None, limit=LIMIT, scalar=()):
    traffic = sum(math.prod(a.shape) * a.dtype.itemsize for a in (*args, *outs))
    near = pl.BlockSpec(memory_space=pltpu.VMEM)
    there = pl.BlockSpec(memory_space=pltpu.HBM)
    return pl.pallas_call(
        kernel,
        out_shape=[jax.ShapeDtypeStruct(o.shape, o.dtype) for o in outs],
        in_specs=[
            pl.BlockSpec(memory_space=pltpu.SMEM) if n in scalar else there if n in far else near
            for n in range(len(args))
        ],
        out_specs=[there if n in far_out else near for n in range(len(outs))],
        scratch_shapes=list(scratch),
        input_output_aliases=aliases or {},
        compiler_params=pltpu.CompilerParams(vmem_limit_bytes=limit),
        cost_estimate=pl.CostEstimate(flops=flops, bytes_accessed=traffic, transcendentals=0),
    )(*args)


def shape(dims, dtype):
    return jax.ShapeDtypeStruct(dims, dtype)


def beside(block, step):
    count = lax.axis_size("gy")
    if step == 0:
        return lax.ppermute(block, "gy", [(0, count - 1), (count - 1, 0)])
    starts = range(count - 1) if step > 0 else range(1, count)
    return lax.ppermute(block, "gy", [(j, j + step) for j in starts])


def send(block, di, dj, ngx, ngy):
    pairs = []
    for i in range(ngx):
        for j in range(ngy):
            pairs.append((i * ngy + j, ((i + di) % ngx) * ngy + (j + dj) % ngy))
    return lax.ppermute(block, AXES, pairs)


def swap(block):
    return lax.ppermute(block, "gx", [(i, i ^ 1) for i in range(lax.axis_size("gx"))])


def exchange(payload, ndev):
    rows, width = payload.shape
    moved = lax.all_to_all(
        payload.reshape(ndev, rows // ndev, width), AXES, split_axis=0, concat_axis=0, tiled=True
    )
    return moved.reshape(rows, width)


def rolled(x, di, dj):
    for axis, shift in ((0, di), (1, dj)):
        if shift == 1:
            head, tail = lax.slice_in_dim(x, 1, None, axis=axis), lax.slice_in_dim(x, 0, 1, axis=axis)
            x = jnp.concatenate([head, tail], axis=axis)
        elif shift == -1:
            count = x.shape[axis]
            head = lax.slice_in_dim(x, count - 1, count, axis=axis)
            x = jnp.concatenate([head, lax.slice_in_dim(x, 0, count - 1, axis=axis)], axis=axis)
    return x


def picked_depth(z, nz):
    depth = lax.broadcasted_iota(I32, (nz, z.shape[1]), 0)
    return jnp.where(depth == z, 1.0, 0.0).astype(BF16)


def rows_in(recv_ref, ndev, cap):
    width = recv_ref.shape[1]
    arrived = recv_ref[...].astype(F32).reshape(ndev, 3, cap, width)
    return [arrived[:, n].reshape(ndev * cap, width).astype(BF16) for n in range(3)]


def stacked(grad):
    nz = grad.shape[1]
    wide = grad.astype(F32)
    return jnp.concatenate(
        [pltpu.roll(wide, nz - 1, 1), wide, pltpu.roll(wide, 1, 1)], axis=0
    ).astype(BF16)


def over_depth(acc):
    chans, nz = acc.shape[0] // 3, acc.shape[1]
    total = acc[chans : 2 * chans] + pltpu.roll(acc[:chans], 1, 1)
    return total + pltpu.roll(acc[2 * chans :], nz - 1, 1)


def finish_row(pre, field, cot):
    sig = jax.nn.sigmoid(pre)
    out = field.astype(F32) + pre * sig
    grad = cot.astype(F32) * sig * (1.0 + pre * (1.0 - sig))
    return out.astype(BF16), grad.astype(BF16)


def first_kernel(
    ngx, ngy, cap, rows_far, counts_far, send_ref, rows_ref, counts_ref, sems
):
    copies = [
        pltpu.make_async_copy(rows_far, rows_ref, sems.at[0]),
        pltpu.make_async_copy(counts_far, counts_ref, sems.at[1]),
    ]
    for copy in copies:
        copy.start()
    for copy in copies:
        copy.wait()
    pick(ngx, ngy, cap, counts_ref, rows_ref, send_ref)


def same_kernel(in_ref, out_ref):
    pass


def both_kernel(first_ref, last_ref, first_out, last_out):
    pass


def pick(ngx, ngy, cap, counts_ref, rows_ref, out_ref):
    ndev = ngx * ngy
    nrows, feats = rows_ref.shape
    slots = ndev * cap
    counts = counts_ref[...].astype(F32)
    owner = lax.broadcasted_iota(I32, (ndev, cap, ndev), 0).reshape(slots, ndev)
    lane = lax.broadcasted_iota(I32, (slots, ndev), 1)
    start = jnp.sum(jnp.where(lane < owner, counts, 0.0), axis=1, keepdims=True)
    held = jnp.sum(jnp.where(lane == owner, counts, 0.0), axis=1, keepdims=True)
    place = lax.broadcasted_iota(I32, (ndev, cap, nrows), 1).reshape(slots, nrows).astype(F32)
    row = lax.broadcasted_iota(I32, (slots, nrows), 1).astype(F32)
    onehot = jnp.where((row == place + start) & (place < held), 1.0, 0.0).astype(BF16)
    raw = mm(onehot, rows_ref[...]).reshape(ngx, ngy, cap, feats)
    parts = [rolled(raw, dx, 0).reshape(ndev, cap, feats) for dx in (-1, 0, 1)]
    out_ref[...] = jnp.stack(parts, axis=1).reshape(out_ref.shape).astype(BF16)


def painted_rows(values, y, onehot, ns, masked):
    chans = values.shape[0]
    for n, row in enumerate(ns):
        masked[pl.ds(n * chans, chans)] = values * jnp.where(y == row, 1.0, 0.0).astype(BF16)
    return mm(masked[pl.ds(0, len(ns) * chans)], onehot, NT)


def add_to_rows(near, far, cot, back, out_ref):
    chans = cot.shape[0]
    rows = 3 * chans
    at, over = (rows, 0) if back else (0, rows)
    out_ref[pl.ds(0, chans)] = over_depth(near[at : at + rows]).astype(BF16)
    out_ref[pl.ds(chans, chans)] = over_depth(near[over : over + rows] + far).astype(BF16)
    out_ref[pl.ds(2 * chans, chans)] = cot


def outer_kernel(
    ndev, cap, spot_ref, recv_ref, own_ref, west_ref, east_ref, own_cells, west_cells, east_cells,
    proj_t_ref, cot_ref, wf_ref, first_ref, last_ref, wrap_ref, values_ref, hot_ref, masked, field,
):
    chans, cy, nz = own_ref.shape
    rows = 3 * chans
    raws = rows_in(recv_ref, ndev, cap)
    ns = (0, 1, cy - 2, cy - 1)
    planes = ((west_ref, west_cells), (own_ref, own_cells), (east_ref, east_cells))
    for dx, (ref, cells_ref) in enumerate(planes):
        values = mm(proj_t_ref[...], raws[dx], NT).astype(BF16)
        y, z = place(cells_ref, nz)
        onehot = picked_depth(z, nz)
        values_ref[dx] = values
        hot_ref[dx] = onehot
        painted = painted_rows(values, y, onehot, ns, masked)
        base = turned(ref)
        for n, row in enumerate(ns):
            part = painted[n * chans : (n + 1) * chans]
            field[n, pl.ds(dx * chans, chans)] = (base[row] + part).astype(BF16)
    near = mm(wf_ref[pl.ds(0, 2 * rows)], field[3])
    add_to_rows(near, mm(wf_ref[pl.ds(0, rows)], field[2]), cot_ref[cy - 1], False, last_ref)
    near = mm(wf_ref[pl.ds(rows, 2 * rows)], field[0])
    add_to_rows(near, mm(wf_ref[pl.ds(2 * rows, rows)], field[1]), cot_ref[0], True, first_ref)

    @pl.when(spot_ref[1] == 1)
    def _():
        wrap_ref[...] = first_ref[...]

    @pl.when(spot_ref[1] != 1)
    def _():
        wrap_ref[...] = last_ref[...]


def place(cells_ref, nz):
    cells = cells_ref[...]
    return cells // nz, cells % nz


def turned(ref):
    return jnp.swapaxes(ref[...].astype(F32), 0, 1)


def conv_kernel(
    values_ref, hot_ref, own_ref, west_ref, east_ref, own_cells, west_cells, east_cells,
    cot_ref, wf_ref, wb_ref,
    x_ref, out_ref, total_ref, pre_ref, slot_ref, plane, acc, grads, back, masked,
):
    cy, chans, nz = cot_ref.shape
    rows = 3 * chans
    planes = ((west_ref, west_cells), (own_ref, own_cells), (east_ref, east_cells))
    for dx, (ref, cells_ref) in enumerate(planes):
        y, _ = place(cells_ref, nz)
        painted = painted_rows(values_ref[dx], y, hot_ref[dx], range(cy), masked)
        field = turned(ref) + painted.reshape(cy, chans, nz)
        x_ref[:, pl.ds(dx * chans, chans)] = field.astype(BF16)
    own = pl.ds(chans, chans)
    zeros = jnp.zeros((rows, nz), BF16)
    for t in (0, 1, cy, cy + 1):
        grads[t] = zeros
    out_ref[0] = zeros[:chans]
    out_ref[cy - 1] = zeros[:chans]
    acc[0] = jnp.zeros((rows, nz), F32)

    def spread(n):
        terms = mm(wf_ref[...], x_ref[n])
        acc[n + 1] = terms[:rows]
        acc[n] += terms[rows : 2 * rows]
        return terms[2 * rows :]

    pre_ref[0] = over_depth(spread(0))
    pre_ref[1] = over_depth(acc[0] + spread(1))

    def forward(n):
        done = spread(n) + acc[n - 1]
        y = n - 1
        out, grad = finish_row(over_depth(done), x_ref[y, own], cot_ref[y])
        out_ref[y] = out
        grads[y + 1] = stacked(grad)

    for n in range(2, cy):
        forward(n)
    pre_ref[2] = over_depth(acc[cy - 1])
    pre_ref[3] = over_depth(acc[cy])
    total_ref[...] = jnp.zeros_like(total_ref)
    back[0] = jnp.zeros((rows, nz), F32)
    back[1] = jnp.zeros((rows, nz), F32)

    def taps(n):
        window = grads[pl.ds(n, 3)].reshape(3 * rows, nz)
        total_ref[...] += mm(window, x_ref[n], NT)

    def spread_back(n):
        terms = mm(wb_ref[...], grads[n + 1])
        back[n + 1] = terms[2 * rows :]
        back[n] += terms[rows : 2 * rows]
        return terms[:rows]

    def backward(n):
        taps(n)
        value = spread_back(n) + back[n - 1]
        for dx in range(3):
            part = value[dx * chans : (dx + 1) * chans]
            if dx == 1:
                part = part + cot_ref[n - 1].astype(F32)
            plane[dx, pl.ds((n - 3) * chans, chans)] = part.astype(BF16)

    taps(0)
    taps(1)
    slot_ref[0] = spread_back(1)
    taps(2)
    slot_ref[1] = spread_back(2) + back[1]
    for n in range(3, cy - 1):
        backward(n)
    taps(cy - 1)
    slot_ref[2] = back[cy - 2]
    slot_ref[3] = back[cy - 1]


def at_slots(part, y, onehot, first):
    found = mm(part, onehot)
    chans = found.shape[0] // len(first)
    total = jnp.zeros((chans, found.shape[1]), F32)
    for n, row in enumerate(first):
        total = total + jnp.where(y == row, found[n * chans : (n + 1) * chans], 0.0)
    return total


def edge_kernel(
    part, spot_ref, pre_ref, total_ref, north_ref, south_ref, wrap_ref, x_ref, cot_ref,
    out_ref, grads_ref, keep_ref, give_ref, total, sums,
):
    cy, chans, nz = cot_ref.shape
    rows = 3 * chans
    own = pl.ds(chans, chans)
    wrap = wrap_ref[...].astype(F32)
    north = jnp.where(spot_ref[1] == 1, wrap, north_ref[...].astype(F32))
    south = jnp.where(spot_ref[2] == 1, wrap, south_ref[...].astype(F32))
    cots = (north[2 * chans :], cot_ref[0], cot_ref[cy - 1], south[2 * chans :])
    ends = []
    for n, (side, at) in enumerate(((north, 1), (north, 0), (south, 0), (south, 1))):
        pre = pre_ref[n] + side[at * chans : (at + 1) * chans]
        ends.append(finish_row(pre, x_ref[0 if n < 2 else cy - 1, own], cots[n]))
    out_ref[0], out_ref[1] = ends[1][0], ends[2][0]
    grads = [stacked(grad) for _, grad in ends]
    for n in range(4):
        grads_ref[n] = grads[n]
    top = mm(jnp.concatenate([grads[0], grads[1]], axis=0), x_ref[0], NT)
    bottom = mm(jnp.concatenate([grads[2], grads[3]], axis=0), x_ref[cy - 1], NT)
    here = [pl.ds(n * rows, rows) for n in range(3)]
    total[here[0]] = total_ref[here[0]] + (top[:rows] + mm(grads[1], x_ref[1], NT))
    total[here[1]] = total_ref[here[1]] + (top[rows:] + bottom[:rows])
    total[here[2]] = total_ref[here[2]] + (bottom[rows:] + mm(grads[2], x_ref[cy - 2], NT))
    full, _, width = keep_ref.shape
    half = 3 * rows // 2
    split = 3 * rows // (2 * part)
    sums[pl.ds(0, split)] = total[:, :width].reshape(split, 2, part, width)
    taps = jnp.concatenate([total[pl.ds(0, half), width:], total[pl.ds(half, half), width:]], axis=1)
    sums[pl.ds(split, full - split)] = taps.reshape(full - split, 2, part, width)
    parity = spot_ref[0]
    keep_ref[...] = sums[:, parity]
    give_ref[...] = sums[:, 1 - parity].astype(BF16)


def slots_kernel(
    ndev, cap, part, full, slot_ref, plane_ref, hot_ref, grads_ref, wb_ref, cot_ref,
    own_cells, west_cells, east_cells, recv_ref, slots_ref, proj_ref,
):
    cy, chans, nz = cot_ref.shape
    rows = 3 * chans
    inner = mm(wb_ref[pl.ds(rows, 2 * rows)], grads_ref[1])
    top = slot_ref[0] + inner[:rows] + mm(wb_ref[pl.ds(2 * rows, rows)], grads_ref[0])
    second = slot_ref[1] + inner[rows:]
    inner = mm(wb_ref[pl.ds(0, 2 * rows)], grads_ref[2])
    third = slot_ref[2] + inner[:rows]
    bottom = slot_ref[3] + inner[rows:] + mm(wb_ref[pl.ds(0, rows)], grads_ref[3])
    at = (0, 1, cy - 2, cy - 1)
    found = []
    for dx, cells_ref in enumerate((west_cells, own_cells, east_cells)):
        parts = [value[dx * chans : (dx + 1) * chans] for value in (top, second, third, bottom)]
        if dx == 1:
            parts = [value + cot_ref[n].astype(F32) for value, n in zip(parts, at)]
        parts = [value.astype(BF16) for value in parts]
        terms = jnp.concatenate([plane_ref[dx], *parts], axis=0)
        y, _ = place(cells_ref, nz)
        found.append(at_slots(terms, y, hot_ref[dx], (*range(2, cy - 2), *at)))
    sides = jnp.concatenate([found[0], found[2]], axis=0).T
    middle = jnp.concatenate([found[1], jnp.zeros_like(found[1])], axis=0).T
    width = recv_ref.shape[1]
    back = [sides.reshape(ndev, cap, width), middle.reshape(ndev, cap, width)]
    slots_ref[...] = jnp.concatenate(back, axis=1).astype(BF16)
    raws = rows_in(recv_ref, ndev, cap)
    proj = sum(mm(found[dx].astype(BF16), raws[dx]) for dx in range(3))
    rest = ndev - full
    pad = jnp.zeros((rest * part - chans, width), F32)
    proj = jnp.concatenate([proj, pad], axis=0).reshape(rest, part, width)
    proj_ref[...] = proj.astype(BF16)


def pair_kernel(keep_ref, got_ref, slots_ref, proj_ref, send_far, sums_send, sems):
    full, part, _ = keep_ref.shape
    ndev, back, _ = slots_ref.shape
    pieces = (
        (slots_ref, send_far.at[:, pl.ds(part, back)]),
        (proj_ref, send_far.at[pl.ds(full, ndev - full), pl.ds(0, part)]),
        (sums_send, send_far.at[pl.ds(0, full), pl.ds(0, part)]),
    )
    copies = [pltpu.make_async_copy(src, dst, sems.at[n]) for n, (src, dst) in enumerate(pieces)]
    copies[0].start()
    copies[1].start()
    sums_send[...] = (keep_ref[...] + got_ref[...].astype(F32)).astype(BF16)
    copies[2].start()
    for copy in copies:
        copy.wait()


def sums_kernel(ngx, ngy, full, cap, recv_ref, index_ref, sums_ref):
    ndev, each, width = recv_ref.shape
    part = each - 2 * cap
    terms = recv_ref[:, pl.ds(0, part)].astype(F32).reshape(ngx // 2, 2, ngy, part, width)
    sums = jnp.sum(terms, axis=(0, 2))
    whole = sums[0] + sums[1]
    high = whole.astype(BF16).astype(F32)
    last = jnp.broadcast_to(index_ref[...], whole.shape) >= full
    sums = [
        jnp.where(last, high, sums[0]).astype(BF16),
        jnp.where(last, whole - high, sums[1]).astype(BF16),
    ]
    for n in range(ndev):
        sums_ref[n] = sums[(n // ngy) % 2]


def rows_kernel(
    ngx, ngy, cap, chans, recv_ref, counts_ref, proj_t_ref, inner_ref, ends_ref, rows_ref, out_ref
):
    ndev = ngx * ngy
    nrows = rows_ref.shape[0]
    width = recv_ref.shape[2]
    slots = ndev * cap
    share = recv_ref.shape[1] - 2 * cap
    arrived = recv_ref[:, pl.ds(share, 2 * cap)].astype(F32)
    sides = arrived[:, :cap].reshape(ngx, ngy, cap, width)
    left = lax.broadcasted_iota(I32, sides.shape, 3) < chans
    sides = jnp.where(left, rolled(sides, 1, 0), rolled(sides, -1, 0)).reshape(slots, width)
    middle = arrived[:, cap:].reshape(slots, width)
    counts = counts_ref[...].astype(F32)
    place = lax.broadcasted_iota(I32, (nrows, ndev), 0).astype(F32)
    lane = lax.broadcasted_iota(I32, (ndev, ndev), 1)
    upto = lax.broadcasted_iota(I32, (ndev, ndev), 0) <= lane
    ends = mm(counts.astype(BF16), jnp.where(upto, 1.0, 0.0).astype(BF16))
    before = ends <= place
    owner = jnp.sum(jnp.where(before, 1.0, 0.0), axis=1, keepdims=True)
    start = jnp.sum(jnp.where(before, counts, 0.0), axis=1, keepdims=True)
    slot = owner * cap + place[:, :1] - start
    onehot = jnp.where(
        lax.broadcasted_iota(I32, (nrows, slots), 1).astype(F32) == slot, 1.0, 0.0
    ).astype(BF16)
    proj_t = proj_t_ref[...]
    both = jnp.concatenate([proj_t, proj_t], axis=0)
    sides = mm(onehot, sides.astype(BF16)).astype(BF16)
    middle = mm(onehot, middle.astype(BF16)).astype(BF16)
    rows_ref[...] = mm(sides, both) + mm(middle, both)
    cy = inner_ref.shape[0]
    field = jnp.concatenate([ends_ref[:1], inner_ref[1 : cy - 1], ends_ref[1:]], axis=0)
    out_ref[...] = jnp.swapaxes(field.astype(F32), 0, 1).astype(BF16)


def finish_kernel(conv_scale, proj_scale, parity_ref, mine_ref, other_ref, conv_ref, proj_ref, both):
    ndev, part, width = mine_ref.shape
    parity = parity_ref[0]
    both[:, parity] = mine_ref[...]
    both[:, 1 - parity] = other_ref[...]
    sums = both[...].astype(F32).reshape(ndev * 2 * part, width)
    taps, chans, _ = conv_ref.shape
    rows = 9 * chans
    half = rows // 2
    packed = sums[rows : rows + half]
    column = jnp.concatenate([packed[:, :chans], packed[:, chans:]], axis=0)
    for b in range(3):
        for dz in range(3):
            first = (b * 3 + dz) * chans
            block = sums[first : first + chans]
            k = (2 - b) * 3 + dz
            conv_ref[k] = block[:, :chans] * conv_scale
            conv_ref[9 + k] = block[:, chans:] * conv_scale
            conv_ref[18 + k] = column[first : first + chans] * conv_scale
    terms = sums[rows + half : rows + half + 2 * chans].reshape(chans // part, 2, part, width)
    proj_ref[...] = jnp.sum(terms, axis=1).reshape(chans, width) * proj_scale


def local(particles, send_counts, cell_lists, base_field, proj_weight, conv_weight, cotangent):
    ngx, ngy = lax.axis_size("gx"), lax.axis_size("gy")
    ndev = ngx * ngy
    nrows, feats = particles.shape
    chans, cx, cy, nz = base_field.shape
    slots = cell_lists.shape[1]
    cap = slots // ndev
    count = cx * cy * nz
    assert cx == 1 and feats == 2 * chans
    proj_t = proj_weight.T
    move = functools.partial(send, ngx=ngx, ngy=ngy)
    rows = 3 * chans
    one = 2 * rows * rows * nz

    base = base_field.reshape(chans, cy, nz)
    west, east = move(base_field, 1, 0), move(base_field, -1, 0)
    planes = (base, west.reshape(base.shape), east.reshape(base.shape))
    lists = (cell_lists, move(cell_lists, 1, 0), move(cell_lists, -1, 0))
    (payload,) = call(
        functools.partial(first_kernel, ngx, ngy, cap),
        [shape((ndev * 3 * cap, feats), BF16)],
        (particles, send_counts),
        2 * slots * nrows * feats,
        (
            pltpu.VMEM(particles.shape, BF16),
            pltpu.VMEM(send_counts.shape, I32),
            pltpu.SemaphoreType.DMA((2,)),
        ),
        far=range(2),
        limit=ALL,
    )
    recv = exchange(payload, ndev)

    cot = cotangent[:, 0].transpose(1, 0, 2)
    taps = conv_weight.reshape(3, 3, 3, chans, chans)
    wf = taps.transpose(1, 2, 3, 0, 4).reshape(9 * chans, rows)
    wb = taps.transpose(1, 0, 4, 2, 3).reshape(9 * chans, rows)

    row, column = lax.axis_index("gx"), lax.axis_index("gy")
    spot = jnp.stack([row % 2, column == 0, column == ngy - 1]).astype(I32)
    first, last, wrap, values, hots = call(
        functools.partial(outer_kernel, ndev, cap),
        [shape((rows, nz), BF16)] * 3
        + [shape((3, chans, slots), BF16), shape((3, nz, slots), BF16)],
        (spot, recv, *planes, *lists, proj_t, cot, wf),
        4 * one,
        (pltpu.VMEM((4 * chans, slots), BF16), pltpu.VMEM((4, rows, nz), BF16)),
        scalar=(0,),
    )
    wrap = beside(wrap, 0)
    first, last = call(both_kernel, [first, last], (first, last), 0, aliases={0: 0, 1: 1})
    south, north = beside(first, -1), beside(last, 1)
    x_all, out_rows, total, pre_edge, slot_edge, plane = call(
        conv_kernel,
        [
            shape((cy, rows, nz), BF16),
            shape((cy, chans, nz), BF16),
            shape((9 * chans, rows), F32),
            shape((4, chans, nz), F32),
            shape((4, rows, nz), F32),
            shape((3, (cy - 4) * chans, nz), BF16),
        ],
        (values, hots, *planes, *lists, cot, wf, wb),
        3 * cy * 3 * one,
        (
            pltpu.VMEM((cy + 1, rows, nz), F32),
            pltpu.VMEM((cy + 2, rows, nz), BF16),
            pltpu.VMEM((cy, rows, nz), F32),
            pltpu.VMEM((cy * chans, slots), BF16),
        ),
    )
    grad_rows = 27 * chans * chans // feats
    part = -(-(grad_rows + 2 * chans) // (32 * ndev)) * 16
    full = grad_rows // (2 * part)
    assert ngx % 2 == 0 and ngy > 1 and full * 2 * part == grad_rows
    out_edge, grads, keep, give = call(
        functools.partial(edge_kernel, part),
        [
            shape((2, chans, nz), BF16),
            shape((4, rows, nz), BF16),
            shape((full, part, feats), F32),
            shape((full, part, feats), BF16),
        ],
        (spot, pre_edge, total, north, south, wrap, x_all, cot),
        6 * one,
        (pltpu.VMEM((9 * chans, rows), F32), pltpu.VMEM((full, 2, part, feats), F32)),
        scalar=(0,),
    )
    got = swap(give)
    back, proj = call(
        functools.partial(slots_kernel, ndev, cap, part, full),
        [shape((ndev, 2 * cap, feats), BF16), shape((ndev - full, part, feats), BF16)],
        (slot_edge, plane, hots, grads, wb, cot, *lists, recv),
        6 * one,
    )
    (payload,) = call(
        pair_kernel,
        [shape((ndev, part + 2 * cap, feats), BF16)],
        (keep, got, back, proj),
        1000,
        (pltpu.VMEM((full, part, feats), BF16), pltpu.SemaphoreType.DMA((3,))),
        far_out=(0,),
    )
    (payload,) = call(same_kernel, [payload], (payload,), 0, far=(0,), far_out=(0,), aliases={0: 0})
    recv = exchange(payload.reshape(-1, feats), ndev).reshape(payload.shape)
    index = (row * ngy + column).astype(I32).reshape(1, 1)
    (sums,) = call(
        functools.partial(sums_kernel, ngx, ngy, full, cap),
        [shape((ndev, part, feats), BF16)],
        (recv, index),
        1000,
    )
    row_grads, out_field = call(
        functools.partial(rows_kernel, ngx, ngy, cap, chans),
        [shape((nrows, feats), F32), shape((chans, cy, nz), BF16)],
        (recv, send_counts, proj_t, out_rows, out_edge),
        2 * nrows * slots * chans,
    )
    mine = exchange(sums.reshape(-1, feats), ndev).reshape(sums.shape)
    mine, row_grads, out_field = lax.optimization_barrier((mine, row_grads, out_field))
    other = swap(mine)
    conv_grad, proj_grad = call(
        functools.partial(
            finish_kernel, 1.0 / math.sqrt(count * ndev), 1.0 / math.sqrt(nrows * ndev)
        ),
        [shape((27, chans, chans), F32), shape((chans, feats), F32)],
        (spot, mine, other),
        1000,
        (pltpu.VMEM((ndev, 2, part, feats), BF16),),
        scalar=(0,),
    )
    return (out_field[:, None], row_grads, conv_grad, proj_grad.T)


def solution(mesh):
    in_specs = (
        P(("gx", "gy"), None),
        P(("gx", "gy"), None),
        P(("gx", "gy"), None),
        P(None, "gx", "gy", None),
        P(),
        P(),
        P(None, "gx", "gy", None),
    )
    out_specs = (P(None, "gx", "gy", None), P(("gx", "gy"), None), P(), P())
    return jax.shard_map(local, mesh=mesh, in_specs=in_specs, out_specs=out_specs, check_vma=False)
```

```python
import functools
import math

import jax
import jax.numpy as jnp
from jax import lax
from jax.experimental import pallas as pl
from jax.experimental.pallas import tpu as pltpu
from jax.sharding import PartitionSpec as P

AXES = ("gx", "gy")
F32, BF16, I32 = jnp.float32, jnp.bfloat16, jnp.int32
LIMIT = 40 * 1024 * 1024
ALL = 60 * 1024 * 1024
NT = (((1,), (1,)), ((), ()))
NN = (((1,), (0,)), ((), ()))


def mm(a, b, dims=NN):
    return lax.dot_general(a, b, dims, preferred_element_type=F32)


def call(kernel, outs, args, flops, scratch=(), far=(), far_out=(), aliases=None, limit=LIMIT, scalar=()):
    traffic = sum(math.prod(a.shape) * a.dtype.itemsize for a in (*args, *outs))
    near = pl.BlockSpec(memory_space=pltpu.VMEM)
    there = pl.BlockSpec(memory_space=pltpu.HBM)
    return pl.pallas_call(
        kernel,
        out_shape=[jax.ShapeDtypeStruct(o.shape, o.dtype) for o in outs],
        in_specs=[
            pl.BlockSpec(memory_space=pltpu.SMEM) if n in scalar else there if n in far else near
            for n in range(len(args))
        ],
        out_specs=[there if n in far_out else near for n in range(len(outs))],
        scratch_shapes=list(scratch),
        input_output_aliases=aliases or {},
        compiler_params=pltpu.CompilerParams(vmem_limit_bytes=limit),
        cost_estimate=pl.CostEstimate(flops=flops, bytes_accessed=traffic, transcendentals=0),
    )(*args)


def shape(dims, dtype):
    return jax.ShapeDtypeStruct(dims, dtype)


def send(block, di, dj, ngx, ngy):
    pairs = []
    for i in range(ngx):
        for j in range(ngy):
            pairs.append((i * ngy + j, ((i + di) % ngx) * ngy + (j + dj) % ngy))
    return lax.ppermute(block, AXES, pairs)


def swap(block):
    return lax.ppermute(block, "gx", [(i, i ^ 1) for i in range(lax.axis_size("gx"))])


def exchange(payload, ndev):
    rows, width = payload.shape
    moved = lax.all_to_all(
        payload.reshape(ndev, rows // ndev, width), AXES, split_axis=0, concat_axis=0, tiled=True
    )
    return moved.reshape(rows, width)


def rolled(x, di, dj):
    for axis, shift in ((0, di), (1, dj)):
        if shift == 1:
            head, tail = lax.slice_in_dim(x, 1, None, axis=axis), lax.slice_in_dim(x, 0, 1, axis=axis)
            x = jnp.concatenate([head, tail], axis=axis)
        elif shift == -1:
            count = x.shape[axis]
            head = lax.slice_in_dim(x, count - 1, count, axis=axis)
            x = jnp.concatenate([head, lax.slice_in_dim(x, 0, count - 1, axis=axis)], axis=axis)
    return x


def picked_depth(z, nz):
    depth = lax.broadcasted_iota(I32, (nz, z.shape[1]), 0)
    return jnp.where(depth == z, 1.0, 0.0).astype(BF16)


def rows_in(recv_ref, ndev, cap):
    width = recv_ref.shape[1]
    arrived = recv_ref[...].astype(F32).reshape(ndev, 3, cap, width)
    return [arrived[:, n].reshape(ndev * cap, width).astype(BF16) for n in range(3)]


def stacked(grad):
    nz = grad.shape[1]
    wide = grad.astype(F32)
    return jnp.concatenate(
        [pltpu.roll(wide, nz - 1, 1), wide, pltpu.roll(wide, 1, 1)], axis=0
    ).astype(BF16)


def over_depth(acc):
    chans, nz = acc.shape[0] // 3, acc.shape[1]
    total = acc[chans : 2 * chans] + pltpu.roll(acc[:chans], 1, 1)
    return total + pltpu.roll(acc[2 * chans :], nz - 1, 1)


def finish_row(pre, field, cot):
    sig = jax.nn.sigmoid(pre)
    out = field.astype(F32) + pre * sig
    grad = cot.astype(F32) * sig * (1.0 + pre * (1.0 - sig))
    return out.astype(BF16), grad.astype(BF16)


def first_kernel(
    ngx, ngy, cap, rows_far, counts_far, send_ref, rows_ref, counts_ref, sems
):
    copies = [
        pltpu.make_async_copy(rows_far, rows_ref, sems.at[0]),
        pltpu.make_async_copy(counts_far, counts_ref, sems.at[1]),
    ]
    for copy in copies:
        copy.start()
    for copy in copies:
        copy.wait()
    pick(ngx, ngy, cap, counts_ref, rows_ref, send_ref)


def same_kernel(in_ref, out_ref):
    pass


def pick(ngx, ngy, cap, counts_ref, rows_ref, out_ref):
    ndev = ngx * ngy
    nrows, feats = rows_ref.shape
    slots = ndev * cap
    counts = counts_ref[...].astype(F32)
    owner = lax.broadcasted_iota(I32, (ndev, cap, ndev), 0).reshape(slots, ndev)
    lane = lax.broadcasted_iota(I32, (slots, ndev), 1)
    start = jnp.sum(jnp.where(lane < owner, counts, 0.0), axis=1, keepdims=True)
    held = jnp.sum(jnp.where(lane == owner, counts, 0.0), axis=1, keepdims=True)
    place = lax.broadcasted_iota(I32, (ndev, cap, nrows), 1).reshape(slots, nrows).astype(F32)
    row = lax.broadcasted_iota(I32, (slots, nrows), 1).astype(F32)
    onehot = jnp.where((row == place + start) & (place < held), 1.0, 0.0).astype(BF16)
    raw = mm(onehot, rows_ref[...]).reshape(ngx, ngy, cap, feats)
    parts = [rolled(raw, dx, 0).reshape(ndev, cap, feats) for dx in (-1, 0, 1)]
    out_ref[...] = jnp.stack(parts, axis=1).reshape(out_ref.shape).astype(BF16)


def painted_rows(values, y, onehot, ns, masked):
    chans = values.shape[0]
    for n, row in enumerate(ns):
        masked[pl.ds(n * chans, chans)] = values * jnp.where(y == row, 1.0, 0.0).astype(BF16)
    return mm(masked[pl.ds(0, len(ns) * chans)], onehot, NT)


def add_to_rows(near, far, cot, back, out_ref):
    chans = cot.shape[0]
    rows = 3 * chans
    at, over = (rows, 0) if back else (0, rows)
    out_ref[pl.ds(0, chans)] = over_depth(near[at : at + rows]).astype(BF16)
    out_ref[pl.ds(chans, chans)] = over_depth(near[over : over + rows] + far).astype(BF16)
    out_ref[pl.ds(2 * chans, chans)] = cot


def outer_kernel(
    ndev, cap, recv_ref, own_ref, west_ref, east_ref, own_cells, west_cells, east_cells,
    proj_t_ref, cot_ref, wf_ref, first_ref, last_ref, values_ref, hot_ref, masked, field,
):
    chans, cy, nz = own_ref.shape
    rows = 3 * chans
    raws = rows_in(recv_ref, ndev, cap)
    ns = (0, 1, cy - 2, cy - 1)
    planes = ((west_ref, west_cells), (own_ref, own_cells), (east_ref, east_cells))
    for dx, (ref, cells_ref) in enumerate(planes):
        values = mm(proj_t_ref[...], raws[dx], NT).astype(BF16)
        y, z = place(cells_ref, nz)
        onehot = picked_depth(z, nz)
        values_ref[dx] = values
        hot_ref[dx] = onehot
        painted = painted_rows(values, y, onehot, ns, masked)
        base = turned(ref)
        for n, row in enumerate(ns):
            part = painted[n * chans : (n + 1) * chans]
            field[n, pl.ds(dx * chans, chans)] = (base[row] + part).astype(BF16)
    near = mm(wf_ref[pl.ds(0, 2 * rows)], field[3])
    add_to_rows(near, mm(wf_ref[pl.ds(0, rows)], field[2]), cot_ref[cy - 1], False, last_ref)
    near = mm(wf_ref[pl.ds(rows, 2 * rows)], field[0])
    add_to_rows(near, mm(wf_ref[pl.ds(2 * rows, rows)], field[1]), cot_ref[0], True, first_ref)


def place(cells_ref, nz):
    cells = cells_ref[...]
    return cells // nz, cells % nz


def turned(ref):
    return jnp.swapaxes(ref[...], 0, 1).astype(F32)


def conv_kernel(
    values_ref, hot_ref, own_ref, west_ref, east_ref, own_cells, west_cells, east_cells,
    cot_ref, wf_ref, wb_ref,
    x_ref, out_ref, total_ref, pre_ref, slot_ref, plane, acc, grads, back, masked,
):
    cy, chans, nz = cot_ref.shape
    rows = 3 * chans
    planes = ((west_ref, west_cells), (own_ref, own_cells), (east_ref, east_cells))
    for dx, (ref, cells_ref) in enumerate(planes):
        y, _ = place(cells_ref, nz)
        painted = painted_rows(values_ref[dx], y, hot_ref[dx], range(cy), masked)
        field = turned(ref) + painted.reshape(cy, chans, nz)
        x_ref[:, pl.ds(dx * chans, chans)] = field.astype(BF16)
    own = pl.ds(chans, chans)
    zeros = jnp.zeros((rows, nz), BF16)
    for t in (0, 1, cy, cy + 1):
        grads[t] = zeros
    out_ref[0] = zeros[:chans]
    out_ref[cy - 1] = zeros[:chans]
    acc[0] = jnp.zeros((rows, nz), F32)

    def spread(n):
        terms = mm(wf_ref[...], x_ref[n])
        acc[n + 1] = terms[:rows]
        acc[n] += terms[rows : 2 * rows]
        return terms[2 * rows :]

    pre_ref[0] = over_depth(spread(0))
    pre_ref[1] = over_depth(acc[0] + spread(1))

    def forward(n):
        done = spread(n) + acc[n - 1]
        y = n - 1
        out, grad = finish_row(over_depth(done), x_ref[y, own], cot_ref[y])
        out_ref[y] = out
        grads[y + 1] = stacked(grad)

    for n in range(2, cy):
        forward(n)
    pre_ref[2] = over_depth(acc[cy - 1])
    pre_ref[3] = over_depth(acc[cy])
    total_ref[...] = jnp.zeros_like(total_ref)
    back[0] = jnp.zeros((rows, nz), F32)
    back[1] = jnp.zeros((rows, nz), F32)

    def taps(n):
        window = grads[pl.ds(n, 3)].reshape(3 * rows, nz)
        total_ref[...] += mm(window, x_ref[n], NT)

    def spread_back(n):
        terms = mm(wb_ref[...], grads[n + 1])
        back[n + 1] = terms[2 * rows :]
        back[n] += terms[rows : 2 * rows]
        return terms[:rows]

    def backward(n):
        taps(n)
        value = spread_back(n) + back[n - 1]
        for dx in range(3):
            part = value[dx * chans : (dx + 1) * chans]
            if dx == 1:
                part = part + cot_ref[n - 1].astype(F32)
            plane[dx, pl.ds((n - 3) * chans, chans)] = part.astype(BF16)

    taps(0)
    taps(1)
    slot_ref[0] = spread_back(1)
    taps(2)
    slot_ref[1] = spread_back(2) + back[1]
    for n in range(3, cy - 1):
        backward(n)
    taps(cy - 1)
    slot_ref[2] = back[cy - 2]
    slot_ref[3] = back[cy - 1]


def at_slots(part, y, onehot, first):
    found = mm(part, onehot)
    chans = found.shape[0] // len(first)
    total = jnp.zeros((chans, found.shape[1]), F32)
    for n, row in enumerate(first):
        total = total + jnp.where(y == row, found[n * chans : (n + 1) * chans], 0.0)
    return total


def edge_kernel(
    part, parity_ref, pre_ref, total_ref, north_ref, south_ref, x_ref, cot_ref,
    out_ref, grads_ref, keep_ref, give_ref, total, sums,
):
    cy, chans, nz = cot_ref.shape
    rows = 3 * chans
    own = pl.ds(chans, chans)
    last = pl.ds(2 * chans, chans)
    cots = (north_ref[last], cot_ref[0], cot_ref[cy - 1], south_ref[last])
    sides = ((north_ref, 1), (north_ref, 0), (south_ref, 0), (south_ref, 1))
    ends = []
    for n, (ref, at) in enumerate(sides):
        pre = pre_ref[n] + ref[pl.ds(at * chans, chans)].astype(F32)
        ends.append(finish_row(pre, x_ref[0 if n < 2 else cy - 1, own], cots[n]))
    out_ref[0], out_ref[1] = ends[1][0], ends[2][0]
    grads = [stacked(grad) for _, grad in ends]
    for n in range(4):
        grads_ref[n] = grads[n]
    top = mm(jnp.concatenate([grads[0], grads[1]], axis=0), x_ref[0], NT)
    bottom = mm(jnp.concatenate([grads[2], grads[3]], axis=0), x_ref[cy - 1], NT)
    here = [pl.ds(n * rows, rows) for n in range(3)]
    total[here[0]] = total_ref[here[0]] + (top[:rows] + mm(grads[1], x_ref[1], NT))
    total[here[1]] = total_ref[here[1]] + (top[rows:] + bottom[:rows])
    total[here[2]] = total_ref[here[2]] + (bottom[rows:] + mm(grads[2], x_ref[cy - 2], NT))
    full, _, width = keep_ref.shape
    half = 3 * rows // 2
    split = 3 * rows // (2 * part)
    sums[pl.ds(0, split)] = total[:, :width].reshape(split, 2, part, width)
    taps = jnp.concatenate([total[pl.ds(0, half), width:], total[pl.ds(half, half), width:]], axis=1)
    sums[pl.ds(split, full - split)] = taps.reshape(full - split, 2, part, width)
    parity = parity_ref[0]
    keep_ref[...] = sums[:, parity]
    give_ref[...] = sums[:, 1 - parity].astype(BF16)


def slots_kernel(
    ndev, cap, part, full, slot_ref, plane_ref, hot_ref, grads_ref, wb_ref, cot_ref,
    own_cells, west_cells, east_cells, recv_ref, slots_ref, proj_ref,
):
    cy, chans, nz = cot_ref.shape
    rows = 3 * chans
    inner = mm(wb_ref[pl.ds(rows, 2 * rows)], grads_ref[1])
    top = slot_ref[0] + inner[:rows] + mm(wb_ref[pl.ds(2 * rows, rows)], grads_ref[0])
    second = slot_ref[1] + inner[rows:]
    inner = mm(wb_ref[pl.ds(0, 2 * rows)], grads_ref[2])
    third = slot_ref[2] + inner[:rows]
    bottom = slot_ref[3] + inner[rows:] + mm(wb_ref[pl.ds(0, rows)], grads_ref[3])
    at = (0, 1, cy - 2, cy - 1)
    found = []
    for dx, cells_ref in enumerate((west_cells, own_cells, east_cells)):
        parts = [value[dx * chans : (dx + 1) * chans] for value in (top, second, third, bottom)]
        if dx == 1:
            parts = [value + cot_ref[n].astype(F32) for value, n in zip(parts, at)]
        parts = [value.astype(BF16) for value in parts]
        terms = jnp.concatenate([plane_ref[dx], *parts], axis=0)
        y, _ = place(cells_ref, nz)
        found.append(at_slots(terms, y, hot_ref[dx], (*range(2, cy - 2), *at)))
    sides = jnp.concatenate([found[0], found[2]], axis=0).T
    middle = jnp.concatenate([found[1], jnp.zeros_like(found[1])], axis=0).T
    width = recv_ref.shape[1]
    back = [sides.reshape(ndev, cap, width), middle.reshape(ndev, cap, width)]
    slots_ref[...] = jnp.concatenate(back, axis=1).astype(BF16)
    raws = rows_in(recv_ref, ndev, cap)
    proj = sum(mm(found[dx].astype(BF16), raws[dx]) for dx in range(3))
    rest = ndev - full
    pad = jnp.zeros((rest * part - chans, width), F32)
    proj = jnp.concatenate([proj, pad], axis=0).reshape(rest, part, width)
    proj_ref[...] = proj.astype(BF16)


def pair_kernel(keep_ref, got_ref, slots_ref, proj_ref, send_far, sums_send, sems):
    full, part, _ = keep_ref.shape
    ndev, back, _ = slots_ref.shape
    pieces = (
        (slots_ref, send_far.at[:, pl.ds(part, back)]),
        (proj_ref, send_far.at[pl.ds(full, ndev - full), pl.ds(0, part)]),
        (sums_send, send_far.at[pl.ds(0, full), pl.ds(0, part)]),
    )
    copies = [pltpu.make_async_copy(src, dst, sems.at[n]) for n, (src, dst) in enumerate(pieces)]
    copies[0].start()
    copies[1].start()
    sums_send[...] = (keep_ref[...] + got_ref[...].astype(F32)).astype(BF16)
    copies[2].start()
    for copy in copies:
        copy.wait()


def sums_kernel(ngx, ngy, full, cap, recv_ref, index_ref, sums_ref):
    ndev, each, width = recv_ref.shape
    part = each - 2 * cap
    terms = recv_ref[:, pl.ds(0, part)].astype(F32).reshape(ngx // 2, 2, ngy, part, width)
    sums = jnp.sum(terms, axis=(0, 2))
    whole = sums[0] + sums[1]
    high = whole.astype(BF16).astype(F32)
    last = jnp.broadcast_to(index_ref[...], whole.shape) >= full
    sums = [
        jnp.where(last, high, sums[0]).astype(BF16),
        jnp.where(last, whole - high, sums[1]).astype(BF16),
    ]
    for n in range(ndev):
        sums_ref[n] = sums[(n // ngy) % 2]


def rows_kernel(
    ngx, ngy, cap, chans, recv_ref, counts_ref, proj_t_ref, inner_ref, ends_ref, rows_ref, out_ref
):
    ndev = ngx * ngy
    nrows = rows_ref.shape[0]
    width = recv_ref.shape[2]
    slots = ndev * cap
    share = recv_ref.shape[1] - 2 * cap
    arrived = recv_ref[:, pl.ds(share, 2 * cap)].astype(F32)
    sides = arrived[:, :cap].reshape(ngx, ngy, cap, width)
    left = lax.broadcasted_iota(I32, sides.shape, 3) < chans
    sides = jnp.where(left, rolled(sides, 1, 0), rolled(sides, -1, 0)).reshape(slots, width)
    middle = arrived[:, cap:].reshape(slots, width)
    counts = counts_ref[...].astype(F32)
    place = lax.broadcasted_iota(I32, (nrows, ndev), 0).astype(F32)
    lane = lax.broadcasted_iota(I32, (ndev, ndev), 1)
    upto = lax.broadcasted_iota(I32, (ndev, ndev), 0) <= lane
    ends = mm(counts.astype(BF16), jnp.where(upto, 1.0, 0.0).astype(BF16))
    before = ends <= place
    owner = jnp.sum(jnp.where(before, 1.0, 0.0), axis=1, keepdims=True)
    start = jnp.sum(jnp.where(before, counts, 0.0), axis=1, keepdims=True)
    slot = owner * cap + place[:, :1] - start
    onehot = jnp.where(
        lax.broadcasted_iota(I32, (nrows, slots), 1).astype(F32) == slot, 1.0, 0.0
    ).astype(BF16)
    proj_t = proj_t_ref[...]
    both = jnp.concatenate([proj_t, proj_t], axis=0)
    sides = mm(onehot, sides.astype(BF16)).astype(BF16)
    middle = mm(onehot, middle.astype(BF16)).astype(BF16)
    rows_ref[...] = mm(sides, both) + mm(middle, both)
    cy = inner_ref.shape[0]
    field = jnp.concatenate([ends_ref[:1], inner_ref[1 : cy - 1], ends_ref[1:]], axis=0)
    out_ref[...] = jnp.swapaxes(field, 0, 1)


def finish_kernel(conv_scale, proj_scale, parity_ref, mine_ref, other_ref, conv_ref, proj_ref, both):
    ndev, part, width = mine_ref.shape
    parity = parity_ref[0]
    both[:, parity] = mine_ref[...]
    both[:, 1 - parity] = other_ref[...]
    sums = both[...].astype(F32).reshape(ndev * 2 * part, width)
    taps, chans, _ = conv_ref.shape
    rows = 9 * chans
    half = rows // 2
    packed = sums[rows : rows + half]
    column = jnp.concatenate([packed[:, :chans], packed[:, chans:]], axis=0)
    for b in range(3):
        for dz in range(3):
            first = (b * 3 + dz) * chans
            block = sums[first : first + chans]
            k = (2 - b) * 3 + dz
            conv_ref[k] = block[:, :chans] * conv_scale
            conv_ref[9 + k] = block[:, chans:] * conv_scale
            conv_ref[18 + k] = column[first : first + chans] * conv_scale
    terms = sums[rows + half : rows + half + 2 * chans].reshape(chans // part, 2, part, width)
    proj_ref[...] = jnp.sum(terms, axis=1).reshape(chans, width) * proj_scale


def local(particles, send_counts, cell_lists, base_field, proj_weight, conv_weight, cotangent):
    ngx, ngy = lax.axis_size("gx"), lax.axis_size("gy")
    ndev = ngx * ngy
    nrows, feats = particles.shape
    chans, cx, cy, nz = base_field.shape
    slots = cell_lists.shape[1]
    cap = slots // ndev
    count = cx * cy * nz
    assert cx == 1 and feats == 2 * chans
    proj_t = proj_weight.T
    move = functools.partial(send, ngx=ngx, ngy=ngy)
    rows = 3 * chans
    one = 2 * rows * rows * nz

    base = base_field.reshape(chans, cy, nz)
    west, east = move(base_field, 1, 0), move(base_field, -1, 0)
    planes = (base, west.reshape(base.shape), east.reshape(base.shape))
    lists = (cell_lists, move(cell_lists, 1, 0), move(cell_lists, -1, 0))
    (payload,) = call(
        functools.partial(first_kernel, ngx, ngy, cap),
        [shape((ndev * 3 * cap, feats), BF16)],
        (particles, send_counts),
        2 * slots * nrows * feats,
        (
            pltpu.VMEM(particles.shape, BF16),
            pltpu.VMEM(send_counts.shape, I32),
            pltpu.SemaphoreType.DMA((2,)),
        ),
        far=range(2),
        limit=ALL,
    )
    recv = exchange(payload, ndev)

    cot = cotangent[:, 0].transpose(1, 0, 2)
    taps = conv_weight.reshape(3, 3, 3, chans, chans)
    wf = taps.transpose(1, 2, 3, 0, 4).reshape(9 * chans, rows)
    wb = taps.transpose(1, 0, 4, 2, 3).reshape(9 * chans, rows)

    first, last, values, hots = call(
        functools.partial(outer_kernel, ndev, cap),
        [shape((rows, nz), BF16)] * 2
        + [shape((3, chans, slots), BF16), shape((3, nz, slots), BF16)],
        (recv, *planes, *lists, proj_t, cot, wf),
        4 * one,
        (pltpu.VMEM((4 * chans, slots), BF16), pltpu.VMEM((4, rows, nz), BF16)),
    )
    south, north = move(first, 0, -1), move(last, 0, 1)
    x_all, out_rows, total, pre_edge, slot_edge, plane = call(
        conv_kernel,
        [
            shape((cy, rows, nz), BF16),
            shape((cy, chans, nz), BF16),
            shape((9 * chans, rows), F32),
            shape((4, chans, nz), F32),
            shape((4, rows, nz), F32),
            shape((3, (cy - 4) * chans, nz), BF16),
        ],
        (values, hots, *planes, *lists, cot, wf, wb),
        3 * cy * 3 * one,
        (
            pltpu.VMEM((cy + 1, rows, nz), F32),
            pltpu.VMEM((cy + 2, rows, nz), BF16),
            pltpu.VMEM((cy, rows, nz), F32),
            pltpu.VMEM((cy * chans, slots), BF16),
        ),
    )
    grad_rows = 27 * chans * chans // feats
    part = -(-(grad_rows + 2 * chans) // (32 * ndev)) * 16
    full = grad_rows // (2 * part)
    assert ngx % 2 == 0 and full * 2 * part == grad_rows
    row = lax.axis_index("gx")
    parity = (row % 2).astype(I32).reshape(1)
    out_edge, grads, keep, give = call(
        functools.partial(edge_kernel, part),
        [
            shape((2, chans, nz), BF16),
            shape((4, rows, nz), BF16),
            shape((full, part, feats), F32),
            shape((full, part, feats), BF16),
        ],
        (parity, pre_edge, total, north, south, x_all, cot),
        6 * one,
        (pltpu.VMEM((9 * chans, rows), F32), pltpu.VMEM((full, 2, part, feats), F32)),
        scalar=(0,),
    )
    got = swap(give)
    back, proj = call(
        functools.partial(slots_kernel, ndev, cap, part, full),
        [shape((ndev, 2 * cap, feats), BF16), shape((ndev - full, part, feats), BF16)],
        (slot_edge, plane, hots, grads, wb, cot, *lists, recv),
        6 * one,
    )
    (payload,) = call(
        pair_kernel,
        [shape((ndev, part + 2 * cap, feats), BF16)],
        (keep, got, back, proj),
        1000,
        (pltpu.VMEM((full, part, feats), BF16), pltpu.SemaphoreType.DMA((3,))),
        far_out=(0,),
    )
    (payload,) = call(same_kernel, [payload], (payload,), 0, far=(0,), far_out=(0,), aliases={0: 0})
    recv = exchange(payload.reshape(-1, feats), ndev).reshape(payload.shape)
    index = (row * ngy + lax.axis_index("gy")).astype(I32).reshape(1, 1)
    (sums,) = call(
        functools.partial(sums_kernel, ngx, ngy, full, cap),
        [shape((ndev, part, feats), BF16)],
        (recv, index),
        1000,
    )
    row_grads, out_field = call(
        functools.partial(rows_kernel, ngx, ngy, cap, chans),
        [shape((nrows, feats), F32), shape((chans, cy, nz), BF16)],
        (recv, send_counts, proj_t, out_rows, out_edge),
        2 * nrows * slots * chans,
    )
    mine = exchange(sums.reshape(-1, feats), ndev).reshape(sums.shape)
    mine, row_grads, out_field = lax.optimization_barrier((mine, row_grads, out_field))
    other = swap(mine)
    conv_grad, proj_grad = call(
        functools.partial(
            finish_kernel, 1.0 / math.sqrt(count * ndev), 1.0 / math.sqrt(nrows * ndev)
        ),
        [shape((27, chans, chans), F32), shape((chans, feats), F32)],
        (parity, mine, other),
        1000,
        (pltpu.VMEM((ndev, 2, part, feats), BF16),),
        scalar=(0,),
    )
    return (out_field[:, None], row_grads, conv_grad, proj_grad.T)


def solution(mesh):
    in_specs = (
        P(("gx", "gy"), None),
        P(("gx", "gy"), None),
        P(("gx", "gy"), None),
        P(None, "gx", "gy", None),
        P(),
        P(),
        P(None, "gx", "gy", None),
    )
    out_specs = (P(None, "gx", "gy", None), P(("gx", "gy"), None), P(), P())
    return jax.shard_map(local, mesh=mesh, in_specs=in_specs, out_specs=out_specs, check_vma=False)
```

```python
import functools
import math

import jax
import jax.numpy as jnp
from jax import lax
from jax.experimental import pallas as pl
from jax.experimental.pallas import tpu as pltpu
from jax.sharding import PartitionSpec as P

AXES = ("gx", "gy")
F32, BF16, I32 = jnp.float32, jnp.bfloat16, jnp.int32
LIMIT = 40 * 1024 * 1024
NT = (((1,), (1,)), ((), ()))
NN = (((1,), (0,)), ((), ()))


def mm(a, b, dims=NN):
    return lax.dot_general(a, b, dims, preferred_element_type=F32)


def call(kernel, outs, args, flops, scratch=(), far=(), far_out=(), aliases=None, scalar=()):
    traffic = sum(math.prod(a.shape) * a.dtype.itemsize for a in (*args, *outs))
    near = pl.BlockSpec(memory_space=pltpu.VMEM)
    there = pl.BlockSpec(memory_space=pltpu.HBM)
    return pl.pallas_call(
        kernel,
        out_shape=[jax.ShapeDtypeStruct(o.shape, o.dtype) for o in outs],
        in_specs=[
            pl.BlockSpec(memory_space=pltpu.SMEM) if n in scalar else there if n in far else near
            for n in range(len(args))
        ],
        out_specs=[there if n in far_out else near for n in range(len(outs))],
        scratch_shapes=list(scratch),
        input_output_aliases=aliases or {},
        compiler_params=pltpu.CompilerParams(vmem_limit_bytes=LIMIT),
        cost_estimate=pl.CostEstimate(flops=flops, bytes_accessed=traffic, transcendentals=0),
    )(*args)


def shape(dims, dtype):
    return jax.ShapeDtypeStruct(dims, dtype)


def send(block, di, dj, ngx, ngy):
    pairs = []
    for i in range(ngx):
        for j in range(ngy):
            pairs.append((i * ngy + j, ((i + di) % ngx) * ngy + (j + dj) % ngy))
    return lax.ppermute(block, AXES, pairs)


def swap(block):
    return lax.ppermute(block, "gx", [(i, i ^ 1) for i in range(lax.axis_size("gx"))])


def exchange(payload, ndev):
    rows, width = payload.shape
    moved = lax.all_to_all(
        payload.reshape(ndev, rows // ndev, width), AXES, split_axis=0, concat_axis=0, tiled=True
    )
    return moved.reshape(rows, width)


def rolled(x, di, dj):
    for axis, shift in ((0, di), (1, dj)):
        if shift == 1:
            head, tail = lax.slice_in_dim(x, 1, None, axis=axis), lax.slice_in_dim(x, 0, 1, axis=axis)
            x = jnp.concatenate([head, tail], axis=axis)
        elif shift == -1:
            count = x.shape[axis]
            head = lax.slice_in_dim(x, count - 1, count, axis=axis)
            x = jnp.concatenate([head, lax.slice_in_dim(x, 0, count - 1, axis=axis)], axis=axis)
    return x


def picked_depth(z, nz):
    depth = lax.broadcasted_iota(I32, (nz, z.shape[1]), 0)
    return jnp.where(depth == z, 1.0, 0.0).astype(BF16)


def rows_in(recv_ref, ndev, cap):
    width = recv_ref.shape[1]
    arrived = recv_ref[...].astype(F32).reshape(ndev, 3, cap, width)
    return [arrived[:, n].reshape(ndev * cap, width).astype(BF16) for n in range(3)]


def stacked(grad):
    nz = grad.shape[1]
    wide = grad.astype(F32)
    return jnp.concatenate(
        [pltpu.roll(wide, nz - 1, 1), wide, pltpu.roll(wide, 1, 1)], axis=0
    ).astype(BF16)


def over_depth(acc):
    chans, nz = acc.shape[0] // 3, acc.shape[1]
    total = acc[chans : 2 * chans] + pltpu.roll(acc[:chans], 1, 1)
    return total + pltpu.roll(acc[2 * chans :], nz - 1, 1)


def finish_row(pre, field, cot):
    sig = jax.nn.sigmoid(pre)
    out = field.astype(F32) + pre * sig
    grad = cot.astype(F32) * sig * (1.0 + pre * (1.0 - sig))
    return out.astype(BF16), grad.astype(BF16)


def same_kernel(in_ref, out_ref):
    pass


def pick(ngx, ngy, cap, counts_ref, rows_ref, out_ref):
    ndev = ngx * ngy
    nrows, feats = rows_ref.shape
    slots = ndev * cap
    counts = counts_ref[...].astype(F32)
    owner = lax.broadcasted_iota(I32, (ndev, cap, ndev), 0).reshape(slots, ndev)
    lane = lax.broadcasted_iota(I32, (slots, ndev), 1)
    start = jnp.sum(jnp.where(lane < owner, counts, 0.0), axis=1, keepdims=True)
    held = jnp.sum(jnp.where(lane == owner, counts, 0.0), axis=1, keepdims=True)
    place = lax.broadcasted_iota(I32, (ndev, cap, nrows), 1).reshape(slots, nrows).astype(F32)
    row = lax.broadcasted_iota(I32, (slots, nrows), 1).astype(F32)
    onehot = jnp.where((row == place + start) & (place < held), 1.0, 0.0).astype(BF16)
    raw = mm(onehot, rows_ref[...]).reshape(ngx, ngy, cap, feats)
    parts = [rolled(raw, dx, 0).reshape(ndev, cap, feats) for dx in (-1, 0, 1)]
    out_ref[...] = jnp.stack(parts, axis=1).reshape(out_ref.shape).astype(BF16)


def painted_rows(values, y, onehot, ns, masked):
    chans = values.shape[0]
    for n, row in enumerate(ns):
        masked[pl.ds(n * chans, chans)] = values * jnp.where(y == row, 1.0, 0.0).astype(BF16)
    return mm(masked[pl.ds(0, len(ns) * chans)], onehot, NT)


def add_to_rows(near, far, cot, back, out_ref):
    chans = cot.shape[0]
    rows = 3 * chans
    at, over = (rows, 0) if back else (0, rows)
    out_ref[pl.ds(0, chans)] = over_depth(near[at : at + rows]).astype(BF16)
    out_ref[pl.ds(chans, chans)] = over_depth(near[over : over + rows] + far).astype(BF16)
    out_ref[pl.ds(2 * chans, chans)] = cot


def outer_kernel(
    ndev, cap, recv_ref, own_ref, west_ref, east_ref, own_cells, west_cells, east_cells,
    proj_t_ref, cot_ref, wf_ref, first_ref, last_ref, values_ref, hot_ref, masked, field,
):
    chans, cy, nz = own_ref.shape
    rows = 3 * chans
    raws = rows_in(recv_ref, ndev, cap)
    ns = (0, 1, cy - 2, cy - 1)
    planes = ((west_ref, west_cells), (own_ref, own_cells), (east_ref, east_cells))
    for dx, (ref, cells_ref) in enumerate(planes):
        values = mm(proj_t_ref[...], raws[dx], NT).astype(BF16)
        y, z = place(cells_ref, nz)
        onehot = picked_depth(z, nz)
        values_ref[dx] = values
        hot_ref[dx] = onehot
        painted = painted_rows(values, y, onehot, ns, masked)
        base = turned(ref)
        for n, row in enumerate(ns):
            part = painted[n * chans : (n + 1) * chans]
            field[n, pl.ds(dx * chans, chans)] = (base[row] + part).astype(BF16)
    near = mm(wf_ref[pl.ds(0, 2 * rows)], field[3])
    add_to_rows(near, mm(wf_ref[pl.ds(0, rows)], field[2]), cot_ref[cy - 1], False, last_ref)
    near = mm(wf_ref[pl.ds(rows, 2 * rows)], field[0])
    add_to_rows(near, mm(wf_ref[pl.ds(2 * rows, rows)], field[1]), cot_ref[0], True, first_ref)


def place(cells_ref, nz):
    cells = cells_ref[...]
    return cells // nz, cells % nz


def turned(ref):
    return jnp.swapaxes(ref[...], 0, 1).astype(F32)


def conv_kernel(
    values_ref, hot_ref, own_ref, west_ref, east_ref, own_cells, west_cells, east_cells,
    cot_ref, wf_ref, wb_ref,
    x_ref, out_ref, total_ref, pre_ref, slot_ref, plane, acc, grads, back, masked,
):
    cy, chans, nz = cot_ref.shape
    rows = 3 * chans
    planes = ((west_ref, west_cells), (own_ref, own_cells), (east_ref, east_cells))
    for dx, (ref, cells_ref) in enumerate(planes):
        y, _ = place(cells_ref, nz)
        painted = painted_rows(values_ref[dx], y, hot_ref[dx], range(cy), masked)
        field = turned(ref) + painted.reshape(cy, chans, nz)
        x_ref[:, pl.ds(dx * chans, chans)] = field.astype(BF16)
    own = pl.ds(chans, chans)
    zeros = jnp.zeros((rows, nz), BF16)
    for t in (0, 1, cy, cy + 1):
        grads[t] = zeros
    out_ref[0] = zeros[:chans]
    out_ref[cy - 1] = zeros[:chans]
    acc[0] = jnp.zeros((rows, nz), F32)

    def spread(n):
        terms = mm(wf_ref[...], x_ref[n])
        acc[n + 1] = terms[:rows]
        acc[n] += terms[rows : 2 * rows]
        return terms[2 * rows :]

    pre_ref[0] = over_depth(spread(0))
    pre_ref[1] = over_depth(acc[0] + spread(1))

    def forward(n):
        done = spread(n) + acc[n - 1]
        y = n - 1
        out, grad = finish_row(over_depth(done), x_ref[y, own], cot_ref[y])
        out_ref[y] = out
        grads[y + 1] = stacked(grad)

    for n in range(2, cy):
        forward(n)
    pre_ref[2] = over_depth(acc[cy - 1])
    pre_ref[3] = over_depth(acc[cy])
    total_ref[...] = jnp.zeros_like(total_ref)
    back[0] = jnp.zeros((rows, nz), F32)
    back[1] = jnp.zeros((rows, nz), F32)

    def taps(n):
        window = grads[pl.ds(n, 3)].reshape(3 * rows, nz)
        total_ref[...] += mm(window, x_ref[n], NT)

    def spread_back(n):
        terms = mm(wb_ref[...], grads[n + 1])
        back[n + 1] = terms[2 * rows :]
        back[n] += terms[rows : 2 * rows]
        return terms[:rows]

    def backward(n):
        taps(n)
        value = spread_back(n) + back[n - 1]
        for dx in range(3):
            part = value[dx * chans : (dx + 1) * chans]
            if dx == 1:
                part = part + cot_ref[n - 1].astype(F32)
            plane[dx, pl.ds((n - 3) * chans, chans)] = part.astype(BF16)

    taps(0)
    taps(1)
    slot_ref[0] = spread_back(1)
    taps(2)
    slot_ref[1] = spread_back(2) + back[1]
    for n in range(3, cy - 1):
        backward(n)
    taps(cy - 1)
    slot_ref[2] = back[cy - 2]
    slot_ref[3] = back[cy - 1]


def at_slots(part, y, onehot, first):
    found = mm(part, onehot)
    chans = found.shape[0] // len(first)
    total = jnp.zeros((chans, found.shape[1]), F32)
    for n, row in enumerate(first):
        total = total + jnp.where(y == row, found[n * chans : (n + 1) * chans], 0.0)
    return total


def edge_kernel(
    part, parity_ref, pre_ref, total_ref, north_ref, south_ref, x_ref, cot_ref,
    out_ref, grads_ref, keep_ref, give_ref, total, sums,
):
    cy, chans, nz = cot_ref.shape
    rows = 3 * chans
    own = pl.ds(chans, chans)
    last = pl.ds(2 * chans, chans)
    cots = (north_ref[last], cot_ref[0], cot_ref[cy - 1], south_ref[last])
    sides = ((north_ref, 1), (north_ref, 0), (south_ref, 0), (south_ref, 1))
    ends = []
    for n, (ref, at) in enumerate(sides):
        pre = pre_ref[n] + ref[pl.ds(at * chans, chans)].astype(F32)
        ends.append(finish_row(pre, x_ref[0 if n < 2 else cy - 1, own], cots[n]))
    out_ref[0], out_ref[1] = ends[1][0], ends[2][0]
    grads = [stacked(grad) for _, grad in ends]
    for n in range(4):
        grads_ref[n] = grads[n]
    top = mm(jnp.concatenate([grads[0], grads[1]], axis=0), x_ref[0], NT)
    bottom = mm(jnp.concatenate([grads[2], grads[3]], axis=0), x_ref[cy - 1], NT)
    here = [pl.ds(n * rows, rows) for n in range(3)]
    total[here[0]] = total_ref[here[0]] + (top[:rows] + mm(grads[1], x_ref[1], NT))
    total[here[1]] = total_ref[here[1]] + (top[rows:] + bottom[:rows])
    total[here[2]] = total_ref[here[2]] + (bottom[rows:] + mm(grads[2], x_ref[cy - 2], NT))
    full, _, width = keep_ref.shape
    half = 3 * rows // 2
    split = 3 * rows // (2 * part)
    sums[pl.ds(0, split)] = total[:, :width].reshape(split, 2, part, width)
    taps = jnp.concatenate([total[pl.ds(0, half), width:], total[pl.ds(half, half), width:]], axis=1)
    sums[pl.ds(split, full - split)] = taps.reshape(full - split, 2, part, width)
    parity = parity_ref[0]
    keep_ref[...] = sums[:, parity]
    give_ref[...] = sums[:, 1 - parity].astype(BF16)


def slots_kernel(
    ndev, cap, part, full, slot_ref, plane_ref, hot_ref, grads_ref, wb_ref, cot_ref,
    own_cells, west_cells, east_cells, recv_ref, slots_ref, proj_ref,
):
    cy, chans, nz = cot_ref.shape
    rows = 3 * chans
    inner = mm(wb_ref[pl.ds(rows, 2 * rows)], grads_ref[1])
    top = slot_ref[0] + inner[:rows] + mm(wb_ref[pl.ds(2 * rows, rows)], grads_ref[0])
    second = slot_ref[1] + inner[rows:]
    inner = mm(wb_ref[pl.ds(0, 2 * rows)], grads_ref[2])
    third = slot_ref[2] + inner[:rows]
    bottom = slot_ref[3] + inner[rows:] + mm(wb_ref[pl.ds(0, rows)], grads_ref[3])
    at = (0, 1, cy - 2, cy - 1)
    found = []
    for dx, cells_ref in enumerate((west_cells, own_cells, east_cells)):
        parts = [value[dx * chans : (dx + 1) * chans] for value in (top, second, third, bottom)]
        if dx == 1:
            parts = [value + cot_ref[n].astype(F32) for value, n in zip(parts, at)]
        parts = [value.astype(BF16) for value in parts]
        terms = jnp.concatenate([plane_ref[dx], *parts], axis=0)
        y, _ = place(cells_ref, nz)
        found.append(at_slots(terms, y, hot_ref[dx], (*range(2, cy - 2), *at)))
    sides = jnp.concatenate([found[0], found[2]], axis=0).T
    middle = jnp.concatenate([found[1], jnp.zeros_like(found[1])], axis=0).T
    width = recv_ref.shape[1]
    back = [sides.reshape(ndev, cap, width), middle.reshape(ndev, cap, width)]
    slots_ref[...] = jnp.concatenate(back, axis=1).astype(BF16)
    raws = rows_in(recv_ref, ndev, cap)
    proj = sum(mm(found[dx].astype(BF16), raws[dx]) for dx in range(3))
    rest = ndev - full
    pad = jnp.zeros((rest * part - chans, width), F32)
    proj = jnp.concatenate([proj, pad], axis=0).reshape(rest, part, width)
    proj_ref[...] = proj.astype(BF16)


def pair_kernel(keep_ref, got_ref, slots_ref, proj_ref, send_far, sums_send, sems):
    full, part, _ = keep_ref.shape
    ndev, back, _ = slots_ref.shape
    pieces = (
        (slots_ref, send_far.at[:, pl.ds(part, back)]),
        (proj_ref, send_far.at[pl.ds(full, ndev - full), pl.ds(0, part)]),
        (sums_send, send_far.at[pl.ds(0, full), pl.ds(0, part)]),
    )
    copies = [pltpu.make_async_copy(src, dst, sems.at[n]) for n, (src, dst) in enumerate(pieces)]
    copies[0].start()
    copies[1].start()
    sums_send[...] = (keep_ref[...] + got_ref[...].astype(F32)).astype(BF16)
    copies[2].start()
    for copy in copies:
        copy.wait()


def sums_kernel(ngx, ngy, full, cap, recv_ref, index_ref, sums_ref):
    ndev, each, width = recv_ref.shape
    part = each - 2 * cap
    terms = recv_ref[:, pl.ds(0, part)].astype(F32).reshape(ngx // 2, 2, ngy, part, width)
    sums = jnp.sum(terms, axis=(0, 2))
    whole = sums[0] + sums[1]
    high = whole.astype(BF16).astype(F32)
    last = jnp.broadcast_to(index_ref[...], whole.shape) >= full
    sums = [
        jnp.where(last, high, sums[0]).astype(BF16),
        jnp.where(last, whole - high, sums[1]).astype(BF16),
    ]
    for n in range(ndev):
        sums_ref[n] = sums[(n // ngy) % 2]


def rows_kernel(
    ngx, ngy, cap, chans, recv_ref, counts_ref, proj_t_ref, inner_ref, ends_ref, rows_ref, out_ref
):
    ndev = ngx * ngy
    nrows = rows_ref.shape[0]
    width = recv_ref.shape[2]
    slots = ndev * cap
    share = recv_ref.shape[1] - 2 * cap
    arrived = recv_ref[:, pl.ds(share, 2 * cap)].astype(F32)
    sides = arrived[:, :cap].reshape(ngx, ngy, cap, width)
    left = lax.broadcasted_iota(I32, sides.shape, 3) < chans
    sides = jnp.where(left, rolled(sides, 1, 0), rolled(sides, -1, 0)).reshape(slots, width)
    middle = arrived[:, cap:].reshape(slots, width)
    counts = counts_ref[...].astype(F32)
    place = lax.broadcasted_iota(I32, (nrows, ndev), 0).astype(F32)
    lane = lax.broadcasted_iota(I32, (ndev, ndev), 1)
    upto = lax.broadcasted_iota(I32, (ndev, ndev), 0) <= lane
    ends = mm(counts.astype(BF16), jnp.where(upto, 1.0, 0.0).astype(BF16))
    before = ends <= place
    owner = jnp.sum(jnp.where(before, 1.0, 0.0), axis=1, keepdims=True)
    start = jnp.sum(jnp.where(before, counts, 0.0), axis=1, keepdims=True)
    slot = owner * cap + place[:, :1] - start
    onehot = jnp.where(
        lax.broadcasted_iota(I32, (nrows, slots), 1).astype(F32) == slot, 1.0, 0.0
    ).astype(BF16)
    proj_t = proj_t_ref[...]
    both = jnp.concatenate([proj_t, proj_t], axis=0)
    sides = mm(onehot, sides.astype(BF16)).astype(BF16)
    middle = mm(onehot, middle.astype(BF16)).astype(BF16)
    rows_ref[...] = mm(sides, both) + mm(middle, both)
    cy = inner_ref.shape[0]
    field = jnp.concatenate([ends_ref[:1], inner_ref[1 : cy - 1], ends_ref[1:]], axis=0)
    out_ref[...] = jnp.swapaxes(field, 0, 1)


def finish_kernel(conv_scale, proj_scale, parity_ref, mine_ref, other_ref, conv_ref, proj_ref, both):
    ndev, part, width = mine_ref.shape
    parity = parity_ref[0]
    both[:, parity] = mine_ref[...]
    both[:, 1 - parity] = other_ref[...]
    sums = both[...].astype(F32).reshape(ndev * 2 * part, width)
    taps, chans, _ = conv_ref.shape
    rows = 9 * chans
    half = rows // 2
    packed = sums[rows : rows + half]
    column = jnp.concatenate([packed[:, :chans], packed[:, chans:]], axis=0)
    for b in range(3):
        for dz in range(3):
            first = (b * 3 + dz) * chans
            block = sums[first : first + chans]
            k = (2 - b) * 3 + dz
            conv_ref[k] = block[:, :chans] * conv_scale
            conv_ref[9 + k] = block[:, chans:] * conv_scale
            conv_ref[18 + k] = column[first : first + chans] * conv_scale
    terms = sums[rows + half : rows + half + 2 * chans].reshape(chans // part, 2, part, width)
    proj_ref[...] = jnp.sum(terms, axis=1).reshape(chans, width) * proj_scale


def local(particles, send_counts, cell_lists, base_field, proj_weight, conv_weight, cotangent):
    ngx, ngy = lax.axis_size("gx"), lax.axis_size("gy")
    ndev = ngx * ngy
    nrows, feats = particles.shape
    chans, cx, cy, nz = base_field.shape
    slots = cell_lists.shape[1]
    cap = slots // ndev
    count = cx * cy * nz
    assert cx == 1 and feats == 2 * chans
    proj_t = proj_weight.T
    move = functools.partial(send, ngx=ngx, ngy=ngy)
    rows = 3 * chans
    one = 2 * rows * rows * nz

    base = base_field.reshape(chans, cy, nz)
    west, east = move(base_field, 1, 0), move(base_field, -1, 0)
    planes = (base, west.reshape(base.shape), east.reshape(base.shape))
    lists = (cell_lists, move(cell_lists, 1, 0), move(cell_lists, -1, 0))
    (payload,) = call(
        functools.partial(pick, ngx, ngy, cap),
        [shape((ndev * 3 * cap, feats), BF16)],
        (send_counts, particles),
        2 * slots * nrows * feats,
    )
    recv = exchange(payload, ndev)

    cot = cotangent[:, 0].transpose(1, 0, 2)
    taps = conv_weight.reshape(3, 3, 3, chans, chans)
    wf = taps.transpose(1, 2, 3, 0, 4).reshape(9 * chans, rows)
    wb = taps.transpose(1, 0, 4, 2, 3).reshape(9 * chans, rows)

    first, last, values, hots = call(
        functools.partial(outer_kernel, ndev, cap),
        [shape((rows, nz), BF16)] * 2
        + [shape((3, chans, slots), BF16), shape((3, nz, slots), BF16)],
        (recv, *planes, *lists, proj_t, cot, wf),
        4 * one,
        (pltpu.VMEM((4 * chans, slots), BF16), pltpu.VMEM((4, rows, nz), BF16)),
    )
    south, north = move(first, 0, -1), move(last, 0, 1)
    x_all, out_rows, total, pre_edge, slot_edge, plane = call(
        conv_kernel,
        [
            shape((cy, rows, nz), BF16),
            shape((cy, chans, nz), BF16),
            shape((9 * chans, rows), F32),
            shape((4, chans, nz), F32),
            shape((4, rows, nz), F32),
            shape((3, (cy - 4) * chans, nz), BF16),
        ],
        (values, hots, *planes, *lists, cot, wf, wb),
        3 * cy * 3 * one,
        (
            pltpu.VMEM((cy + 1, rows, nz), F32),
            pltpu.VMEM((cy + 2, rows, nz), BF16),
            pltpu.VMEM((cy, rows, nz), F32),
            pltpu.VMEM((cy * chans, slots), BF16),
        ),
    )
    grad_rows = 27 * chans * chans // feats
    part = -(-(grad_rows + 2 * chans) // (32 * ndev)) * 16
    full = grad_rows // (2 * part)
    assert ngx % 2 == 0 and full * 2 * part == grad_rows
    row = lax.axis_index("gx")
    parity = (row % 2).astype(I32).reshape(1)
    out_edge, grads, keep, give = call(
        functools.partial(edge_kernel, part),
        [
            shape((2, chans, nz), BF16),
            shape((4, rows, nz), BF16),
            shape((full, part, feats), F32),
            shape((full, part, feats), BF16),
        ],
        (parity, pre_edge, total, north, south, x_all, cot),
        6 * one,
        (pltpu.VMEM((9 * chans, rows), F32), pltpu.VMEM((full, 2, part, feats), F32)),
        scalar=(0,),
    )
    got = swap(give)
    back, proj = call(
        functools.partial(slots_kernel, ndev, cap, part, full),
        [shape((ndev, 2 * cap, feats), BF16), shape((ndev - full, part, feats), BF16)],
        (slot_edge, plane, hots, grads, wb, cot, *lists, recv),
        6 * one,
    )
    (payload,) = call(
        pair_kernel,
        [shape((ndev, part + 2 * cap, feats), BF16)],
        (keep, got, back, proj),
        1000,
        (pltpu.VMEM((full, part, feats), BF16), pltpu.SemaphoreType.DMA((3,))),
        far_out=(0,),
    )
    (payload,) = call(same_kernel, [payload], (payload,), 0, far=(0,), far_out=(0,), aliases={0: 0})
    recv = exchange(payload.reshape(-1, feats), ndev).reshape(payload.shape)
    index = (row * ngy + lax.axis_index("gy")).astype(I32).reshape(1, 1)
    (sums,) = call(
        functools.partial(sums_kernel, ngx, ngy, full, cap),
        [shape((ndev, part, feats), BF16)],
        (recv, index),
        1000,
    )
    row_grads, out_field = call(
        functools.partial(rows_kernel, ngx, ngy, cap, chans),
        [shape((nrows, feats), F32), shape((chans, cy, nz), BF16)],
        (recv, send_counts, proj_t, out_rows, out_edge),
        2 * nrows * slots * chans,
    )
    mine = exchange(sums.reshape(-1, feats), ndev).reshape(sums.shape)
    mine, row_grads, out_field = lax.optimization_barrier((mine, row_grads, out_field))
    other = swap(mine)
    conv_grad, proj_grad = call(
        functools.partial(
            finish_kernel, 1.0 / math.sqrt(count * ndev), 1.0 / math.sqrt(nrows * ndev)
        ),
        [shape((27, chans, chans), F32), shape((chans, feats), F32)],
        (parity, mine, other),
        1000,
        (pltpu.VMEM((ndev, 2, part, feats), BF16),),
        scalar=(0,),
    )
    return (out_field[:, None], row_grads, conv_grad, proj_grad.T)


def solution(mesh):
    in_specs = (
        P(("gx", "gy"), None),
        P(("gx", "gy"), None),
        P(("gx", "gy"), None),
        P(None, "gx", "gy", None),
        P(),
        P(),
        P(None, "gx", "gy", None),
    )
    out_specs = (P(None, "gx", "gy", None), P(("gx", "gy"), None), P(), P())
    return jax.shard_map(local, mesh=mesh, in_specs=in_specs, out_specs=out_specs, check_vma=False)
```

```python
import functools
import math

import jax
import jax.numpy as jnp
from jax import lax
from jax.experimental import pallas as pl
from jax.experimental.pallas import tpu as pltpu
from jax.sharding import PartitionSpec as P

AXES = ("gx", "gy")
F32, BF16, I32 = jnp.float32, jnp.bfloat16, jnp.int32
LIMIT = 40 * 1024 * 1024
ALL = 60 * 1024 * 1024
NT = (((1,), (1,)), ((), ()))
NN = (((1,), (0,)), ((), ()))


def mm(a, b, dims=NN):
    return lax.dot_general(a, b, dims, preferred_element_type=F32)


def call(kernel, outs, args, flops, scratch=(), far=(), far_out=(), aliases=None, limit=LIMIT, scalar=()):
    traffic = sum(math.prod(a.shape) * a.dtype.itemsize for a in (*args, *outs))
    near = pl.BlockSpec(memory_space=pltpu.VMEM)
    there = pl.BlockSpec(memory_space=pltpu.HBM)
    return pl.pallas_call(
        kernel,
        out_shape=[jax.ShapeDtypeStruct(o.shape, o.dtype) for o in outs],
        in_specs=[
            pl.BlockSpec(memory_space=pltpu.SMEM) if n in scalar else there if n in far else near
            for n in range(len(args))
        ],
        out_specs=[there if n in far_out else near for n in range(len(outs))],
        scratch_shapes=list(scratch),
        input_output_aliases=aliases or {},
        compiler_params=pltpu.CompilerParams(vmem_limit_bytes=limit),
        cost_estimate=pl.CostEstimate(flops=flops, bytes_accessed=traffic, transcendentals=0),
    )(*args)


def shape(dims, dtype):
    return jax.ShapeDtypeStruct(dims, dtype)


def send(block, di, dj, ngx, ngy):
    pairs = []
    for i in range(ngx):
        for j in range(ngy):
            pairs.append((i * ngy + j, ((i + di) % ngx) * ngy + (j + dj) % ngy))
    return lax.ppermute(block, AXES, pairs)


def swap(block):
    return lax.ppermute(block, "gx", [(i, i ^ 1) for i in range(lax.axis_size("gx"))])


def exchange(payload, ndev):
    rows, width = payload.shape
    moved = lax.all_to_all(
        payload.reshape(ndev, rows // ndev, width), AXES, split_axis=0, concat_axis=0, tiled=True
    )
    return moved.reshape(rows, width)


def rolled(x, di, dj):
    for axis, shift in ((0, di), (1, dj)):
        if shift == 1:
            head, tail = lax.slice_in_dim(x, 1, None, axis=axis), lax.slice_in_dim(x, 0, 1, axis=axis)
            x = jnp.concatenate([head, tail], axis=axis)
        elif shift == -1:
            count = x.shape[axis]
            head = lax.slice_in_dim(x, count - 1, count, axis=axis)
            x = jnp.concatenate([head, lax.slice_in_dim(x, 0, count - 1, axis=axis)], axis=axis)
    return x


def picked_depth(z, nz):
    depth = lax.broadcasted_iota(I32, (nz, z.shape[1]), 0)
    return jnp.where(depth == z, 1.0, 0.0).astype(BF16)


def rows_in(recv_ref, ndev, cap):
    width = recv_ref.shape[1]
    arrived = recv_ref[...].astype(F32).reshape(ndev, 3, cap, width)
    return [arrived[:, n].reshape(ndev * cap, width).astype(BF16) for n in range(3)]


def stacked(grad):
    nz = grad.shape[1]
    wide = grad.astype(F32)
    return jnp.concatenate(
        [pltpu.roll(wide, nz - 1, 1), wide, pltpu.roll(wide, 1, 1)], axis=0
    ).astype(BF16)


def over_depth(acc):
    chans, nz = acc.shape[0] // 3, acc.shape[1]
    total = acc[chans : 2 * chans] + pltpu.roll(acc[:chans], 1, 1)
    return total + pltpu.roll(acc[2 * chans :], nz - 1, 1)


def finish_row(pre, field, cot):
    sig = jax.nn.sigmoid(pre)
    out = field.astype(F32) + pre * sig
    grad = cot.astype(F32) * sig * (1.0 + pre * (1.0 - sig))
    return out.astype(BF16), grad.astype(BF16)


def first_kernel(
    ngx, ngy, cap, rows_far, counts_far, base_far, send_ref, again_far, rows_ref, counts_ref, sems
):
    again = pltpu.make_async_copy(base_far, again_far, sems.at[2])
    copies = [
        pltpu.make_async_copy(rows_far, rows_ref, sems.at[0]),
        pltpu.make_async_copy(counts_far, counts_ref, sems.at[1]),
    ]
    for copy in copies:
        copy.start()
    again.start()
    for copy in copies:
        copy.wait()
    pick(ngx, ngy, cap, counts_ref, rows_ref, send_ref)
    again.wait()


def same_kernel(in_ref, out_ref):
    pass


def pick(ngx, ngy, cap, counts_ref, rows_ref, out_ref):
    ndev = ngx * ngy
    nrows, feats = rows_ref.shape
    slots = ndev * cap
    counts = counts_ref[...].astype(F32)
    owner = lax.broadcasted_iota(I32, (ndev, cap, ndev), 0).reshape(slots, ndev)
    lane = lax.broadcasted_iota(I32, (slots, ndev), 1)
    start = jnp.sum(jnp.where(lane < owner, counts, 0.0), axis=1, keepdims=True)
    held = jnp.sum(jnp.where(lane == owner, counts, 0.0), axis=1, keepdims=True)
    place = lax.broadcasted_iota(I32, (ndev, cap, nrows), 1).reshape(slots, nrows).astype(F32)
    row = lax.broadcasted_iota(I32, (slots, nrows), 1).astype(F32)
    onehot = jnp.where((row == place + start) & (place < held), 1.0, 0.0).astype(BF16)
    raw = mm(onehot, rows_ref[...]).reshape(ngx, ngy, cap, feats)
    parts = [rolled(raw, dx, 0).reshape(ndev, cap, feats) for dx in (-1, 0, 1)]
    out_ref[...] = jnp.stack(parts, axis=1).reshape(out_ref.shape).astype(BF16)


def painted_rows(values, y, onehot, ns, masked):
    chans = values.shape[0]
    for n, row in enumerate(ns):
        masked[pl.ds(n * chans, chans)] = values * jnp.where(y == row, 1.0, 0.0).astype(BF16)
    return mm(masked[pl.ds(0, len(ns) * chans)], onehot, NT)


def add_to_rows(near, far, cot, back, out_ref):
    chans = cot.shape[0]
    rows = 3 * chans
    at, over = (rows, 0) if back else (0, rows)
    out_ref[pl.ds(0, chans)] = over_depth(near[at : at + rows]).astype(BF16)
    out_ref[pl.ds(chans, chans)] = over_depth(near[over : over + rows] + far).astype(BF16)
    out_ref[pl.ds(2 * chans, chans)] = cot


def outer_kernel(
    ndev, cap, recv_ref, own_ref, west_ref, east_ref, own_cells, west_cells, east_cells,
    proj_t_ref, cot_ref, wf_ref, first_ref, last_ref, values_ref, hot_ref, masked, field,
):
    chans, cy, nz = own_ref.shape
    rows = 3 * chans
    raws = rows_in(recv_ref, ndev, cap)
    ns = (0, 1, cy - 2, cy - 1)
    planes = ((west_ref, west_cells), (own_ref, own_cells), (east_ref, east_cells))
    for dx, (ref, cells_ref) in enumerate(planes):
        values = mm(proj_t_ref[...], raws[dx], NT).astype(BF16)
        y, z = place(cells_ref, nz)
        onehot = picked_depth(z, nz)
        values_ref[dx] = values
        hot_ref[dx] = onehot
        painted = painted_rows(values, y, onehot, ns, masked)
        base = turned(ref)
        for n, row in enumerate(ns):
            part = painted[n * chans : (n + 1) * chans]
            field[n, pl.ds(dx * chans, chans)] = (base[row] + part).astype(BF16)
    near = mm(wf_ref[pl.ds(0, 2 * rows)], field[3])
    add_to_rows(near, mm(wf_ref[pl.ds(0, rows)], field[2]), cot_ref[cy - 1], False, last_ref)
    near = mm(wf_ref[pl.ds(rows, 2 * rows)], field[0])
    add_to_rows(near, mm(wf_ref[pl.ds(2 * rows, rows)], field[1]), cot_ref[0], True, first_ref)


def place(cells_ref, nz):
    cells = cells_ref[...]
    return cells // nz, cells % nz


def turned(ref):
    return jnp.swapaxes(ref[...], 0, 1).astype(F32)


def conv_kernel(
    values_ref, hot_ref, own_ref, west_ref, east_ref, own_cells, west_cells, east_cells,
    cot_ref, wf_ref, wb_ref,
    x_ref, out_ref, total_ref, pre_ref, slot_ref, plane, acc, grads, back, masked,
):
    cy, chans, nz = cot_ref.shape
    rows = 3 * chans
    planes = ((west_ref, west_cells), (own_ref, own_cells), (east_ref, east_cells))
    for dx, (ref, cells_ref) in enumerate(planes):
        y, _ = place(cells_ref, nz)
        painted = painted_rows(values_ref[dx], y, hot_ref[dx], range(cy), masked)
        field = turned(ref) + painted.reshape(cy, chans, nz)
        x_ref[:, pl.ds(dx * chans, chans)] = field.astype(BF16)
    own = pl.ds(chans, chans)
    zeros = jnp.zeros((rows, nz), BF16)
    for t in (0, 1, cy, cy + 1):
        grads[t] = zeros
    out_ref[0] = zeros[:chans]
    out_ref[cy - 1] = zeros[:chans]
    acc[0] = jnp.zeros((rows, nz), F32)

    def spread(n):
        terms = mm(wf_ref[...], x_ref[n])
        acc[n + 1] = terms[:rows]
        acc[n] += terms[rows : 2 * rows]
        return terms[2 * rows :]

    pre_ref[0] = over_depth(spread(0))
    pre_ref[1] = over_depth(acc[0] + spread(1))

    def forward(n):
        done = spread(n) + acc[n - 1]
        y = n - 1
        out, grad = finish_row(over_depth(done), x_ref[y, own], cot_ref[y])
        out_ref[y] = out
        grads[y + 1] = stacked(grad)

    for n in range(2, cy):
        forward(n)
    pre_ref[2] = over_depth(acc[cy - 1])
    pre_ref[3] = over_depth(acc[cy])
    total_ref[...] = jnp.zeros_like(total_ref)
    back[0] = jnp.zeros((rows, nz), F32)
    back[1] = jnp.zeros((rows, nz), F32)

    def taps(n):
        window = grads[pl.ds(n, 3)].reshape(3 * rows, nz)
        total_ref[...] += mm(window, x_ref[n], NT)

    def spread_back(n):
        terms = mm(wb_ref[...], grads[n + 1])
        back[n + 1] = terms[2 * rows :]
        back[n] += terms[rows : 2 * rows]
        return terms[:rows]

    def backward(n):
        taps(n)
        value = spread_back(n) + back[n - 1]
        for dx in range(3):
            part = value[dx * chans : (dx + 1) * chans]
            if dx == 1:
                part = part + cot_ref[n - 1].astype(F32)
            plane[dx, pl.ds((n - 3) * chans, chans)] = part.astype(BF16)

    taps(0)
    taps(1)
    slot_ref[0] = spread_back(1)
    taps(2)
    slot_ref[1] = spread_back(2) + back[1]
    for n in range(3, cy - 1):
        backward(n)
    taps(cy - 1)
    slot_ref[2] = back[cy - 2]
    slot_ref[3] = back[cy - 1]


def at_slots(part, y, onehot, first):
    found = mm(part, onehot)
    chans = found.shape[0] // len(first)
    total = jnp.zeros((chans, found.shape[1]), F32)
    for n, row in enumerate(first):
        total = total + jnp.where(y == row, found[n * chans : (n + 1) * chans], 0.0)
    return total


def edge_kernel(
    part, parity_ref, pre_ref, total_ref, north_ref, south_ref, x_ref, cot_ref,
    out_ref, grads_ref, keep_ref, give_ref, total, sums,
):
    cy, chans, nz = cot_ref.shape
    rows = 3 * chans
    own = pl.ds(chans, chans)
    last = pl.ds(2 * chans, chans)
    cots = (north_ref[last], cot_ref[0], cot_ref[cy - 1], south_ref[last])
    sides = ((north_ref, 1), (north_ref, 0), (south_ref, 0), (south_ref, 1))
    ends = []
    for n, (ref, at) in enumerate(sides):
        pre = pre_ref[n] + ref[pl.ds(at * chans, chans)].astype(F32)
        ends.append(finish_row(pre, x_ref[0 if n < 2 else cy - 1, own], cots[n]))
    out_ref[0], out_ref[1] = ends[1][0], ends[2][0]
    grads = [stacked(grad) for _, grad in ends]
    for n in range(4):
        grads_ref[n] = grads[n]
    top = mm(jnp.concatenate([grads[0], grads[1]], axis=0), x_ref[0], NT)
    bottom = mm(jnp.concatenate([grads[2], grads[3]], axis=0), x_ref[cy - 1], NT)
    here = [pl.ds(n * rows, rows) for n in range(3)]
    total[here[0]] = total_ref[here[0]] + (top[:rows] + mm(grads[1], x_ref[1], NT))
    total[here[1]] = total_ref[here[1]] + (top[rows:] + bottom[:rows])
    total[here[2]] = total_ref[here[2]] + (bottom[rows:] + mm(grads[2], x_ref[cy - 2], NT))
    full, _, width = keep_ref.shape
    half = 3 * rows // 2
    split = 3 * rows // (2 * part)
    sums[pl.ds(0, split)] = total[:, :width].reshape(split, 2, part, width)
    taps = jnp.concatenate([total[pl.ds(0, half), width:], total[pl.ds(half, half), width:]], axis=1)
    sums[pl.ds(split, full - split)] = taps.reshape(full - split, 2, part, width)
    parity = parity_ref[0]
    keep_ref[...] = sums[:, parity]
    give_ref[...] = sums[:, 1 - parity].astype(BF16)


def slots_kernel(
    ndev, cap, part, full, slot_ref, plane_ref, hot_ref, grads_ref, wb_ref, cot_ref,
    own_cells, west_cells, east_cells, recv_ref, slots_ref, proj_ref,
):
    cy, chans, nz = cot_ref.shape
    rows = 3 * chans
    inner = mm(wb_ref[pl.ds(rows, 2 * rows)], grads_ref[1])
    top = slot_ref[0] + inner[:rows] + mm(wb_ref[pl.ds(2 * rows, rows)], grads_ref[0])
    second = slot_ref[1] + inner[rows:]
    inner = mm(wb_ref[pl.ds(0, 2 * rows)], grads_ref[2])
    third = slot_ref[2] + inner[:rows]
    bottom = slot_ref[3] + inner[rows:] + mm(wb_ref[pl.ds(0, rows)], grads_ref[3])
    at = (0, 1, cy - 2, cy - 1)
    found = []
    for dx, cells_ref in enumerate((west_cells, own_cells, east_cells)):
        parts = [value[dx * chans : (dx + 1) * chans] for value in (top, second, third, bottom)]
        if dx == 1:
            parts = [value + cot_ref[n].astype(F32) for value, n in zip(parts, at)]
        parts = [value.astype(BF16) for value in parts]
        terms = jnp.concatenate([plane_ref[dx], *parts], axis=0)
        y, _ = place(cells_ref, nz)
        found.append(at_slots(terms, y, hot_ref[dx], (*range(2, cy - 2), *at)))
    sides = jnp.concatenate([found[0], found[2]], axis=0).T
    middle = jnp.concatenate([found[1], jnp.zeros_like(found[1])], axis=0).T
    width = recv_ref.shape[1]
    back = [sides.reshape(ndev, cap, width), middle.reshape(ndev, cap, width)]
    slots_ref[...] = jnp.concatenate(back, axis=1).astype(BF16)
    raws = rows_in(recv_ref, ndev, cap)
    proj = sum(mm(found[dx].astype(BF16), raws[dx]) for dx in range(3))
    rest = ndev - full
    pad = jnp.zeros((rest * part - chans, width), F32)
    proj = jnp.concatenate([proj, pad], axis=0).reshape(rest, part, width)
    proj_ref[...] = proj.astype(BF16)


def pair_kernel(keep_ref, got_ref, slots_ref, proj_ref, send_far, sums_send, sems):
    full, part, _ = keep_ref.shape
    ndev, back, _ = slots_ref.shape
    pieces = (
        (slots_ref, send_far.at[:, pl.ds(part, back)]),
        (proj_ref, send_far.at[pl.ds(full, ndev - full), pl.ds(0, part)]),
        (sums_send, send_far.at[pl.ds(0, full), pl.ds(0, part)]),
    )
    copies = [pltpu.make_async_copy(src, dst, sems.at[n]) for n, (src, dst) in enumerate(pieces)]
    copies[0].start()
    copies[1].start()
    sums_send[...] = (keep_ref[...] + got_ref[...].astype(F32)).astype(BF16)
    copies[2].start()
    for copy in copies:
        copy.wait()


def sums_kernel(ngx, ngy, full, cap, recv_ref, index_ref, sums_ref):
    ndev, each, width = recv_ref.shape
    part = each - 2 * cap
    terms = recv_ref[:, pl.ds(0, part)].astype(F32).reshape(ngx // 2, 2, ngy, part, width)
    sums = jnp.sum(terms, axis=(0, 2))
    whole = sums[0] + sums[1]
    high = whole.astype(BF16).astype(F32)
    last = jnp.broadcast_to(index_ref[...], whole.shape) >= full
    sums = [
        jnp.where(last, high, sums[0]).astype(BF16),
        jnp.where(last, whole - high, sums[1]).astype(BF16),
    ]
    for n in range(ndev):
        sums_ref[n] = sums[(n // ngy) % 2]


def rows_kernel(
    ngx, ngy, cap, chans, recv_ref, counts_ref, proj_t_ref, inner_ref, ends_ref, rows_ref, out_ref
):
    ndev = ngx * ngy
    nrows = rows_ref.shape[0]
    width = recv_ref.shape[2]
    slots = ndev * cap
    share = recv_ref.shape[1] - 2 * cap
    arrived = recv_ref[:, pl.ds(share, 2 * cap)].astype(F32)
    sides = arrived[:, :cap].reshape(ngx, ngy, cap, width)
    left = lax.broadcasted_iota(I32, sides.shape, 3) < chans
    sides = jnp.where(left, rolled(sides, 1, 0), rolled(sides, -1, 0)).reshape(slots, width)
    middle = arrived[:, cap:].reshape(slots, width)
    counts = counts_ref[...].astype(F32)
    place = lax.broadcasted_iota(I32, (nrows, ndev), 0).astype(F32)
    lane = lax.broadcasted_iota(I32, (ndev, ndev), 1)
    upto = lax.broadcasted_iota(I32, (ndev, ndev), 0) <= lane
    ends = mm(counts.astype(BF16), jnp.where(upto, 1.0, 0.0).astype(BF16))
    before = ends <= place
    owner = jnp.sum(jnp.where(before, 1.0, 0.0), axis=1, keepdims=True)
    start = jnp.sum(jnp.where(before, counts, 0.0), axis=1, keepdims=True)
    slot = owner * cap + place[:, :1] - start
    onehot = jnp.where(
        lax.broadcasted_iota(I32, (nrows, slots), 1).astype(F32) == slot, 1.0, 0.0
    ).astype(BF16)
    proj_t = proj_t_ref[...]
    both = jnp.concatenate([proj_t, proj_t], axis=0)
    sides = mm(onehot, sides.astype(BF16)).astype(BF16)
    middle = mm(onehot, middle.astype(BF16)).astype(BF16)
    rows_ref[...] = mm(sides, both) + mm(middle, both)
    cy = inner_ref.shape[0]
    field = jnp.concatenate([ends_ref[:1], inner_ref[1 : cy - 1], ends_ref[1:]], axis=0)
    out_ref[...] = jnp.swapaxes(field, 0, 1)


def finish_kernel(conv_scale, proj_scale, parity_ref, mine_ref, other_ref, conv_ref, proj_ref, both):
    ndev, part, width = mine_ref.shape
    parity = parity_ref[0]
    both[:, parity] = mine_ref[...]
    both[:, 1 - parity] = other_ref[...]
    sums = both[...].astype(F32).reshape(ndev * 2 * part, width)
    taps, chans, _ = conv_ref.shape
    rows = 9 * chans
    half = rows // 2
    packed = sums[rows : rows + half]
    column = jnp.concatenate([packed[:, :chans], packed[:, chans:]], axis=0)
    for b in range(3):
        for dz in range(3):
            first = (b * 3 + dz) * chans
            block = sums[first : first + chans]
            k = (2 - b) * 3 + dz
            conv_ref[k] = block[:, :chans] * conv_scale
            conv_ref[9 + k] = block[:, chans:] * conv_scale
            conv_ref[18 + k] = column[first : first + chans] * conv_scale
    terms = sums[rows + half : rows + half + 2 * chans].reshape(chans // part, 2, part, width)
    proj_ref[...] = jnp.sum(terms, axis=1).reshape(chans, width) * proj_scale


def local(particles, send_counts, cell_lists, base_field, proj_weight, conv_weight, cotangent):
    ngx, ngy = lax.axis_size("gx"), lax.axis_size("gy")
    ndev = ngx * ngy
    nrows, feats = particles.shape
    chans, cx, cy, nz = base_field.shape
    slots = cell_lists.shape[1]
    cap = slots // ndev
    count = cx * cy * nz
    assert cx == 1 and feats == 2 * chans
    proj_t = proj_weight.T
    move = functools.partial(send, ngx=ngx, ngy=ngy)
    rows = 3 * chans
    one = 2 * rows * rows * nz

    base = base_field.reshape(chans, cy, nz)
    west = move(base, 1, 0)
    lists = (cell_lists, move(cell_lists, 1, 0), move(cell_lists, -1, 0))
    payload, again = call(
        functools.partial(first_kernel, ngx, ngy, cap),
        [shape((ndev * 3 * cap, feats), BF16), base],
        (particles, send_counts, base),
        2 * slots * nrows * feats,
        (
            pltpu.VMEM(particles.shape, BF16),
            pltpu.VMEM(send_counts.shape, I32),
            pltpu.SemaphoreType.DMA((3,)),
        ),
        far=range(3),
        far_out=(1,),
        limit=ALL,
    )
    planes = (base, west, move(again, -1, 0))
    recv = exchange(payload, ndev)

    cot = cotangent[:, 0].transpose(1, 0, 2)
    taps = conv_weight.reshape(3, 3, 3, chans, chans)
    wf = taps.transpose(1, 2, 3, 0, 4).reshape(9 * chans, rows)
    wb = taps.transpose(1, 0, 4, 2, 3).reshape(9 * chans, rows)

    first, last, values, hots = call(
        functools.partial(outer_kernel, ndev, cap),
        [shape((rows, nz), BF16)] * 2
        + [shape((3, chans, slots), BF16), shape((3, nz, slots), BF16)],
        (recv, *planes, *lists, proj_t, cot, wf),
        4 * one,
        (pltpu.VMEM((4 * chans, slots), BF16), pltpu.VMEM((4, rows, nz), BF16)),
    )
    south, north = move(first, 0, -1), move(last, 0, 1)
    x_all, out_rows, total, pre_edge, slot_edge, plane = call(
        conv_kernel,
        [
            shape((cy, rows, nz), BF16),
            shape((cy, chans, nz), BF16),
            shape((9 * chans, rows), F32),
            shape((4, chans, nz), F32),
            shape((4, rows, nz), F32),
            shape((3, (cy - 4) * chans, nz), BF16),
        ],
        (values, hots, *planes, *lists, cot, wf, wb),
        3 * cy * 3 * one,
        (
            pltpu.VMEM((cy + 1, rows, nz), F32),
            pltpu.VMEM((cy + 2, rows, nz), BF16),
            pltpu.VMEM((cy, rows, nz), F32),
            pltpu.VMEM((cy * chans, slots), BF16),
        ),
    )
    grad_rows = 27 * chans * chans // feats
    part = -(-(grad_rows + 2 * chans) // (32 * ndev)) * 16
    full = grad_rows // (2 * part)
    assert ngx % 2 == 0 and full * 2 * part == grad_rows
    row = lax.axis_index("gx")
    parity = (row % 2).astype(I32).reshape(1)
    out_edge, grads, keep, give = call(
        functools.partial(edge_kernel, part),
        [
            shape((2, chans, nz), BF16),
            shape((4, rows, nz), BF16),
            shape((full, part, feats), F32),
            shape((full, part, feats), BF16),
        ],
        (parity, pre_edge, total, north, south, x_all, cot),
        6 * one,
        (pltpu.VMEM((9 * chans, rows), F32), pltpu.VMEM((full, 2, part, feats), F32)),
        scalar=(0,),
    )
    got = swap(give)
    back, proj = call(
        functools.partial(slots_kernel, ndev, cap, part, full),
        [shape((ndev, 2 * cap, feats), BF16), shape((ndev - full, part, feats), BF16)],
        (slot_edge, plane, hots, grads, wb, cot, *lists, recv),
        6 * one,
    )
    (payload,) = call(
        pair_kernel,
        [shape((ndev, part + 2 * cap, feats), BF16)],
        (keep, got, back, proj),
        1000,
        (pltpu.VMEM((full, part, feats), BF16), pltpu.SemaphoreType.DMA((3,))),
        far_out=(0,),
    )
    (payload,) = call(same_kernel, [payload], (payload,), 0, far=(0,), far_out=(0,), aliases={0: 0})
    recv = exchange(payload.reshape(-1, feats), ndev).reshape(payload.shape)
    index = (row * ngy + lax.axis_index("gy")).astype(I32).reshape(1, 1)
    (sums,) = call(
        functools.partial(sums_kernel, ngx, ngy, full, cap),
        [shape((ndev, part, feats), BF16)],
        (recv, index),
        1000,
    )
    row_grads, out_field = call(
        functools.partial(rows_kernel, ngx, ngy, cap, chans),
        [shape((nrows, feats), F32), shape((chans, cy, nz), BF16)],
        (recv, send_counts, proj_t, out_rows, out_edge),
        2 * nrows * slots * chans,
    )
    mine = exchange(sums.reshape(-1, feats), ndev).reshape(sums.shape)
    mine, row_grads, out_field = lax.optimization_barrier((mine, row_grads, out_field))
    other = swap(mine)
    conv_grad, proj_grad = call(
        functools.partial(
            finish_kernel, 1.0 / math.sqrt(count * ndev), 1.0 / math.sqrt(nrows * ndev)
        ),
        [shape((27, chans, chans), F32), shape((chans, feats), F32)],
        (parity, mine, other),
        1000,
        (pltpu.VMEM((ndev, 2, part, feats), BF16),),
        scalar=(0,),
    )
    return (out_field[:, None], row_grads, conv_grad, proj_grad.T)


def solution(mesh):
    in_specs = (
        P(("gx", "gy"), None),
        P(("gx", "gy"), None),
        P(("gx", "gy"), None),
        P(None, "gx", "gy", None),
        P(),
        P(),
        P(None, "gx", "gy", None),
    )
    out_specs = (P(None, "gx", "gy", None), P(("gx", "gy"), None), P(), P())
    return jax.shard_map(local, mesh=mesh, in_specs=in_specs, out_specs=out_specs, check_vma=False)
```

```python
import functools
import math

import jax
import jax.numpy as jnp
from jax import lax
from jax.experimental import pallas as pl
from jax.experimental.pallas import tpu as pltpu
from jax.sharding import PartitionSpec as P

AXES = ("gx", "gy")
F32, BF16, I32 = jnp.float32, jnp.bfloat16, jnp.int32
LIMIT = 40 * 1024 * 1024
ALL = 60 * 1024 * 1024
NT = (((1,), (1,)), ((), ()))
NN = (((1,), (0,)), ((), ()))


def mm(a, b, dims=NN):
    return lax.dot_general(a, b, dims, preferred_element_type=F32)


def call(kernel, outs, args, flops, scratch=(), far=(), far_out=(), aliases=None, limit=LIMIT, scalar=()):
    traffic = sum(math.prod(a.shape) * a.dtype.itemsize for a in (*args, *outs))
    near = pl.BlockSpec(memory_space=pltpu.VMEM)
    there = pl.BlockSpec(memory_space=pltpu.HBM)
    return pl.pallas_call(
        kernel,
        out_shape=[jax.ShapeDtypeStruct(o.shape, o.dtype) for o in outs],
        in_specs=[
            pl.BlockSpec(memory_space=pltpu.SMEM) if n in scalar else there if n in far else near
            for n in range(len(args))
        ],
        out_specs=[there if n in far_out else near for n in range(len(outs))],
        scratch_shapes=list(scratch),
        input_output_aliases=aliases or {},
        compiler_params=pltpu.CompilerParams(vmem_limit_bytes=limit),
        cost_estimate=pl.CostEstimate(flops=flops, bytes_accessed=traffic, transcendentals=0),
    )(*args)


def shape(dims, dtype):
    return jax.ShapeDtypeStruct(dims, dtype)


def send(block, di, dj, ngx, ngy):
    pairs = []
    for i in range(ngx):
        for j in range(ngy):
            pairs.append((i * ngy + j, ((i + di) % ngx) * ngy + (j + dj) % ngy))
    return lax.ppermute(block, AXES, pairs)


def swap(block):
    return lax.ppermute(block, "gx", [(i, i ^ 1) for i in range(lax.axis_size("gx"))])


def exchange(payload, ndev):
    rows, width = payload.shape
    moved = lax.all_to_all(
        payload.reshape(ndev, rows // ndev, width), AXES, split_axis=0, concat_axis=0, tiled=True
    )
    return moved.reshape(rows, width)


def rolled(x, di, dj):
    for axis, shift in ((0, di), (1, dj)):
        if shift == 1:
            head, tail = lax.slice_in_dim(x, 1, None, axis=axis), lax.slice_in_dim(x, 0, 1, axis=axis)
            x = jnp.concatenate([head, tail], axis=axis)
        elif shift == -1:
            count = x.shape[axis]
            head = lax.slice_in_dim(x, count - 1, count, axis=axis)
            x = jnp.concatenate([head, lax.slice_in_dim(x, 0, count - 1, axis=axis)], axis=axis)
    return x


def picked_depth(z, nz):
    depth = lax.broadcasted_iota(I32, (nz, z.shape[1]), 0)
    return jnp.where(depth == z, 1.0, 0.0).astype(BF16)


def rows_in(recv_ref, ndev, cap):
    width = recv_ref.shape[1]
    arrived = recv_ref[...].astype(F32).reshape(ndev, 3, cap, width)
    return [arrived[:, n].reshape(ndev * cap, width).astype(BF16) for n in range(3)]


def stacked(grad):
    nz = grad.shape[1]
    wide = grad.astype(F32)
    return jnp.concatenate(
        [pltpu.roll(wide, nz - 1, 1), wide, pltpu.roll(wide, 1, 1)], axis=0
    ).astype(BF16)


def over_depth(acc):
    chans, nz = acc.shape[0] // 3, acc.shape[1]
    total = acc[chans : 2 * chans] + pltpu.roll(acc[:chans], 1, 1)
    return total + pltpu.roll(acc[2 * chans :], nz - 1, 1)


def finish_row(pre, field, cot):
    sig = jax.nn.sigmoid(pre)
    out = field.astype(F32) + pre * sig
    grad = cot.astype(F32) * sig * (1.0 + pre * (1.0 - sig))
    return out.astype(BF16), grad.astype(BF16)


def first_kernel(
    ngx, ngy, cap, rows_far, counts_far, send_ref, rows_ref, counts_ref, sems
):
    copies = [
        pltpu.make_async_copy(rows_far, rows_ref, sems.at[0]),
        pltpu.make_async_copy(counts_far, counts_ref, sems.at[1]),
    ]
    for copy in copies:
        copy.start()
    copies[1].wait()
    pick(ngx, ngy, cap, counts_ref, rows_ref, send_ref, copies[0])


def turns_kernel(weight_ref, cot_ref, wf_ref, wb_ref, cot_out):
    cot_out[...] = jnp.swapaxes(cot_ref[...], 0, 1)
    chans = cot_ref.shape[0]
    three = range(3)
    for dy in three:
        for n in three:
            rows = pl.ds((dy * 3 + n) * chans, chans)
            taps = [weight_ref[dx * 9 + dy * 3 + n] for dx in three]
            wf_ref[rows] = jnp.concatenate(taps, axis=1)
            taps = [weight_ref[n * 9 + dy * 3 + dz].astype(F32).T for dz in three]
            wb_ref[rows] = jnp.concatenate(taps, axis=1).astype(BF16)


def same_kernel(in_ref, out_ref):
    pass


def pick(ngx, ngy, cap, counts_ref, rows_ref, out_ref, rows_copy):
    ndev = ngx * ngy
    nrows, feats = rows_ref.shape
    slots = ndev * cap
    counts = counts_ref[...].astype(F32)
    owner = lax.broadcasted_iota(I32, (ndev, cap, ndev), 0).reshape(slots, ndev)
    lane = lax.broadcasted_iota(I32, (slots, ndev), 1)
    start = jnp.sum(jnp.where(lane < owner, counts, 0.0), axis=1, keepdims=True)
    held = jnp.sum(jnp.where(lane == owner, counts, 0.0), axis=1, keepdims=True)
    place = lax.broadcasted_iota(I32, (ndev, cap, nrows), 1).reshape(slots, nrows).astype(F32)
    row = lax.broadcasted_iota(I32, (slots, nrows), 1).astype(F32)
    onehot = jnp.where((row == place + start) & (place < held), 1.0, 0.0).astype(BF16)
    rows_copy.wait()
    raw = mm(onehot, rows_ref[...]).reshape(ngx, ngy, cap, feats)
    parts = [rolled(raw, dx, 0).reshape(ndev, cap, feats) for dx in (-1, 0, 1)]
    out_ref[...] = jnp.stack(parts, axis=1).reshape(out_ref.shape).astype(BF16)


def painted_rows(values, y, onehot, ns, masked):
    chans = values.shape[0]
    for n, row in enumerate(ns):
        masked[pl.ds(n * chans, chans)] = values * jnp.where(y == row, 1.0, 0.0).astype(BF16)
    return mm(masked[pl.ds(0, len(ns) * chans)], onehot, NT)


def add_to_rows(near, far, cot, back, out_ref):
    chans = cot.shape[0]
    rows = 3 * chans
    at, over = (rows, 0) if back else (0, rows)
    out_ref[pl.ds(0, chans)] = over_depth(near[at : at + rows]).astype(BF16)
    out_ref[pl.ds(chans, chans)] = over_depth(near[over : over + rows] + far).astype(BF16)
    out_ref[pl.ds(2 * chans, chans)] = cot


def outer_kernel(
    ndev, cap, recv_ref, own_ref, west_ref, east_ref, own_cells, west_cells, east_cells,
    proj_t_ref, cot_ref, wf_ref, first_ref, last_ref, values_ref, hot_ref, masked, field,
):
    chans, cy, nz = own_ref.shape
    rows = 3 * chans
    raws = rows_in(recv_ref, ndev, cap)
    ns = (0, 1, cy - 2, cy - 1)
    planes = ((west_ref, west_cells), (own_ref, own_cells), (east_ref, east_cells))
    for dx, (ref, cells_ref) in enumerate(planes):
        values = mm(proj_t_ref[...], raws[dx], NT).astype(BF16)
        y, z = place(cells_ref, nz)
        onehot = picked_depth(z, nz)
        values_ref[dx] = values
        hot_ref[dx] = onehot
        painted = painted_rows(values, y, onehot, ns, masked)
        base = turned(ref)
        for n, row in enumerate(ns):
            part = painted[n * chans : (n + 1) * chans]
            field[n, pl.ds(dx * chans, chans)] = (base[row] + part).astype(BF16)
    near = mm(wf_ref[pl.ds(0, 2 * rows)], field[3])
    add_to_rows(near, mm(wf_ref[pl.ds(0, rows)], field[2]), cot_ref[cy - 1], False, last_ref)
    near = mm(wf_ref[pl.ds(rows, 2 * rows)], field[0])
    add_to_rows(near, mm(wf_ref[pl.ds(2 * rows, rows)], field[1]), cot_ref[0], True, first_ref)


def place(cells_ref, nz):
    cells = cells_ref[...]
    return cells // nz, cells % nz


def turned(ref):
    return jnp.swapaxes(ref[...], 0, 1).astype(F32)


def conv_kernel(
    values_ref, hot_ref, own_ref, west_ref, east_ref, own_cells, west_cells, east_cells,
    cot_ref, wf_ref, wb_ref,
    x_ref, out_ref, total_ref, pre_ref, slot_ref, plane, acc, grads, back, masked,
):
    cy, chans, nz = cot_ref.shape
    rows = 3 * chans
    planes = ((west_ref, west_cells), (own_ref, own_cells), (east_ref, east_cells))
    for dx, (ref, cells_ref) in enumerate(planes):
        y, _ = place(cells_ref, nz)
        painted = painted_rows(values_ref[dx], y, hot_ref[dx], range(cy), masked)
        field = turned(ref) + painted.reshape(cy, chans, nz)
        x_ref[:, pl.ds(dx * chans, chans)] = field.astype(BF16)
    own = pl.ds(chans, chans)
    zeros = jnp.zeros((rows, nz), BF16)
    for t in (0, 1, cy, cy + 1):
        grads[t] = zeros
    out_ref[0] = zeros[:chans]
    out_ref[cy - 1] = zeros[:chans]
    acc[0] = jnp.zeros((rows, nz), F32)

    def spread(n):
        terms = mm(wf_ref[...], x_ref[n])
        acc[n + 1] = terms[:rows]
        acc[n] += terms[rows : 2 * rows]
        return terms[2 * rows :]

    pre_ref[0] = over_depth(spread(0))
    pre_ref[1] = over_depth(acc[0] + spread(1))

    def forward(n):
        done = spread(n) + acc[n - 1]
        y = n - 1
        out, grad = finish_row(over_depth(done), x_ref[y, own], cot_ref[y])
        out_ref[y] = out
        grads[y + 1] = stacked(grad)

    for n in range(2, cy):
        forward(n)
    pre_ref[2] = over_depth(acc[cy - 1])
    pre_ref[3] = over_depth(acc[cy])
    total_ref[...] = jnp.zeros_like(total_ref)
    back[0] = jnp.zeros((rows, nz), F32)
    back[1] = jnp.zeros((rows, nz), F32)

    def taps(n):
        window = grads[pl.ds(n, 3)].reshape(3 * rows, nz)
        total_ref[...] += mm(window, x_ref[n], NT)

    def spread_back(n):
        terms = mm(wb_ref[...], grads[n + 1])
        back[n + 1] = terms[2 * rows :]
        back[n] += terms[rows : 2 * rows]
        return terms[:rows]

    def backward(n):
        taps(n)
        value = spread_back(n) + back[n - 1]
        for dx in range(3):
            part = value[dx * chans : (dx + 1) * chans]
            if dx == 1:
                part = part + cot_ref[n - 1].astype(F32)
            plane[dx, pl.ds((n - 3) * chans, chans)] = part.astype(BF16)

    taps(0)
    taps(1)
    slot_ref[0] = spread_back(1)
    taps(2)
    slot_ref[1] = spread_back(2) + back[1]
    for n in range(3, cy - 1):
        backward(n)
    taps(cy - 1)
    slot_ref[2] = back[cy - 2]
    slot_ref[3] = back[cy - 1]


def at_slots(part, y, onehot, first):
    found = mm(part, onehot)
    chans = found.shape[0] // len(first)
    total = jnp.zeros((chans, found.shape[1]), F32)
    for n, row in enumerate(first):
        total = total + jnp.where(y == row, found[n * chans : (n + 1) * chans], 0.0)
    return total


def edge_kernel(
    part, parity_ref, pre_ref, total_ref, north_ref, south_ref, x_ref, cot_ref,
    out_ref, grads_ref, keep_ref, give_ref, total, sums,
):
    cy, chans, nz = cot_ref.shape
    rows = 3 * chans
    own = pl.ds(chans, chans)
    last = pl.ds(2 * chans, chans)
    cots = (north_ref[last], cot_ref[0], cot_ref[cy - 1], south_ref[last])
    sides = ((north_ref, 1), (north_ref, 0), (south_ref, 0), (south_ref, 1))
    ends = []
    for n, (ref, at) in enumerate(sides):
        pre = pre_ref[n] + ref[pl.ds(at * chans, chans)].astype(F32)
        ends.append(finish_row(pre, x_ref[0 if n < 2 else cy - 1, own], cots[n]))
    out_ref[0], out_ref[1] = ends[1][0], ends[2][0]
    grads = [stacked(grad) for _, grad in ends]
    for n in range(4):
        grads_ref[n] = grads[n]
    top = mm(jnp.concatenate([grads[0], grads[1]], axis=0), x_ref[0], NT)
    bottom = mm(jnp.concatenate([grads[2], grads[3]], axis=0), x_ref[cy - 1], NT)
    here = [pl.ds(n * rows, rows) for n in range(3)]
    total[here[0]] = total_ref[here[0]] + (top[:rows] + mm(grads[1], x_ref[1], NT))
    total[here[1]] = total_ref[here[1]] + (top[rows:] + bottom[:rows])
    total[here[2]] = total_ref[here[2]] + (bottom[rows:] + mm(grads[2], x_ref[cy - 2], NT))
    full, _, width = keep_ref.shape
    half = 3 * rows // 2
    split = 3 * rows // (2 * part)
    sums[pl.ds(0, split)] = total[:, :width].reshape(split, 2, part, width)
    taps = jnp.concatenate([total[pl.ds(0, half), width:], total[pl.ds(half, half), width:]], axis=1)
    sums[pl.ds(split, full - split)] = taps.reshape(full - split, 2, part, width)
    parity = parity_ref[0]
    keep_ref[...] = sums[:, parity]
    give_ref[...] = sums[:, 1 - parity].astype(BF16)


def slots_kernel(
    ndev, cap, part, full, slot_ref, plane_ref, hot_ref, grads_ref, wb_ref, cot_ref,
    own_cells, west_cells, east_cells, recv_ref, slots_ref, proj_ref,
):
    cy, chans, nz = cot_ref.shape
    rows = 3 * chans
    inner = mm(wb_ref[pl.ds(rows, 2 * rows)], grads_ref[1])
    top = slot_ref[0] + inner[:rows] + mm(wb_ref[pl.ds(2 * rows, rows)], grads_ref[0])
    second = slot_ref[1] + inner[rows:]
    inner = mm(wb_ref[pl.ds(0, 2 * rows)], grads_ref[2])
    third = slot_ref[2] + inner[:rows]
    bottom = slot_ref[3] + inner[rows:] + mm(wb_ref[pl.ds(0, rows)], grads_ref[3])
    at = (0, 1, cy - 2, cy - 1)
    found = []
    for dx, cells_ref in enumerate((west_cells, own_cells, east_cells)):
        parts = [value[dx * chans : (dx + 1) * chans] for value in (top, second, third, bottom)]
        if dx == 1:
            parts = [value + cot_ref[n].astype(F32) for value, n in zip(parts, at)]
        parts = [value.astype(BF16) for value in parts]
        terms = jnp.concatenate([plane_ref[dx], *parts], axis=0)
        y, _ = place(cells_ref, nz)
        found.append(at_slots(terms, y, hot_ref[dx], (*range(2, cy - 2), *at)))
    sides = jnp.concatenate([found[0], found[2]], axis=0).T
    middle = jnp.concatenate([found[1], jnp.zeros_like(found[1])], axis=0).T
    width = recv_ref.shape[1]
    back = [sides.reshape(ndev, cap, width), middle.reshape(ndev, cap, width)]
    slots_ref[...] = jnp.concatenate(back, axis=1).astype(BF16)
    raws = rows_in(recv_ref, ndev, cap)
    proj = sum(mm(found[dx].astype(BF16), raws[dx]) for dx in range(3))
    rest = ndev - full
    pad = jnp.zeros((rest * part - chans, width), F32)
    proj = jnp.concatenate([proj, pad], axis=0).reshape(rest, part, width)
    proj_ref[...] = proj.astype(BF16)


def pair_kernel(keep_ref, got_ref, slots_ref, proj_ref, send_far, sums_send, sems):
    full, part, _ = keep_ref.shape
    ndev, back, _ = slots_ref.shape
    pieces = (
        (slots_ref, send_far.at[:, pl.ds(part, back)]),
        (proj_ref, send_far.at[pl.ds(full, ndev - full), pl.ds(0, part)]),
        (sums_send, send_far.at[pl.ds(0, full), pl.ds(0, part)]),
    )
    copies = [pltpu.make_async_copy(src, dst, sems.at[n]) for n, (src, dst) in enumerate(pieces)]
    copies[0].start()
    copies[1].start()
    sums_send[...] = (keep_ref[...] + got_ref[...].astype(F32)).astype(BF16)
    copies[2].start()
    for copy in copies:
        copy.wait()


def sums_kernel(ngx, ngy, full, cap, recv_ref, index_ref, sums_ref):
    ndev, each, width = recv_ref.shape
    part = each - 2 * cap
    terms = recv_ref[:, pl.ds(0, part)].astype(F32).reshape(ngx // 2, 2, ngy, part, width)
    sums = jnp.sum(terms, axis=(0, 2))
    whole = sums[0] + sums[1]
    high = whole.astype(BF16).astype(F32)
    last = jnp.broadcast_to(index_ref[...], whole.shape) >= full
    sums = [
        jnp.where(last, high, sums[0]).astype(BF16),
        jnp.where(last, whole - high, sums[1]).astype(BF16),
    ]
    for n in range(ndev):
        sums_ref[n] = sums[(n // ngy) % 2]


def rows_kernel(
    ngx, ngy, cap, chans, recv_ref, counts_ref, proj_t_ref, inner_ref, ends_ref, rows_ref, out_ref
):
    ndev = ngx * ngy
    nrows = rows_ref.shape[0]
    width = recv_ref.shape[2]
    slots = ndev * cap
    share = recv_ref.shape[1] - 2 * cap
    arrived = recv_ref[:, pl.ds(share, 2 * cap)].astype(F32)
    sides = arrived[:, :cap].reshape(ngx, ngy, cap, width)
    left = lax.broadcasted_iota(I32, sides.shape, 3) < chans
    sides = jnp.where(left, rolled(sides, 1, 0), rolled(sides, -1, 0)).reshape(slots, width)
    middle = arrived[:, cap:].reshape(slots, width)
    counts = counts_ref[...].astype(F32)
    place = lax.broadcasted_iota(I32, (nrows, ndev), 0).astype(F32)
    lane = lax.broadcasted_iota(I32, (ndev, ndev), 1)
    upto = lax.broadcasted_iota(I32, (ndev, ndev), 0) <= lane
    ends = mm(counts.astype(BF16), jnp.where(upto, 1.0, 0.0).astype(BF16))
    before = ends <= place
    owner = jnp.sum(jnp.where(before, 1.0, 0.0), axis=1, keepdims=True)
    start = jnp.sum(jnp.where(before, counts, 0.0), axis=1, keepdims=True)
    slot = owner * cap + place[:, :1] - start
    onehot = jnp.where(
        lax.broadcasted_iota(I32, (nrows, slots), 1).astype(F32) == slot, 1.0, 0.0
    ).astype(BF16)
    proj_t = proj_t_ref[...]
    both = jnp.concatenate([proj_t, proj_t], axis=0)
    sides = mm(onehot, sides.astype(BF16)).astype(BF16)
    middle = mm(onehot, middle.astype(BF16)).astype(BF16)
    rows_ref[...] = mm(sides, both) + mm(middle, both)
    cy = inner_ref.shape[0]
    field = jnp.concatenate([ends_ref[:1], inner_ref[1 : cy - 1], ends_ref[1:]], axis=0)
    out_ref[...] = jnp.swapaxes(field, 0, 1)


def finish_kernel(conv_scale, proj_scale, parity_ref, mine_ref, other_ref, conv_ref, proj_ref, both):
    ndev, part, width = mine_ref.shape
    parity = parity_ref[0]
    both[:, parity] = mine_ref[...]
    both[:, 1 - parity] = other_ref[...]
    sums = both[...].astype(F32).reshape(ndev * 2 * part, width)
    taps, chans, _ = conv_ref.shape
    rows = 9 * chans
    half = rows // 2
    packed = sums[rows : rows + half]
    column = jnp.concatenate([packed[:, :chans], packed[:, chans:]], axis=0)
    for b in range(3):
        for dz in range(3):
            first = (b * 3 + dz) * chans
            block = sums[first : first + chans]
            k = (2 - b) * 3 + dz
            conv_ref[k] = block[:, :chans] * conv_scale
            conv_ref[9 + k] = block[:, chans:] * conv_scale
            conv_ref[18 + k] = column[first : first + chans] * conv_scale
    terms = sums[rows + half : rows + half + 2 * chans].reshape(chans // part, 2, part, width)
    proj_ref[...] = jnp.sum(terms, axis=1).reshape(chans, width) * proj_scale


def local(particles, send_counts, cell_lists, base_field, proj_weight, conv_weight, cotangent):
    ngx, ngy = lax.axis_size("gx"), lax.axis_size("gy")
    ndev = ngx * ngy
    nrows, feats = particles.shape
    chans, cx, cy, nz = base_field.shape
    slots = cell_lists.shape[1]
    cap = slots // ndev
    count = cx * cy * nz
    assert cx == 1 and feats == 2 * chans
    proj_t = proj_weight.T
    move = functools.partial(send, ngx=ngx, ngy=ngy)
    rows = 3 * chans
    one = 2 * rows * rows * nz

    base = base_field.reshape(chans, cy, nz)
    west, east = move(base_field, 1, 0), move(base_field, -1, 0)
    planes = (base, west.reshape(base.shape), east.reshape(base.shape))
    lists = (cell_lists, move(cell_lists, 1, 0), move(cell_lists, -1, 0))
    (payload,) = call(
        functools.partial(first_kernel, ngx, ngy, cap),
        [shape((ndev * 3 * cap, feats), BF16)],
        (particles, send_counts),
        2 * slots * nrows * feats,
        (
            pltpu.VMEM(particles.shape, BF16),
            pltpu.VMEM(send_counts.shape, I32),
            pltpu.SemaphoreType.DMA((2,)),
        ),
        far=range(2),
        limit=ALL,
    )
    recv = exchange(payload, ndev)

    wf, wb, cot = call(
        turns_kernel,
        [shape((9 * chans, rows), BF16)] * 2 + [shape((cy, chans, nz), BF16)],
        (conv_weight, cotangent.reshape(chans, cy, nz)),
        1000,
    )

    first, last, values, hots = call(
        functools.partial(outer_kernel, ndev, cap),
        [shape((rows, nz), BF16)] * 2
        + [shape((3, chans, slots), BF16), shape((3, nz, slots), BF16)],
        (recv, *planes, *lists, proj_t, cot, wf),
        4 * one,
        (pltpu.VMEM((4 * chans, slots), BF16), pltpu.VMEM((4, rows, nz), BF16)),
    )
    south, north = move(first, 0, -1), move(last, 0, 1)
    x_all, out_rows, total, pre_edge, slot_edge, plane = call(
        conv_kernel,
        [
            shape((cy, rows, nz), BF16),
            shape((cy, chans, nz), BF16),
            shape((9 * chans, rows), F32),
            shape((4, chans, nz), F32),
            shape((4, rows, nz), F32),
            shape((3, (cy - 4) * chans, nz), BF16),
        ],
        (values, hots, *planes, *lists, cot, wf, wb),
        3 * cy * 3 * one,
        (
            pltpu.VMEM((cy + 1, rows, nz), F32),
            pltpu.VMEM((cy + 2, rows, nz), BF16),
            pltpu.VMEM((cy, rows, nz), F32),
            pltpu.VMEM((cy * chans, slots), BF16),
        ),
    )
    grad_rows = 27 * chans * chans // feats
    part = -(-(grad_rows + 2 * chans) // (32 * ndev)) * 16
    full = grad_rows // (2 * part)
    assert ngx % 2 == 0 and full * 2 * part == grad_rows
    row = lax.axis_index("gx")
    parity = (row % 2).astype(I32).reshape(1)
    out_edge, grads, keep, give = call(
        functools.partial(edge_kernel, part),
        [
            shape((2, chans, nz), BF16),
            shape((4, rows, nz), BF16),
            shape((full, part, feats), F32),
            shape((full, part, feats), BF16),
        ],
        (parity, pre_edge, total, north, south, x_all, cot),
        6 * one,
        (pltpu.VMEM((9 * chans, rows), F32), pltpu.VMEM((full, 2, part, feats), F32)),
        scalar=(0,),
    )
    got = swap(give)
    back, proj = call(
        functools.partial(slots_kernel, ndev, cap, part, full),
        [shape((ndev, 2 * cap, feats), BF16), shape((ndev - full, part, feats), BF16)],
        (slot_edge, plane, hots, grads, wb, cot, *lists, recv),
        6 * one,
    )
    (payload,) = call(
        pair_kernel,
        [shape((ndev, part + 2 * cap, feats), BF16)],
        (keep, got, back, proj),
        1000,
        (pltpu.VMEM((full, part, feats), BF16), pltpu.SemaphoreType.DMA((3,))),
        far_out=(0,),
    )
    (payload,) = call(same_kernel, [payload], (payload,), 0, far=(0,), far_out=(0,), aliases={0: 0})
    recv = exchange(payload.reshape(-1, feats), ndev).reshape(payload.shape)
    index = (row * ngy + lax.axis_index("gy")).astype(I32).reshape(1, 1)
    (sums,) = call(
        functools.partial(sums_kernel, ngx, ngy, full, cap),
        [shape((ndev, part, feats), BF16)],
        (recv, index),
        1000,
    )
    row_grads, out_field = call(
        functools.partial(rows_kernel, ngx, ngy, cap, chans),
        [shape((nrows, feats), F32), shape((chans, cy, nz), BF16)],
        (recv, send_counts, proj_t, out_rows, out_edge),
        2 * nrows * slots * chans,
    )
    mine = exchange(sums.reshape(-1, feats), ndev).reshape(sums.shape)
    mine, row_grads, out_field = lax.optimization_barrier((mine, row_grads, out_field))
    other = swap(mine)
    conv_grad, proj_grad = call(
        functools.partial(
            finish_kernel, 1.0 / math.sqrt(count * ndev), 1.0 / math.sqrt(nrows * ndev)
        ),
        [shape((27, chans, chans), F32), shape((chans, feats), F32)],
        (parity, mine, other),
        1000,
        (pltpu.VMEM((ndev, 2, part, feats), BF16),),
        scalar=(0,),
    )
    return (out_field[:, None], row_grads, conv_grad, proj_grad.T)


def solution(mesh):
    in_specs = (
        P(("gx", "gy"), None),
        P(("gx", "gy"), None),
        P(("gx", "gy"), None),
        P(None, "gx", "gy", None),
        P(),
        P(),
        P(None, "gx", "gy", None),
    )
    out_specs = (P(None, "gx", "gy", None), P(("gx", "gy"), None), P(), P())
    return jax.shard_map(local, mesh=mesh, in_specs=in_specs, out_specs=out_specs, check_vma=False)
```

```python
import functools
import math

import jax
import jax.numpy as jnp
from jax import lax
from jax.experimental import pallas as pl
from jax.experimental.pallas import tpu as pltpu
from jax.sharding import PartitionSpec as P

AXES = ("gx", "gy")
F32, BF16, I32 = jnp.float32, jnp.bfloat16, jnp.int32
LIMIT = 40 * 1024 * 1024
ALL = 60 * 1024 * 1024
NT = (((1,), (1,)), ((), ()))
NN = (((1,), (0,)), ((), ()))


def mm(a, b, dims=NN):
    return lax.dot_general(a, b, dims, preferred_element_type=F32)


def call(kernel, outs, args, flops, scratch=(), far=(), far_out=(), aliases=None, limit=LIMIT, scalar=()):
    traffic = sum(math.prod(a.shape) * a.dtype.itemsize for a in (*args, *outs))
    near = pl.BlockSpec(memory_space=pltpu.VMEM)
    there = pl.BlockSpec(memory_space=pltpu.HBM)
    return pl.pallas_call(
        kernel,
        out_shape=[jax.ShapeDtypeStruct(o.shape, o.dtype) for o in outs],
        in_specs=[
            pl.BlockSpec(memory_space=pltpu.SMEM) if n in scalar else there if n in far else near
            for n in range(len(args))
        ],
        out_specs=[there if n in far_out else near for n in range(len(outs))],
        scratch_shapes=list(scratch),
        input_output_aliases=aliases or {},
        compiler_params=pltpu.CompilerParams(vmem_limit_bytes=limit),
        cost_estimate=pl.CostEstimate(flops=flops, bytes_accessed=traffic, transcendentals=0),
    )(*args)


def shape(dims, dtype):
    return jax.ShapeDtypeStruct(dims, dtype)


def send(block, di, dj, ngx, ngy):
    pairs = []
    for i in range(ngx):
        for j in range(ngy):
            pairs.append((i * ngy + j, ((i + di) % ngx) * ngy + (j + dj) % ngy))
    return lax.ppermute(block, AXES, pairs)


def swap(block):
    return lax.ppermute(block, "gx", [(i, i ^ 1) for i in range(lax.axis_size("gx"))])


def exchange(payload, ndev):
    rows, width = payload.shape
    moved = lax.all_to_all(
        payload.reshape(ndev, rows // ndev, width), AXES, split_axis=0, concat_axis=0, tiled=True
    )
    return moved.reshape(rows, width)


def rolled(x, di, dj):
    for axis, shift in ((0, di), (1, dj)):
        if shift == 1:
            head, tail = lax.slice_in_dim(x, 1, None, axis=axis), lax.slice_in_dim(x, 0, 1, axis=axis)
            x = jnp.concatenate([head, tail], axis=axis)
        elif shift == -1:
            count = x.shape[axis]
            head = lax.slice_in_dim(x, count - 1, count, axis=axis)
            x = jnp.concatenate([head, lax.slice_in_dim(x, 0, count - 1, axis=axis)], axis=axis)
    return x


def picked_depth(z, nz):
    depth = lax.broadcasted_iota(I32, (nz, z.shape[1]), 0)
    return jnp.where(depth == z, 1.0, 0.0).astype(BF16)


def rows_in(recv_ref, ndev, cap):
    width = recv_ref.shape[1]
    arrived = recv_ref[...].astype(F32).reshape(ndev, 3, cap, width)
    return [arrived[:, n].reshape(ndev * cap, width).astype(BF16) for n in range(3)]


def stacked(grad):
    nz = grad.shape[1]
    wide = grad.astype(F32)
    return jnp.concatenate(
        [pltpu.roll(wide, nz - 1, 1), wide, pltpu.roll(wide, 1, 1)], axis=0
    ).astype(BF16)


def over_depth(acc):
    chans, nz = acc.shape[0] // 3, acc.shape[1]
    total = acc[chans : 2 * chans] + pltpu.roll(acc[:chans], 1, 1)
    return total + pltpu.roll(acc[2 * chans :], nz - 1, 1)


def finish_row(pre, field, cot):
    sig = jax.nn.sigmoid(pre)
    out = field.astype(F32) + pre * sig
    grad = cot.astype(F32) * sig * (1.0 + pre * (1.0 - sig))
    return out.astype(BF16), grad.astype(BF16)


def first_kernel(
    ngx, ngy, cap, rows_far, counts_far, send_ref, rows_ref, counts_ref, sems
):
    copies = [
        pltpu.make_async_copy(rows_far, rows_ref, sems.at[0]),
        pltpu.make_async_copy(counts_far, counts_ref, sems.at[1]),
    ]
    for copy in copies:
        copy.start()
    copies[1].wait()
    pick(ngx, ngy, cap, counts_ref, rows_ref, send_ref, copies[0])


def turns_kernel(weight_ref, cot_ref, wf_ref, wb_ref, cot_out):
    cot_out[...] = jnp.swapaxes(cot_ref[...], 0, 1)
    chans = cot_ref.shape[0]
    three = range(3)
    for dy in three:
        for n in three:
            rows = pl.ds((dy * 3 + n) * chans, chans)
            taps = [weight_ref[dx * 9 + dy * 3 + n] for dx in three]
            wf_ref[rows] = jnp.concatenate(taps, axis=1)
            taps = [weight_ref[n * 9 + dy * 3 + dz].astype(F32).T for dz in three]
            wb_ref[rows] = jnp.concatenate(taps, axis=1).astype(BF16)


def same_kernel(in_ref, out_ref):
    pass


def pick(ngx, ngy, cap, counts_ref, rows_ref, out_ref, rows_copy):
    ndev = ngx * ngy
    nrows, feats = rows_ref.shape
    slots = ndev * cap
    counts = counts_ref[...].astype(F32)
    owner = lax.broadcasted_iota(I32, (ndev, cap, ndev), 0).reshape(slots, ndev)
    lane = lax.broadcasted_iota(I32, (slots, ndev), 1)
    start = jnp.sum(jnp.where(lane < owner, counts, 0.0), axis=1, keepdims=True)
    held = jnp.sum(jnp.where(lane == owner, counts, 0.0), axis=1, keepdims=True)
    place = lax.broadcasted_iota(I32, (ndev, cap, nrows), 1).reshape(slots, nrows).astype(F32)
    row = lax.broadcasted_iota(I32, (slots, nrows), 1).astype(F32)
    onehot = jnp.where((row == place + start) & (place < held), 1.0, 0.0).astype(BF16)
    rows_copy.wait()
    raw = mm(onehot, rows_ref[...]).reshape(ngx, ngy, cap, feats)
    parts = [rolled(raw, dx, 0).reshape(ndev, cap, feats) for dx in (-1, 0, 1)]
    out_ref[...] = jnp.stack(parts, axis=1).reshape(out_ref.shape).astype(BF16)


def painted_rows(values, y, onehot, ns, masked):
    chans = values.shape[0]
    for n, row in enumerate(ns):
        masked[pl.ds(n * chans, chans)] = values * jnp.where(y == row, 1.0, 0.0).astype(BF16)
    return mm(masked[pl.ds(0, len(ns) * chans)], onehot, NT)


def add_to_rows(near, far, cot, back, out_ref):
    chans = cot.shape[0]
    rows = 3 * chans
    at, over = (rows, 0) if back else (0, rows)
    out_ref[pl.ds(0, chans)] = over_depth(near[at : at + rows]).astype(BF16)
    out_ref[pl.ds(chans, chans)] = over_depth(near[over : over + rows] + far).astype(BF16)
    out_ref[pl.ds(2 * chans, chans)] = cot


def outer_kernel(
    ndev, cap, recv_ref, own_ref, west_ref, east_ref, own_cells, west_cells, east_cells,
    proj_t_ref, cot_ref, wf_ref, first_ref, last_ref, values_ref, hot_ref, masked, field,
):
    chans, cy, nz = own_ref.shape
    rows = 3 * chans
    raws = rows_in(recv_ref, ndev, cap)
    ns = (0, 1, cy - 2, cy - 1)
    planes = ((west_ref, west_cells), (own_ref, own_cells), (east_ref, east_cells))
    for dx, (ref, cells_ref) in enumerate(planes):
        values = mm(proj_t_ref[...], raws[dx], NT).astype(BF16)
        y, z = place(cells_ref, nz)
        onehot = picked_depth(z, nz)
        values_ref[dx] = values
        hot_ref[dx] = onehot
        painted = painted_rows(values, y, onehot, ns, masked)
        base = turned(ref)
        for n, row in enumerate(ns):
            part = painted[n * chans : (n + 1) * chans]
            field[n, pl.ds(dx * chans, chans)] = (base[row] + part).astype(BF16)
    near = mm(wf_ref[pl.ds(0, 2 * rows)], field[3])
    add_to_rows(near, mm(wf_ref[pl.ds(0, rows)], field[2]), cot_ref[cy - 1], False, last_ref)
    near = mm(wf_ref[pl.ds(rows, 2 * rows)], field[0])
    add_to_rows(near, mm(wf_ref[pl.ds(2 * rows, rows)], field[1]), cot_ref[0], True, first_ref)


def place(cells_ref, nz):
    cells = cells_ref[...]
    return cells // nz, cells % nz


def turned(ref):
    return jnp.swapaxes(ref[...], 0, 1).astype(F32)


def conv_kernel(
    values_ref, hot_ref, own_ref, west_ref, east_ref, own_cells, west_cells, east_cells,
    cot_ref, wf_ref, wb_ref,
    x_ref, out_ref, total_ref, pre_ref, slot_ref, plane, acc, grads, back, masked,
):
    cy, chans, nz = cot_ref.shape
    rows = 3 * chans
    planes = ((west_ref, west_cells), (own_ref, own_cells), (east_ref, east_cells))
    for dx, (ref, cells_ref) in enumerate(planes):
        y, _ = place(cells_ref, nz)
        painted = painted_rows(values_ref[dx], y, hot_ref[dx], range(cy), masked)
        field = turned(ref) + painted.reshape(cy, chans, nz)
        x_ref[:, pl.ds(dx * chans, chans)] = field.astype(BF16)
    own = pl.ds(chans, chans)
    zeros = jnp.zeros((rows, nz), BF16)
    for t in (0, 1, cy, cy + 1):
        grads[t] = zeros
    out_ref[0] = zeros[:chans]
    out_ref[cy - 1] = zeros[:chans]
    acc[0] = jnp.zeros((rows, nz), F32)

    def spread(n):
        terms = mm(wf_ref[...], x_ref[n])
        acc[n + 1] = terms[:rows]
        acc[n] += terms[rows : 2 * rows]
        return terms[2 * rows :]

    pre_ref[0] = over_depth(spread(0))
    pre_ref[1] = over_depth(acc[0] + spread(1))

    def forward(n):
        done = spread(n) + acc[n - 1]
        y = n - 1
        out, grad = finish_row(over_depth(done), x_ref[y, own], cot_ref[y])
        out_ref[y] = out
        grads[y + 1] = stacked(grad)

    for n in range(2, cy):
        forward(n)
    pre_ref[2] = over_depth(acc[cy - 1])
    pre_ref[3] = over_depth(acc[cy])
    total_ref[...] = jnp.zeros_like(total_ref)
    back[0] = jnp.zeros((rows, nz), F32)
    back[1] = jnp.zeros((rows, nz), F32)

    def taps(n):
        window = grads[pl.ds(n, 3)].reshape(3 * rows, nz)
        total_ref[...] += mm(window, x_ref[n], NT)

    def spread_back(n):
        terms = mm(wb_ref[...], grads[n + 1])
        back[n + 1] = terms[2 * rows :]
        back[n] += terms[rows : 2 * rows]
        return terms[:rows]

    def backward(n):
        taps(n)
        value = spread_back(n) + back[n - 1]
        for dx in range(3):
            part = value[dx * chans : (dx + 1) * chans]
            if dx == 1:
                part = part + cot_ref[n - 1].astype(F32)
            plane[dx, pl.ds((n - 3) * chans, chans)] = part.astype(BF16)

    taps(0)
    taps(1)
    slot_ref[0] = spread_back(1)
    taps(2)
    slot_ref[1] = spread_back(2) + back[1]
    for n in range(3, cy - 1):
        backward(n)
    taps(cy - 1)
    slot_ref[2] = back[cy - 2]
    slot_ref[3] = back[cy - 1]


def at_slots(part, y, onehot, first):
    found = mm(part, onehot)
    chans = found.shape[0] // len(first)
    total = jnp.zeros((chans, found.shape[1]), F32)
    for n, row in enumerate(first):
        total = total + jnp.where(y == row, found[n * chans : (n + 1) * chans], 0.0)
    return total


def edge_kernel(
    part, parity_ref, pre_ref, total_ref, north_ref, south_ref, x_ref, cot_ref,
    out_ref, grads_ref, keep_ref, give_ref, total, sums,
):
    cy, chans, nz = cot_ref.shape
    rows = 3 * chans
    own = pl.ds(chans, chans)
    last = pl.ds(2 * chans, chans)
    cots = (north_ref[last], cot_ref[0], cot_ref[cy - 1], south_ref[last])
    sides = ((north_ref, 1), (north_ref, 0), (south_ref, 0), (south_ref, 1))
    ends = []
    for n, (ref, at) in enumerate(sides):
        pre = pre_ref[n] + ref[pl.ds(at * chans, chans)].astype(F32)
        ends.append(finish_row(pre, x_ref[0 if n < 2 else cy - 1, own], cots[n]))
    out_ref[0], out_ref[1] = ends[1][0], ends[2][0]
    grads = [stacked(grad) for _, grad in ends]
    for n in range(4):
        grads_ref[n] = grads[n]
    top = mm(jnp.concatenate([grads[0], grads[1]], axis=0), x_ref[0], NT)
    bottom = mm(jnp.concatenate([grads[2], grads[3]], axis=0), x_ref[cy - 1], NT)
    here = [pl.ds(n * rows, rows) for n in range(3)]
    total[here[0]] = total_ref[here[0]] + (top[:rows] + mm(grads[1], x_ref[1], NT))
    total[here[1]] = total_ref[here[1]] + (top[rows:] + bottom[:rows])
    total[here[2]] = total_ref[here[2]] + (bottom[rows:] + mm(grads[2], x_ref[cy - 2], NT))
    full, _, width = keep_ref.shape
    half = 3 * rows // 2
    split = 3 * rows // (2 * part)
    sums[pl.ds(0, split)] = total[:, :width].reshape(split, 2, part, width)
    taps = jnp.concatenate([total[pl.ds(0, half), width:], total[pl.ds(half, half), width:]], axis=1)
    sums[pl.ds(split, full - split)] = taps.reshape(full - split, 2, part, width)
    parity = parity_ref[0]
    keep_ref[...] = sums[:, parity]
    give_ref[...] = sums[:, 1 - parity].astype(BF16)


def slots_kernel(
    ndev, cap, part, full, slot_ref, plane_ref, hot_ref, grads_ref, wb_ref, cot_ref,
    own_cells, west_cells, east_cells, recv_ref, slots_ref, proj_ref,
):
    cy, chans, nz = cot_ref.shape
    rows = 3 * chans
    inner = mm(wb_ref[pl.ds(rows, 2 * rows)], grads_ref[1])
    top = slot_ref[0] + inner[:rows] + mm(wb_ref[pl.ds(2 * rows, rows)], grads_ref[0])
    second = slot_ref[1] + inner[rows:]
    inner = mm(wb_ref[pl.ds(0, 2 * rows)], grads_ref[2])
    third = slot_ref[2] + inner[:rows]
    bottom = slot_ref[3] + inner[rows:] + mm(wb_ref[pl.ds(0, rows)], grads_ref[3])
    at = (0, 1, cy - 2, cy - 1)
    found = []
    for dx, cells_ref in enumerate((west_cells, own_cells, east_cells)):
        parts = [value[dx * chans : (dx + 1) * chans] for value in (top, second, third, bottom)]
        if dx == 1:
            parts = [value + cot_ref[n].astype(F32) for value, n in zip(parts, at)]
        parts = [value.astype(BF16) for value in parts]
        terms = jnp.concatenate([plane_ref[dx], *parts], axis=0)
        y, _ = place(cells_ref, nz)
        found.append(at_slots(terms, y, hot_ref[dx], (*range(2, cy - 2), *at)))
    sides = jnp.concatenate([found[0], found[2]], axis=0).T
    middle = jnp.concatenate([found[1], jnp.zeros_like(found[1])], axis=0).T
    width = recv_ref.shape[1]
    back = [sides.reshape(ndev, cap, width), middle.reshape(ndev, cap, width)]
    slots_ref[...] = jnp.concatenate(back, axis=1).astype(BF16)
    raws = rows_in(recv_ref, ndev, cap)
    proj = sum(mm(found[dx].astype(BF16), raws[dx]) for dx in range(3))
    rest = ndev - full
    pad = jnp.zeros((rest * part - chans, width), F32)
    proj = jnp.concatenate([proj, pad], axis=0).reshape(rest, part, width)
    proj_ref[...] = proj.astype(BF16)


def pair_kernel(keep_ref, got_ref, slots_ref, proj_ref, send_far, sums_send, sems):
    full, part, _ = keep_ref.shape
    ndev, back, _ = slots_ref.shape
    pieces = (
        (slots_ref, send_far.at[:, pl.ds(part, back)]),
        (proj_ref, send_far.at[pl.ds(full, ndev - full), pl.ds(0, part)]),
        (sums_send, send_far.at[pl.ds(0, full), pl.ds(0, part)]),
    )
    copies = [pltpu.make_async_copy(src, dst, sems.at[n]) for n, (src, dst) in enumerate(pieces)]
    copies[0].start()
    copies[1].start()
    sums_send[...] = (keep_ref[...] + got_ref[...].astype(F32)).astype(BF16)
    copies[2].start()
    for copy in copies:
        copy.wait()


def sums_kernel(ngx, ngy, full, cap, recv_ref, index_ref, sums_ref):
    ndev, each, width = recv_ref.shape
    part = each - 2 * cap
    terms = recv_ref[:, pl.ds(0, part)].astype(F32).reshape(ngx // 2, 2, ngy, part, width)
    sums = jnp.sum(terms, axis=(0, 2))
    whole = sums[0] + sums[1]
    high = whole.astype(BF16).astype(F32)
    last = jnp.broadcast_to(index_ref[...], whole.shape) >= full
    sums = [
        jnp.where(last, high, sums[0]).astype(BF16),
        jnp.where(last, whole - high, sums[1]).astype(BF16),
    ]
    for n in range(ndev):
        sums_ref[n] = sums[(n // ngy) % 2]


def rows_kernel(
    ngx, ngy, cap, chans, recv_ref, counts_ref, proj_t_ref, inner_ref, ends_ref, rows_ref, out_ref
):
    ndev = ngx * ngy
    nrows = rows_ref.shape[0]
    width = recv_ref.shape[2]
    slots = ndev * cap
    share = recv_ref.shape[1] - 2 * cap
    arrived = recv_ref[:, pl.ds(share, 2 * cap)].astype(F32)
    sides = arrived[:, :cap].reshape(ngx, ngy, cap, width)
    left = lax.broadcasted_iota(I32, sides.shape, 3) < chans
    sides = jnp.where(left, rolled(sides, 1, 0), rolled(sides, -1, 0)).reshape(slots, width)
    middle = arrived[:, cap:].reshape(slots, width)
    counts = counts_ref[...].astype(F32)
    place = lax.broadcasted_iota(I32, (nrows, ndev), 0).astype(F32)
    lane = lax.broadcasted_iota(I32, (ndev, ndev), 1)
    upto = lax.broadcasted_iota(I32, (ndev, ndev), 0) <= lane
    ends = mm(counts.astype(BF16), jnp.where(upto, 1.0, 0.0).astype(BF16))
    before = ends <= place
    owner = jnp.sum(jnp.where(before, 1.0, 0.0), axis=1, keepdims=True)
    start = jnp.sum(jnp.where(before, counts, 0.0), axis=1, keepdims=True)
    slot = owner * cap + place[:, :1] - start
    onehot = jnp.where(
        lax.broadcasted_iota(I32, (nrows, slots), 1).astype(F32) == slot, 1.0, 0.0
    ).astype(BF16)
    proj_t = proj_t_ref[...]
    both = jnp.concatenate([proj_t, proj_t], axis=0)
    sides = mm(onehot, sides.astype(BF16)).astype(BF16)
    middle = mm(onehot, middle.astype(BF16)).astype(BF16)
    rows_ref[...] = mm(sides, both) + mm(middle, both)
    cy = inner_ref.shape[0]
    field = jnp.concatenate([ends_ref[:1], inner_ref[1 : cy - 1], ends_ref[1:]], axis=0)
    out_ref[...] = jnp.swapaxes(field, 0, 1)


def finish_kernel(conv_scale, proj_scale, parity_ref, mine_ref, other_ref, conv_ref, proj_ref, both):
    ndev, part, width = mine_ref.shape
    parity = parity_ref[0]
    both[:, parity] = mine_ref[...]
    both[:, 1 - parity] = other_ref[...]
    sums = both[...].astype(F32).reshape(ndev * 2 * part, width)
    taps, chans, _ = conv_ref.shape
    rows = 9 * chans
    half = rows // 2
    packed = sums[rows : rows + half]
    column = jnp.concatenate([packed[:, :chans], packed[:, chans:]], axis=0)
    for b in range(3):
        for dz in range(3):
            first = (b * 3 + dz) * chans
            block = sums[first : first + chans]
            k = (2 - b) * 3 + dz
            conv_ref[k] = block[:, :chans] * conv_scale
            conv_ref[9 + k] = block[:, chans:] * conv_scale
            conv_ref[18 + k] = column[first : first + chans] * conv_scale
    terms = sums[rows + half : rows + half + 2 * chans].reshape(chans // part, 2, part, width)
    proj_ref[...] = jnp.sum(terms, axis=1).reshape(chans, width) * proj_scale


def local(particles, send_counts, cell_lists, base_field, proj_weight, conv_weight, cotangent):
    ngx, ngy = lax.axis_size("gx"), lax.axis_size("gy")
    ndev = ngx * ngy
    nrows, feats = particles.shape
    chans, cx, cy, nz = base_field.shape
    slots = cell_lists.shape[1]
    cap = slots // ndev
    count = cx * cy * nz
    assert cx == 1 and feats == 2 * chans
    proj_t = proj_weight.T
    move = functools.partial(send, ngx=ngx, ngy=ngy)
    rows = 3 * chans
    one = 2 * rows * rows * nz

    base = base_field.reshape(chans, cy, nz)
    west, east = move(base_field, 1, 0), move(base_field, -1, 0)
    planes = (base, west.reshape(base.shape), east.reshape(base.shape))
    lists = (cell_lists, move(cell_lists, 1, 0), move(cell_lists, -1, 0))
    (payload,) = call(
        functools.partial(first_kernel, ngx, ngy, cap),
        [shape((ndev * 3 * cap, feats), BF16)],
        (particles, send_counts),
        2 * slots * nrows * feats,
        (
            pltpu.VMEM(particles.shape, BF16),
            pltpu.VMEM(send_counts.shape, I32),
            pltpu.SemaphoreType.DMA((2,)),
        ),
        far=range(2),
        limit=ALL,
    )
    recv = exchange(payload, ndev)

    wf, wb, cot = call(
        turns_kernel,
        [shape((9 * chans, rows), BF16)] * 2 + [shape((cy, chans, nz), BF16)],
        (conv_weight, cotangent.reshape(chans, cy, nz)),
        1000,
    )

    first, last, values, hots = call(
        functools.partial(outer_kernel, ndev, cap),
        [shape((rows, nz), BF16)] * 2
        + [shape((3, chans, slots), BF16), shape((3, nz, slots), BF16)],
        (recv, *planes, *lists, proj_t, cot, wf),
        4 * one,
        (pltpu.VMEM((4 * chans, slots), BF16), pltpu.VMEM((4, rows, nz), BF16)),
    )
    south = move(first, 0, -1)
    (last,) = call(same_kernel, [last], (last,), 0, aliases={0: 0})
    north = move(last, 0, 1)
    x_all, out_rows, total, pre_edge, slot_edge, plane = call(
        conv_kernel,
        [
            shape((cy, rows, nz), BF16),
            shape((cy, chans, nz), BF16),
            shape((9 * chans, rows), F32),
            shape((4, chans, nz), F32),
            shape((4, rows, nz), F32),
            shape((3, (cy - 4) * chans, nz), BF16),
        ],
        (values, hots, *planes, *lists, cot, wf, wb),
        3 * cy * 3 * one,
        (
            pltpu.VMEM((cy + 1, rows, nz), F32),
            pltpu.VMEM((cy + 2, rows, nz), BF16),
            pltpu.VMEM((cy, rows, nz), F32),
            pltpu.VMEM((cy * chans, slots), BF16),
        ),
    )
    grad_rows = 27 * chans * chans // feats
    part = -(-(grad_rows + 2 * chans) // (32 * ndev)) * 16
    full = grad_rows // (2 * part)
    assert ngx % 2 == 0 and full * 2 * part == grad_rows
    row = lax.axis_index("gx")
    parity = (row % 2).astype(I32).reshape(1)
    out_edge, grads, keep, give = call(
        functools.partial(edge_kernel, part),
        [
            shape((2, chans, nz), BF16),
            shape((4, rows, nz), BF16),
            shape((full, part, feats), F32),
            shape((full, part, feats), BF16),
        ],
        (parity, pre_edge, total, north, south, x_all, cot),
        6 * one,
        (pltpu.VMEM((9 * chans, rows), F32), pltpu.VMEM((full, 2, part, feats), F32)),
        scalar=(0,),
    )
    got = swap(give)
    back, proj = call(
        functools.partial(slots_kernel, ndev, cap, part, full),
        [shape((ndev, 2 * cap, feats), BF16), shape((ndev - full, part, feats), BF16)],
        (slot_edge, plane, hots, grads, wb, cot, *lists, recv),
        6 * one,
    )
    (payload,) = call(
        pair_kernel,
        [shape((ndev, part + 2 * cap, feats), BF16)],
        (keep, got, back, proj),
        1000,
        (pltpu.VMEM((full, part, feats), BF16), pltpu.SemaphoreType.DMA((3,))),
        far_out=(0,),
    )
    (payload,) = call(same_kernel, [payload], (payload,), 0, far=(0,), far_out=(0,), aliases={0: 0})
    recv = exchange(payload.reshape(-1, feats), ndev).reshape(payload.shape)
    index = (row * ngy + lax.axis_index("gy")).astype(I32).reshape(1, 1)
    (sums,) = call(
        functools.partial(sums_kernel, ngx, ngy, full, cap),
        [shape((ndev, part, feats), BF16)],
        (recv, index),
        1000,
    )
    row_grads, out_field = call(
        functools.partial(rows_kernel, ngx, ngy, cap, chans),
        [shape((nrows, feats), F32), shape((chans, cy, nz), BF16)],
        (recv, send_counts, proj_t, out_rows, out_edge),
        2 * nrows * slots * chans,
    )
    mine = exchange(sums.reshape(-1, feats), ndev).reshape(sums.shape)
    mine, row_grads, out_field = lax.optimization_barrier((mine, row_grads, out_field))
    other = swap(mine)
    conv_grad, proj_grad = call(
        functools.partial(
            finish_kernel, 1.0 / math.sqrt(count * ndev), 1.0 / math.sqrt(nrows * ndev)
        ),
        [shape((27, chans, chans), F32), shape((chans, feats), F32)],
        (parity, mine, other),
        1000,
        (pltpu.VMEM((ndev, 2, part, feats), BF16),),
        scalar=(0,),
    )
    return (out_field[:, None], row_grads, conv_grad, proj_grad.T)


def solution(mesh):
    in_specs = (
        P(("gx", "gy"), None),
        P(("gx", "gy"), None),
        P(("gx", "gy"), None),
        P(None, "gx", "gy", None),
        P(),
        P(),
        P(None, "gx", "gy", None),
    )
    out_specs = (P(None, "gx", "gy", None), P(("gx", "gy"), None), P(), P())
    return jax.shard_map(local, mesh=mesh, in_specs=in_specs, out_specs=out_specs, check_vma=False)
```

```python
import functools
import math

import jax
import jax.numpy as jnp
from jax import lax
from jax.experimental import pallas as pl
from jax.experimental.pallas import tpu as pltpu
from jax.sharding import PartitionSpec as P

AXES = ("gx", "gy")
F32, BF16, I32 = jnp.float32, jnp.bfloat16, jnp.int32
LIMIT = 40 * 1024 * 1024
ALL = 60 * 1024 * 1024
NT = (((1,), (1,)), ((), ()))
NN = (((1,), (0,)), ((), ()))


def mm(a, b, dims=NN):
    return lax.dot_general(a, b, dims, preferred_element_type=F32)


def call(kernel, outs, args, flops, scratch=(), far=(), far_out=(), aliases=None, limit=LIMIT, scalar=()):
    traffic = sum(math.prod(a.shape) * a.dtype.itemsize for a in (*args, *outs))
    near = pl.BlockSpec(memory_space=pltpu.VMEM)
    there = pl.BlockSpec(memory_space=pltpu.HBM)
    return pl.pallas_call(
        kernel,
        out_shape=[jax.ShapeDtypeStruct(o.shape, o.dtype) for o in outs],
        in_specs=[
            pl.BlockSpec(memory_space=pltpu.SMEM) if n in scalar else there if n in far else near
            for n in range(len(args))
        ],
        out_specs=[there if n in far_out else near for n in range(len(outs))],
        scratch_shapes=list(scratch),
        input_output_aliases=aliases or {},
        compiler_params=pltpu.CompilerParams(vmem_limit_bytes=limit),
        cost_estimate=pl.CostEstimate(flops=flops, bytes_accessed=traffic, transcendentals=0),
    )(*args)


def shape(dims, dtype):
    return jax.ShapeDtypeStruct(dims, dtype)


def send(block, di, dj, ngx, ngy):
    pairs = []
    for i in range(ngx):
        for j in range(ngy):
            pairs.append((i * ngy + j, ((i + di) % ngx) * ngy + (j + dj) % ngy))
    return lax.ppermute(block, AXES, pairs)


def swap(block):
    return lax.ppermute(block, "gx", [(i, i ^ 1) for i in range(lax.axis_size("gx"))])


def exchange(payload, ndev):
    rows, width = payload.shape
    moved = lax.all_to_all(
        payload.reshape(ndev, rows // ndev, width), AXES, split_axis=0, concat_axis=0, tiled=True
    )
    return moved.reshape(rows, width)


def rolled(x, di, dj):
    for axis, shift in ((0, di), (1, dj)):
        if shift == 1:
            head, tail = lax.slice_in_dim(x, 1, None, axis=axis), lax.slice_in_dim(x, 0, 1, axis=axis)
            x = jnp.concatenate([head, tail], axis=axis)
        elif shift == -1:
            count = x.shape[axis]
            head = lax.slice_in_dim(x, count - 1, count, axis=axis)
            x = jnp.concatenate([head, lax.slice_in_dim(x, 0, count - 1, axis=axis)], axis=axis)
    return x


def picked_depth(z, nz):
    depth = lax.broadcasted_iota(I32, (nz, z.shape[1]), 0)
    return jnp.where(depth == z, 1.0, 0.0).astype(BF16)


def rows_in(recv_ref, ndev, cap):
    width = recv_ref.shape[1]
    arrived = recv_ref[...].astype(F32).reshape(ndev, 3, cap, width)
    return [arrived[:, n].reshape(ndev * cap, width).astype(BF16) for n in range(3)]


def stacked(grad):
    nz = grad.shape[1]
    wide = grad.astype(F32)
    return jnp.concatenate(
        [pltpu.roll(wide, nz - 1, 1), wide, pltpu.roll(wide, 1, 1)], axis=0
    ).astype(BF16)


def over_depth(acc):
    chans, nz = acc.shape[0] // 3, acc.shape[1]
    total = acc[chans : 2 * chans] + pltpu.roll(acc[:chans], 1, 1)
    return total + pltpu.roll(acc[2 * chans :], nz - 1, 1)


def finish_row(pre, field, cot):
    sig = jax.nn.sigmoid(pre)
    out = field.astype(F32) + pre * sig
    grad = cot.astype(F32) * sig * (1.0 + pre * (1.0 - sig))
    return out.astype(BF16), grad.astype(BF16)


def first_kernel(
    ngx, ngy, cap, rows_far, counts_far, send_ref, rows_ref, counts_ref, sems
):
    copies = [
        pltpu.make_async_copy(rows_far, rows_ref, sems.at[0]),
        pltpu.make_async_copy(counts_far, counts_ref, sems.at[1]),
    ]
    for copy in copies:
        copy.start()
    copies[1].wait()
    pick(ngx, ngy, cap, counts_ref, rows_ref, send_ref, copies[0])


def turns_kernel(weight_ref, cot_ref, wf_ref, wb_ref, cot_out):
    cot_out[...] = jnp.swapaxes(cot_ref[...], 0, 1)
    chans = cot_ref.shape[0]
    three = range(3)
    for dy in three:
        for n in three:
            rows = pl.ds((dy * 3 + n) * chans, chans)
            taps = [weight_ref[dx * 9 + dy * 3 + n] for dx in three]
            wf_ref[rows] = jnp.concatenate(taps, axis=1)
            taps = [weight_ref[n * 9 + dy * 3 + dz].astype(F32).T for dz in three]
            wb_ref[rows] = jnp.concatenate(taps, axis=1).astype(BF16)


def same_kernel(in_ref, out_ref):
    pass


def pick(ngx, ngy, cap, counts_ref, rows_ref, out_ref, rows_copy):
    ndev = ngx * ngy
    nrows, feats = rows_ref.shape
    slots = ndev * cap
    counts = counts_ref[...].astype(F32)
    owner = lax.broadcasted_iota(I32, (ndev, cap, ndev), 0).reshape(slots, ndev)
    lane = lax.broadcasted_iota(I32, (slots, ndev), 1)
    start = jnp.sum(jnp.where(lane < owner, counts, 0.0), axis=1, keepdims=True)
    held = jnp.sum(jnp.where(lane == owner, counts, 0.0), axis=1, keepdims=True)
    place = lax.broadcasted_iota(I32, (ndev, cap, nrows), 1).reshape(slots, nrows).astype(F32)
    row = lax.broadcasted_iota(I32, (slots, nrows), 1).astype(F32)
    onehot = jnp.where((row == place + start) & (place < held), 1.0, 0.0).astype(BF16)
    rows_copy.wait()
    raw = mm(onehot, rows_ref[...]).reshape(ngx, ngy, cap, feats)
    parts = [rolled(raw, dx, 0).reshape(ndev, cap, feats) for dx in (-1, 0, 1)]
    out_ref[...] = jnp.stack(parts, axis=1).reshape(out_ref.shape).astype(BF16)


def painted_rows(values, y, onehot, ns, masked):
    chans = values.shape[0]
    for n, row in enumerate(ns):
        masked[pl.ds(n * chans, chans)] = values * jnp.where(y == row, 1.0, 0.0).astype(BF16)
    return mm(masked[pl.ds(0, len(ns) * chans)], onehot, NT)


def add_to_rows(near, far, cot, back, out_ref):
    chans = cot.shape[0]
    rows = 3 * chans
    at, over = (rows, 0) if back else (0, rows)
    out_ref[pl.ds(0, chans)] = over_depth(near[at : at + rows]).astype(BF16)
    out_ref[pl.ds(chans, chans)] = over_depth(near[over : over + rows] + far).astype(BF16)
    out_ref[pl.ds(2 * chans, chans)] = cot


def outer_kernel(
    ndev, cap, recv_ref, own_ref, west_ref, east_ref, own_cells, west_cells, east_cells,
    proj_t_ref, cot_ref, wf_ref, first_ref, last_ref, values_ref, hot_ref, masked, field,
):
    chans, cy, nz = own_ref.shape
    rows = 3 * chans
    raws = rows_in(recv_ref, ndev, cap)
    ns = (0, 1, cy - 2, cy - 1)
    planes = ((west_ref, west_cells), (own_ref, own_cells), (east_ref, east_cells))
    for dx, (ref, cells_ref) in enumerate(planes):
        values = mm(proj_t_ref[...], raws[dx], NT).astype(BF16)
        y, z = place(cells_ref, nz)
        onehot = picked_depth(z, nz)
        values_ref[dx] = values
        hot_ref[dx] = onehot
        painted = painted_rows(values, y, onehot, ns, masked)
        base = turned(ref)
        for n, row in enumerate(ns):
            part = painted[n * chans : (n + 1) * chans]
            field[n, pl.ds(dx * chans, chans)] = (base[row] + part).astype(BF16)
    near = mm(wf_ref[pl.ds(0, 2 * rows)], field[3])
    add_to_rows(near, mm(wf_ref[pl.ds(0, rows)], field[2]), cot_ref[cy - 1], False, last_ref)
    near = mm(wf_ref[pl.ds(rows, 2 * rows)], field[0])
    add_to_rows(near, mm(wf_ref[pl.ds(2 * rows, rows)], field[1]), cot_ref[0], True, first_ref)


def place(cells_ref, nz):
    cells = cells_ref[...]
    return cells // nz, cells % nz


def turned(ref):
    return jnp.swapaxes(ref[...], 0, 1).astype(F32)


def conv_kernel(
    values_ref, hot_ref, own_ref, west_ref, east_ref, own_cells, west_cells, east_cells,
    cot_ref, wf_ref, wb_ref,
    x_ref, out_ref, total_ref, pre_ref, slot_ref, plane, grads, acc, back, masked,
):
    cy, chans, nz = cot_ref.shape
    rows = 3 * chans
    planes = ((west_ref, west_cells), (own_ref, own_cells), (east_ref, east_cells))
    for dx, (ref, cells_ref) in enumerate(planes):
        y, _ = place(cells_ref, nz)
        painted = painted_rows(values_ref[dx], y, hot_ref[dx], range(cy), masked)
        field = turned(ref) + painted.reshape(cy, chans, nz)
        x_ref[:, pl.ds(dx * chans, chans)] = field.astype(BF16)
    own = pl.ds(chans, chans)
    zeros = jnp.zeros((rows, nz), BF16)
    for t in (0, 1, cy, cy + 1):
        grads[t] = zeros
    out_ref[0] = zeros[:chans]
    out_ref[cy - 1] = zeros[:chans]
    acc[0] = jnp.zeros((rows, nz), F32)

    def spread(n):
        terms = mm(wf_ref[...], x_ref[n])
        acc[n + 1] = terms[:rows]
        acc[n] += terms[rows : 2 * rows]
        return terms[2 * rows :]

    pre_ref[0] = over_depth(spread(0))
    pre_ref[1] = over_depth(acc[0] + spread(1))

    def forward(n):
        done = spread(n) + acc[n - 1]
        y = n - 1
        out, grad = finish_row(over_depth(done), x_ref[y, own], cot_ref[y])
        out_ref[y] = out
        grads[y + 1] = stacked(grad)

    for n in range(2, cy):
        forward(n)
    pre_ref[2] = over_depth(acc[cy - 1])
    pre_ref[3] = over_depth(acc[cy])
    total_ref[...] = jnp.zeros_like(total_ref)
    back[0] = jnp.zeros((rows, nz), F32)
    back[1] = jnp.zeros((rows, nz), F32)

    def taps(n):
        window = grads[pl.ds(n, 3)].reshape(3 * rows, nz)
        total_ref[...] += mm(window, x_ref[n], NT)

    def spread_back(n):
        terms = mm(wb_ref[...], grads[n + 1])
        back[n + 1] = terms[2 * rows :]
        back[n] += terms[rows : 2 * rows]
        return terms[:rows]

    def backward(n):
        taps(n)
        value = spread_back(n) + back[n - 1]
        for dx in range(3):
            part = value[dx * chans : (dx + 1) * chans]
            if dx == 1:
                part = part + cot_ref[n - 1].astype(F32)
            plane[dx, pl.ds((n - 3) * chans, chans)] = part.astype(BF16)

    taps(0)
    taps(1)
    slot_ref[0] = spread_back(1)
    taps(2)
    slot_ref[1] = spread_back(2) + back[1]
    late = plane.shape[1] // chans + 2
    for n in range(3, late + 1):
        backward(n)
    for n in range(late + 1, cy):
        taps(n)
    slot_ref[2] = back[late]
    slot_ref[3] = back[late + 1]


def at_slots(part, y, onehot, first):
    found = mm(part, onehot)
    chans = found.shape[0] // len(first)
    total = jnp.zeros((chans, found.shape[1]), F32)
    for n, row in enumerate(first):
        total = total + jnp.where(y == row, found[n * chans : (n + 1) * chans], 0.0)
    return total


def edge_kernel(
    part, parity_ref, pre_ref, total_ref, north_ref, south_ref, x_ref, cot_ref,
    out_ref, grads_ref, keep_ref, give_ref, total, sums,
):
    cy, chans, nz = cot_ref.shape
    rows = 3 * chans
    own = pl.ds(chans, chans)
    last = pl.ds(2 * chans, chans)
    cots = (north_ref[last], cot_ref[0], cot_ref[cy - 1], south_ref[last])
    sides = ((north_ref, 1), (north_ref, 0), (south_ref, 0), (south_ref, 1))
    ends = []
    for n, (ref, at) in enumerate(sides):
        pre = pre_ref[n] + ref[pl.ds(at * chans, chans)].astype(F32)
        ends.append(finish_row(pre, x_ref[0 if n < 2 else cy - 1, own], cots[n]))
    out_ref[0], out_ref[1] = ends[1][0], ends[2][0]
    grads = [stacked(grad) for _, grad in ends]
    for n in range(4):
        grads_ref[n] = grads[n]
    top = mm(jnp.concatenate([grads[0], grads[1]], axis=0), x_ref[0], NT)
    bottom = mm(jnp.concatenate([grads[2], grads[3]], axis=0), x_ref[cy - 1], NT)
    here = [pl.ds(n * rows, rows) for n in range(3)]
    total[here[0]] = total_ref[here[0]] + (top[:rows] + mm(grads[1], x_ref[1], NT))
    total[here[1]] = total_ref[here[1]] + (top[rows:] + bottom[:rows])
    total[here[2]] = total_ref[here[2]] + (bottom[rows:] + mm(grads[2], x_ref[cy - 2], NT))
    full, _, width = keep_ref.shape
    half = 3 * rows // 2
    split = 3 * rows // (2 * part)
    sums[pl.ds(0, split)] = total[:, :width].reshape(split, 2, part, width)
    taps = jnp.concatenate([total[pl.ds(0, half), width:], total[pl.ds(half, half), width:]], axis=1)
    sums[pl.ds(split, full - split)] = taps.reshape(full - split, 2, part, width)
    parity = parity_ref[0]
    keep_ref[...] = sums[:, parity]
    give_ref[...] = sums[:, 1 - parity].astype(BF16)


def slots_kernel(
    ndev, cap, part, full, slot_ref, plane_ref, inner_ref, hot_ref, grads_ref, wb_ref, cot_ref,
    own_cells, west_cells, east_cells, recv_ref, slots_ref, proj_ref,
):
    cy, chans, nz = cot_ref.shape
    rows = 3 * chans
    inner = mm(wb_ref[pl.ds(rows, 2 * rows)], grads_ref[1])
    top = slot_ref[0] + inner[:rows] + mm(wb_ref[pl.ds(2 * rows, rows)], grads_ref[0])
    second = slot_ref[1] + inner[rows:]
    late = plane_ref.shape[1] // chans + 2
    third, bottom = slot_ref[2], slot_ref[3]
    values = {}
    for n in range(late + 1, cy - 1):
        terms = mm(wb_ref[...], inner_ref[n + 1])
        values[n - 1] = third + terms[:rows]
        third, bottom = bottom + terms[rows : 2 * rows], terms[2 * rows :]
    inner = mm(wb_ref[pl.ds(0, 2 * rows)], grads_ref[2])
    third = third + inner[:rows]
    bottom = bottom + inner[rows:] + mm(wb_ref[pl.ds(0, rows)], grads_ref[3])
    values.update({0: top, 1: second, cy - 2: third, cy - 1: bottom})
    found = []
    for dx, cells_ref in enumerate((west_cells, own_cells, east_cells)):
        parts = [value[dx * chans : (dx + 1) * chans] for value in values.values()]
        if dx == 1:
            parts = [part + cot_ref[n].astype(F32) for part, n in zip(parts, values)]
        parts = [part.astype(BF16) for part in parts]
        terms = jnp.concatenate([plane_ref[dx], *parts], axis=0)
        y, _ = place(cells_ref, nz)
        found.append(at_slots(terms, y, hot_ref[dx], (*range(2, late), *values)))
    sides = jnp.concatenate([found[0], found[2]], axis=0).T
    middle = jnp.concatenate([found[1], jnp.zeros_like(found[1])], axis=0).T
    width = recv_ref.shape[1]
    back = [sides.reshape(ndev, cap, width), middle.reshape(ndev, cap, width)]
    slots_ref[...] = jnp.concatenate(back, axis=1).astype(BF16)
    raws = rows_in(recv_ref, ndev, cap)
    proj = sum(mm(found[dx].astype(BF16), raws[dx]) for dx in range(3))
    rest = ndev - full
    pad = jnp.zeros((rest * part - chans, width), F32)
    proj = jnp.concatenate([proj, pad], axis=0).reshape(rest, part, width)
    proj_ref[...] = proj.astype(BF16)


def pair_kernel(keep_ref, got_ref, slots_ref, proj_ref, send_far, sums_send, sems):
    full, part, _ = keep_ref.shape
    ndev, back, _ = slots_ref.shape
    pieces = (
        (slots_ref, send_far.at[:, pl.ds(part, back)]),
        (proj_ref, send_far.at[pl.ds(full, ndev - full), pl.ds(0, part)]),
        (sums_send, send_far.at[pl.ds(0, full), pl.ds(0, part)]),
    )
    copies = [pltpu.make_async_copy(src, dst, sems.at[n]) for n, (src, dst) in enumerate(pieces)]
    copies[0].start()
    copies[1].start()
    sums_send[...] = (keep_ref[...] + got_ref[...].astype(F32)).astype(BF16)
    copies[2].start()
    for copy in copies:
        copy.wait()


def sums_kernel(ngx, ngy, full, cap, recv_ref, index_ref, sums_ref):
    ndev, each, width = recv_ref.shape
    part = each - 2 * cap
    terms = recv_ref[:, pl.ds(0, part)].astype(F32).reshape(ngx // 2, 2, ngy, part, width)
    sums = jnp.sum(terms, axis=(0, 2))
    whole = sums[0] + sums[1]
    high = whole.astype(BF16).astype(F32)
    last = jnp.broadcast_to(index_ref[...], whole.shape) >= full
    sums = [
        jnp.where(last, high, sums[0]).astype(BF16),
        jnp.where(last, whole - high, sums[1]).astype(BF16),
    ]
    for n in range(ndev):
        sums_ref[n] = sums[(n // ngy) % 2]


def rows_kernel(
    ngx, ngy, cap, chans, recv_ref, counts_ref, proj_t_ref, inner_ref, ends_ref, rows_ref, out_ref
):
    ndev = ngx * ngy
    nrows = rows_ref.shape[0]
    width = recv_ref.shape[2]
    slots = ndev * cap
    share = recv_ref.shape[1] - 2 * cap
    arrived = recv_ref[:, pl.ds(share, 2 * cap)].astype(F32)
    sides = arrived[:, :cap].reshape(ngx, ngy, cap, width)
    left = lax.broadcasted_iota(I32, sides.shape, 3) < chans
    sides = jnp.where(left, rolled(sides, 1, 0), rolled(sides, -1, 0)).reshape(slots, width)
    middle = arrived[:, cap:].reshape(slots, width)
    counts = counts_ref[...].astype(F32)
    place = lax.broadcasted_iota(I32, (nrows, ndev), 0).astype(F32)
    lane = lax.broadcasted_iota(I32, (ndev, ndev), 1)
    upto = lax.broadcasted_iota(I32, (ndev, ndev), 0) <= lane
    ends = mm(counts.astype(BF16), jnp.where(upto, 1.0, 0.0).astype(BF16))
    before = ends <= place
    owner = jnp.sum(jnp.where(before, 1.0, 0.0), axis=1, keepdims=True)
    start = jnp.sum(jnp.where(before, counts, 0.0), axis=1, keepdims=True)
    slot = owner * cap + place[:, :1] - start
    onehot = jnp.where(
        lax.broadcasted_iota(I32, (nrows, slots), 1).astype(F32) == slot, 1.0, 0.0
    ).astype(BF16)
    proj_t = proj_t_ref[...]
    both = jnp.concatenate([proj_t, proj_t], axis=0)
    sides = mm(onehot, sides.astype(BF16)).astype(BF16)
    middle = mm(onehot, middle.astype(BF16)).astype(BF16)
    rows_ref[...] = mm(sides, both) + mm(middle, both)
    cy = inner_ref.shape[0]
    field = jnp.concatenate([ends_ref[:1], inner_ref[1 : cy - 1], ends_ref[1:]], axis=0)
    out_ref[...] = jnp.swapaxes(field, 0, 1)


def finish_kernel(conv_scale, proj_scale, parity_ref, mine_ref, other_ref, conv_ref, proj_ref, both):
    ndev, part, width = mine_ref.shape
    parity = parity_ref[0]
    both[:, parity] = mine_ref[...]
    both[:, 1 - parity] = other_ref[...]
    sums = both[...].astype(F32).reshape(ndev * 2 * part, width)
    taps, chans, _ = conv_ref.shape
    rows = 9 * chans
    half = rows // 2
    packed = sums[rows : rows + half]
    column = jnp.concatenate([packed[:, :chans], packed[:, chans:]], axis=0)
    for b in range(3):
        for dz in range(3):
            first = (b * 3 + dz) * chans
            block = sums[first : first + chans]
            k = (2 - b) * 3 + dz
            conv_ref[k] = block[:, :chans] * conv_scale
            conv_ref[9 + k] = block[:, chans:] * conv_scale
            conv_ref[18 + k] = column[first : first + chans] * conv_scale
    terms = sums[rows + half : rows + half + 2 * chans].reshape(chans // part, 2, part, width)
    proj_ref[...] = jnp.sum(terms, axis=1).reshape(chans, width) * proj_scale


def local(particles, send_counts, cell_lists, base_field, proj_weight, conv_weight, cotangent):
    ngx, ngy = lax.axis_size("gx"), lax.axis_size("gy")
    ndev = ngx * ngy
    nrows, feats = particles.shape
    chans, cx, cy, nz = base_field.shape
    slots = cell_lists.shape[1]
    cap = slots // ndev
    count = cx * cy * nz
    assert cx == 1 and feats == 2 * chans
    proj_t = proj_weight.T
    move = functools.partial(send, ngx=ngx, ngy=ngy)
    rows = 3 * chans
    one = 2 * rows * rows * nz

    base = base_field.reshape(chans, cy, nz)
    west, east = move(base_field, 1, 0), move(base_field, -1, 0)
    planes = (base, west.reshape(base.shape), east.reshape(base.shape))
    lists = (cell_lists, move(cell_lists, 1, 0), move(cell_lists, -1, 0))
    (payload,) = call(
        functools.partial(first_kernel, ngx, ngy, cap),
        [shape((ndev * 3 * cap, feats), BF16)],
        (particles, send_counts),
        2 * slots * nrows * feats,
        (
            pltpu.VMEM(particles.shape, BF16),
            pltpu.VMEM(send_counts.shape, I32),
            pltpu.SemaphoreType.DMA((2,)),
        ),
        far=range(2),
        limit=ALL,
    )
    recv = exchange(payload, ndev)

    wf, wb, cot = call(
        turns_kernel,
        [shape((9 * chans, rows), BF16)] * 2 + [shape((cy, chans, nz), BF16)],
        (conv_weight, cotangent.reshape(chans, cy, nz)),
        1000,
    )

    first, last, values, hots = call(
        functools.partial(outer_kernel, ndev, cap),
        [shape((rows, nz), BF16)] * 2
        + [shape((3, chans, slots), BF16), shape((3, nz, slots), BF16)],
        (recv, *planes, *lists, proj_t, cot, wf),
        4 * one,
        (pltpu.VMEM((4 * chans, slots), BF16), pltpu.VMEM((4, rows, nz), BF16)),
    )
    south, north = move(first, 0, -1), move(last, 0, 1)
    late = cy // 2 + 1
    x_all, out_rows, total, pre_edge, slot_edge, plane, inner = call(
        conv_kernel,
        [
            shape((cy, rows, nz), BF16),
            shape((cy, chans, nz), BF16),
            shape((9 * chans, rows), F32),
            shape((4, chans, nz), F32),
            shape((4, rows, nz), F32),
            shape((3, (late - 2) * chans, nz), BF16),
            shape((cy + 2, rows, nz), BF16),
        ],
        (values, hots, *planes, *lists, cot, wf, wb),
        3 * cy * 3 * one,
        (
            pltpu.VMEM((cy + 1, rows, nz), F32),
            pltpu.VMEM((cy, rows, nz), F32),
            pltpu.VMEM((cy * chans, slots), BF16),
        ),
    )
    grad_rows = 27 * chans * chans // feats
    part = -(-(grad_rows + 2 * chans) // (32 * ndev)) * 16
    full = grad_rows // (2 * part)
    assert ngx % 2 == 0 and full * 2 * part == grad_rows
    row = lax.axis_index("gx")
    parity = (row % 2).astype(I32).reshape(1)
    out_edge, grads, keep, give = call(
        functools.partial(edge_kernel, part),
        [
            shape((2, chans, nz), BF16),
            shape((4, rows, nz), BF16),
            shape((full, part, feats), F32),
            shape((full, part, feats), BF16),
        ],
        (parity, pre_edge, total, north, south, x_all, cot),
        6 * one,
        (pltpu.VMEM((9 * chans, rows), F32), pltpu.VMEM((full, 2, part, feats), F32)),
        scalar=(0,),
    )
    got = swap(give)
    back, proj = call(
        functools.partial(slots_kernel, ndev, cap, part, full),
        [shape((ndev, 2 * cap, feats), BF16), shape((ndev - full, part, feats), BF16)],
        (slot_edge, plane, inner, hots, grads, wb, cot, *lists, recv),
        6 * one,
    )
    (payload,) = call(
        pair_kernel,
        [shape((ndev, part + 2 * cap, feats), BF16)],
        (keep, got, back, proj),
        1000,
        (pltpu.VMEM((full, part, feats), BF16), pltpu.SemaphoreType.DMA((3,))),
        far_out=(0,),
    )
    (payload,) = call(same_kernel, [payload], (payload,), 0, far=(0,), far_out=(0,), aliases={0: 0})
    recv = exchange(payload.reshape(-1, feats), ndev).reshape(payload.shape)
    index = (row * ngy + lax.axis_index("gy")).astype(I32).reshape(1, 1)
    (sums,) = call(
        functools.partial(sums_kernel, ngx, ngy, full, cap),
        [shape((ndev, part, feats), BF16)],
        (recv, index),
        1000,
    )
    row_grads, out_field = call(
        functools.partial(rows_kernel, ngx, ngy, cap, chans),
        [shape((nrows, feats), F32), shape((chans, cy, nz), BF16)],
        (recv, send_counts, proj_t, out_rows, out_edge),
        2 * nrows * slots * chans,
    )
    mine = exchange(sums.reshape(-1, feats), ndev).reshape(sums.shape)
    mine, row_grads, out_field = lax.optimization_barrier((mine, row_grads, out_field))
    other = swap(mine)
    conv_grad, proj_grad = call(
        functools.partial(
            finish_kernel, 1.0 / math.sqrt(count * ndev), 1.0 / math.sqrt(nrows * ndev)
        ),
        [shape((27, chans, chans), F32), shape((chans, feats), F32)],
        (parity, mine, other),
        1000,
        (pltpu.VMEM((ndev, 2, part, feats), BF16),),
        scalar=(0,),
    )
    return (out_field[:, None], row_grads, conv_grad, proj_grad.T)


def solution(mesh):
    in_specs = (
        P(("gx", "gy"), None),
        P(("gx", "gy"), None),
        P(("gx", "gy"), None),
        P(None, "gx", "gy", None),
        P(),
        P(),
        P(None, "gx", "gy", None),
    )
    out_specs = (P(None, "gx", "gy", None), P(("gx", "gy"), None), P(), P())
    return jax.shard_map(local, mesh=mesh, in_specs=in_specs, out_specs=out_specs, check_vma=False)
```

```python
import functools
import math

import jax
import jax.numpy as jnp
from jax import lax
from jax.experimental import pallas as pl
from jax.experimental.pallas import tpu as pltpu
from jax.sharding import PartitionSpec as P

AXES = ("gx", "gy")
F32, BF16, I32 = jnp.float32, jnp.bfloat16, jnp.int32
LIMIT = 40 * 1024 * 1024
ALL = 60 * 1024 * 1024
NT = (((1,), (1,)), ((), ()))
NN = (((1,), (0,)), ((), ()))


def mm(a, b, dims=NN):
    return lax.dot_general(a, b, dims, preferred_element_type=F32)


def call(kernel, outs, args, flops, scratch=(), far=(), far_out=(), aliases=None, limit=LIMIT, scalar=()):
    traffic = sum(math.prod(a.shape) * a.dtype.itemsize for a in (*args, *outs))
    near = pl.BlockSpec(memory_space=pltpu.VMEM)
    there = pl.BlockSpec(memory_space=pltpu.HBM)
    return pl.pallas_call(
        kernel,
        out_shape=[jax.ShapeDtypeStruct(o.shape, o.dtype) for o in outs],
        in_specs=[
            pl.BlockSpec(memory_space=pltpu.SMEM) if n in scalar else there if n in far else near
            for n in range(len(args))
        ],
        out_specs=[there if n in far_out else near for n in range(len(outs))],
        scratch_shapes=list(scratch),
        input_output_aliases=aliases or {},
        compiler_params=pltpu.CompilerParams(vmem_limit_bytes=limit),
        cost_estimate=pl.CostEstimate(flops=flops, bytes_accessed=traffic, transcendentals=0),
    )(*args)


def shape(dims, dtype):
    return jax.ShapeDtypeStruct(dims, dtype)


def send(block, di, dj, ngx, ngy):
    pairs = []
    for i in range(ngx):
        for j in range(ngy):
            pairs.append((i * ngy + j, ((i + di) % ngx) * ngy + (j + dj) % ngy))
    return lax.ppermute(block, AXES, pairs)


def swap(block):
    return lax.ppermute(block, "gx", [(i, i ^ 1) for i in range(lax.axis_size("gx"))])


def exchange(payload, ndev):
    rows, width = payload.shape
    moved = lax.all_to_all(
        payload.reshape(ndev, rows // ndev, width), AXES, split_axis=0, concat_axis=0, tiled=True
    )
    return moved.reshape(rows, width)


def rolled(x, di, dj):
    for axis, shift in ((0, di), (1, dj)):
        if shift == 1:
            head, tail = lax.slice_in_dim(x, 1, None, axis=axis), lax.slice_in_dim(x, 0, 1, axis=axis)
            x = jnp.concatenate([head, tail], axis=axis)
        elif shift == -1:
            count = x.shape[axis]
            head = lax.slice_in_dim(x, count - 1, count, axis=axis)
            x = jnp.concatenate([head, lax.slice_in_dim(x, 0, count - 1, axis=axis)], axis=axis)
    return x


def picked_depth(z, nz):
    depth = lax.broadcasted_iota(I32, (nz, z.shape[1]), 0)
    return jnp.where(depth == z, 1.0, 0.0).astype(BF16)


def rows_in(recv_ref, ndev, cap):
    width = recv_ref.shape[1]
    arrived = recv_ref[...].astype(F32).reshape(ndev, 3, cap, width)
    return [arrived[:, n].reshape(ndev * cap, width).astype(BF16) for n in range(3)]


def stacked(grad):
    nz = grad.shape[1]
    wide = grad.astype(F32)
    return jnp.concatenate(
        [pltpu.roll(wide, nz - 1, 1), wide, pltpu.roll(wide, 1, 1)], axis=0
    ).astype(BF16)


def over_depth(acc):
    chans, nz = acc.shape[0] // 3, acc.shape[1]
    total = acc[chans : 2 * chans] + pltpu.roll(acc[:chans], 1, 1)
    return total + pltpu.roll(acc[2 * chans :], nz - 1, 1)


def finish_row(pre, field, cot):
    sig = jax.nn.sigmoid(pre)
    out = field.astype(F32) + pre * sig
    grad = cot.astype(F32) * sig * (1.0 + pre * (1.0 - sig))
    return out.astype(BF16), grad.astype(BF16)


def first_kernel(
    ngx, ngy, cap, rows_far, counts_far, send_ref, rows_ref, counts_ref, sems
):
    copies = [
        pltpu.make_async_copy(rows_far, rows_ref, sems.at[0]),
        pltpu.make_async_copy(counts_far, counts_ref, sems.at[1]),
    ]
    for copy in copies:
        copy.start()
    copies[1].wait()
    pick(ngx, ngy, cap, counts_ref, rows_ref, send_ref, copies[0])


def turns_kernel(weight_ref, cot_ref, wf_ref, wb_ref, cot_out):
    cot_out[...] = jnp.swapaxes(cot_ref[...], 0, 1)
    chans = cot_ref.shape[0]
    three = range(3)
    for dy in three:
        for n in three:
            rows = pl.ds((dy * 3 + n) * chans, chans)
            taps = [weight_ref[dx * 9 + dy * 3 + n] for dx in three]
            wf_ref[rows] = jnp.concatenate(taps, axis=1)
            taps = [weight_ref[n * 9 + dy * 3 + dz].astype(F32).T for dz in three]
            wb_ref[rows] = jnp.concatenate(taps, axis=1).astype(BF16)


def same_kernel(in_ref, out_ref):
    pass


def pick(ngx, ngy, cap, counts_ref, rows_ref, out_ref, rows_copy):
    ndev = ngx * ngy
    nrows, feats = rows_ref.shape
    slots = ndev * cap
    counts = counts_ref[...].astype(F32)
    owner = lax.broadcasted_iota(I32, (ndev, cap, ndev), 0).reshape(slots, ndev)
    lane = lax.broadcasted_iota(I32, (slots, ndev), 1)
    start = jnp.sum(jnp.where(lane < owner, counts, 0.0), axis=1, keepdims=True)
    held = jnp.sum(jnp.where(lane == owner, counts, 0.0), axis=1, keepdims=True)
    place = lax.broadcasted_iota(I32, (ndev, cap, nrows), 1).reshape(slots, nrows).astype(F32)
    row = lax.broadcasted_iota(I32, (slots, nrows), 1).astype(F32)
    onehot = jnp.where((row == place + start) & (place < held), 1.0, 0.0).astype(BF16)
    rows_copy.wait()
    raw = mm(onehot, rows_ref[...]).reshape(ngx, ngy, cap, feats)
    parts = [rolled(raw, dx, 0).reshape(ndev, cap, feats) for dx in (-1, 0, 1)]
    out_ref[...] = jnp.stack(parts, axis=1).reshape(out_ref.shape).astype(BF16)


def painted_rows(values, y, onehot, ns, masked):
    chans = values.shape[0]
    for n, row in enumerate(ns):
        masked[pl.ds(n * chans, chans)] = values * jnp.where(y == row, 1.0, 0.0).astype(BF16)
    return mm(masked[pl.ds(0, len(ns) * chans)], onehot, NT)


def add_to_rows(near, far, cot, back, out_ref):
    chans = cot.shape[0]
    rows = 3 * chans
    at, over = (rows, 0) if back else (0, rows)
    out_ref[pl.ds(0, chans)] = over_depth(near[at : at + rows]).astype(BF16)
    out_ref[pl.ds(chans, chans)] = over_depth(near[over : over + rows] + far).astype(BF16)
    out_ref[pl.ds(2 * chans, chans)] = cot


def planes_kernel(
    own_ref, west_ref, east_ref, own_cells, west_cells, east_cells, turned_ref, hot_ref
):
    planes = ((west_ref, west_cells), (own_ref, own_cells), (east_ref, east_cells))
    for dx, (ref, cells_ref) in enumerate(planes):
        turned_ref[dx] = jnp.swapaxes(ref[...], 0, 1)
        _, z = place(cells_ref, ref.shape[2])
        hot_ref[dx] = picked_depth(z, ref.shape[2])


def outer_kernel(
    ndev, cap, recv_ref, turned_ref, hot_ref, own_cells, west_cells, east_cells,
    proj_t_ref, cot_ref, wf_ref, first_ref, last_ref, values_ref, masked, field,
):
    cy, chans, nz = cot_ref.shape
    rows = 3 * chans
    raws = rows_in(recv_ref, ndev, cap)
    ns = (0, 1, cy - 2, cy - 1)
    for dx, cells_ref in enumerate((west_cells, own_cells, east_cells)):
        values = mm(proj_t_ref[...], raws[dx], NT).astype(BF16)
        y, _ = place(cells_ref, nz)
        values_ref[dx] = values
        painted = painted_rows(values, y, hot_ref[dx], ns, masked)
        for n, row in enumerate(ns):
            part = painted[n * chans : (n + 1) * chans]
            base = turned_ref[dx, row].astype(F32)
            field[n, pl.ds(dx * chans, chans)] = (base + part).astype(BF16)
    near = mm(wf_ref[pl.ds(0, 2 * rows)], field[3])
    add_to_rows(near, mm(wf_ref[pl.ds(0, rows)], field[2]), cot_ref[cy - 1], False, last_ref)
    near = mm(wf_ref[pl.ds(rows, 2 * rows)], field[0])
    add_to_rows(near, mm(wf_ref[pl.ds(2 * rows, rows)], field[1]), cot_ref[0], True, first_ref)


def place(cells_ref, nz):
    cells = cells_ref[...]
    return cells // nz, cells % nz


def conv_kernel(
    values_ref, hot_ref, turned_ref, own_cells, west_cells, east_cells, cot_ref, wf_ref, wb_ref,
    x_ref, out_ref, total_ref, pre_ref, slot_ref, plane, acc, grads, back, masked,
):
    cy, chans, nz = cot_ref.shape
    rows = 3 * chans
    for dx, cells_ref in enumerate((west_cells, own_cells, east_cells)):
        y, _ = place(cells_ref, nz)
        painted = painted_rows(values_ref[dx], y, hot_ref[dx], range(cy), masked)
        field = turned_ref[dx].astype(F32) + painted.reshape(cy, chans, nz)
        x_ref[:, pl.ds(dx * chans, chans)] = field.astype(BF16)
    own = pl.ds(chans, chans)
    zeros = jnp.zeros((rows, nz), BF16)
    for t in (0, 1, cy, cy + 1):
        grads[t] = zeros
    out_ref[0] = zeros[:chans]
    out_ref[cy - 1] = zeros[:chans]
    acc[0] = jnp.zeros((rows, nz), F32)

    def spread(n):
        terms = mm(wf_ref[...], x_ref[n])
        acc[n + 1] = terms[:rows]
        acc[n] += terms[rows : 2 * rows]
        return terms[2 * rows :]

    pre_ref[0] = over_depth(spread(0))
    pre_ref[1] = over_depth(acc[0] + spread(1))

    def forward(n):
        done = spread(n) + acc[n - 1]
        y = n - 1
        out, grad = finish_row(over_depth(done), x_ref[y, own], cot_ref[y])
        out_ref[y] = out
        grads[y + 1] = stacked(grad)

    for n in range(2, cy):
        forward(n)
    pre_ref[2] = over_depth(acc[cy - 1])
    pre_ref[3] = over_depth(acc[cy])
    total_ref[...] = jnp.zeros_like(total_ref)
    back[0] = jnp.zeros((rows, nz), F32)
    back[1] = jnp.zeros((rows, nz), F32)

    def taps(n):
        window = grads[pl.ds(n, 3)].reshape(3 * rows, nz)
        total_ref[...] += mm(window, x_ref[n], NT)

    def spread_back(n):
        terms = mm(wb_ref[...], grads[n + 1])
        back[n + 1] = terms[2 * rows :]
        back[n] += terms[rows : 2 * rows]
        return terms[:rows]

    def backward(n):
        taps(n)
        value = spread_back(n) + back[n - 1]
        for dx in range(3):
            part = value[dx * chans : (dx + 1) * chans]
            if dx == 1:
                part = part + cot_ref[n - 1].astype(F32)
            plane[dx, pl.ds((n - 3) * chans, chans)] = part.astype(BF16)

    taps(0)
    taps(1)
    slot_ref[0] = spread_back(1)
    taps(2)
    slot_ref[1] = spread_back(2) + back[1]
    for n in range(3, cy - 1):
        backward(n)
    taps(cy - 1)
    slot_ref[2] = back[cy - 2]
    slot_ref[3] = back[cy - 1]


def at_slots(part, y, onehot, first):
    found = mm(part, onehot)
    chans = found.shape[0] // len(first)
    total = jnp.zeros((chans, found.shape[1]), F32)
    for n, row in enumerate(first):
        total = total + jnp.where(y == row, found[n * chans : (n + 1) * chans], 0.0)
    return total


def edge_kernel(
    part, parity_ref, pre_ref, total_ref, north_ref, south_ref, x_ref, cot_ref,
    out_ref, grads_ref, keep_ref, give_ref, total, sums,
):
    cy, chans, nz = cot_ref.shape
    rows = 3 * chans
    own = pl.ds(chans, chans)
    last = pl.ds(2 * chans, chans)
    cots = (north_ref[last], cot_ref[0], cot_ref[cy - 1], south_ref[last])
    sides = ((north_ref, 1), (north_ref, 0), (south_ref, 0), (south_ref, 1))
    ends = []
    for n, (ref, at) in enumerate(sides):
        pre = pre_ref[n] + ref[pl.ds(at * chans, chans)].astype(F32)
        ends.append(finish_row(pre, x_ref[0 if n < 2 else cy - 1, own], cots[n]))
    out_ref[0], out_ref[1] = ends[1][0], ends[2][0]
    grads = [stacked(grad) for _, grad in ends]
    for n in range(4):
        grads_ref[n] = grads[n]
    top = mm(jnp.concatenate([grads[0], grads[1]], axis=0), x_ref[0], NT)
    bottom = mm(jnp.concatenate([grads[2], grads[3]], axis=0), x_ref[cy - 1], NT)
    here = [pl.ds(n * rows, rows) for n in range(3)]
    total[here[0]] = total_ref[here[0]] + (top[:rows] + mm(grads[1], x_ref[1], NT))
    total[here[1]] = total_ref[here[1]] + (top[rows:] + bottom[:rows])
    total[here[2]] = total_ref[here[2]] + (bottom[rows:] + mm(grads[2], x_ref[cy - 2], NT))
    full, _, width = keep_ref.shape
    half = 3 * rows // 2
    split = 3 * rows // (2 * part)
    sums[pl.ds(0, split)] = total[:, :width].reshape(split, 2, part, width)
    taps = jnp.concatenate([total[pl.ds(0, half), width:], total[pl.ds(half, half), width:]], axis=1)
    sums[pl.ds(split, full - split)] = taps.reshape(full - split, 2, part, width)
    parity = parity_ref[0]
    keep_ref[...] = sums[:, parity]
    give_ref[...] = sums[:, 1 - parity].astype(BF16)


def slots_kernel(
    ndev, cap, part, full, slot_ref, plane_ref, hot_ref, grads_ref, wb_ref, cot_ref,
    own_cells, west_cells, east_cells, recv_ref, slots_ref, proj_ref,
):
    cy, chans, nz = cot_ref.shape
    rows = 3 * chans
    inner = mm(wb_ref[pl.ds(rows, 2 * rows)], grads_ref[1])
    top = slot_ref[0] + inner[:rows] + mm(wb_ref[pl.ds(2 * rows, rows)], grads_ref[0])
    second = slot_ref[1] + inner[rows:]
    inner = mm(wb_ref[pl.ds(0, 2 * rows)], grads_ref[2])
    third = slot_ref[2] + inner[:rows]
    bottom = slot_ref[3] + inner[rows:] + mm(wb_ref[pl.ds(0, rows)], grads_ref[3])
    at = (0, 1, cy - 2, cy - 1)
    found = []
    for dx, cells_ref in enumerate((west_cells, own_cells, east_cells)):
        parts = [value[dx * chans : (dx + 1) * chans] for value in (top, second, third, bottom)]
        if dx == 1:
            parts = [value + cot_ref[n].astype(F32) for value, n in zip(parts, at)]
        parts = [value.astype(BF16) for value in parts]
        terms = jnp.concatenate([plane_ref[dx], *parts], axis=0)
        y, _ = place(cells_ref, nz)
        found.append(at_slots(terms, y, hot_ref[dx], (*range(2, cy - 2), *at)))
    sides = jnp.concatenate([found[0], found[2]], axis=0).T
    middle = jnp.concatenate([found[1], jnp.zeros_like(found[1])], axis=0).T
    width = recv_ref.shape[1]
    back = [sides.reshape(ndev, cap, width), middle.reshape(ndev, cap, width)]
    slots_ref[...] = jnp.concatenate(back, axis=1).astype(BF16)
    raws = rows_in(recv_ref, ndev, cap)
    proj = sum(mm(found[dx].astype(BF16), raws[dx]) for dx in range(3))
    rest = ndev - full
    pad = jnp.zeros((rest * part - chans, width), F32)
    proj = jnp.concatenate([proj, pad], axis=0).reshape(rest, part, width)
    proj_ref[...] = proj.astype(BF16)


def pair_kernel(keep_ref, got_ref, slots_ref, proj_ref, send_far, sums_send, sems):
    full, part, _ = keep_ref.shape
    ndev, back, _ = slots_ref.shape
    pieces = (
        (slots_ref, send_far.at[:, pl.ds(part, back)]),
        (proj_ref, send_far.at[pl.ds(full, ndev - full), pl.ds(0, part)]),
        (sums_send, send_far.at[pl.ds(0, full), pl.ds(0, part)]),
    )
    copies = [pltpu.make_async_copy(src, dst, sems.at[n]) for n, (src, dst) in enumerate(pieces)]
    copies[0].start()
    copies[1].start()
    sums_send[...] = (keep_ref[...] + got_ref[...].astype(F32)).astype(BF16)
    copies[2].start()
    for copy in copies:
        copy.wait()


def sums_kernel(ngx, ngy, full, cap, recv_ref, index_ref, sums_ref):
    ndev, each, width = recv_ref.shape
    part = each - 2 * cap
    terms = recv_ref[:, pl.ds(0, part)].astype(F32).reshape(ngx // 2, 2, ngy, part, width)
    sums = jnp.sum(terms, axis=(0, 2))
    whole = sums[0] + sums[1]
    high = whole.astype(BF16).astype(F32)
    last = jnp.broadcast_to(index_ref[...], whole.shape) >= full
    sums = [
        jnp.where(last, high, sums[0]).astype(BF16),
        jnp.where(last, whole - high, sums[1]).astype(BF16),
    ]
    for n in range(ndev):
        sums_ref[n] = sums[(n // ngy) % 2]


def rows_kernel(
    ngx, ngy, cap, chans, recv_ref, counts_ref, proj_t_ref, inner_ref, ends_ref, rows_ref, out_ref
):
    ndev = ngx * ngy
    nrows = rows_ref.shape[0]
    width = recv_ref.shape[2]
    slots = ndev * cap
    share = recv_ref.shape[1] - 2 * cap
    arrived = recv_ref[:, pl.ds(share, 2 * cap)].astype(F32)
    sides = arrived[:, :cap].reshape(ngx, ngy, cap, width)
    left = lax.broadcasted_iota(I32, sides.shape, 3) < chans
    sides = jnp.where(left, rolled(sides, 1, 0), rolled(sides, -1, 0)).reshape(slots, width)
    middle = arrived[:, cap:].reshape(slots, width)
    counts = counts_ref[...].astype(F32)
    place = lax.broadcasted_iota(I32, (nrows, ndev), 0).astype(F32)
    lane = lax.broadcasted_iota(I32, (ndev, ndev), 1)
    upto = lax.broadcasted_iota(I32, (ndev, ndev), 0) <= lane
    ends = mm(counts.astype(BF16), jnp.where(upto, 1.0, 0.0).astype(BF16))
    before = ends <= place
    owner = jnp.sum(jnp.where(before, 1.0, 0.0), axis=1, keepdims=True)
    start = jnp.sum(jnp.where(before, counts, 0.0), axis=1, keepdims=True)
    slot = owner * cap + place[:, :1] - start
    onehot = jnp.where(
        lax.broadcasted_iota(I32, (nrows, slots), 1).astype(F32) == slot, 1.0, 0.0
    ).astype(BF16)
    proj_t = proj_t_ref[...]
    both = jnp.concatenate([proj_t, proj_t], axis=0)
    sides = mm(onehot, sides.astype(BF16)).astype(BF16)
    middle = mm(onehot, middle.astype(BF16)).astype(BF16)
    rows_ref[...] = mm(sides, both) + mm(middle, both)
    cy = inner_ref.shape[0]
    field = jnp.concatenate([ends_ref[:1], inner_ref[1 : cy - 1], ends_ref[1:]], axis=0)
    out_ref[...] = jnp.swapaxes(field, 0, 1)


def finish_kernel(conv_scale, proj_scale, parity_ref, mine_ref, other_ref, conv_ref, proj_ref, both):
    ndev, part, width = mine_ref.shape
    parity = parity_ref[0]
    both[:, parity] = mine_ref[...]
    both[:, 1 - parity] = other_ref[...]
    sums = both[...].astype(F32).reshape(ndev * 2 * part, width)
    taps, chans, _ = conv_ref.shape
    rows = 9 * chans
    half = rows // 2
    packed = sums[rows : rows + half]
    column = jnp.concatenate([packed[:, :chans], packed[:, chans:]], axis=0)
    for b in range(3):
        for dz in range(3):
            first = (b * 3 + dz) * chans
            block = sums[first : first + chans]
            k = (2 - b) * 3 + dz
            conv_ref[k] = block[:, :chans] * conv_scale
            conv_ref[9 + k] = block[:, chans:] * conv_scale
            conv_ref[18 + k] = column[first : first + chans] * conv_scale
    terms = sums[rows + half : rows + half + 2 * chans].reshape(chans // part, 2, part, width)
    proj_ref[...] = jnp.sum(terms, axis=1).reshape(chans, width) * proj_scale


def local(particles, send_counts, cell_lists, base_field, proj_weight, conv_weight, cotangent):
    ngx, ngy = lax.axis_size("gx"), lax.axis_size("gy")
    ndev = ngx * ngy
    nrows, feats = particles.shape
    chans, cx, cy, nz = base_field.shape
    slots = cell_lists.shape[1]
    cap = slots // ndev
    count = cx * cy * nz
    assert cx == 1 and feats == 2 * chans
    proj_t = proj_weight.T
    move = functools.partial(send, ngx=ngx, ngy=ngy)
    rows = 3 * chans
    one = 2 * rows * rows * nz

    base = base_field.reshape(chans, cy, nz)
    west, east = move(base_field, 1, 0), move(base_field, -1, 0)
    planes = (base, west.reshape(base.shape), east.reshape(base.shape))
    lists = (cell_lists, move(cell_lists, 1, 0), move(cell_lists, -1, 0))
    (payload,) = call(
        functools.partial(first_kernel, ngx, ngy, cap),
        [shape((ndev * 3 * cap, feats), BF16)],
        (particles, send_counts),
        2 * slots * nrows * feats,
        (
            pltpu.VMEM(particles.shape, BF16),
            pltpu.VMEM(send_counts.shape, I32),
            pltpu.SemaphoreType.DMA((2,)),
        ),
        far=range(2),
        limit=ALL,
    )
    recv = exchange(payload, ndev)

    wf, wb, cot = call(
        turns_kernel,
        [shape((9 * chans, rows), BF16)] * 2 + [shape((cy, chans, nz), BF16)],
        (conv_weight, cotangent.reshape(chans, cy, nz)),
        1000,
    )

    turned, hots = call(
        planes_kernel,
        [shape((3, cy, chans, nz), BF16), shape((3, nz, slots), BF16)],
        (*planes, *lists),
        1000,
    )
    first, last, values = call(
        functools.partial(outer_kernel, ndev, cap),
        [shape((rows, nz), BF16)] * 2 + [shape((3, chans, slots), BF16)],
        (recv, turned, hots, *lists, proj_t, cot, wf),
        4 * one,
        (pltpu.VMEM((4 * chans, slots), BF16), pltpu.VMEM((4, rows, nz), BF16)),
    )
    south, north = move(first, 0, -1), move(last, 0, 1)
    x_all, out_rows, total, pre_edge, slot_edge, plane = call(
        conv_kernel,
        [
            shape((cy, rows, nz), BF16),
            shape((cy, chans, nz), BF16),
            shape((9 * chans, rows), F32),
            shape((4, chans, nz), F32),
            shape((4, rows, nz), F32),
            shape((3, (cy - 4) * chans, nz), BF16),
        ],
        (values, hots, turned, *lists, cot, wf, wb),
        3 * cy * 3 * one,
        (
            pltpu.VMEM((cy + 1, rows, nz), F32),
            pltpu.VMEM((cy + 2, rows, nz), BF16),
            pltpu.VMEM((cy, rows, nz), F32),
            pltpu.VMEM((cy * chans, slots), BF16),
        ),
    )
    grad_rows = 27 * chans * chans // feats
    part = -(-(grad_rows + 2 * chans) // (32 * ndev)) * 16
    full = grad_rows // (2 * part)
    assert ngx % 2 == 0 and full * 2 * part == grad_rows
    row = lax.axis_index("gx")
    parity = (row % 2).astype(I32).reshape(1)
    out_edge, grads, keep, give = call(
        functools.partial(edge_kernel, part),
        [
            shape((2, chans, nz), BF16),
            shape((4, rows, nz), BF16),
            shape((full, part, feats), F32),
            shape((full, part, feats), BF16),
        ],
        (parity, pre_edge, total, north, south, x_all, cot),
        6 * one,
        (pltpu.VMEM((9 * chans, rows), F32), pltpu.VMEM((full, 2, part, feats), F32)),
        scalar=(0,),
    )
    got = swap(give)
    back, proj = call(
        functools.partial(slots_kernel, ndev, cap, part, full),
        [shape((ndev, 2 * cap, feats), BF16), shape((ndev - full, part, feats), BF16)],
        (slot_edge, plane, hots, grads, wb, cot, *lists, recv),
        6 * one,
    )
    (payload,) = call(
        pair_kernel,
        [shape((ndev, part + 2 * cap, feats), BF16)],
        (keep, got, back, proj),
        1000,
        (pltpu.VMEM((full, part, feats), BF16), pltpu.SemaphoreType.DMA((3,))),
        far_out=(0,),
    )
    (payload,) = call(same_kernel, [payload], (payload,), 0, far=(0,), far_out=(0,), aliases={0: 0})
    recv = exchange(payload.reshape(-1, feats), ndev).reshape(payload.shape)
    index = (row * ngy + lax.axis_index("gy")).astype(I32).reshape(1, 1)
    (sums,) = call(
        functools.partial(sums_kernel, ngx, ngy, full, cap),
        [shape((ndev, part, feats), BF16)],
        (recv, index),
        1000,
    )
    row_grads, out_field = call(
        functools.partial(rows_kernel, ngx, ngy, cap, chans),
        [shape((nrows, feats), F32), shape((chans, cy, nz), BF16)],
        (recv, send_counts, proj_t, out_rows, out_edge),
        2 * nrows * slots * chans,
    )
    mine = exchange(sums.reshape(-1, feats), ndev).reshape(sums.shape)
    mine, row_grads, out_field = lax.optimization_barrier((mine, row_grads, out_field))
    other = swap(mine)
    conv_grad, proj_grad = call(
        functools.partial(
            finish_kernel, 1.0 / math.sqrt(count * ndev), 1.0 / math.sqrt(nrows * ndev)
        ),
        [shape((27, chans, chans), F32), shape((chans, feats), F32)],
        (parity, mine, other),
        1000,
        (pltpu.VMEM((ndev, 2, part, feats), BF16),),
        scalar=(0,),
    )
    return (out_field[:, None], row_grads, conv_grad, proj_grad.T)


def solution(mesh):
    in_specs = (
        P(("gx", "gy"), None),
        P(("gx", "gy"), None),
        P(("gx", "gy"), None),
        P(None, "gx", "gy", None),
        P(),
        P(),
        P(None, "gx", "gy", None),
    )
    out_specs = (P(None, "gx", "gy", None), P(("gx", "gy"), None), P(), P())
    return jax.shard_map(local, mesh=mesh, in_specs=in_specs, out_specs=out_specs, check_vma=False)
```

```python
import functools
import math

import jax
import jax.numpy as jnp
from jax import lax
from jax.experimental import pallas as pl
from jax.experimental.pallas import tpu as pltpu
from jax.sharding import PartitionSpec as P

AXES = ("gx", "gy")
F32, BF16, I32 = jnp.float32, jnp.bfloat16, jnp.int32
LIMIT = 40 * 1024 * 1024
ALL = 50 * 1024 * 1024
NT = (((1,), (1,)), ((), ()))
NN = (((1,), (0,)), ((), ()))


def mm(a, b, dims=NN):
    return lax.dot_general(a, b, dims, preferred_element_type=F32)


def call(kernel, outs, args, flops, scratch=(), far=(), far_out=(), aliases=None, limit=LIMIT, scalar=()):
    traffic = sum(math.prod(a.shape) * a.dtype.itemsize for a in (*args, *outs))
    near = pl.BlockSpec(memory_space=pltpu.VMEM)
    there = pl.BlockSpec(memory_space=pltpu.HBM)
    return pl.pallas_call(
        kernel,
        out_shape=[jax.ShapeDtypeStruct(o.shape, o.dtype) for o in outs],
        in_specs=[
            pl.BlockSpec(memory_space=pltpu.SMEM) if n in scalar else there if n in far else near
            for n in range(len(args))
        ],
        out_specs=[there if n in far_out else near for n in range(len(outs))],
        scratch_shapes=list(scratch),
        input_output_aliases=aliases or {},
        compiler_params=pltpu.CompilerParams(vmem_limit_bytes=limit),
        cost_estimate=pl.CostEstimate(flops=flops, bytes_accessed=traffic, transcendentals=0),
    )(*args)


def shape(dims, dtype):
    return jax.ShapeDtypeStruct(dims, dtype)


def send(block, di, dj, ngx, ngy):
    pairs = []
    for i in range(ngx):
        for j in range(ngy):
            pairs.append((i * ngy + j, ((i + di) % ngx) * ngy + (j + dj) % ngy))
    return lax.ppermute(block, AXES, pairs)


def swap(block):
    return lax.ppermute(block, "gx", [(i, i ^ 1) for i in range(lax.axis_size("gx"))])


def exchange(payload, ndev):
    rows, width = payload.shape
    moved = lax.all_to_all(
        payload.reshape(ndev, rows // ndev, width), AXES, split_axis=0, concat_axis=0, tiled=True
    )
    return moved.reshape(rows, width)


def rolled(x, di, dj):
    for axis, shift in ((0, di), (1, dj)):
        if shift == 1:
            head, tail = lax.slice_in_dim(x, 1, None, axis=axis), lax.slice_in_dim(x, 0, 1, axis=axis)
            x = jnp.concatenate([head, tail], axis=axis)
        elif shift == -1:
            count = x.shape[axis]
            head = lax.slice_in_dim(x, count - 1, count, axis=axis)
            x = jnp.concatenate([head, lax.slice_in_dim(x, 0, count - 1, axis=axis)], axis=axis)
    return x


def picked_depth(z, nz):
    depth = lax.broadcasted_iota(I32, (nz, z.shape[1]), 0)
    return jnp.where(depth == z, 1.0, 0.0).astype(BF16)


def rows_in(recv_ref, ndev, cap):
    width = recv_ref.shape[1]
    arrived = recv_ref[...].astype(F32).reshape(ndev, 3, cap, width)
    return [arrived[:, n].reshape(ndev * cap, width).astype(BF16) for n in range(3)]


def stacked(grad):
    nz = grad.shape[1]
    wide = grad.astype(F32)
    return jnp.concatenate(
        [pltpu.roll(wide, nz - 1, 1), wide, pltpu.roll(wide, 1, 1)], axis=0
    ).astype(BF16)


def over_depth(acc):
    chans, nz = acc.shape[0] // 3, acc.shape[1]
    total = acc[chans : 2 * chans] + pltpu.roll(acc[:chans], 1, 1)
    return total + pltpu.roll(acc[2 * chans :], nz - 1, 1)


def finish_row(pre, field, cot):
    sig = jax.nn.sigmoid(pre)
    out = field.astype(F32) + pre * sig
    grad = cot.astype(F32) * sig * (1.0 + pre * (1.0 - sig))
    return out.astype(BF16), grad.astype(BF16)


def first_kernel(
    ngx, ngy, cap, rows_far, counts_far, send_ref, rows_ref, counts_ref, sems
):
    copies = [
        pltpu.make_async_copy(rows_far, rows_ref, sems.at[0]),
        pltpu.make_async_copy(counts_far, counts_ref, sems.at[1]),
    ]
    for copy in copies:
        copy.start()
    copies[1].wait()
    pick(ngx, ngy, cap, counts_ref, rows_ref, send_ref, copies[0])


def turns_kernel(weight_ref, cot_ref, wf_ref, wb_ref, cot_out):
    cot_out[...] = jnp.swapaxes(cot_ref[...], 0, 1)
    chans = cot_ref.shape[0]
    three = range(3)
    for dy in three:
        for n in three:
            rows = pl.ds((dy * 3 + n) * chans, chans)
            taps = [weight_ref[dx * 9 + dy * 3 + n] for dx in three]
            wf_ref[rows] = jnp.concatenate(taps, axis=1)
            taps = [weight_ref[n * 9 + dy * 3 + dz].astype(F32).T for dz in three]
            wb_ref[rows] = jnp.concatenate(taps, axis=1).astype(BF16)


def same_kernel(in_ref, out_ref):
    pass


def pick(ngx, ngy, cap, counts_ref, rows_ref, out_ref, rows_copy):
    ndev = ngx * ngy
    nrows, feats = rows_ref.shape
    slots = ndev * cap
    counts = counts_ref[...].astype(F32)
    owner = lax.broadcasted_iota(I32, (ndev, cap, ndev), 0).reshape(slots, ndev)
    lane = lax.broadcasted_iota(I32, (slots, ndev), 1)
    start = jnp.sum(jnp.where(lane < owner, counts, 0.0), axis=1, keepdims=True)
    held = jnp.sum(jnp.where(lane == owner, counts, 0.0), axis=1, keepdims=True)
    place = lax.broadcasted_iota(I32, (ndev, cap, nrows), 1).reshape(slots, nrows).astype(F32)
    row = lax.broadcasted_iota(I32, (slots, nrows), 1).astype(F32)
    onehot = jnp.where((row == place + start) & (place < held), 1.0, 0.0).astype(BF16)
    rows_copy.wait()
    raw = mm(onehot, rows_ref[...]).reshape(ngx, ngy, cap, feats)
    parts = [rolled(raw, dx, 0).reshape(ndev, cap, feats) for dx in (-1, 0, 1)]
    out_ref[...] = jnp.stack(parts, axis=1).reshape(out_ref.shape).astype(BF16)


def painted_rows(values, y, onehot, ns, masked):
    chans = values.shape[0]
    for n, row in enumerate(ns):
        masked[pl.ds(n * chans, chans)] = values * jnp.where(y == row, 1.0, 0.0).astype(BF16)
    return mm(masked[pl.ds(0, len(ns) * chans)], onehot, NT)


def add_to_rows(near, far, cot, back, out_ref):
    chans = cot.shape[0]
    rows = 3 * chans
    at, over = (rows, 0) if back else (0, rows)
    out_ref[pl.ds(0, chans)] = over_depth(near[at : at + rows]).astype(BF16)
    out_ref[pl.ds(chans, chans)] = over_depth(near[over : over + rows] + far).astype(BF16)
    out_ref[pl.ds(2 * chans, chans)] = cot


def planes_kernel(
    own_ref, west_ref, east_ref, own_cells, west_cells, east_cells, turned_ref, hot_ref
):
    planes = ((west_ref, west_cells), (own_ref, own_cells), (east_ref, east_cells))
    for dx, (ref, cells_ref) in enumerate(planes):
        turned_ref[dx] = jnp.swapaxes(ref[...], 0, 1)
        _, z = place(cells_ref, ref.shape[2])
        hot_ref[dx] = picked_depth(z, ref.shape[2])


def outer_kernel(
    ndev, cap, recv_ref, turned_ref, hot_ref, own_cells, west_cells, east_cells,
    proj_t_ref, cot_ref, wf_ref, first_ref, last_ref, values_ref, masked, field,
):
    cy, chans, nz = cot_ref.shape
    rows = 3 * chans
    raws = rows_in(recv_ref, ndev, cap)
    ns = (0, 1, cy - 2, cy - 1)
    for dx, cells_ref in enumerate((west_cells, own_cells, east_cells)):
        values = mm(proj_t_ref[...], raws[dx], NT).astype(BF16)
        y, _ = place(cells_ref, nz)
        values_ref[dx] = values
        painted = painted_rows(values, y, hot_ref[dx], ns, masked)
        for n, row in enumerate(ns):
            part = painted[n * chans : (n + 1) * chans]
            base = turned_ref[dx, row].astype(F32)
            field[n, pl.ds(dx * chans, chans)] = (base + part).astype(BF16)
    near = mm(wf_ref[pl.ds(0, 2 * rows)], field[3])
    add_to_rows(near, mm(wf_ref[pl.ds(0, rows)], field[2]), cot_ref[cy - 1], False, last_ref)
    near = mm(wf_ref[pl.ds(rows, 2 * rows)], field[0])
    add_to_rows(near, mm(wf_ref[pl.ds(2 * rows, rows)], field[1]), cot_ref[0], True, first_ref)


def place(cells_ref, nz):
    cells = cells_ref[...]
    return cells // nz, cells % nz


def conv_kernel(
    values_ref, hot_ref, turned_ref, own_cells, west_cells, east_cells, cot_ref, wf_ref, wb_ref,
    x_ref, out_ref, total_ref, pre_ref, slot_ref, plane, acc, grads, back, masked,
):
    cy, chans, nz = cot_ref.shape
    rows = 3 * chans
    for dx, cells_ref in enumerate((west_cells, own_cells, east_cells)):
        y, _ = place(cells_ref, nz)
        painted = painted_rows(values_ref[dx], y, hot_ref[dx], range(cy), masked)
        field = turned_ref[dx].astype(F32) + painted.reshape(cy, chans, nz)
        x_ref[:, pl.ds(dx * chans, chans)] = field.astype(BF16)
    own = pl.ds(chans, chans)
    zeros = jnp.zeros((rows, nz), BF16)
    for t in (0, 1, cy, cy + 1):
        grads[t] = zeros
    out_ref[0] = zeros[:chans]
    out_ref[cy - 1] = zeros[:chans]
    acc[0] = jnp.zeros((rows, nz), F32)

    def spread(n):
        terms = mm(wf_ref[...], x_ref[n])
        acc[n + 1] = terms[:rows]
        acc[n] += terms[rows : 2 * rows]
        return terms[2 * rows :]

    pre_ref[0] = over_depth(spread(0))
    pre_ref[1] = over_depth(acc[0] + spread(1))

    def forward(n):
        done = spread(n) + acc[n - 1]
        y = n - 1
        out, grad = finish_row(over_depth(done), x_ref[y, own], cot_ref[y])
        out_ref[y] = out
        grads[y + 1] = stacked(grad)

    for n in range(2, cy):
        forward(n)
    pre_ref[2] = over_depth(acc[cy - 1])
    pre_ref[3] = over_depth(acc[cy])
    total_ref[...] = jnp.zeros_like(total_ref)
    back[0] = jnp.zeros((rows, nz), F32)
    back[1] = jnp.zeros((rows, nz), F32)

    def taps(n):
        window = grads[pl.ds(n, 3)].reshape(3 * rows, nz)
        total_ref[...] += mm(window, x_ref[n], NT)

    def spread_back(n):
        terms = mm(wb_ref[...], grads[n + 1])
        back[n + 1] = terms[2 * rows :]
        back[n] += terms[rows : 2 * rows]
        return terms[:rows]

    def backward(n):
        taps(n)
        value = spread_back(n) + back[n - 1]
        for dx in range(3):
            part = value[dx * chans : (dx + 1) * chans]
            if dx == 1:
                part = part + cot_ref[n - 1].astype(F32)
            plane[dx, pl.ds((n - 3) * chans, chans)] = part.astype(BF16)

    taps(0)
    taps(1)
    slot_ref[0] = spread_back(1)
    taps(2)
    slot_ref[1] = spread_back(2) + back[1]
    for n in range(3, cy - 1):
        backward(n)
    taps(cy - 1)
    slot_ref[2] = back[cy - 2]
    slot_ref[3] = back[cy - 1]


def at_slots(part, y, onehot, first):
    found = mm(part, onehot)
    chans = found.shape[0] // len(first)
    total = jnp.zeros((chans, found.shape[1]), F32)
    for n, row in enumerate(first):
        total = total + jnp.where(y == row, found[n * chans : (n + 1) * chans], 0.0)
    return total


def edge_kernel(
    part, parity_ref, pre_ref, total_ref, north_ref, south_ref, x_ref, cot_ref,
    out_ref, grads_ref, keep_ref, give_ref, total, sums,
):
    cy, chans, nz = cot_ref.shape
    rows = 3 * chans
    own = pl.ds(chans, chans)
    last = pl.ds(2 * chans, chans)
    cots = (north_ref[last], cot_ref[0], cot_ref[cy - 1], south_ref[last])
    sides = ((north_ref, 1), (north_ref, 0), (south_ref, 0), (south_ref, 1))
    ends = []
    for n, (ref, at) in enumerate(sides):
        pre = pre_ref[n] + ref[pl.ds(at * chans, chans)].astype(F32)
        ends.append(finish_row(pre, x_ref[0 if n < 2 else cy - 1, own], cots[n]))
    out_ref[0], out_ref[1] = ends[1][0], ends[2][0]
    grads = [stacked(grad) for _, grad in ends]
    for n in range(4):
        grads_ref[n] = grads[n]
    top = mm(jnp.concatenate([grads[0], grads[1]], axis=0), x_ref[0], NT)
    bottom = mm(jnp.concatenate([grads[2], grads[3]], axis=0), x_ref[cy - 1], NT)
    here = [pl.ds(n * rows, rows) for n in range(3)]
    total[here[0]] = total_ref[here[0]] + (top[:rows] + mm(grads[1], x_ref[1], NT))
    total[here[1]] = total_ref[here[1]] + (top[rows:] + bottom[:rows])
    total[here[2]] = total_ref[here[2]] + (bottom[rows:] + mm(grads[2], x_ref[cy - 2], NT))
    full, _, width = keep_ref.shape
    half = 3 * rows // 2
    split = 3 * rows // (2 * part)
    sums[pl.ds(0, split)] = total[:, :width].reshape(split, 2, part, width)
    taps = jnp.concatenate([total[pl.ds(0, half), width:], total[pl.ds(half, half), width:]], axis=1)
    sums[pl.ds(split, full - split)] = taps.reshape(full - split, 2, part, width)
    parity = parity_ref[0]
    keep_ref[...] = sums[:, parity]
    give_ref[...] = sums[:, 1 - parity].astype(BF16)


def slots_kernel(
    ndev, cap, part, full, slot_ref, plane_ref, hot_ref, grads_ref, wb_ref, cot_ref,
    own_cells, west_cells, east_cells, recv_ref, slots_ref, proj_ref,
):
    cy, chans, nz = cot_ref.shape
    rows = 3 * chans
    inner = mm(wb_ref[pl.ds(rows, 2 * rows)], grads_ref[1])
    top = slot_ref[0] + inner[:rows] + mm(wb_ref[pl.ds(2 * rows, rows)], grads_ref[0])
    second = slot_ref[1] + inner[rows:]
    inner = mm(wb_ref[pl.ds(0, 2 * rows)], grads_ref[2])
    third = slot_ref[2] + inner[:rows]
    bottom = slot_ref[3] + inner[rows:] + mm(wb_ref[pl.ds(0, rows)], grads_ref[3])
    at = (0, 1, cy - 2, cy - 1)
    found = []
    for dx, cells_ref in enumerate((west_cells, own_cells, east_cells)):
        parts = [value[dx * chans : (dx + 1) * chans] for value in (top, second, third, bottom)]
        if dx == 1:
            parts = [value + cot_ref[n].astype(F32) for value, n in zip(parts, at)]
        parts = [value.astype(BF16) for value in parts]
        terms = jnp.concatenate([plane_ref[dx], *parts], axis=0)
        y, _ = place(cells_ref, nz)
        found.append(at_slots(terms, y, hot_ref[dx], (*range(2, cy - 2), *at)))
    sides = jnp.concatenate([found[0], found[2]], axis=0).T
    middle = jnp.concatenate([found[1], jnp.zeros_like(found[1])], axis=0).T
    width = recv_ref.shape[1]
    back = [sides.reshape(ndev, cap, width), middle.reshape(ndev, cap, width)]
    slots_ref[...] = jnp.concatenate(back, axis=1).astype(BF16)
    raws = rows_in(recv_ref, ndev, cap)
    proj = sum(mm(found[dx].astype(BF16), raws[dx]) for dx in range(3))
    rest = ndev - full
    pad = jnp.zeros((rest * part - chans, width), F32)
    proj = jnp.concatenate([proj, pad], axis=0).reshape(rest, part, width)
    proj_ref[...] = proj.astype(BF16)


def pair_kernel(keep_ref, got_ref, slots_ref, proj_ref, send_far, sums_send, sems):
    full, part, _ = keep_ref.shape
    ndev, back, _ = slots_ref.shape
    pieces = (
        (slots_ref, send_far.at[:, pl.ds(part, back)]),
        (proj_ref, send_far.at[pl.ds(full, ndev - full), pl.ds(0, part)]),
        (sums_send, send_far.at[pl.ds(0, full), pl.ds(0, part)]),
    )
    copies = [pltpu.make_async_copy(src, dst, sems.at[n]) for n, (src, dst) in enumerate(pieces)]
    copies[0].start()
    copies[1].start()
    sums_send[...] = (keep_ref[...] + got_ref[...].astype(F32)).astype(BF16)
    copies[2].start()
    for copy in copies:
        copy.wait()


def sums_kernel(ngx, ngy, full, cap, recv_ref, index_ref, sums_ref):
    ndev, each, width = recv_ref.shape
    part = each - 2 * cap
    terms = recv_ref[:, pl.ds(0, part)].astype(F32).reshape(ngx // 2, 2, ngy, part, width)
    sums = jnp.sum(terms, axis=(0, 2))
    whole = sums[0] + sums[1]
    high = whole.astype(BF16).astype(F32)
    last = jnp.broadcast_to(index_ref[...], whole.shape) >= full
    sums = [
        jnp.where(last, high, sums[0]).astype(BF16),
        jnp.where(last, whole - high, sums[1]).astype(BF16),
    ]
    for n in range(ndev):
        sums_ref[n] = sums[(n // ngy) % 2]


def rows_kernel(
    ngx, ngy, cap, chans, recv_ref, counts_ref, proj_t_ref, inner_ref, ends_ref, rows_ref, out_ref
):
    ndev = ngx * ngy
    nrows = rows_ref.shape[0]
    width = recv_ref.shape[2]
    slots = ndev * cap
    share = recv_ref.shape[1] - 2 * cap
    arrived = recv_ref[:, pl.ds(share, 2 * cap)].astype(F32)
    sides = arrived[:, :cap].reshape(ngx, ngy, cap, width)
    left = lax.broadcasted_iota(I32, sides.shape, 3) < chans
    sides = jnp.where(left, rolled(sides, 1, 0), rolled(sides, -1, 0)).reshape(slots, width)
    middle = arrived[:, cap:].reshape(slots, width)
    counts = counts_ref[...].astype(F32)
    place = lax.broadcasted_iota(I32, (nrows, ndev), 0).astype(F32)
    lane = lax.broadcasted_iota(I32, (ndev, ndev), 1)
    upto = lax.broadcasted_iota(I32, (ndev, ndev), 0) <= lane
    ends = mm(counts.astype(BF16), jnp.where(upto, 1.0, 0.0).astype(BF16))
    before = ends <= place
    owner = jnp.sum(jnp.where(before, 1.0, 0.0), axis=1, keepdims=True)
    start = jnp.sum(jnp.where(before, counts, 0.0), axis=1, keepdims=True)
    slot = owner * cap + place[:, :1] - start
    onehot = jnp.where(
        lax.broadcasted_iota(I32, (nrows, slots), 1).astype(F32) == slot, 1.0, 0.0
    ).astype(BF16)
    proj_t = proj_t_ref[...]
    both = jnp.concatenate([proj_t, proj_t], axis=0)
    sides = mm(onehot, sides.astype(BF16)).astype(BF16)
    middle = mm(onehot, middle.astype(BF16)).astype(BF16)
    rows_ref[...] = mm(sides, both) + mm(middle, both)
    cy = inner_ref.shape[0]
    field = jnp.concatenate([ends_ref[:1], inner_ref[1 : cy - 1], ends_ref[1:]], axis=0)
    out_ref[...] = jnp.swapaxes(field, 0, 1)


def finish_kernel(conv_scale, proj_scale, parity_ref, mine_ref, other_ref, conv_ref, proj_ref, both):
    ndev, part, width = mine_ref.shape
    parity = parity_ref[0]
    both[:, parity] = mine_ref[...]
    both[:, 1 - parity] = other_ref[...]
    sums = both[...].astype(F32).reshape(ndev * 2 * part, width)
    taps, chans, _ = conv_ref.shape
    rows = 9 * chans
    half = rows // 2
    packed = sums[rows : rows + half]
    column = jnp.concatenate([packed[:, :chans], packed[:, chans:]], axis=0)
    for b in range(3):
        for dz in range(3):
            first = (b * 3 + dz) * chans
            block = sums[first : first + chans]
            k = (2 - b) * 3 + dz
            conv_ref[k] = block[:, :chans] * conv_scale
            conv_ref[9 + k] = block[:, chans:] * conv_scale
            conv_ref[18 + k] = column[first : first + chans] * conv_scale
    terms = sums[rows + half : rows + half + 2 * chans].reshape(chans // part, 2, part, width)
    proj_ref[...] = jnp.sum(terms, axis=1).reshape(chans, width) * proj_scale


def local(particles, send_counts, cell_lists, base_field, proj_weight, conv_weight, cotangent):
    ngx, ngy = lax.axis_size("gx"), lax.axis_size("gy")
    ndev = ngx * ngy
    nrows, feats = particles.shape
    chans, cx, cy, nz = base_field.shape
    slots = cell_lists.shape[1]
    cap = slots // ndev
    count = cx * cy * nz
    assert cx == 1 and feats == 2 * chans
    proj_t = proj_weight.T
    move = functools.partial(send, ngx=ngx, ngy=ngy)
    rows = 3 * chans
    one = 2 * rows * rows * nz

    base = base_field.reshape(chans, cy, nz)
    west, east = move(base_field, 1, 0), move(base_field, -1, 0)
    planes = (base, west.reshape(base.shape), east.reshape(base.shape))
    lists = (cell_lists, move(cell_lists, 1, 0), move(cell_lists, -1, 0))
    (payload,) = call(
        functools.partial(first_kernel, ngx, ngy, cap),
        [shape((ndev * 3 * cap, feats), BF16)],
        (particles, send_counts),
        2 * slots * nrows * feats,
        (
            pltpu.VMEM(particles.shape, BF16),
            pltpu.VMEM(send_counts.shape, I32),
            pltpu.SemaphoreType.DMA((2,)),
        ),
        far=range(2),
        limit=ALL,
    )
    recv = exchange(payload, ndev)

    wf, wb, cot = call(
        turns_kernel,
        [shape((9 * chans, rows), BF16)] * 2 + [shape((cy, chans, nz), BF16)],
        (conv_weight, cotangent.reshape(chans, cy, nz)),
        1000,
    )

    turned, hots = call(
        planes_kernel,
        [shape((3, cy, chans, nz), BF16), shape((3, nz, slots), BF16)],
        (*planes, *lists),
        1000,
    )
    first, last, values = call(
        functools.partial(outer_kernel, ndev, cap),
        [shape((rows, nz), BF16)] * 2 + [shape((3, chans, slots), BF16)],
        (recv, turned, hots, *lists, proj_t, cot, wf),
        4 * one,
        (pltpu.VMEM((4 * chans, slots), BF16), pltpu.VMEM((4, rows, nz), BF16)),
    )
    south, north = move(first, 0, -1), move(last, 0, 1)
    x_all, out_rows, total, pre_edge, slot_edge, plane = call(
        conv_kernel,
        [
            shape((cy, rows, nz), BF16),
            shape((cy, chans, nz), BF16),
            shape((9 * chans, rows), F32),
            shape((4, chans, nz), F32),
            shape((4, rows, nz), F32),
            shape((3, (cy - 4) * chans, nz), BF16),
        ],
        (values, hots, turned, *lists, cot, wf, wb),
        3 * cy * 3 * one,
        (
            pltpu.VMEM((cy + 1, rows, nz), F32),
            pltpu.VMEM((cy + 2, rows, nz), BF16),
            pltpu.VMEM((cy, rows, nz), F32),
            pltpu.VMEM((cy * chans, slots), BF16),
        ),
    )
    grad_rows = 27 * chans * chans // feats
    part = -(-(grad_rows + 2 * chans) // (32 * ndev)) * 16
    full = grad_rows // (2 * part)
    assert ngx % 2 == 0 and full * 2 * part == grad_rows
    row = lax.axis_index("gx")
    parity = (row % 2).astype(I32).reshape(1)
    out_edge, grads, keep, give = call(
        functools.partial(edge_kernel, part),
        [
            shape((2, chans, nz), BF16),
            shape((4, rows, nz), BF16),
            shape((full, part, feats), F32),
            shape((full, part, feats), BF16),
        ],
        (parity, pre_edge, total, north, south, x_all, cot),
        6 * one,
        (pltpu.VMEM((9 * chans, rows), F32), pltpu.VMEM((full, 2, part, feats), F32)),
        scalar=(0,),
    )
    got = swap(give)
    back, proj = call(
        functools.partial(slots_kernel, ndev, cap, part, full),
        [shape((ndev, 2 * cap, feats), BF16), shape((ndev - full, part, feats), BF16)],
        (slot_edge, plane, hots, grads, wb, cot, *lists, recv),
        6 * one,
    )
    (payload,) = call(
        pair_kernel,
        [shape((ndev, part + 2 * cap, feats), BF16)],
        (keep, got, back, proj),
        1000,
        (pltpu.VMEM((full, part, feats), BF16), pltpu.SemaphoreType.DMA((3,))),
        far_out=(0,),
    )
    (payload,) = call(same_kernel, [payload], (payload,), 0, far=(0,), far_out=(0,), aliases={0: 0})
    recv = exchange(payload.reshape(-1, feats), ndev).reshape(payload.shape)
    index = (row * ngy + lax.axis_index("gy")).astype(I32).reshape(1, 1)
    (sums,) = call(
        functools.partial(sums_kernel, ngx, ngy, full, cap),
        [shape((ndev, part, feats), BF16)],
        (recv, index),
        1000,
    )
    row_grads, out_field = call(
        functools.partial(rows_kernel, ngx, ngy, cap, chans),
        [shape((nrows, feats), F32), shape((chans, cy, nz), BF16)],
        (recv, send_counts, proj_t, out_rows, out_edge),
        2 * nrows * slots * chans,
    )
    mine = exchange(sums.reshape(-1, feats), ndev).reshape(sums.shape)
    mine, row_grads, out_field = lax.optimization_barrier((mine, row_grads, out_field))
    other = swap(mine)
    conv_grad, proj_grad = call(
        functools.partial(
            finish_kernel, 1.0 / math.sqrt(count * ndev), 1.0 / math.sqrt(nrows * ndev)
        ),
        [shape((27, chans, chans), F32), shape((chans, feats), F32)],
        (parity, mine, other),
        1000,
        (pltpu.VMEM((ndev, 2, part, feats), BF16),),
        scalar=(0,),
    )
    return (out_field[:, None], row_grads, conv_grad, proj_grad.T)


def solution(mesh):
    in_specs = (
        P(("gx", "gy"), None),
        P(("gx", "gy"), None),
        P(("gx", "gy"), None),
        P(None, "gx", "gy", None),
        P(),
        P(),
        P(None, "gx", "gy", None),
    )
    out_specs = (P(None, "gx", "gy", None), P(("gx", "gy"), None), P(), P())
    return jax.shard_map(local, mesh=mesh, in_specs=in_specs, out_specs=out_specs, check_vma=False)
```

```python
import functools
import math

import jax
import jax.numpy as jnp
from jax import lax
from jax.experimental import pallas as pl
from jax.experimental.pallas import tpu as pltpu
from jax.sharding import PartitionSpec as P

AXES = ("gx", "gy")
F32, BF16, I32 = jnp.float32, jnp.bfloat16, jnp.int32
LIMIT = 40 * 1024 * 1024
ALL = 60 * 1024 * 1024
NT = (((1,), (1,)), ((), ()))
NN = (((1,), (0,)), ((), ()))


def mm(a, b, dims=NN):
    return lax.dot_general(a, b, dims, preferred_element_type=F32)


def call(kernel, outs, args, flops, scratch=(), far=(), far_out=(), aliases=None, limit=LIMIT, scalar=()):
    traffic = sum(math.prod(a.shape) * a.dtype.itemsize for a in (*args, *outs))
    near = pl.BlockSpec(memory_space=pltpu.VMEM)
    there = pl.BlockSpec(memory_space=pltpu.HBM)
    return pl.pallas_call(
        kernel,
        out_shape=[jax.ShapeDtypeStruct(o.shape, o.dtype) for o in outs],
        in_specs=[
            pl.BlockSpec(memory_space=pltpu.SMEM) if n in scalar else there if n in far else near
            for n in range(len(args))
        ],
        out_specs=[there if n in far_out else near for n in range(len(outs))],
        scratch_shapes=list(scratch),
        input_output_aliases=aliases or {},
        compiler_params=pltpu.CompilerParams(vmem_limit_bytes=limit),
        cost_estimate=pl.CostEstimate(flops=flops, bytes_accessed=traffic, transcendentals=0),
    )(*args)


def shape(dims, dtype):
    return jax.ShapeDtypeStruct(dims, dtype)


def send(block, di, dj, ngx, ngy):
    pairs = []
    for i in range(ngx):
        for j in range(ngy):
            pairs.append((i * ngy + j, ((i + di) % ngx) * ngy + (j + dj) % ngy))
    return lax.ppermute(block, AXES, pairs)


def swap(block):
    return lax.ppermute(block, "gx", [(i, i ^ 1) for i in range(lax.axis_size("gx"))])


def exchange(payload, ndev):
    rows, width = payload.shape
    moved = lax.all_to_all(
        payload.reshape(ndev, rows // ndev, width), AXES, split_axis=0, concat_axis=0, tiled=True
    )
    return moved.reshape(rows, width)


def rolled(x, di, dj):
    for axis, shift in ((0, di), (1, dj)):
        if shift == 1:
            head, tail = lax.slice_in_dim(x, 1, None, axis=axis), lax.slice_in_dim(x, 0, 1, axis=axis)
            x = jnp.concatenate([head, tail], axis=axis)
        elif shift == -1:
            count = x.shape[axis]
            head = lax.slice_in_dim(x, count - 1, count, axis=axis)
            x = jnp.concatenate([head, lax.slice_in_dim(x, 0, count - 1, axis=axis)], axis=axis)
    return x


def picked_depth(z, nz):
    depth = lax.broadcasted_iota(I32, (nz, z.shape[1]), 0)
    return jnp.where(depth == z, 1.0, 0.0).astype(BF16)


def rows_in(recv_ref, ndev, cap):
    width = recv_ref.shape[1]
    arrived = recv_ref[...].astype(F32).reshape(ndev, 3, cap, width)
    return [arrived[:, n].reshape(ndev * cap, width).astype(BF16) for n in range(3)]


def stacked(grad):
    nz = grad.shape[1]
    wide = grad.astype(F32)
    return jnp.concatenate(
        [pltpu.roll(wide, nz - 1, 1), wide, pltpu.roll(wide, 1, 1)], axis=0
    ).astype(BF16)


def over_depth(acc):
    chans, nz = acc.shape[0] // 3, acc.shape[1]
    total = acc[chans : 2 * chans] + pltpu.roll(acc[:chans], 1, 1)
    return total + pltpu.roll(acc[2 * chans :], nz - 1, 1)


def finish_row(pre, field, cot):
    sig = jax.nn.sigmoid(pre)
    out = field.astype(F32) + pre * sig
    grad = cot.astype(F32) * sig * (1.0 + pre * (1.0 - sig))
    return out.astype(BF16), grad.astype(BF16)


def first_kernel(
    ngx, ngy, cap, rows_far, counts_far, send_ref, rows_ref, counts_ref, sems
):
    copies = [
        pltpu.make_async_copy(rows_far, rows_ref, sems.at[0]),
        pltpu.make_async_copy(counts_far, counts_ref, sems.at[1]),
    ]
    for copy in copies:
        copy.start()
    copies[1].wait()
    pick(ngx, ngy, cap, counts_ref, rows_ref, send_ref, copies[0])


def turns_kernel(weight_ref, cot_ref, wf_ref, wb_ref, cot_out):
    cot_out[...] = jnp.swapaxes(cot_ref[...], 0, 1)
    chans = cot_ref.shape[0]
    three = range(3)
    for dy in three:
        for n in three:
            rows = pl.ds((dy * 3 + n) * chans, chans)
            taps = [weight_ref[dx * 9 + dy * 3 + n] for dx in three]
            wf_ref[rows] = jnp.concatenate(taps, axis=1)
            taps = [weight_ref[n * 9 + dy * 3 + dz].astype(F32).T for dz in three]
            wb_ref[rows] = jnp.concatenate(taps, axis=1).astype(BF16)


def same_kernel(in_ref, out_ref):
    pass


def pick(ngx, ngy, cap, counts_ref, rows_ref, out_ref, rows_copy):
    ndev = ngx * ngy
    nrows, feats = rows_ref.shape
    slots = ndev * cap
    counts = counts_ref[...].astype(F32)
    owner = lax.broadcasted_iota(I32, (ndev, cap, ndev), 0).reshape(slots, ndev)
    lane = lax.broadcasted_iota(I32, (slots, ndev), 1)
    start = jnp.sum(jnp.where(lane < owner, counts, 0.0), axis=1, keepdims=True)
    held = jnp.sum(jnp.where(lane == owner, counts, 0.0), axis=1, keepdims=True)
    place = lax.broadcasted_iota(I32, (ndev, cap, nrows), 1).reshape(slots, nrows).astype(F32)
    row = lax.broadcasted_iota(I32, (slots, nrows), 1).astype(F32)
    onehot = jnp.where((row == place + start) & (place < held), 1.0, 0.0).astype(BF16)
    rows_copy.wait()
    raw = mm(onehot, rows_ref[...]).reshape(ngx, ngy, cap, feats)
    parts = [rolled(raw, dx, 0).reshape(ndev, cap, feats) for dx in (-1, 0, 1)]
    out_ref[...] = jnp.stack(parts, axis=1).reshape(out_ref.shape).astype(BF16)


def painted_rows(values, y, onehot, ns, masked):
    chans = values.shape[0]
    for n, row in enumerate(ns):
        masked[pl.ds(n * chans, chans)] = values * jnp.where(y == row, 1.0, 0.0).astype(BF16)
    return mm(masked[pl.ds(0, len(ns) * chans)], onehot, NT)


def add_to_rows(near, far, cot, back, out_ref):
    chans = cot.shape[0]
    rows = 3 * chans
    at, over = (rows, 0) if back else (0, rows)
    out_ref[pl.ds(0, chans)] = over_depth(near[at : at + rows]).astype(BF16)
    out_ref[pl.ds(chans, chans)] = over_depth(near[over : over + rows] + far).astype(BF16)
    out_ref[pl.ds(2 * chans, chans)] = cot


def outer_kernel(
    ndev, cap, recv_ref, own_ref, west_ref, east_ref, own_cells, west_cells, east_cells,
    proj_t_ref, cot_ref, wf_ref, first_ref, last_ref, values_ref, hot_ref, masked, field,
):
    chans, cy, nz = own_ref.shape
    rows = 3 * chans
    raws = rows_in(recv_ref, ndev, cap)
    ns = (0, 1, cy - 2, cy - 1)
    planes = ((west_ref, west_cells), (own_ref, own_cells), (east_ref, east_cells))
    for dx, (ref, cells_ref) in enumerate(planes):
        values = mm(proj_t_ref[...], raws[dx], NT).astype(BF16)
        y, z = place(cells_ref, nz)
        onehot = picked_depth(z, nz)
        values_ref[dx] = values
        hot_ref[dx] = onehot
        painted = painted_rows(values, y, onehot, ns, masked)
        base = turned(ref)
        for n, row in enumerate(ns):
            part = painted[n * chans : (n + 1) * chans]
            field[n, pl.ds(dx * chans, chans)] = (base[row] + part).astype(BF16)
    near = mm(wf_ref[pl.ds(0, 2 * rows)], field[3])
    add_to_rows(near, mm(wf_ref[pl.ds(0, rows)], field[2]), cot_ref[cy - 1], False, last_ref)
    near = mm(wf_ref[pl.ds(rows, 2 * rows)], field[0])
    add_to_rows(near, mm(wf_ref[pl.ds(2 * rows, rows)], field[1]), cot_ref[0], True, first_ref)


def place(cells_ref, nz):
    cells = cells_ref[...]
    return cells // nz, cells % nz


def turned(ref):
    return jnp.swapaxes(ref[...], 0, 1).astype(F32)


def conv_kernel(
    values_ref, hot_ref, own_ref, west_ref, east_ref, own_cells, west_cells, east_cells,
    cot_ref, wf_ref, wb_ref,
    x_ref, out_ref, total_ref, pre_ref, slot_ref, plane, acc, grads, back, masked,
):
    cy, chans, nz = cot_ref.shape
    rows = 3 * chans
    planes = ((west_ref, west_cells), (own_ref, own_cells), (east_ref, east_cells))
    for dx, (ref, cells_ref) in enumerate(planes):
        y, _ = place(cells_ref, nz)
        painted = painted_rows(values_ref[dx], y, hot_ref[dx], range(cy), masked)
        field = turned(ref) + painted.reshape(cy, chans, nz)
        x_ref[:, pl.ds(dx * chans, chans)] = field.astype(BF16)
    own = pl.ds(chans, chans)
    zeros = jnp.zeros((rows, nz), BF16)
    for t in (0, 1, cy, cy + 1):
        grads[t] = zeros
    out_ref[0] = zeros[:chans]
    out_ref[cy - 1] = zeros[:chans]
    acc[0] = jnp.zeros((rows, nz), F32)

    def spread(n):
        terms = mm(wf_ref[...], x_ref[n])
        acc[n + 1] = terms[:rows]
        acc[n] += terms[rows : 2 * rows]
        return terms[2 * rows :]

    pre_ref[0] = over_depth(spread(0))
    pre_ref[1] = over_depth(acc[0] + spread(1))

    def forward(n):
        done = spread(n) + acc[n - 1]
        y = n - 1
        out, grad = finish_row(over_depth(done), x_ref[y, own], cot_ref[y])
        out_ref[y] = out
        grads[y + 1] = stacked(grad)

    for n in range(2, cy):
        forward(n)
    pre_ref[2] = over_depth(acc[cy - 1])
    pre_ref[3] = over_depth(acc[cy])
    total_ref[...] = jnp.zeros_like(total_ref)
    back[0] = jnp.zeros((rows, nz), F32)
    back[1] = jnp.zeros((rows, nz), F32)

    def taps(n):
        window = grads[pl.ds(n, 3)].reshape(3 * rows, nz)
        total_ref[...] += mm(window, x_ref[n], NT)

    def spread_back(n):
        terms = mm(wb_ref[...], grads[n + 1])
        back[n + 1] = terms[2 * rows :]
        back[n] += terms[rows : 2 * rows]
        return terms[:rows]

    def backward(n):
        taps(n)
        value = spread_back(n) + back[n - 1]
        for dx in range(3):
            part = value[dx * chans : (dx + 1) * chans]
            if dx == 1:
                part = part + cot_ref[n - 1].astype(F32)
            plane[dx, pl.ds((n - 3) * chans, chans)] = part.astype(BF16)

    taps(0)
    taps(1)
    slot_ref[0] = spread_back(1)
    taps(2)
    slot_ref[1] = spread_back(2) + back[1]
    for n in range(3, cy - 1):
        backward(n)
    taps(cy - 1)
    slot_ref[2] = back[cy - 2]
    slot_ref[3] = back[cy - 1]


def at_slots(part, y, onehot, first):
    found = mm(part, onehot)
    chans = found.shape[0] // len(first)
    total = jnp.zeros((chans, found.shape[1]), F32)
    for n, row in enumerate(first):
        total = total + jnp.where(y == row, found[n * chans : (n + 1) * chans], 0.0)
    return total


def edge_kernel(
    part, parity_ref, pre_ref, total_ref, north_ref, south_ref, x_ref, cot_ref,
    out_ref, grads_ref, keep_ref, give_ref, total, sums,
):
    cy, chans, nz = cot_ref.shape
    rows = 3 * chans
    own = pl.ds(chans, chans)
    last = pl.ds(2 * chans, chans)
    cots = (north_ref[last], cot_ref[0], cot_ref[cy - 1], south_ref[last])
    sides = ((north_ref, 1), (north_ref, 0), (south_ref, 0), (south_ref, 1))
    ends = []
    for n, (ref, at) in enumerate(sides):
        pre = pre_ref[n] + ref[pl.ds(at * chans, chans)].astype(F32)
        ends.append(finish_row(pre, x_ref[0 if n < 2 else cy - 1, own], cots[n]))
    out_ref[0], out_ref[1] = ends[1][0], ends[2][0]
    grads = [stacked(grad) for _, grad in ends]
    for n in range(4):
        grads_ref[n] = grads[n]
    top = mm(jnp.concatenate([grads[0], grads[1]], axis=0), x_ref[0], NT)
    bottom = mm(jnp.concatenate([grads[2], grads[3]], axis=0), x_ref[cy - 1], NT)
    here = [pl.ds(n * rows, rows) for n in range(3)]
    total[here[0]] = total_ref[here[0]] + (top[:rows] + mm(grads[1], x_ref[1], NT))
    total[here[1]] = total_ref[here[1]] + (top[rows:] + bottom[:rows])
    total[here[2]] = total_ref[here[2]] + (bottom[rows:] + mm(grads[2], x_ref[cy - 2], NT))
    full, _, width = keep_ref.shape
    half = 3 * rows // 2
    split = 3 * rows // (2 * part)
    sums[pl.ds(0, split)] = total[:, :width].reshape(split, 2, part, width)
    taps = jnp.concatenate([total[pl.ds(0, half), width:], total[pl.ds(half, half), width:]], axis=1)
    sums[pl.ds(split, full - split)] = taps.reshape(full - split, 2, part, width)
    parity = parity_ref[0]
    keep_ref[...] = sums[:, parity]
    give_ref[...] = sums[:, 1 - parity].astype(BF16)


def slots_kernel(
    ndev, cap, part, full, slot_ref, plane_ref, hot_ref, grads_ref, wb_ref, cot_ref,
    own_cells, west_cells, east_cells, recv_ref, slots_ref, proj_ref,
):
    cy, chans, nz = cot_ref.shape
    rows = 3 * chans
    inner = mm(wb_ref[pl.ds(rows, 2 * rows)], grads_ref[1])
    top = slot_ref[0] + inner[:rows] + mm(wb_ref[pl.ds(2 * rows, rows)], grads_ref[0])
    second = slot_ref[1] + inner[rows:]
    inner = mm(wb_ref[pl.ds(0, 2 * rows)], grads_ref[2])
    third = slot_ref[2] + inner[:rows]
    bottom = slot_ref[3] + inner[rows:] + mm(wb_ref[pl.ds(0, rows)], grads_ref[3])
    at = (0, 1, cy - 2, cy - 1)
    found = []
    for dx, cells_ref in enumerate((west_cells, own_cells, east_cells)):
        parts = [value[dx * chans : (dx + 1) * chans] for value in (top, second, third, bottom)]
        if dx == 1:
            parts = [value + cot_ref[n].astype(F32) for value, n in zip(parts, at)]
        parts = [value.astype(BF16) for value in parts]
        terms = jnp.concatenate([plane_ref[dx], *parts], axis=0)
        y, _ = place(cells_ref, nz)
        found.append(at_slots(terms, y, hot_ref[dx], (*range(2, cy - 2), *at)))
    sides = jnp.concatenate([found[0], found[2]], axis=0).T
    middle = jnp.concatenate([found[1], jnp.zeros_like(found[1])], axis=0).T
    width = recv_ref.shape[1]
    back = [sides.reshape(ndev, cap, width), middle.reshape(ndev, cap, width)]
    slots_ref[...] = jnp.concatenate(back, axis=1).astype(BF16)
    raws = rows_in(recv_ref, ndev, cap)
    proj = sum(mm(found[dx].astype(BF16), raws[dx]) for dx in range(3))
    rest = ndev - full
    pad = jnp.zeros((rest * part - chans, width), F32)
    proj = jnp.concatenate([proj, pad], axis=0).reshape(rest, part, width)
    proj_ref[...] = proj.astype(BF16)


def pair_kernel(keep_ref, got_ref, slots_ref, proj_ref, send_ref):
    full, part, _ = keep_ref.shape
    ndev, back, _ = slots_ref.shape
    send_ref[:, pl.ds(part, back)] = slots_ref[...]
    send_ref[pl.ds(full, ndev - full), pl.ds(0, part)] = proj_ref[...]
    sums = keep_ref[...] + got_ref[...].astype(F32)
    send_ref[pl.ds(0, full), pl.ds(0, part)] = sums.astype(BF16)


def sums_kernel(ngx, ngy, full, cap, recv_ref, index_ref, sums_ref):
    ndev, each, width = recv_ref.shape
    part = each - 2 * cap
    terms = recv_ref[:, pl.ds(0, part)].astype(F32).reshape(ngx // 2, 2, ngy, part, width)
    sums = jnp.sum(terms, axis=(0, 2))
    whole = sums[0] + sums[1]
    high = whole.astype(BF16).astype(F32)
    last = jnp.broadcast_to(index_ref[...], whole.shape) >= full
    sums = [
        jnp.where(last, high, sums[0]).astype(BF16),
        jnp.where(last, whole - high, sums[1]).astype(BF16),
    ]
    for n in range(ndev):
        sums_ref[n] = sums[(n // ngy) % 2]


def rows_kernel(
    ngx, ngy, cap, chans, recv_ref, counts_ref, proj_t_ref, inner_ref, ends_ref, rows_ref, out_ref
):
    ndev = ngx * ngy
    nrows = rows_ref.shape[0]
    width = recv_ref.shape[2]
    slots = ndev * cap
    share = recv_ref.shape[1] - 2 * cap
    arrived = recv_ref[:, pl.ds(share, 2 * cap)].astype(F32)
    sides = arrived[:, :cap].reshape(ngx, ngy, cap, width)
    left = lax.broadcasted_iota(I32, sides.shape, 3) < chans
    sides = jnp.where(left, rolled(sides, 1, 0), rolled(sides, -1, 0)).reshape(slots, width)
    middle = arrived[:, cap:].reshape(slots, width)
    counts = counts_ref[...].astype(F32)
    place = lax.broadcasted_iota(I32, (nrows, ndev), 0).astype(F32)
    lane = lax.broadcasted_iota(I32, (ndev, ndev), 1)
    upto = lax.broadcasted_iota(I32, (ndev, ndev), 0) <= lane
    ends = mm(counts.astype(BF16), jnp.where(upto, 1.0, 0.0).astype(BF16))
    before = ends <= place
    owner = jnp.sum(jnp.where(before, 1.0, 0.0), axis=1, keepdims=True)
    start = jnp.sum(jnp.where(before, counts, 0.0), axis=1, keepdims=True)
    slot = owner * cap + place[:, :1] - start
    onehot = jnp.where(
        lax.broadcasted_iota(I32, (nrows, slots), 1).astype(F32) == slot, 1.0, 0.0
    ).astype(BF16)
    proj_t = proj_t_ref[...]
    both = jnp.concatenate([proj_t, proj_t], axis=0)
    sides = mm(onehot, sides.astype(BF16)).astype(BF16)
    middle = mm(onehot, middle.astype(BF16)).astype(BF16)
    rows_ref[...] = mm(sides, both) + mm(middle, both)
    cy = inner_ref.shape[0]
    field = jnp.concatenate([ends_ref[:1], inner_ref[1 : cy - 1], ends_ref[1:]], axis=0)
    out_ref[...] = jnp.swapaxes(field, 0, 1)


def finish_kernel(conv_scale, proj_scale, parity_ref, mine_ref, other_ref, conv_ref, proj_ref, both):
    ndev, part, width = mine_ref.shape
    parity = parity_ref[0]
    both[:, parity] = mine_ref[...]
    both[:, 1 - parity] = other_ref[...]
    sums = both[...].astype(F32).reshape(ndev * 2 * part, width)
    taps, chans, _ = conv_ref.shape
    rows = 9 * chans
    half = rows // 2
    packed = sums[rows : rows + half]
    column = jnp.concatenate([packed[:, :chans], packed[:, chans:]], axis=0)
    for b in range(3):
        for dz in range(3):
            first = (b * 3 + dz) * chans
            block = sums[first : first + chans]
            k = (2 - b) * 3 + dz
            conv_ref[k] = block[:, :chans] * conv_scale
            conv_ref[9 + k] = block[:, chans:] * conv_scale
            conv_ref[18 + k] = column[first : first + chans] * conv_scale
    terms = sums[rows + half : rows + half + 2 * chans].reshape(chans // part, 2, part, width)
    proj_ref[...] = jnp.sum(terms, axis=1).reshape(chans, width) * proj_scale


def local(particles, send_counts, cell_lists, base_field, proj_weight, conv_weight, cotangent):
    ngx, ngy = lax.axis_size("gx"), lax.axis_size("gy")
    ndev = ngx * ngy
    nrows, feats = particles.shape
    chans, cx, cy, nz = base_field.shape
    slots = cell_lists.shape[1]
    cap = slots // ndev
    count = cx * cy * nz
    assert cx == 1 and feats == 2 * chans
    proj_t = proj_weight.T
    move = functools.partial(send, ngx=ngx, ngy=ngy)
    rows = 3 * chans
    one = 2 * rows * rows * nz

    base = base_field.reshape(chans, cy, nz)
    west, east = move(base_field, 1, 0), move(base_field, -1, 0)
    planes = (base, west.reshape(base.shape), east.reshape(base.shape))
    lists = (cell_lists, move(cell_lists, 1, 0), move(cell_lists, -1, 0))
    (payload,) = call(
        functools.partial(first_kernel, ngx, ngy, cap),
        [shape((ndev * 3 * cap, feats), BF16)],
        (particles, send_counts),
        2 * slots * nrows * feats,
        (
            pltpu.VMEM(particles.shape, BF16),
            pltpu.VMEM(send_counts.shape, I32),
            pltpu.SemaphoreType.DMA((2,)),
        ),
        far=range(2),
        limit=ALL,
    )
    recv = exchange(payload, ndev)

    wf, wb, cot = call(
        turns_kernel,
        [shape((9 * chans, rows), BF16)] * 2 + [shape((cy, chans, nz), BF16)],
        (conv_weight, cotangent.reshape(chans, cy, nz)),
        1000,
    )

    first, last, values, hots = call(
        functools.partial(outer_kernel, ndev, cap),
        [shape((rows, nz), BF16)] * 2
        + [shape((3, chans, slots), BF16), shape((3, nz, slots), BF16)],
        (recv, *planes, *lists, proj_t, cot, wf),
        4 * one,
        (pltpu.VMEM((4 * chans, slots), BF16), pltpu.VMEM((4, rows, nz), BF16)),
    )
    south, north = move(first, 0, -1), move(last, 0, 1)
    x_all, out_rows, total, pre_edge, slot_edge, plane = call(
        conv_kernel,
        [
            shape((cy, rows, nz), BF16),
            shape((cy, chans, nz), BF16),
            shape((9 * chans, rows), F32),
            shape((4, chans, nz), F32),
            shape((4, rows, nz), F32),
            shape((3, (cy - 4) * chans, nz), BF16),
        ],
        (values, hots, *planes, *lists, cot, wf, wb),
        3 * cy * 3 * one,
        (
            pltpu.VMEM((cy + 1, rows, nz), F32),
            pltpu.VMEM((cy + 2, rows, nz), BF16),
            pltpu.VMEM((cy, rows, nz), F32),
            pltpu.VMEM((cy * chans, slots), BF16),
        ),
    )
    grad_rows = 27 * chans * chans // feats
    part = -(-(grad_rows + 2 * chans) // (32 * ndev)) * 16
    full = grad_rows // (2 * part)
    assert ngx % 2 == 0 and full * 2 * part == grad_rows
    row = lax.axis_index("gx")
    parity = (row % 2).astype(I32).reshape(1)
    out_edge, grads, keep, give = call(
        functools.partial(edge_kernel, part),
        [
            shape((2, chans, nz), BF16),
            shape((4, rows, nz), BF16),
            shape((full, part, feats), F32),
            shape((full, part, feats), BF16),
        ],
        (parity, pre_edge, total, north, south, x_all, cot),
        6 * one,
        (pltpu.VMEM((9 * chans, rows), F32), pltpu.VMEM((full, 2, part, feats), F32)),
        scalar=(0,),
    )
    got = swap(give)
    back, proj = call(
        functools.partial(slots_kernel, ndev, cap, part, full),
        [shape((ndev, 2 * cap, feats), BF16), shape((ndev - full, part, feats), BF16)],
        (slot_edge, plane, hots, grads, wb, cot, *lists, recv),
        6 * one,
    )
    (payload,) = call(
        pair_kernel,
        [shape((ndev, part + 2 * cap, feats), BF16)],
        (keep, got, back, proj),
        1000,
    )
    (payload,) = call(same_kernel, [payload], (payload,), 0, far=(0,), far_out=(0,), aliases={0: 0})
    recv = exchange(payload.reshape(-1, feats), ndev).reshape(payload.shape)
    index = (row * ngy + lax.axis_index("gy")).astype(I32).reshape(1, 1)
    (sums,) = call(
        functools.partial(sums_kernel, ngx, ngy, full, cap),
        [shape((ndev, part, feats), BF16)],
        (recv, index),
        1000,
    )
    row_grads, out_field = call(
        functools.partial(rows_kernel, ngx, ngy, cap, chans),
        [shape((nrows, feats), F32), shape((chans, cy, nz), BF16)],
        (recv, send_counts, proj_t, out_rows, out_edge),
        2 * nrows * slots * chans,
    )
    mine = exchange(sums.reshape(-1, feats), ndev).reshape(sums.shape)
    mine, row_grads, out_field = lax.optimization_barrier((mine, row_grads, out_field))
    other = swap(mine)
    conv_grad, proj_grad = call(
        functools.partial(
            finish_kernel, 1.0 / math.sqrt(count * ndev), 1.0 / math.sqrt(nrows * ndev)
        ),
        [shape((27, chans, chans), F32), shape((chans, feats), F32)],
        (parity, mine, other),
        1000,
        (pltpu.VMEM((ndev, 2, part, feats), BF16),),
        scalar=(0,),
    )
    return (out_field[:, None], row_grads, conv_grad, proj_grad.T)


def solution(mesh):
    in_specs = (
        P(("gx", "gy"), None),
        P(("gx", "gy"), None),
        P(("gx", "gy"), None),
        P(None, "gx", "gy", None),
        P(),
        P(),
        P(None, "gx", "gy", None),
    )
    out_specs = (P(None, "gx", "gy", None), P(("gx", "gy"), None), P(), P())
    return jax.shard_map(local, mesh=mesh, in_specs=in_specs, out_specs=out_specs, check_vma=False)
```

```python
import functools
import math

import jax
import jax.numpy as jnp
from jax import lax
from jax.experimental import pallas as pl
from jax.experimental.pallas import tpu as pltpu
from jax.sharding import PartitionSpec as P

AXES = ("gx", "gy")
F32, BF16, I32 = jnp.float32, jnp.bfloat16, jnp.int32
LIMIT = 40 * 1024 * 1024
ALL = 60 * 1024 * 1024
NT = (((1,), (1,)), ((), ()))
NN = (((1,), (0,)), ((), ()))


def mm(a, b, dims=NN):
    return lax.dot_general(a, b, dims, preferred_element_type=F32)


def call(kernel, outs, args, flops, scratch=(), far=(), far_out=(), aliases=None, limit=LIMIT, scalar=()):
    traffic = sum(math.prod(a.shape) * a.dtype.itemsize for a in (*args, *outs))
    near = pl.BlockSpec(memory_space=pltpu.VMEM)
    there = pl.BlockSpec(memory_space=pltpu.HBM)
    return pl.pallas_call(
        kernel,
        out_shape=[jax.ShapeDtypeStruct(o.shape, o.dtype) for o in outs],
        in_specs=[
            pl.BlockSpec(memory_space=pltpu.SMEM) if n in scalar else there if n in far else near
            for n in range(len(args))
        ],
        out_specs=[there if n in far_out else near for n in range(len(outs))],
        scratch_shapes=list(scratch),
        input_output_aliases=aliases or {},
        compiler_params=pltpu.CompilerParams(vmem_limit_bytes=limit),
        cost_estimate=pl.CostEstimate(flops=flops, bytes_accessed=traffic, transcendentals=0),
    )(*args)


def shape(dims, dtype):
    return jax.ShapeDtypeStruct(dims, dtype)


def send(block, di, dj, ngx, ngy):
    pairs = []
    for i in range(ngx):
        for j in range(ngy):
            pairs.append((i * ngy + j, ((i + di) % ngx) * ngy + (j + dj) % ngy))
    return lax.ppermute(block, AXES, pairs)


def swap(block):
    return lax.ppermute(block, "gx", [(i, i ^ 1) for i in range(lax.axis_size("gx"))])


def exchange(payload, ndev):
    rows, width = payload.shape
    moved = lax.all_to_all(
        payload.reshape(ndev, rows // ndev, width), AXES, split_axis=0, concat_axis=0, tiled=True
    )
    return moved.reshape(rows, width)


def rolled(x, di, dj):
    for axis, shift in ((0, di), (1, dj)):
        if shift == 1:
            head, tail = lax.slice_in_dim(x, 1, None, axis=axis), lax.slice_in_dim(x, 0, 1, axis=axis)
            x = jnp.concatenate([head, tail], axis=axis)
        elif shift == -1:
            count = x.shape[axis]
            head = lax.slice_in_dim(x, count - 1, count, axis=axis)
            x = jnp.concatenate([head, lax.slice_in_dim(x, 0, count - 1, axis=axis)], axis=axis)
    return x


def picked_depth(z, nz):
    depth = lax.broadcasted_iota(I32, (nz, z.shape[1]), 0)
    return jnp.where(depth == z, 1.0, 0.0).astype(BF16)


def rows_in(recv_ref, ndev, cap):
    width = recv_ref.shape[1]
    arrived = recv_ref[...].astype(F32).reshape(ndev, 3, cap, width)
    return [arrived[:, n].reshape(ndev * cap, width).astype(BF16) for n in range(3)]


def stacked(grad):
    nz = grad.shape[1]
    wide = grad.astype(F32)
    return jnp.concatenate(
        [pltpu.roll(wide, nz - 1, 1), wide, pltpu.roll(wide, 1, 1)], axis=0
    ).astype(BF16)


def over_depth(acc):
    chans, nz = acc.shape[0] // 3, acc.shape[1]
    total = acc[chans : 2 * chans] + pltpu.roll(acc[:chans], 1, 1)
    return total + pltpu.roll(acc[2 * chans :], nz - 1, 1)


def finish_row(pre, field, cot):
    sig = jax.nn.sigmoid(pre)
    out = field.astype(F32) + pre * sig
    grad = cot.astype(F32) * sig * (1.0 + pre * (1.0 - sig))
    return out.astype(BF16), grad.astype(BF16)


def first_kernel(
    ngx, ngy, cap, rows_far, counts_far, send_ref, rows_ref, counts_ref, sems
):
    copies = [
        pltpu.make_async_copy(rows_far, rows_ref, sems.at[0]),
        pltpu.make_async_copy(counts_far, counts_ref, sems.at[1]),
    ]
    for copy in copies:
        copy.start()
    copies[1].wait()
    pick(ngx, ngy, cap, counts_ref, rows_ref, send_ref, copies[0])


def turns_kernel(weight_ref, cot_ref, wf_ref, wb_ref, cot_out):
    cot_out[...] = jnp.swapaxes(cot_ref[...], 0, 1)
    chans = cot_ref.shape[0]
    three = range(3)
    for dy in three:
        for n in three:
            rows = pl.ds((dy * 3 + n) * chans, chans)
            taps = [weight_ref[dx * 9 + dy * 3 + n] for dx in three]
            wf_ref[rows] = jnp.concatenate(taps, axis=1)
            taps = [weight_ref[n * 9 + dy * 3 + dz].astype(F32).T for dz in three]
            wb_ref[rows] = jnp.concatenate(taps, axis=1).astype(BF16)


def same_kernel(in_ref, out_ref):
    pass


def pick(ngx, ngy, cap, counts_ref, rows_ref, out_ref, rows_copy):
    ndev = ngx * ngy
    nrows, feats = rows_ref.shape
    slots = ndev * cap
    counts = counts_ref[...].astype(F32)
    owner = lax.broadcasted_iota(I32, (ndev, cap, ndev), 0).reshape(slots, ndev)
    lane = lax.broadcasted_iota(I32, (slots, ndev), 1)
    start = jnp.sum(jnp.where(lane < owner, counts, 0.0), axis=1, keepdims=True)
    held = jnp.sum(jnp.where(lane == owner, counts, 0.0), axis=1, keepdims=True)
    place = lax.broadcasted_iota(I32, (ndev, cap, nrows), 1).reshape(slots, nrows).astype(F32)
    row = lax.broadcasted_iota(I32, (slots, nrows), 1).astype(F32)
    onehot = jnp.where((row == place + start) & (place < held), 1.0, 0.0).astype(BF16)
    rows_copy.wait()
    raw = mm(onehot, rows_ref[...]).reshape(ngx, ngy, cap, feats)
    parts = [rolled(raw, dx, 0).reshape(ndev, cap, feats) for dx in (-1, 0, 1)]
    out_ref[...] = jnp.stack(parts, axis=1).reshape(out_ref.shape).astype(BF16)


def painted_rows(values, y, onehot, ns, masked):
    chans = values.shape[0]
    for n, row in enumerate(ns):
        masked[pl.ds(n * chans, chans)] = values * jnp.where(y == row, 1.0, 0.0).astype(BF16)
    return mm(masked[pl.ds(0, len(ns) * chans)], onehot, NT)


def add_to_rows(near, far, cot, back, out_ref):
    chans = cot.shape[0]
    rows = 3 * chans
    at, over = (rows, 0) if back else (0, rows)
    out_ref[pl.ds(0, chans)] = over_depth(near[at : at + rows]).astype(BF16)
    out_ref[pl.ds(chans, chans)] = over_depth(near[over : over + rows] + far).astype(BF16)
    out_ref[pl.ds(2 * chans, chans)] = cot


def outer_kernel(
    ndev, cap, recv_ref, own_ref, west_ref, east_ref, own_cells, west_cells, east_cells,
    proj_t_ref, cot_ref, wf_ref, first_ref, last_ref, values_ref, hot_ref, masked, field,
):
    chans, cy, nz = own_ref.shape
    rows = 3 * chans
    raws = rows_in(recv_ref, ndev, cap)
    ns = (0, 1, cy - 2, cy - 1)
    planes = ((west_ref, west_cells), (own_ref, own_cells), (east_ref, east_cells))
    for dx, (ref, cells_ref) in enumerate(planes):
        values = mm(proj_t_ref[...], raws[dx], NT).astype(BF16)
        y, z = place(cells_ref, nz)
        onehot = picked_depth(z, nz)
        values_ref[dx] = values
        hot_ref[dx] = onehot
        painted = painted_rows(values, y, onehot, ns, masked)
        base = turned(ref)
        for n, row in enumerate(ns):
            part = painted[n * chans : (n + 1) * chans]
            field[n, pl.ds(dx * chans, chans)] = (base[row] + part).astype(BF16)
    near = mm(wf_ref[pl.ds(0, 2 * rows)], field[3])
    add_to_rows(near, mm(wf_ref[pl.ds(0, rows)], field[2]), cot_ref[cy - 1], False, last_ref)
    near = mm(wf_ref[pl.ds(rows, 2 * rows)], field[0])
    add_to_rows(near, mm(wf_ref[pl.ds(2 * rows, rows)], field[1]), cot_ref[0], True, first_ref)


def place(cells_ref, nz):
    cells = cells_ref[...]
    return cells // nz, cells % nz


def turned(ref):
    return jnp.swapaxes(ref[...], 0, 1).astype(F32)


def conv_kernel(
    values_ref, hot_ref, own_ref, west_ref, east_ref, own_cells, west_cells, east_cells,
    cot_ref, wf_ref, wb_ref,
    x_ref, out_ref, total_ref, pre_ref, slot_ref, plane, acc, grads, back, masked,
):
    cy, chans, nz = cot_ref.shape
    rows = 3 * chans
    planes = ((west_ref, west_cells), (own_ref, own_cells), (east_ref, east_cells))
    for dx, (ref, cells_ref) in enumerate(planes):
        y, _ = place(cells_ref, nz)
        painted = painted_rows(values_ref[dx], y, hot_ref[dx], range(cy), masked)
        field = turned(ref) + painted.reshape(cy, chans, nz)
        x_ref[:, pl.ds(dx * chans, chans)] = field.astype(BF16)
    own = pl.ds(chans, chans)
    zeros = jnp.zeros((rows, nz), BF16)
    for t in (0, 1, cy, cy + 1):
        grads[t] = zeros
    out_ref[0] = zeros[:chans]
    out_ref[cy - 1] = zeros[:chans]
    acc[0] = jnp.zeros((rows, nz), F32)

    def spread(n):
        terms = mm(wf_ref[...], x_ref[n])
        acc[n + 1] = terms[:rows]
        acc[n] += terms[rows : 2 * rows]
        return terms[2 * rows :]

    pre_ref[0] = over_depth(spread(0))
    pre_ref[1] = over_depth(acc[0] + spread(1))

    def forward(n):
        done = spread(n) + acc[n - 1]
        y = n - 1
        out, grad = finish_row(over_depth(done), x_ref[y, own], cot_ref[y])
        out_ref[y] = out
        grads[y + 1] = stacked(grad)

    for n in range(2, cy):
        forward(n)
    pre_ref[2] = over_depth(acc[cy - 1])
    pre_ref[3] = over_depth(acc[cy])
    total_ref[...] = jnp.zeros_like(total_ref)
    back[0] = jnp.zeros((rows, nz), F32)
    back[1] = jnp.zeros((rows, nz), F32)

    def taps(n):
        window = grads[pl.ds(n, 3)].reshape(3 * rows, nz)
        total_ref[...] += mm(window, x_ref[n], NT)

    def spread_back(n):
        terms = mm(wb_ref[...], grads[n + 1])
        back[n + 1] = terms[2 * rows :]
        back[n] += terms[rows : 2 * rows]
        return terms[:rows]

    def backward(n):
        taps(n)
        value = spread_back(n) + back[n - 1]
        for dx in range(3):
            part = value[dx * chans : (dx + 1) * chans]
            if dx == 1:
                part = part + cot_ref[n - 1].astype(F32)
            plane[dx, pl.ds((n - 3) * chans, chans)] = part.astype(BF16)

    taps(0)
    taps(1)
    slot_ref[0] = spread_back(1)
    taps(2)
    slot_ref[1] = spread_back(2) + back[1]
    for n in range(3, cy - 1):
        backward(n)
    taps(cy - 1)
    slot_ref[2] = back[cy - 2]
    slot_ref[3] = back[cy - 1]


def at_slots(part, y, onehot, first):
    found = mm(part, onehot)
    chans = found.shape[0] // len(first)
    total = jnp.zeros((chans, found.shape[1]), F32)
    for n, row in enumerate(first):
        total = total + jnp.where(y == row, found[n * chans : (n + 1) * chans], 0.0)
    return total


def edge_kernel(
    part, parity_ref, pre_ref, total_ref, south_ref, north_ref, x_ref, cot_ref,
    out_ref, grads_ref, keep_ref, give_ref, total, sums,
):
    cy, chans, nz = cot_ref.shape
    rows = 3 * chans
    own = pl.ds(chans, chans)
    last = pl.ds(2 * chans, chans)
    cots = (north_ref[last], cot_ref[0], cot_ref[cy - 1], south_ref[last])
    sides = ((north_ref, 1), (north_ref, 0), (south_ref, 0), (south_ref, 1))
    ends = []
    for n, (ref, at) in enumerate(sides):
        pre = pre_ref[n] + ref[pl.ds(at * chans, chans)].astype(F32)
        ends.append(finish_row(pre, x_ref[0 if n < 2 else cy - 1, own], cots[n]))
    out_ref[0], out_ref[1] = ends[1][0], ends[2][0]
    grads = [stacked(grad) for _, grad in ends]
    for n in range(4):
        grads_ref[n] = grads[n]
    top = mm(jnp.concatenate([grads[0], grads[1]], axis=0), x_ref[0], NT)
    bottom = mm(jnp.concatenate([grads[2], grads[3]], axis=0), x_ref[cy - 1], NT)
    here = [pl.ds(n * rows, rows) for n in range(3)]
    total[here[0]] = total_ref[here[0]] + (top[:rows] + mm(grads[1], x_ref[1], NT))
    total[here[1]] = total_ref[here[1]] + (top[rows:] + bottom[:rows])
    total[here[2]] = total_ref[here[2]] + (bottom[rows:] + mm(grads[2], x_ref[cy - 2], NT))
    full, _, width = keep_ref.shape
    half = 3 * rows // 2
    split = 3 * rows // (2 * part)
    sums[pl.ds(0, split)] = total[:, :width].reshape(split, 2, part, width)
    taps = jnp.concatenate([total[pl.ds(0, half), width:], total[pl.ds(half, half), width:]], axis=1)
    sums[pl.ds(split, full - split)] = taps.reshape(full - split, 2, part, width)
    parity = parity_ref[0]
    keep_ref[...] = sums[:, parity]
    give_ref[...] = sums[:, 1 - parity].astype(BF16)


def slots_kernel(
    ndev, cap, part, full, slot_ref, plane_ref, hot_ref, grads_ref, wb_ref, cot_ref,
    own_cells, west_cells, east_cells, recv_ref, slots_ref, proj_ref,
):
    cy, chans, nz = cot_ref.shape
    rows = 3 * chans
    inner = mm(wb_ref[pl.ds(rows, 2 * rows)], grads_ref[1])
    top = slot_ref[0] + inner[:rows] + mm(wb_ref[pl.ds(2 * rows, rows)], grads_ref[0])
    second = slot_ref[1] + inner[rows:]
    inner = mm(wb_ref[pl.ds(0, 2 * rows)], grads_ref[2])
    third = slot_ref[2] + inner[:rows]
    bottom = slot_ref[3] + inner[rows:] + mm(wb_ref[pl.ds(0, rows)], grads_ref[3])
    at = (0, 1, cy - 2, cy - 1)
    found = []
    for dx, cells_ref in enumerate((west_cells, own_cells, east_cells)):
        parts = [value[dx * chans : (dx + 1) * chans] for value in (top, second, third, bottom)]
        if dx == 1:
            parts = [value + cot_ref[n].astype(F32) for value, n in zip(parts, at)]
        parts = [value.astype(BF16) for value in parts]
        terms = jnp.concatenate([plane_ref[dx], *parts], axis=0)
        y, _ = place(cells_ref, nz)
        found.append(at_slots(terms, y, hot_ref[dx], (*range(2, cy - 2), *at)))
    sides = jnp.concatenate([found[0], found[2]], axis=0).T
    middle = jnp.concatenate([found[1], jnp.zeros_like(found[1])], axis=0).T
    width = recv_ref.shape[1]
    back = [sides.reshape(ndev, cap, width), middle.reshape(ndev, cap, width)]
    slots_ref[...] = jnp.concatenate(back, axis=1).astype(BF16)
    raws = rows_in(recv_ref, ndev, cap)
    proj = sum(mm(found[dx].astype(BF16), raws[dx]) for dx in range(3))
    rest = ndev - full
    pad = jnp.zeros((rest * part - chans, width), F32)
    proj = jnp.concatenate([proj, pad], axis=0).reshape(rest, part, width)
    proj_ref[...] = proj.astype(BF16)


def pair_kernel(keep_ref, got_ref, slots_ref, proj_ref, send_far, sums_send, sems):
    full, part, _ = keep_ref.shape
    ndev, back, _ = slots_ref.shape
    pieces = (
        (slots_ref, send_far.at[:, pl.ds(part, back)]),
        (proj_ref, send_far.at[pl.ds(full, ndev - full), pl.ds(0, part)]),
        (sums_send, send_far.at[pl.ds(0, full), pl.ds(0, part)]),
    )
    copies = [pltpu.make_async_copy(src, dst, sems.at[n]) for n, (src, dst) in enumerate(pieces)]
    copies[0].start()
    copies[1].start()
    sums_send[...] = (keep_ref[...] + got_ref[...].astype(F32)).astype(BF16)
    copies[2].start()
    for copy in copies:
        copy.wait()


def sums_kernel(ngx, ngy, full, cap, recv_ref, index_ref, sums_ref):
    ndev, each, width = recv_ref.shape
    part = each - 2 * cap
    terms = recv_ref[:, pl.ds(0, part)].astype(F32).reshape(ngx // 2, 2, ngy, part, width)
    sums = jnp.sum(terms, axis=(0, 2))
    whole = sums[0] + sums[1]
    high = whole.astype(BF16).astype(F32)
    last = jnp.broadcast_to(index_ref[...], whole.shape) >= full
    sums = [
        jnp.where(last, high, sums[0]).astype(BF16),
        jnp.where(last, whole - high, sums[1]).astype(BF16),
    ]
    for n in range(ndev):
        sums_ref[n] = sums[(n // ngy) % 2]


def rows_kernel(
    ngx, ngy, cap, chans, recv_ref, counts_ref, proj_t_ref, inner_ref, ends_ref, rows_ref, out_ref
):
    ndev = ngx * ngy
    nrows = rows_ref.shape[0]
    width = recv_ref.shape[2]
    slots = ndev * cap
    share = recv_ref.shape[1] - 2 * cap
    arrived = recv_ref[:, pl.ds(share, 2 * cap)].astype(F32)
    sides = arrived[:, :cap].reshape(ngx, ngy, cap, width)
    left = lax.broadcasted_iota(I32, sides.shape, 3) < chans
    sides = jnp.where(left, rolled(sides, 1, 0), rolled(sides, -1, 0)).reshape(slots, width)
    middle = arrived[:, cap:].reshape(slots, width)
    counts = counts_ref[...].astype(F32)
    place = lax.broadcasted_iota(I32, (nrows, ndev), 0).astype(F32)
    lane = lax.broadcasted_iota(I32, (ndev, ndev), 1)
    upto = lax.broadcasted_iota(I32, (ndev, ndev), 0) <= lane
    ends = mm(counts.astype(BF16), jnp.where(upto, 1.0, 0.0).astype(BF16))
    before = ends <= place
    owner = jnp.sum(jnp.where(before, 1.0, 0.0), axis=1, keepdims=True)
    start = jnp.sum(jnp.where(before, counts, 0.0), axis=1, keepdims=True)
    slot = owner * cap + place[:, :1] - start
    onehot = jnp.where(
        lax.broadcasted_iota(I32, (nrows, slots), 1).astype(F32) == slot, 1.0, 0.0
    ).astype(BF16)
    proj_t = proj_t_ref[...]
    both = jnp.concatenate([proj_t, proj_t], axis=0)
    sides = mm(onehot, sides.astype(BF16)).astype(BF16)
    middle = mm(onehot, middle.astype(BF16)).astype(BF16)
    rows_ref[...] = mm(sides, both) + mm(middle, both)
    cy = inner_ref.shape[0]
    field = jnp.concatenate([ends_ref[:1], inner_ref[1 : cy - 1], ends_ref[1:]], axis=0)
    out_ref[...] = jnp.swapaxes(field, 0, 1)


def finish_kernel(conv_scale, proj_scale, parity_ref, mine_ref, other_ref, conv_ref, proj_ref, both):
    ndev, part, width = mine_ref.shape
    parity = parity_ref[0]
    both[:, parity] = mine_ref[...]
    both[:, 1 - parity] = other_ref[...]
    sums = both[...].astype(F32).reshape(ndev * 2 * part, width)
    taps, chans, _ = conv_ref.shape
    rows = 9 * chans
    half = rows // 2
    packed = sums[rows : rows + half]
    column = jnp.concatenate([packed[:, :chans], packed[:, chans:]], axis=0)
    for b in range(3):
        for dz in range(3):
            first = (b * 3 + dz) * chans
            block = sums[first : first + chans]
            k = (2 - b) * 3 + dz
            conv_ref[k] = block[:, :chans] * conv_scale
            conv_ref[9 + k] = block[:, chans:] * conv_scale
            conv_ref[18 + k] = column[first : first + chans] * conv_scale
    terms = sums[rows + half : rows + half + 2 * chans].reshape(chans // part, 2, part, width)
    proj_ref[...] = jnp.sum(terms, axis=1).reshape(chans, width) * proj_scale


def local(particles, send_counts, cell_lists, base_field, proj_weight, conv_weight, cotangent):
    ngx, ngy = lax.axis_size("gx"), lax.axis_size("gy")
    ndev = ngx * ngy
    nrows, feats = particles.shape
    chans, cx, cy, nz = base_field.shape
    slots = cell_lists.shape[1]
    cap = slots // ndev
    count = cx * cy * nz
    assert cx == 1 and feats == 2 * chans
    proj_t = proj_weight.T
    move = functools.partial(send, ngx=ngx, ngy=ngy)
    rows = 3 * chans
    one = 2 * rows * rows * nz

    base = base_field.reshape(chans, cy, nz)
    west, east = move(base_field, 1, 0), move(base_field, -1, 0)
    planes = (base, west.reshape(base.shape), east.reshape(base.shape))
    lists = (cell_lists, move(cell_lists, 1, 0), move(cell_lists, -1, 0))
    (payload,) = call(
        functools.partial(first_kernel, ngx, ngy, cap),
        [shape((ndev * 3 * cap, feats), BF16)],
        (particles, send_counts),
        2 * slots * nrows * feats,
        (
            pltpu.VMEM(particles.shape, BF16),
            pltpu.VMEM(send_counts.shape, I32),
            pltpu.SemaphoreType.DMA((2,)),
        ),
        far=range(2),
        limit=ALL,
    )
    recv = exchange(payload, ndev)

    wf, wb, cot = call(
        turns_kernel,
        [shape((9 * chans, rows), BF16)] * 2 + [shape((cy, chans, nz), BF16)],
        (conv_weight, cotangent.reshape(chans, cy, nz)),
        1000,
    )

    first, last, values, hots = call(
        functools.partial(outer_kernel, ndev, cap),
        [shape((rows, nz), BF16)] * 2
        + [shape((3, chans, slots), BF16), shape((3, nz, slots), BF16)],
        (recv, *planes, *lists, proj_t, cot, wf),
        4 * one,
        (pltpu.VMEM((4 * chans, slots), BF16), pltpu.VMEM((4, rows, nz), BF16)),
    )
    north, south = move(last, 0, 1), move(first, 0, -1)
    x_all, out_rows, total, pre_edge, slot_edge, plane = call(
        conv_kernel,
        [
            shape((cy, rows, nz), BF16),
            shape((cy, chans, nz), BF16),
            shape((9 * chans, rows), F32),
            shape((4, chans, nz), F32),
            shape((4, rows, nz), F32),
            shape((3, (cy - 4) * chans, nz), BF16),
        ],
        (values, hots, *planes, *lists, cot, wf, wb),
        3 * cy * 3 * one,
        (
            pltpu.VMEM((cy + 1, rows, nz), F32),
            pltpu.VMEM((cy + 2, rows, nz), BF16),
            pltpu.VMEM((cy, rows, nz), F32),
            pltpu.VMEM((cy * chans, slots), BF16),
        ),
    )
    grad_rows = 27 * chans * chans // feats
    part = -(-(grad_rows + 2 * chans) // (32 * ndev)) * 16
    full = grad_rows // (2 * part)
    assert ngx % 2 == 0 and full * 2 * part == grad_rows
    row = lax.axis_index("gx")
    parity = (row % 2).astype(I32).reshape(1)
    out_edge, grads, keep, give = call(
        functools.partial(edge_kernel, part),
        [
            shape((2, chans, nz), BF16),
            shape((4, rows, nz), BF16),
            shape((full, part, feats), F32),
            shape((full, part, feats), BF16),
        ],
        (parity, pre_edge, total, south, north, x_all, cot),
        6 * one,
        (pltpu.VMEM((9 * chans, rows), F32), pltpu.VMEM((full, 2, part, feats), F32)),
        scalar=(0,),
    )
    got = swap(give)
    back, proj = call(
        functools.partial(slots_kernel, ndev, cap, part, full),
        [shape((ndev, 2 * cap, feats), BF16), shape((ndev - full, part, feats), BF16)],
        (slot_edge, plane, hots, grads, wb, cot, *lists, recv),
        6 * one,
    )
    (payload,) = call(
        pair_kernel,
        [shape((ndev, part + 2 * cap, feats), BF16)],
        (keep, got, back, proj),
        1000,
        (pltpu.VMEM((full, part, feats), BF16), pltpu.SemaphoreType.DMA((3,))),
        far_out=(0,),
    )
    (payload,) = call(same_kernel, [payload], (payload,), 0, far=(0,), far_out=(0,), aliases={0: 0})
    recv = exchange(payload.reshape(-1, feats), ndev).reshape(payload.shape)
    index = (row * ngy + lax.axis_index("gy")).astype(I32).reshape(1, 1)
    (sums,) = call(
        functools.partial(sums_kernel, ngx, ngy, full, cap),
        [shape((ndev, part, feats), BF16)],
        (recv, index),
        1000,
    )
    row_grads, out_field = call(
        functools.partial(rows_kernel, ngx, ngy, cap, chans),
        [shape((nrows, feats), F32), shape((chans, cy, nz), BF16)],
        (recv, send_counts, proj_t, out_rows, out_edge),
        2 * nrows * slots * chans,
    )
    mine = exchange(sums.reshape(-1, feats), ndev).reshape(sums.shape)
    mine, row_grads, out_field = lax.optimization_barrier((mine, row_grads, out_field))
    other = swap(mine)
    conv_grad, proj_grad = call(
        functools.partial(
            finish_kernel, 1.0 / math.sqrt(count * ndev), 1.0 / math.sqrt(nrows * ndev)
        ),
        [shape((27, chans, chans), F32), shape((chans, feats), F32)],
        (parity, mine, other),
        1000,
        (pltpu.VMEM((ndev, 2, part, feats), BF16),),
        scalar=(0,),
    )
    return (out_field[:, None], row_grads, conv_grad, proj_grad.T)


def solution(mesh):
    in_specs = (
        P(("gx", "gy"), None),
        P(("gx", "gy"), None),
        P(("gx", "gy"), None),
        P(None, "gx", "gy", None),
        P(),
        P(),
        P(None, "gx", "gy", None),
    )
    out_specs = (P(None, "gx", "gy", None), P(("gx", "gy"), None), P(), P())
    return jax.shard_map(local, mesh=mesh, in_specs=in_specs, out_specs=out_specs, check_vma=False)
```
